32 devices in a mesh: seq: 8 (over z, core), batch: 4 (over y, x).
Axes of the slice: x: 2, y: 2, z: 4, core: 2. Of those that a mesh axis runs over, the one named last changes fastest.
Arguments:
- layer_inputs: bfloat16 [16, 2048, 768], P('batch', 'seq'), may hold values from -6 to 6
- document_openings: int32 [16, 2048], P('batch', 'seq'), may hold values from 0 to 1, as said below
- mixing_lookup_projection: bfloat16 [768, 768], P(('seq', 'batch')), may hold values from -0.21875 to 0.21875
- mixing_payload_projection: bfloat16 [768, 768], P(('seq', 'batch')), may hold values from -0.21875 to 0.21875
- mixing_acceptor_projection: bfloat16 [768, 768], P(('seq', 'batch')), may hold values from -0.21875 to 0.21875
- mixing_result_projection: bfloat16 [768, 768], P(('seq', 'batch')), may hold values from -0.875 to 0.875
- feedforward_lookup_projection: bfloat16 [768, 3072], P(('seq', 'batch')), may hold values from -0.21875 to 0.21875
- feedforward_acceptor_projection: bfloat16 [768, 768], P(('seq', 'batch')), may hold values from -0.21875 to 0.21875
- feedforward_payload_projection: bfloat16 [3072, 768], P(('seq', 'batch')), may hold values from -0.15625 to 0.15625
- premix_layer_scaling: bfloat16 [768], P(('seq', 'batch')), may hold values from 0.25 to 1.75
- premix_layer_offset: bfloat16 [768], P(('seq', 'batch')), may hold values from -3 to 3
- postmix_layer_scaling: bfloat16 [768], P(('seq', 'batch')), may hold values from 0.25 to 1.75
- postmix_layer_offset: bfloat16 [768], P(('seq', 'batch')), may hold values from -3 to 3
- mixing_lookup_blend: bfloat16 [768], P(('seq', 'batch')), may hold values from 0.049804688 to 0.94921875
- mixing_payload_blend: bfloat16 [768], P(('seq', 'batch')), may hold values from 0.049804688 to 0.94921875
- mixing_acceptor_blend: bfloat16 [768], P(('seq', 'batch')), may hold values from 0.049804688 to 0.94921875
- feedforward_lookup_blend: bfloat16 [768], P(('seq', 'batch')), may hold values from 0.049804688 to 0.94921875
- feedforward_acceptor_blend: bfloat16 [768], P(('seq', 'batch')), may hold values from 0.049804688 to 0.94921875
- feature_fading_speed: bfloat16 [768], P(('seq', 'batch')), may hold values from 9.765625e-05 to 0.08, as said below
- present_token_reward: bfloat16 [768], P(('seq', 'batch')), may hold values from -1 to 1
- upstream_adjoint: bfloat16 [16, 2048, 768], P('batch', 'seq'), may hold values from -6 to 6
Outputs:
- block_out: bfloat16 [16, 2048, 768], P('batch', 'seq')
- tokens_grad: float32 [16, 2048, 768], P('batch', 'seq')
- key_weight_grad: float32 [768, 768], P(('seq', 'batch'))
- value_weight_grad: float32 [768, 768], P(('seq', 'batch'))
- gate_weight_grad: float32 [768, 768], P(('seq', 'batch'))
- output_weight_grad: float32 [768, 768], P(('seq', 'batch'))
- expand_weight_grad: float32 [768, 3072], P(('seq', 'batch'))
- select_weight_grad: float32 [768, 768], P(('seq', 'batch'))
- contract_weight_grad: float32 [3072, 768], P(('seq', 'batch'))
- attn_gain_grad: float32 [768], P(('seq', 'batch'))
- attn_bias_grad: float32 [768], P(('seq', 'batch'))
- chan_gain_grad: float32 [768], P(('seq', 'batch'))
- chan_bias_grad: float32 [768], P(('seq', 'batch'))
- key_ratio_grad: float32 [768], P(('seq', 'batch'))
- value_ratio_grad: float32 [768], P(('seq', 'batch'))
- gate_ratio_grad: float32 [768], P(('seq', 'batch'))
- expand_ratio_grad: float32 [768], P(('seq', 'batch'))
- select_ratio_grad: float32 [768], P(('seq', 'batch'))
- decay_rate_grad: float32 [768], P(('seq', 'batch'))
- bonus_term_grad: float32 [768], P(('seq', 'batch'))
The draws below stay inside these ranges and needn't reach their ends.
Inputs may be any that keep to these rules, and one draw needn't show every extreme that they name: `document_openings`: 1 marks a token that begins a document; in each aligned group of 4 sequences one sequence, drawn from the seed, holds no 1 at all. `feature_fading_speed`: positive per-channel rates.
All inputs are finite; a program needn't handle non-finite values.
Results may differ from the reference program's by a relative error of at most 0.013.
Values may be sent and summed in bfloat16 or wider, within the bound.
A program may use at most 256 MiB of HBM per device.

```python
import jax
import jax.numpy as jnp
from jax import lax

EMBED_DIMENSION = 768
FF = 3072
CH = 256
SEQ_DEV = 4
LEN = 2048
SEQS = 16


def draw_feature_fading_speed(key, part):
    key = jax.random.fold_in(key, 7)
    spread = jax.random.fold_in(key, 1)
    unit = jax.random.uniform(spread, (EMBED_DIMENSION,), jnp.float32)
    lowest = jnp.log(0.5 / LEN)
    return jnp.exp(lowest + unit * (jnp.log(0.08) - lowest)).astype(jnp.bfloat16)


def draw_document_openings(key, part):
    key = jax.random.fold_in(key, 13)
    first_key, second_key = jax.random.split(key)
    marks = jax.random.randint(first_key, (SEQS, LEN), 0, 2 * CH)
    chosen = jax.random.randint(second_key, (SEQS // SEQ_DEV,), 0, SEQ_DEV)
    unbroken = jnp.repeat(chosen, SEQ_DEV) == jnp.arange(SEQS) % SEQ_DEV
    return jnp.where(unbroken[:, None] | (marks != 0), 0, 1).astype(jnp.int32)


def level_of(own_key, shape, cuts, least, largest):
    factor_of, own = 1.0, jax.random.fold_in(own_key, 6)
    for position, shards_of in cuts:
        heights = jnp.exp(jax.random.uniform(jax.random.fold_in(own, position), (shards_of,), jnp.float32, least / len(cuts), largest / len(cuts)))
        factor_of = factor_of * jnp.repeat(heights, shape[position] // shards_of).reshape([-1 if axis == position else 1 for axis in range(len(shape))])
    return factor_of


def normal_values(key, extent, scale, reach, shards=(), dtype=jnp.bfloat16):
    array = jax.random.normal(key, extent, jnp.float32) * scale
    if len(shards) > 0:
        array = level_of(key, extent, shards, -0.22, 0.18) * array
    return jnp.clip(array, min=-reach, max=reach).astype(dtype)


def setup_inputs(seed: int = 0) -> dict:
    key_list = jax.random.split(jax.random.key(seed), 22)
    layer_inputs = normal_values(key_list[0], (SEQS, LEN, EMBED_DIMENSION), 1.0, 6.0, ((0, 4), (1, 8)))
    document_openings = draw_document_openings(jax.random.fold_in(key_list[21], 71), 0)
    mixing_lookup_projection = normal_values(key_list[2], (EMBED_DIMENSION, EMBED_DIMENSION), EMBED_DIMENSION ** -0.5, 0.21875, ((0, 32),))
    mixing_payload_projection = normal_values(key_list[3], (EMBED_DIMENSION, EMBED_DIMENSION), EMBED_DIMENSION ** -0.5, 0.21875, ((0, 32),))
    mixing_acceptor_projection = normal_values(key_list[4], (EMBED_DIMENSION, EMBED_DIMENSION), EMBED_DIMENSION ** -0.5, 0.21875, ((0, 32),))
    mixing_result_projection = normal_values(key_list[5], (EMBED_DIMENSION, EMBED_DIMENSION), (EMBED_DIMENSION // 16) ** -0.5, 0.875, ((0, 32),))
    feedforward_lookup_projection = normal_values(key_list[6], (EMBED_DIMENSION, FF), EMBED_DIMENSION ** -0.5, 0.21875, ((0, 32),))
    feedforward_acceptor_projection = normal_values(key_list[7], (EMBED_DIMENSION, EMBED_DIMENSION), EMBED_DIMENSION ** -0.5, 0.21875, ((0, 32),))
    feedforward_payload_projection = normal_values(key_list[8], (FF, EMBED_DIMENSION), (FF // 2) ** -0.5, 0.15625, ((0, 32),))
    premix_layer_scaling = jnp.clip(1.0 + 0.15 * jax.random.normal(key_list[9], (EMBED_DIMENSION,), jnp.float32), 0.25, 1.75).astype(jnp.bfloat16)
    premix_layer_offset = normal_values(key_list[10], (EMBED_DIMENSION,), 0.3, 3.0, ((0, 32),))
    postmix_layer_scaling = jnp.clip(1.0 + 0.15 * jax.random.normal(key_list[11], (EMBED_DIMENSION,), jnp.float32), 0.25, 1.75).astype(jnp.bfloat16)
    postmix_layer_offset = normal_values(key_list[12], (EMBED_DIMENSION,), 0.3, 3.0, ((0, 32),))
    mixing_lookup_blend = jnp.clip(0.049804688 + 0.89941406 * jax.random.uniform(key_list[13], (EMBED_DIMENSION,), jnp.float32) ** level_of(key_list[13], (EMBED_DIMENSION,), ((0, 32),), -0.2, 0.2), 0.049804688, 0.94921875).astype(jnp.bfloat16)
    mixing_payload_blend = jnp.clip(0.049804688 + 0.89941406 * jax.random.uniform(key_list[14], (EMBED_DIMENSION,), jnp.float32) ** level_of(key_list[14], (EMBED_DIMENSION,), ((0, 32),), -0.2, 0.2), 0.049804688, 0.94921875).astype(jnp.bfloat16)
    mixing_acceptor_blend = jnp.clip(0.049804688 + 0.89941406 * jax.random.uniform(key_list[15], (EMBED_DIMENSION,), jnp.float32) ** level_of(key_list[15], (EMBED_DIMENSION,), ((0, 32),), -0.2, 0.2), 0.049804688, 0.94921875).astype(jnp.bfloat16)
    feedforward_lookup_blend = jnp.clip(0.049804688 + 0.89941406 * jax.random.uniform(key_list[16], (EMBED_DIMENSION,), jnp.float32) ** level_of(key_list[16], (EMBED_DIMENSION,), ((0, 32),), -0.2, 0.2), 0.049804688, 0.94921875).astype(jnp.bfloat16)
    feedforward_acceptor_blend = jnp.clip(0.049804688 + 0.89941406 * jax.random.uniform(key_list[17], (EMBED_DIMENSION,), jnp.float32) ** level_of(key_list[17], (EMBED_DIMENSION,), ((0, 32),), -0.2, 0.2), 0.049804688, 0.94921875).astype(jnp.bfloat16)
    feature_fading_speed = draw_feature_fading_speed(jax.random.fold_in(key_list[21], 71), 0)
    present_token_reward = jnp.clip(jax.random.uniform(key_list[19], (EMBED_DIMENSION,), jnp.float32, -1.0, 1.0) * level_of(key_list[19], (EMBED_DIMENSION,), ((0, 32),), -0.4, 0.0), -1.0, 1.0).astype(jnp.bfloat16)
    upstream_adjoint = normal_values(key_list[20], (SEQS, LEN, EMBED_DIMENSION), 1.0, 6.0, ((0, 4), (1, 8)))
    return dict(layer_inputs=layer_inputs, document_openings=document_openings, mixing_lookup_projection=mixing_lookup_projection, mixing_payload_projection=mixing_payload_projection, mixing_acceptor_projection=mixing_acceptor_projection, mixing_result_projection=mixing_result_projection, feedforward_lookup_projection=feedforward_lookup_projection, feedforward_acceptor_projection=feedforward_acceptor_projection, feedforward_payload_projection=feedforward_payload_projection, premix_layer_scaling=premix_layer_scaling, premix_layer_offset=premix_layer_offset, postmix_layer_scaling=postmix_layer_scaling, postmix_layer_offset=postmix_layer_offset, mixing_lookup_blend=mixing_lookup_blend, mixing_payload_blend=mixing_payload_blend, mixing_acceptor_blend=mixing_acceptor_blend, feedforward_lookup_blend=feedforward_lookup_blend, feedforward_acceptor_blend=feedforward_acceptor_blend, feature_fading_speed=feature_fading_speed, present_token_reward=present_token_reward, upstream_adjoint=upstream_adjoint)


@jax.custom_vjp
def low(v):
    return lax.optimization_barrier(v.astype(jnp.bfloat16)).astype(jnp.float32)

@jax.custom_vjp
def low_back(v):
    return v

def low_keep(v):
    return (low(v), None)

def low_pass(kept, grad):
    return (grad,)

def back_keep(v):
    return (v, None)

def back_low(kept, grad):
    return (low(grad),)
low.defvjp(low_keep, low_pass)
low_back.defvjp(back_keep, back_low)

def layer_norm(values, gain, offset):
    center = values - lax.optimization_barrier(jnp.mean(values, axis=-1, keepdims=True))
    factor = lax.rsqrt(lax.optimization_barrier(jnp.mean(center * center, axis=-1, keepdims=True)) + 1e-05)
    return center * factor * gain + offset

def previous(values, persisting_indicator):
    moved = jnp.concatenate([jnp.zeros_like(values[:1]), values[:-1]], axis=0)
    return moved * persisting_indicator[:, None]

def blend(current, before, ratio):
    return current * ratio + before * (1.0 - ratio)

def matmul(left, right):
    return jnp.dot(left, right, precision=lax.Precision.HIGHEST)

def recurrent_average_prefix(lookup_table_lines, payload_table_lines, persisting_indicator, fading_multiplier, present_reward_term):
    shrink = jnp.exp(-fading_multiplier)

    def inner(state, stream_element):
        present_lookup, present_payload, keep_now = stream_element
        running_dividend = state[0] * keep_now
        running_divisor = state[1] * keep_now
        reward_scaled_pairs = jnp.exp(present_reward_term + present_lookup)
        returned_pair = (running_dividend + reward_scaled_pairs * present_payload) / (running_divisor + reward_scaled_pairs)
        exponentiated_lookup = jnp.exp(present_lookup)
        return ((shrink * running_dividend + exponentiated_lookup * present_payload, shrink * running_divisor + exponentiated_lookup), returned_pair)

    def outer(state, block):
        return lax.scan(inner, state, block)
    outer = jax.checkpoint(outer)
    zeros = jnp.zeros_like(lookup_table_lines[0])
    shaped = (lookup_table_lines.reshape(LEN // CH, CH, -1), payload_table_lines.reshape(LEN // CH, CH, -1), persisting_indicator.reshape(LEN // CH, CH))
    final, results = lax.scan(outer, (zeros, zeros), shaped)
    return results.reshape(LEN, -1)

def block_forward(rows, persisting_indicator, layer_settings):
    mixing_lookup_projection, mixing_payload_projection, mixing_acceptor_projection, mixing_result_projection, feedforward_lookup_projection, feedforward_acceptor_projection, feedforward_payload_projection, premix_layer_scaling, premix_layer_offset, postmix_layer_scaling, postmix_layer_offset, mixing_lookup_blend, mixing_payload_blend, mixing_acceptor_blend, feedforward_lookup_blend, feedforward_acceptor_blend, feature_fading_speed, present_token_reward = layer_settings
    normed_a = layer_norm(rows, premix_layer_scaling, premix_layer_offset)
    before_a = previous(normed_a, persisting_indicator)
    key_in = low(blend(normed_a, before_a, mixing_lookup_blend))
    value_in = low(blend(normed_a, before_a, mixing_payload_blend))
    gate_in = low(blend(normed_a, before_a, mixing_acceptor_blend))
    lookup_table_lines = low_back(matmul(key_in, mixing_lookup_projection))
    payload_table_lines = low_back(matmul(value_in, mixing_payload_projection))
    gate_rows = low_back(matmul(gate_in, mixing_acceptor_projection))
    recurrent_average = recurrent_average_prefix(lookup_table_lines, payload_table_lines, persisting_indicator, feature_fading_speed, present_token_reward)
    mixed = low(jax.nn.sigmoid(gate_rows) * recurrent_average)
    first = rows + low_back(matmul(mixed, mixing_result_projection))
    normed_b = layer_norm(first, postmix_layer_scaling, postmix_layer_offset)
    before_b = previous(normed_b, persisting_indicator)
    expand_in = low(blend(normed_b, before_b, feedforward_lookup_blend))
    select_in = low(blend(normed_b, before_b, feedforward_acceptor_blend))
    expanded = low_back(matmul(expand_in, feedforward_lookup_projection))
    selected = low_back(matmul(select_in, feedforward_acceptor_projection))
    positive = jax.nn.relu(expanded)
    squared = low(positive * positive)
    contracted = low_back(matmul(squared, feedforward_payload_projection))
    return first + jax.nn.sigmoid(selected) * contracted

def reference(layer_inputs, document_openings, mixing_lookup_projection, mixing_payload_projection, mixing_acceptor_projection, mixing_result_projection, feedforward_lookup_projection, feedforward_acceptor_projection, feedforward_payload_projection, premix_layer_scaling, premix_layer_offset, postmix_layer_scaling, postmix_layer_offset, mixing_lookup_blend, mixing_payload_blend, mixing_acceptor_blend, feedforward_lookup_blend, feedforward_acceptor_blend, feature_fading_speed, present_token_reward, upstream_adjoint):
    layer_settings = tuple((stream_element.astype(jnp.float32) for stream_element in (mixing_lookup_projection, mixing_payload_projection, mixing_acceptor_projection, mixing_result_projection, feedforward_lookup_projection, feedforward_acceptor_projection, feedforward_payload_projection, premix_layer_scaling, premix_layer_offset, postmix_layer_scaling, postmix_layer_offset, mixing_lookup_blend, mixing_payload_blend, mixing_acceptor_blend, feedforward_lookup_blend, feedforward_acceptor_blend, feature_fading_speed, present_token_reward)))

    def one_sequence(totals, stream_element):
        rows, marks, upstream = stream_element
        persisting_indicator = 1.0 - marks.astype(jnp.float32)
        returned_pair, pull = jax.vjp(lambda inputs, weights: block_forward(inputs, persisting_indicator, weights), rows.astype(jnp.float32), layer_settings)
        grad_rows, grad_params = pull(upstream.astype(jnp.float32))
        totals = jax.tree.map(lambda accumulated_sum, fresh: accumulated_sum + fresh, totals, grad_params)
        return (totals, (returned_pair.astype(jnp.bfloat16), grad_rows))
    zeros = jax.tree.map(jnp.zeros_like, layer_settings)
    grads, (outputs, input_grads) = lax.scan(one_sequence, zeros, (layer_inputs, document_openings, upstream_adjoint))
    return (outputs, input_grads, grads[0], grads[1], grads[2], grads[3], grads[4], grads[5], grads[6], grads[7], grads[8], grads[9], grads[10], grads[11], grads[12], grads[13], grads[14], grads[15], grads[16], grads[17])
```

```python
import functools

import jax
import jax.numpy as jnp
from jax import lax
from jax.experimental import pallas as pl
from jax.experimental.pallas import tpu as pltpu
from jax.sharding import PartitionSpec as P

MESH = pl.DeviceIdType.MESH
BF = jnp.bfloat16
F32 = jnp.float32
WIDE = 768
ROWS_MAIN = 224
ROWS_LAST = 96
GATHER_CHUNKS = ((0, 0, 80, 48), (0, 80, 48, 16), (0, 128, 48, 32), (0, 176, 48, 16), (1, 0, 48, 32), (1, 48, 48, 16))
SCATTER_CHUNKS = ((1, 0, 48, 32), (1, 48, 48, 16), (0, 128, 48, 32), (0, 176, 48, 16), (0, 80, 48, 16), (0, 0, 80, 48))
COUNT = len(GATHER_CHUNKS)
GATHER_SEMS = 20
SCATTER_SEMS = 16


class Place:
    def __init__(self):
        self.s = lax.axis_index("seq")
        self.b = lax.axis_index("batch")
        self.z, self.c = self.s // 2, self.s % 2
        y, x = self.b // 2, self.b % 2
        self.bx, self.by, self.bd = y * 2 + 1 - x, (1 - y) * 2 + x, (1 - y) * 2 + 1 - x
        self.depth = lax.axis_size("seq") // 2
        self.x, self.y = (self.s, self.bx), (self.s, self.by)
        self.core = (self.z * 2 + 1 - self.c, self.b)

    def along(self, step):
        z = lax.rem(self.z + step, self.depth)
        return z, (z * 2 + self.c, self.b)

    def back(self, step):
        return lax.rem(self.z + self.depth - step, self.depth)


def rdma(src, dst, sems, send, recv, to):
    return pltpu.make_async_remote_copy(
        src_ref=src, dst_ref=dst, send_sem=sems.at[send], recv_sem=sems.at[recv], device_id=to, device_id_type=MESH
    )


def enter(place):
    barrier = pltpu.get_barrier_semaphore()
    count = 0
    peers = [place.x, place.y, place.core] + [place.along(d)[1] for d in range(1, place.depth)]
    for peer in peers:
        pl.semaphore_signal(barrier, inc=1, device_id=peer, device_id_type=MESH)
    pl.semaphore_wait(barrier, len(peers))


class Gather:
    def __init__(self, place, arrays, sems):
        self.p, self.arrays, self.sems = place, arrays, sems

    def copies(self, k):
        p, sems = self.p, self.sems.at[k]
        a, r0, n, nx = GATHER_CHUNKS[k]
        ref = self.arrays[a]
        whole, part_x, part_y = pl.ds(r0, n), pl.ds(r0, nx), pl.ds(r0 + nx, n - nx)
        own = ref.at[p.z, p.c, p.b, whole]
        col = lambda c, b, rows: ref.at[:, c, b, rows]
        out = {}
        for d in range(1, p.depth):
            out["z", d] = rdma(own, own, sems, 2 * d - 2, 2 * d - 1, p.along(d)[1])
        out["x"] = rdma(col(p.c, p.b, whole), col(p.c, p.b, whole), sems, 6, 7, p.x)
        out["y"] = rdma(col(p.c, p.b, whole), col(p.c, p.b, whole), sems, 8, 9, p.y)
        out["dx"] = rdma(col(p.c, p.by, part_x), col(p.c, p.by, part_x), sems, 10, 11, p.x)
        out["dy"] = rdma(col(p.c, p.bx, part_y), col(p.c, p.bx, part_y), sems, 12, 13, p.y)
        for j, b in enumerate((p.b, p.bx, p.by)):
            pass
        out["c", 0] = rdma(col(p.c, p.b, whole), col(p.c, p.b, whole), sems, 14, 15, p.core)
        out["c", 1] = rdma(col(p.c, p.bx, whole), col(p.c, p.bx, whole), sems, 16, 17, p.core)
        out["c", 2] = rdma(col(p.c, p.by, whole), col(p.c, p.by, whole), sems, 18, 19, p.core)
        out["c", 3] = rdma(col(p.c, p.bd, whole), col(p.c, p.bd, whole), sems, 20, 21, p.core)
        return out

    def arrivals(self, k):
        p, sems = self.p, self.sems.at[k]
        a, r0, n, nx = GATHER_CHUNKS[k]
        ref = self.arrays[a]
        whole, part_x, part_y = pl.ds(r0, n), pl.ds(r0, nx), pl.ds(r0 + nx, n - nx)
        col = lambda c, b, rows: ref.at[:, c, b, rows]
        at = lambda view, recv, to: rdma(view, view, sems, recv - 1, recv, to)
        out = {}
        for d in range(1, p.depth):
            out["z", d] = at(ref.at[p.back(d), p.c, p.b, whole], 2 * d - 1, p.along(d)[1])
        out["x"] = at(col(p.c, p.bx, whole), 7, p.x)
        out["y"] = at(col(p.c, p.by, whole), 9, p.y)
        out["dx"] = at(col(p.c, p.bd, part_x), 11, p.x)
        out["dy"] = at(col(p.c, p.bd, part_y), 13, p.y)
        for j, b in enumerate((p.b, p.bx, p.by, p.bd)):
            out["c", j] = at(col(1 - p.c, b, whole), 15 + 2 * j, p.core)
        return out

    def stage(self, number, k):
        if not 0 <= k < COUNT:
            return
        send, come = self.copies(k), self.arrivals(k)
        if number == 0:
            for d in range(1, self.p.depth):
                send["z", d].start()
        elif number == 1:
            for d in range(1, self.p.depth):
                come["z", d].wait_recv()
            send["x"].start()
            send["y"].start()
            send["c", 0].start()
        elif number == 2:
            come["x"].wait_recv()
            come["y"].wait_recv()
            send["dx"].start()
            send["dy"].start()
            send["c", 1].start()
            send["c", 2].start()
        elif number == 3:
            come["dx"].wait_recv()
            come["dy"].wait_recv()
            send["c", 3].start()
        elif number == 4:
            for j in range(4):
                come["c", j].wait_recv()
        elif number == 5:
            for copy in send.values():
                copy.wait_send()

    def tick(self, t):
        for number in range(5):
            self.stage(number, t - number)


class Scatter:
    def __init__(self, place, packed, from_core, near, diag, line, out, sems):
        self.p, self.packed, self.from_core, self.near = place, packed, from_core, near
        self.diag, self.line, self.out, self.sems = diag, line, out, sems

    def parts(self, k):
        p, sems = self.p, self.sems.at[k]
        a, r0, n, nx = SCATTER_CHUNKS[k]
        ref = self.packed[a]
        f0 = r0 if a == 0 else r0 + ROWS_MAIN
        whole, part_x, part_y = pl.ds(r0, n), pl.ds(r0, nx), pl.ds(r0 + nx, n - nx)
        fw, fx, fy = pl.ds(f0, n), pl.ds(f0, nx), pl.ds(f0 + nx, n - nx)
        out = {}
        out["c"] = rdma(ref.at[:, 1 - p.c, :, whole], self.from_core.at[:, :, fw], sems, 0, 1, p.core)
        out["dx"] = rdma(ref.at[:, p.c, p.bd, part_x], self.diag.at[:, fx], sems, 2, 3, p.x)
        out["dy"] = rdma(ref.at[:, p.c, p.bd, part_y], self.diag.at[:, fy], sems, 4, 5, p.y)
        out["x"] = rdma(ref.at[:, p.c, p.bx, whole], self.near.at[0, :, fw], sems, 6, 7, p.x)
        out["y"] = rdma(ref.at[:, p.c, p.by, whole], self.near.at[1, :, fw], sems, 8, 9, p.y)
        for d in range(1, p.depth):
            z, to = p.along(d)
            out["z", d] = rdma(ref.at[z, p.c, p.b, whole], self.line.at[d - 1, fw], sems, 8 + 2 * d, 9 + 2 * d, to)
        return out

    def add(self, dst, src, rows_dst, rows_src, other):
        pass

    def stage(self, number, k):
        if not 0 <= k < COUNT:
            return
        p = self.p
        copy = self.parts(k)
        a, r0, n, nx = SCATTER_CHUNKS[k]
        ref = self.packed[a]
        f0 = r0 if a == 0 else r0 + ROWS_MAIN
        depth = ref.shape[0]
        if number == 0:
            copy["c"].start()
        elif number == 1:
            copy["c"].wait_recv()

            @pl.loop(0, depth * 4)
            def _(i):
                z, b = i // 4, i % 4
                ref[z, p.c, b, pl.ds(r0, n)] = (
                    ref[z, p.c, b, pl.ds(r0, n)].astype(F32) + self.from_core[z, b, pl.ds(f0, n)].astype(F32)
                ).astype(BF)

            copy["dx"].start()
            copy["dy"].start()
        elif number == 2:
            copy["dx"].wait_recv()
            copy["dy"].wait_recv()

            @pl.loop(0, depth)
            def _(z):
                for b, s0, m in ((p.by, 0, nx), (p.bx, nx, n - nx)):
                    ref[z, p.c, b, pl.ds(r0 + s0, m)] = (
                        ref[z, p.c, b, pl.ds(r0 + s0, m)].astype(F32) + self.diag[z, pl.ds(f0 + s0, m)].astype(F32)
                    ).astype(BF)

            copy["x"].start()
            copy["y"].start()
        elif number == 3:
            copy["x"].wait_recv()
            copy["y"].wait_recv()

            @pl.loop(0, depth)
            def _(z):
                ref[z, p.c, p.b, pl.ds(r0, n)] = (
                    ref[z, p.c, p.b, pl.ds(r0, n)].astype(F32)
                    + self.near[0, z, pl.ds(f0, n)].astype(F32)
                    + self.near[1, z, pl.ds(f0, n)].astype(F32)
                ).astype(BF)

            for d in range(1, p.depth):
                copy["z", d].start()
        elif number == 4:
            for d in range(1, p.depth):
                copy["z", d].wait_recv()
            total = ref[p.z, p.c, p.b, pl.ds(r0, n)].astype(F32)
            for d in range(1, p.depth):
                total = total + self.line[d - 1, pl.ds(f0, n)].astype(F32)
            self.out[pl.ds(f0, n)] = total
            for each in copy.values():
                each.wait_send()

    def tick(self, t):
        for number in range(5):
            self.stage(number, t - number)


def gather_kernel(main_in, last_in, main, last, sems, lsem):
    place = Place()
    a = pltpu.make_async_copy(main_in, main.at[place.z, place.c, place.b], lsem.at[0])
    b = pltpu.make_async_copy(last_in, last.at[place.z, place.c, place.b], lsem.at[1])
    a.start(); b.start()
    enter(place)
    a.wait(); b.wait()
    g = Gather(place, (main, last), sems)
    for t in range(COUNT + 4):
        g.tick(t)
    for k in range(COUNT):
        g.stage(5, k)


def gather_call(main_in, last_in, depth):
    hbm = pl.BlockSpec(memory_space=pl.ANY)
    return pl.pallas_call(
        gather_kernel,
        out_shape=(jax.ShapeDtypeStruct((depth, 2, 4, ROWS_MAIN, WIDE), BF), jax.ShapeDtypeStruct((depth, 2, 4, ROWS_LAST, WIDE), BF)),
        in_specs=[hbm, hbm], out_specs=(hbm, hbm),
        scratch_shapes=[pltpu.SemaphoreType.DMA((COUNT, 22)), pltpu.SemaphoreType.DMA((2,))],
        compiler_params=pltpu.CompilerParams(collective_id=0, has_side_effects=True, vmem_limit_bytes=60 << 20),
    )(main_in, last_in)


def scatter_kernel(main_in, last_in, out, main, last, from_core, near, diag, line, sems, lsem):
    place = Place()
    a = pltpu.make_async_copy(main_in, main, lsem.at[0])
    b = pltpu.make_async_copy(last_in, last, lsem.at[1])
    a.start(); b.start()
    enter(place)
    a.wait(); b.wait()
    r = Scatter(place, (main, last), from_core, near, diag, line, out, sems)
    for t in range(COUNT + 4):
        r.tick(t)


def scatter_call(main_in, last_in, depth):
    hbm = pl.BlockSpec(memory_space=pl.ANY)
    rows = ROWS_MAIN + ROWS_LAST
    return pl.pallas_call(
        scatter_kernel,
        out_shape=jax.ShapeDtypeStruct((rows, WIDE), F32),
        in_specs=[hbm, hbm], out_specs=pl.BlockSpec(memory_space=pltpu.VMEM),
        scratch_shapes=[
            pltpu.VMEM((depth, 2, 4, ROWS_MAIN, WIDE), BF), pltpu.VMEM((depth, 2, 4, ROWS_LAST, WIDE), BF),
            pltpu.VMEM((depth, 4, rows, WIDE), BF), pltpu.VMEM((2, depth, rows, WIDE), BF),
            pltpu.VMEM((depth, rows, WIDE), BF), pltpu.VMEM((depth - 1, rows, WIDE), BF),
            pltpu.SemaphoreType.DMA((COUNT, 16)), pltpu.SemaphoreType.DMA((2,))],
        compiler_params=pltpu.CompilerParams(collective_id=1, has_side_effects=True, vmem_limit_bytes=60 << 20),
    )(main_in, last_in)


EPSILON = 1e-05


def from_behind(block, axis, distance):
    devices = range(lax.axis_size(axis))
    route = [(i - distance, i) for i in devices if i - distance in devices]
    return lax.ppermute(block, axis, route)


def prefix(part, axis, combine, identity, reverse):
    count = lax.axis_size(axis)
    place = lax.axis_index(axis)
    ahead = count - 1 - place if reverse else place
    gathered = jax.tree.map(lambda a: lax.all_gather(a, axis), part)
    state = jax.tree.map(lambda a, e: jnp.zeros_like(a) + jnp.asarray(e, a.dtype), part, identity)

    def one(turn, state):
        source = count - 1 - turn if reverse else turn
        return combine(
            state, jax.tree.map(lambda a: lax.dynamic_index_in_dim(a, source, 0, False), gathered)
        )

    return lax.fori_loop(0, ahead, one, state)


def layer_norm(values, gain, offset):
    center = values - jnp.mean(values, axis=-1, keepdims=True)
    factor = lax.rsqrt(jnp.mean(center * center, axis=-1, keepdims=True) + EPSILON)
    normed = center * factor
    return (normed * gain + offset, normed, factor)


def norm_back(grad_out, normed, factor, gain):
    scaled = grad_out * gain
    centered = scaled - jnp.mean(scaled, axis=-1, keepdims=True)
    grad_in = factor * (centered - normed * jnp.mean(scaled * normed, axis=-1, keepdims=True))
    return (grad_in, jnp.sum(grad_out * normed, axis=(0, 1)), jnp.sum(grad_out, axis=(0, 1)))


def product(left, right):
    return jnp.einsum("scd,de->sce", left, right, preferred_element_type=jnp.float32)


def product_back(grad, right):
    return jnp.einsum("sce,de->scd", grad, right, preferred_element_type=jnp.float32)


def outer_sum(left, grad):
    return jnp.einsum("scd,sce->de", left, grad, preferred_element_type=jnp.float32)


def attach_previous(values, arriving, persisting_indicator):
    return jnp.concatenate([arriving, values[:, :-1]], axis=1) * persisting_indicator[..., None]


def attach_next(masked, arriving):
    return jnp.concatenate([masked[:, 1:], arriving], axis=1)


def make_combine(fading_multiplier):

    def combine(earlier, later):
        early_numer, early_denom, early_length, early_cut = earlier
        late_numer, late_denom, late_length, late_cut = later
        fading = jnp.exp(-late_length * fading_multiplier) * (1.0 - late_cut)
        return (
            late_numer + fading * early_numer,
            late_denom + fading * early_denom,
            early_length + late_length,
            jnp.maximum(early_cut, late_cut),
        )

    return combine


def affine_compose(first_step, second_step):
    first_mult, first_numer, first_denom = first_step
    second_mult, second_numer, second_denom = second_step
    return (
        first_mult * second_mult,
        second_mult * first_numer + second_numer,
        second_mult * first_denom + second_denom,
    )


def forward_sweep(exponentiated_lookup, payload_table_lines, persisting_indicator, shrink):
    multiplier = persisting_indicator[..., None] * shrink
    inclusive = lax.associative_scan(
        affine_compose,
        (multiplier, exponentiated_lookup * payload_table_lines, exponentiated_lookup),
        axis=1,
    )
    zeros = jnp.zeros_like(exponentiated_lookup[:, :1])
    numer_all = (
        jnp.concatenate([zeros, inclusive[1][:, :-1]], axis=1) * persisting_indicator[..., None]
    )
    denom_all = (
        jnp.concatenate([zeros, inclusive[2][:, :-1]], axis=1) * persisting_indicator[..., None]
    )
    return (numer_all, denom_all, inclusive[1][:, -1], inclusive[2][:, -1])


def reverse_sweep(adjoint_dividend, grad_denom, persisting_indicator, shrink):
    keep_now = persisting_indicator[..., None]
    inclusive = lax.associative_scan(
        affine_compose,
        (keep_now * shrink, keep_now * adjoint_dividend, keep_now * grad_denom),
        axis=1,
        reverse=True,
    )
    zeros = jnp.zeros_like(adjoint_dividend[:, :1])
    following_dividend = jnp.concatenate([inclusive[1][:, 1:], zeros], axis=1)
    next_denom = jnp.concatenate([inclusive[2][:, 1:], zeros], axis=1)
    return (following_dividend, next_denom, inclusive[1][:, 0], inclusive[2][:, 0])


def body(
    layer_inputs,
    document_openings,
    mixing_lookup_projection,
    mixing_payload_projection,
    mixing_acceptor_projection,
    mixing_result_projection,
    feedforward_lookup_projection,
    feedforward_acceptor_projection,
    feedforward_payload_projection,
    premix_layer_scaling,
    premix_layer_offset,
    postmix_layer_scaling,
    postmix_layer_offset,
    mixing_lookup_blend,
    mixing_payload_blend,
    mixing_acceptor_blend,
    feedforward_lookup_blend,
    feedforward_acceptor_blend,
    feature_fading_speed,
    present_token_reward,
    upstream_adjoint,
):
    gathered = (
        lax.all_gather(mixing_lookup_projection, ("seq", "batch"), axis=0, tiled=True),
        lax.all_gather(mixing_payload_projection, ("seq", "batch"), axis=0, tiled=True),
        lax.all_gather(mixing_acceptor_projection, ("seq", "batch"), axis=0, tiled=True),
        lax.all_gather(mixing_result_projection, ("seq", "batch"), axis=0, tiled=True),
        lax.all_gather(feedforward_lookup_projection, ("seq", "batch"), axis=0, tiled=True),
        lax.all_gather(feedforward_acceptor_projection, ("seq", "batch"), axis=0, tiled=True),
        lax.all_gather(feedforward_payload_projection, ("seq", "batch"), axis=0, tiled=True),
        lax.all_gather(premix_layer_scaling, ("seq", "batch"), axis=0, tiled=True),
        lax.all_gather(premix_layer_offset, ("seq", "batch"), axis=0, tiled=True),
        lax.all_gather(postmix_layer_scaling, ("seq", "batch"), axis=0, tiled=True),
        lax.all_gather(postmix_layer_offset, ("seq", "batch"), axis=0, tiled=True),
        lax.all_gather(mixing_lookup_blend, ("seq", "batch"), axis=0, tiled=True),
        lax.all_gather(mixing_payload_blend, ("seq", "batch"), axis=0, tiled=True),
        lax.all_gather(mixing_acceptor_blend, ("seq", "batch"), axis=0, tiled=True),
        lax.all_gather(feedforward_lookup_blend, ("seq", "batch"), axis=0, tiled=True),
        lax.all_gather(feedforward_acceptor_blend, ("seq", "batch"), axis=0, tiled=True),
        lax.all_gather(feature_fading_speed, ("seq", "batch"), axis=0, tiled=True),
        lax.all_gather(present_token_reward, ("seq", "batch"), axis=0, tiled=True),
    )
    full_key, full_value, full_gate, full_output, full_expand, full_select, full_contract = (
        gathered[:7]
    )
    vectors = [stream_element.astype(jnp.float32) for stream_element in gathered[7:]]
    (
        gain_first,
        bias_first,
        gain_second,
        bias_second,
        ratio_key,
        ratio_value,
        ratio_gate,
        ratio_expand,
        ratio_select,
        fading_multiplier,
        present_reward_term,
    ) = vectors
    inputs = layer_inputs.astype(jnp.float32)
    flags = document_openings.astype(jnp.float32)
    persisting_indicator = 1.0 - flags
    sequences = layer_inputs.shape[0]
    block_len = layer_inputs.shape[1]
    width = layer_inputs.shape[2]
    normed_a, unit_a, factor_a = layer_norm(inputs, gain_first, bias_first)
    arriving_a = from_behind(normed_a[:, -1:, :], "seq", 1)
    before_a = attach_previous(normed_a, arriving_a, persisting_indicator)
    spread_a = normed_a - before_a
    key_in = (before_a + spread_a * ratio_key).astype(jnp.bfloat16)
    value_in = (before_a + spread_a * ratio_value).astype(jnp.bfloat16)
    gate_in = (before_a + spread_a * ratio_gate).astype(jnp.bfloat16)
    lookup_table_lines = product(key_in, full_key)
    payload_table_lines = product(value_in, full_value)
    gate_rows = product(gate_in, full_gate)
    shrink = jnp.exp(-fading_multiplier)
    exponentiated_lookup = jnp.exp(lookup_table_lines)
    reward_scaled_pairs = jnp.exp(present_reward_term + lookup_table_lines)
    local_numer, local_denom, end_numer, end_denom = forward_sweep(
        exponentiated_lookup, payload_table_lines, persisting_indicator, shrink
    )
    cut = jnp.max(flags, axis=1, keepdims=True)
    length = jnp.full((1,), float(block_len), jnp.float32)
    zero_state = jnp.zeros((sequences, width), jnp.float32)
    identity = (
        zero_state,
        zero_state,
        jnp.zeros((1,), jnp.float32),
        jnp.zeros((sequences, 1), jnp.float32),
    )
    combine = make_combine(fading_multiplier)
    arrived = prefix((end_numer, end_denom, length, cut), "seq", combine, identity, False)
    positions = jnp.arange(block_len, dtype=jnp.float32)
    alive = 1.0 - lax.cummax(flags, axis=1)
    rising = jnp.exp(-positions[:, None] * fading_multiplier[None, :])
    running_dividend = local_numer + alive[..., None] * rising[None] * arrived[0][:, None, :]
    running_divisor = local_denom + alive[..., None] * rising[None] * arrived[1][:, None, :]
    accumulated_sum = running_divisor + reward_scaled_pairs
    recurrent_average = (
        running_dividend + reward_scaled_pairs * payload_table_lines
    ) / accumulated_sum
    gate_sig = jax.nn.sigmoid(gate_rows)
    mixed = (gate_sig * recurrent_average).astype(jnp.bfloat16)
    first = inputs + product(mixed, full_output)
    normed_b, unit_b, factor_b = layer_norm(first, gain_second, bias_second)
    arriving_b = from_behind(normed_b[:, -1:, :], "seq", 1)
    before_b = attach_previous(normed_b, arriving_b, persisting_indicator)
    spread_b = normed_b - before_b
    expand_in = (before_b + spread_b * ratio_expand).astype(jnp.bfloat16)
    select_in = (before_b + spread_b * ratio_select).astype(jnp.bfloat16)
    expanded = product(expand_in, full_expand)
    selected = product(select_in, full_select)
    positive = jax.nn.relu(expanded)
    squared = (positive * positive).astype(jnp.bfloat16)
    contracted = product(squared, full_contract)
    select_sig = jax.nn.sigmoid(selected)
    block_out = (first + select_sig * contracted).astype(jnp.bfloat16)
    again = (
        lax.all_gather(mixing_lookup_projection, ("seq", "batch"), axis=0, tiled=True),
        lax.all_gather(mixing_payload_projection, ("seq", "batch"), axis=0, tiled=True),
        lax.all_gather(mixing_acceptor_projection, ("seq", "batch"), axis=0, tiled=True),
        lax.all_gather(mixing_result_projection, ("seq", "batch"), axis=0, tiled=True),
        lax.all_gather(feedforward_lookup_projection, ("seq", "batch"), axis=0, tiled=True),
        lax.all_gather(feedforward_acceptor_projection, ("seq", "batch"), axis=0, tiled=True),
        lax.all_gather(feedforward_payload_projection, ("seq", "batch"), axis=0, tiled=True),
    )
    full_key, full_value, full_gate, full_output, full_expand, full_select, full_contract = again
    upstream = upstream_adjoint.astype(jnp.float32)
    grad_contracted = (upstream * select_sig).astype(jnp.bfloat16)
    grad_selected = (upstream * contracted * select_sig * (1.0 - select_sig)).astype(jnp.bfloat16)
    grad_squared = product_back(grad_contracted, full_contract)
    grad_expanded = (2.0 * positive * grad_squared).astype(jnp.bfloat16)
    contract_grad = jnp.einsum(
        "scf,scd->fd", squared, grad_contracted, preferred_element_type=jnp.float32
    )
    expand_grad = outer_sum(expand_in, grad_expanded)
    select_grad = outer_sum(select_in, grad_selected)
    grad_expand_in = product_back(grad_expanded, full_expand)
    grad_select_in = product_back(grad_selected, full_select)
    expand_ratio_grad = jnp.sum(grad_expand_in * spread_b, axis=(0, 1))
    select_ratio_grad = jnp.sum(grad_select_in * spread_b, axis=(0, 1))
    grad_before_b = (
        grad_expand_in * (1.0 - ratio_expand) + grad_select_in * (1.0 - ratio_select)
    ) * persisting_indicator[..., None]
    arriving_gb = from_behind(grad_before_b[:, :1, :], "seq", -1)
    grad_normed_b = (
        grad_expand_in * ratio_expand
        + grad_select_in * ratio_select
        + attach_next(grad_before_b, arriving_gb)
    )
    grad_from_b, chan_gain_grad, chan_bias_grad = norm_back(
        grad_normed_b, unit_b, factor_b, gain_second
    )
    grad_first = upstream + grad_from_b
    grad_attended = grad_first.astype(jnp.bfloat16)
    output_grad = outer_sum(mixed, grad_attended)
    grad_mixed = product_back(grad_attended, full_output)
    grad_gates = (grad_mixed * recurrent_average * gate_sig * (1.0 - gate_sig)).astype(jnp.bfloat16)
    grad_wkv = grad_mixed * gate_sig
    adjoint_dividend = grad_wkv / accumulated_sum
    grad_denom = -grad_wkv * recurrent_average / accumulated_sum
    following_dividend, next_denom, lead_numer, lead_denom = reverse_sweep(
        adjoint_dividend, grad_denom, persisting_indicator, shrink
    )
    behind = prefix((lead_numer, lead_denom, length, cut), "seq", combine, identity, True)
    after = jnp.concatenate([flags[:, 1:], jnp.zeros_like(flags[:, :1])], axis=1)
    later_alive = 1.0 - lax.cummax(after, axis=1, reverse=True)
    falling = jnp.exp(-(block_len - 1.0 - positions)[:, None] * fading_multiplier[None, :])
    following_dividend = (
        following_dividend + later_alive[..., None] * falling[None] * behind[0][:, None, :]
    )
    next_denom = next_denom + later_alive[..., None] * falling[None] * behind[1][:, None, :]
    immediate_term = adjoint_dividend * payload_table_lines + grad_denom
    grad_keys = (
        exponentiated_lookup * (following_dividend * payload_table_lines + next_denom)
        + reward_scaled_pairs * immediate_term
    ).astype(jnp.bfloat16)
    adjoint_payloads = (
        exponentiated_lookup * following_dividend + reward_scaled_pairs * adjoint_dividend
    ).astype(jnp.bfloat16)
    present_reward_adjoint = jnp.sum(reward_scaled_pairs * immediate_term, axis=(0, 1))
    decay_grad = -shrink * jnp.sum(
        following_dividend * running_dividend + next_denom * running_divisor, axis=(0, 1)
    )
    key_grad = outer_sum(key_in, grad_keys)
    value_grad = outer_sum(value_in, adjoint_payloads)
    gate_grad = outer_sum(gate_in, grad_gates)
    grad_key_in = product_back(grad_keys, full_key)
    grad_value_in = product_back(adjoint_payloads, full_value)
    grad_gate_in = product_back(grad_gates, full_gate)
    key_ratio_grad = jnp.sum(grad_key_in * spread_a, axis=(0, 1))
    value_ratio_grad = jnp.sum(grad_value_in * spread_a, axis=(0, 1))
    gate_ratio_grad = jnp.sum(grad_gate_in * spread_a, axis=(0, 1))
    grad_before_a = (
        grad_key_in * (1.0 - ratio_key)
        + grad_value_in * (1.0 - ratio_value)
        + grad_gate_in * (1.0 - ratio_gate)
    ) * persisting_indicator[..., None]
    arriving_ga = from_behind(grad_before_a[:, :1, :], "seq", -1)
    grad_normed_a = (
        grad_key_in * ratio_key
        + grad_value_in * ratio_value
        + grad_gate_in * ratio_gate
        + attach_next(grad_before_a, arriving_ga)
    )
    grad_from_a, attn_gain_grad, attn_bias_grad = norm_back(
        grad_normed_a, unit_a, factor_a, gain_first
    )
    tokens_grad = grad_first + grad_from_a
    shares = (
        lax.psum_scatter(key_grad, ("seq", "batch"), scatter_dimension=0, tiled=True),
        lax.psum_scatter(value_grad, ("seq", "batch"), scatter_dimension=0, tiled=True),
        lax.psum_scatter(gate_grad, ("seq", "batch"), scatter_dimension=0, tiled=True),
        lax.psum_scatter(output_grad, ("seq", "batch"), scatter_dimension=0, tiled=True),
        lax.psum_scatter(expand_grad, ("seq", "batch"), scatter_dimension=0, tiled=True),
        lax.psum_scatter(select_grad, ("seq", "batch"), scatter_dimension=0, tiled=True),
        lax.psum_scatter(contract_grad, ("seq", "batch"), scatter_dimension=0, tiled=True),
        lax.psum_scatter(attn_gain_grad, ("seq", "batch"), scatter_dimension=0, tiled=True),
        lax.psum_scatter(attn_bias_grad, ("seq", "batch"), scatter_dimension=0, tiled=True),
        lax.psum_scatter(chan_gain_grad, ("seq", "batch"), scatter_dimension=0, tiled=True),
        lax.psum_scatter(chan_bias_grad, ("seq", "batch"), scatter_dimension=0, tiled=True),
        lax.psum_scatter(key_ratio_grad, ("seq", "batch"), scatter_dimension=0, tiled=True),
        lax.psum_scatter(value_ratio_grad, ("seq", "batch"), scatter_dimension=0, tiled=True),
        lax.psum_scatter(gate_ratio_grad, ("seq", "batch"), scatter_dimension=0, tiled=True),
        lax.psum_scatter(expand_ratio_grad, ("seq", "batch"), scatter_dimension=0, tiled=True),
        lax.psum_scatter(select_ratio_grad, ("seq", "batch"), scatter_dimension=0, tiled=True),
        lax.psum_scatter(decay_grad, ("seq", "batch"), scatter_dimension=0, tiled=True),
        lax.psum_scatter(present_reward_adjoint, ("seq", "batch"), scatter_dimension=0, tiled=True),
    )
    return (
        block_out,
        tokens_grad,
        shares[0],
        shares[1],
        shares[2],
        shares[3],
        shares[4],
        shares[5],
        shares[6],
        shares[7],
        shares[8],
        shares[9],
        shares[10],
        shares[11],
        shares[12],
        shares[13],
        shares[14],
        shares[15],
        shares[16],
        shares[17],
    )


def fast_body(
    layer_inputs,
    document_openings,
    mixing_lookup_projection,
    mixing_payload_projection,
    mixing_acceptor_projection,
    mixing_result_projection,
    feedforward_lookup_projection,
    feedforward_acceptor_projection,
    feedforward_payload_projection,
    premix_layer_scaling,
    premix_layer_offset,
    postmix_layer_scaling,
    postmix_layer_offset,
    mixing_lookup_blend,
    mixing_payload_blend,
    mixing_acceptor_blend,
    feedforward_lookup_blend,
    feedforward_acceptor_blend,
    feature_fading_speed,
    present_token_reward,
    upstream_adjoint,
):
    depth = lax.axis_size("seq") // 2
    pad = jnp.zeros((8, WIDE), BF)
    e = feedforward_lookup_projection
    packed_main = jnp.concatenate(
        [mixing_lookup_projection, mixing_payload_projection, mixing_acceptor_projection, pad,
         mixing_result_projection, feedforward_acceptor_projection]
        + [e[:, i * WIDE : (i + 1) * WIDE] for i in range(4)], axis=0)
    main, last = gather_call(packed_main, feedforward_payload_projection, depth)
    main = main.reshape(-1, ROWS_MAIN, WIDE)
    square = lambda r: main[:, r : r + 24].reshape(-1, WIDE)
    full_key, full_value, full_gate, full_output, full_select = (square(r) for r in (0, 24, 48, 80, 104))
    full_expand = jnp.concatenate([square(128 + 24 * i) for i in range(4)], axis=1)
    full_contract = last.reshape(-1, WIDE)
    small = jnp.stack([premix_layer_scaling, premix_layer_offset, postmix_layer_scaling, postmix_layer_offset, mixing_lookup_blend,
        mixing_payload_blend, mixing_acceptor_blend, feedforward_lookup_blend, feedforward_acceptor_blend, feature_fading_speed, present_token_reward])
    small = lax.all_gather(small, ("seq", "batch"), axis=1, tiled=True)
    gathered = [None] * 7 + [small[i] for i in range(11)]
    vectors = [stream_element.astype(jnp.float32) for stream_element in gathered[7:]]
    (
        gain_first,
        bias_first,
        gain_second,
        bias_second,
        ratio_key,
        ratio_value,
        ratio_gate,
        ratio_expand,
        ratio_select,
        fading_multiplier,
        present_reward_term,
    ) = vectors
    inputs = layer_inputs.astype(jnp.float32)
    flags = document_openings.astype(jnp.float32)
    persisting_indicator = 1.0 - flags
    sequences = layer_inputs.shape[0]
    block_len = layer_inputs.shape[1]
    width = layer_inputs.shape[2]
    normed_a, unit_a, factor_a = layer_norm(inputs, gain_first, bias_first)
    arriving_a = from_behind(normed_a[:, -1:, :], "seq", 1)
    before_a = attach_previous(normed_a, arriving_a, persisting_indicator)
    spread_a = normed_a - before_a
    key_in = (before_a + spread_a * ratio_key).astype(jnp.bfloat16)
    value_in = (before_a + spread_a * ratio_value).astype(jnp.bfloat16)
    gate_in = (before_a + spread_a * ratio_gate).astype(jnp.bfloat16)
    lookup_table_lines = product(key_in, full_key)
    payload_table_lines = product(value_in, full_value)
    gate_rows = product(gate_in, full_gate)
    shrink = jnp.exp(-fading_multiplier)
    exponentiated_lookup = jnp.exp(lookup_table_lines)
    reward_scaled_pairs = jnp.exp(present_reward_term + lookup_table_lines)
    local_numer, local_denom, end_numer, end_denom = forward_sweep(
        exponentiated_lookup, payload_table_lines, persisting_indicator, shrink
    )
    cut = jnp.max(flags, axis=1, keepdims=True)
    length = jnp.full((1,), float(block_len), jnp.float32)
    zero_state = jnp.zeros((sequences, width), jnp.float32)
    identity = (
        zero_state,
        zero_state,
        jnp.zeros((1,), jnp.float32),
        jnp.zeros((sequences, 1), jnp.float32),
    )
    combine = make_combine(fading_multiplier)
    arrived = prefix((end_numer, end_denom, length, cut), "seq", combine, identity, False)
    positions = jnp.arange(block_len, dtype=jnp.float32)
    alive = 1.0 - lax.cummax(flags, axis=1)
    rising = jnp.exp(-positions[:, None] * fading_multiplier[None, :])
    running_dividend = local_numer + alive[..., None] * rising[None] * arrived[0][:, None, :]
    running_divisor = local_denom + alive[..., None] * rising[None] * arrived[1][:, None, :]
    accumulated_sum = running_divisor + reward_scaled_pairs
    recurrent_average = (
        running_dividend + reward_scaled_pairs * payload_table_lines
    ) / accumulated_sum
    gate_sig = jax.nn.sigmoid(gate_rows)
    mixed = (gate_sig * recurrent_average).astype(jnp.bfloat16)
    first = inputs + product(mixed, full_output)
    normed_b, unit_b, factor_b = layer_norm(first, gain_second, bias_second)
    arriving_b = from_behind(normed_b[:, -1:, :], "seq", 1)
    before_b = attach_previous(normed_b, arriving_b, persisting_indicator)
    spread_b = normed_b - before_b
    expand_in = (before_b + spread_b * ratio_expand).astype(jnp.bfloat16)
    select_in = (before_b + spread_b * ratio_select).astype(jnp.bfloat16)
    expanded = product(expand_in, full_expand)
    selected = product(select_in, full_select)
    positive = jax.nn.relu(expanded)
    squared = (positive * positive).astype(jnp.bfloat16)
    contracted = product(squared, full_contract)
    select_sig = jax.nn.sigmoid(selected)
    block_out = (first + select_sig * contracted).astype(jnp.bfloat16)
    upstream = upstream_adjoint.astype(jnp.float32)
    grad_contracted = (upstream * select_sig).astype(jnp.bfloat16)
    grad_selected = (upstream * contracted * select_sig * (1.0 - select_sig)).astype(jnp.bfloat16)
    grad_squared = product_back(grad_contracted, full_contract)
    grad_expanded = (2.0 * positive * grad_squared).astype(jnp.bfloat16)
    contract_grad = jnp.einsum(
        "scf,scd->fd", squared, grad_contracted, preferred_element_type=jnp.float32
    )
    expand_grad = outer_sum(expand_in, grad_expanded)
    select_grad = outer_sum(select_in, grad_selected)
    grad_expand_in = product_back(grad_expanded, full_expand)
    grad_select_in = product_back(grad_selected, full_select)
    expand_ratio_grad = jnp.sum(grad_expand_in * spread_b, axis=(0, 1))
    select_ratio_grad = jnp.sum(grad_select_in * spread_b, axis=(0, 1))
    grad_before_b = (
        grad_expand_in * (1.0 - ratio_expand) + grad_select_in * (1.0 - ratio_select)
    ) * persisting_indicator[..., None]
    arriving_gb = from_behind(grad_before_b[:, :1, :], "seq", -1)
    grad_normed_b = (
        grad_expand_in * ratio_expand
        + grad_select_in * ratio_select
        + attach_next(grad_before_b, arriving_gb)
    )
    grad_from_b, chan_gain_grad, chan_bias_grad = norm_back(
        grad_normed_b, unit_b, factor_b, gain_second
    )
    grad_first = upstream + grad_from_b
    grad_attended = grad_first.astype(jnp.bfloat16)
    output_grad = outer_sum(mixed, grad_attended)
    grad_mixed = product_back(grad_attended, full_output)
    grad_gates = (grad_mixed * recurrent_average * gate_sig * (1.0 - gate_sig)).astype(jnp.bfloat16)
    grad_wkv = grad_mixed * gate_sig
    adjoint_dividend = grad_wkv / accumulated_sum
    grad_denom = -grad_wkv * recurrent_average / accumulated_sum
    following_dividend, next_denom, lead_numer, lead_denom = reverse_sweep(
        adjoint_dividend, grad_denom, persisting_indicator, shrink
    )
    behind = prefix((lead_numer, lead_denom, length, cut), "seq", combine, identity, True)
    after = jnp.concatenate([flags[:, 1:], jnp.zeros_like(flags[:, :1])], axis=1)
    later_alive = 1.0 - lax.cummax(after, axis=1, reverse=True)
    falling = jnp.exp(-(block_len - 1.0 - positions)[:, None] * fading_multiplier[None, :])
    following_dividend = (
        following_dividend + later_alive[..., None] * falling[None] * behind[0][:, None, :]
    )
    next_denom = next_denom + later_alive[..., None] * falling[None] * behind[1][:, None, :]
    immediate_term = adjoint_dividend * payload_table_lines + grad_denom
    grad_keys = (
        exponentiated_lookup * (following_dividend * payload_table_lines + next_denom)
        + reward_scaled_pairs * immediate_term
    ).astype(jnp.bfloat16)
    adjoint_payloads = (
        exponentiated_lookup * following_dividend + reward_scaled_pairs * adjoint_dividend
    ).astype(jnp.bfloat16)
    present_reward_adjoint = jnp.sum(reward_scaled_pairs * immediate_term, axis=(0, 1))
    decay_grad = -shrink * jnp.sum(
        following_dividend * running_dividend + next_denom * running_divisor, axis=(0, 1)
    )
    key_grad = outer_sum(key_in, grad_keys)
    value_grad = outer_sum(value_in, adjoint_payloads)
    gate_grad = outer_sum(gate_in, grad_gates)
    grad_key_in = product_back(grad_keys, full_key)
    grad_value_in = product_back(adjoint_payloads, full_value)
    grad_gate_in = product_back(grad_gates, full_gate)
    key_ratio_grad = jnp.sum(grad_key_in * spread_a, axis=(0, 1))
    value_ratio_grad = jnp.sum(grad_value_in * spread_a, axis=(0, 1))
    gate_ratio_grad = jnp.sum(grad_gate_in * spread_a, axis=(0, 1))
    grad_before_a = (
        grad_key_in * (1.0 - ratio_key)
        + grad_value_in * (1.0 - ratio_value)
        + grad_gate_in * (1.0 - ratio_gate)
    ) * persisting_indicator[..., None]
    arriving_ga = from_behind(grad_before_a[:, :1, :], "seq", -1)
    grad_normed_a = (
        grad_key_in * ratio_key
        + grad_value_in * ratio_value
        + grad_gate_in * ratio_gate
        + attach_next(grad_before_a, arriving_ga)
    )
    grad_from_a, attn_gain_grad, attn_bias_grad = norm_back(
        grad_normed_a, unit_a, factor_a, gain_first
    )
    tokens_grad = grad_first + grad_from_a
    slots = lambda g: g.reshape(-1, 24, WIDE).astype(BF)
    n = lax.axis_size("seq") * 4
    zeros = jnp.zeros((n, 8, WIDE), BF)
    packed = jnp.concatenate([slots(key_grad), slots(value_grad), slots(gate_grad), zeros, slots(output_grad), slots(select_grad)]
        + [slots(expand_grad[:, i * WIDE : (i + 1) * WIDE]) for i in range(4)], axis=1)
    out = scatter_call(packed.reshape(depth, 2, 4, ROWS_MAIN, WIDE), contract_grad.astype(BF).reshape(depth, 2, 4, ROWS_LAST, WIDE), depth)
    vec = jnp.stack([attn_gain_grad, attn_bias_grad, chan_gain_grad, chan_bias_grad, key_ratio_grad, value_ratio_grad, gate_ratio_grad,
        expand_ratio_grad, select_ratio_grad, decay_grad, present_reward_adjoint])
    vec = lax.psum_scatter(vec, ("seq", "batch"), scatter_dimension=1, tiled=True)
    shares = [out[0:24], out[24:48], out[48:72], out[80:104], jnp.concatenate([out[128 + 24 * i : 152 + 24 * i] for i in range(4)], axis=1),
        out[104:128], out[224:320]] + [vec[i] for i in range(11)]
    return (
        block_out,
        tokens_grad,
        shares[0],
        shares[1],
        shares[2],
        shares[3],
        shares[4],
        shares[5],
        shares[6],
        shares[7],
        shares[8],
        shares[9],
        shares[10],
        shares[11],
        shares[12],
        shares[13],
        shares[14],
        shares[15],
        shares[16],
        shares[17],
    )


def solution(mesh):
    fits = mesh.shape["seq"] == 8 and mesh.shape["batch"] == 4
    return jax.shard_map(
        fast_body if fits else body,
        mesh=mesh,
        in_specs=(
            P("batch", "seq", None),
            P("batch", "seq"),
            P(("seq", "batch"), None),
            P(("seq", "batch"), None),
            P(("seq", "batch"), None),
            P(("seq", "batch"), None),
            P(("seq", "batch"), None),
            P(("seq", "batch"), None),
            P(("seq", "batch"), None),
            P(("seq", "batch")),
            P(("seq", "batch")),
            P(("seq", "batch")),
            P(("seq", "batch")),
            P(("seq", "batch")),
            P(("seq", "batch")),
            P(("seq", "batch")),
            P(("seq", "batch")),
            P(("seq", "batch")),
            P(("seq", "batch")),
            P(("seq", "batch")),
            P("batch", "seq", None),
        ),
        out_specs=(
            P("batch", "seq", None),
            P("batch", "seq", None),
            P(("seq", "batch"), None),
            P(("seq", "batch"), None),
            P(("seq", "batch"), None),
            P(("seq", "batch"), None),
            P(("seq", "batch"), None),
            P(("seq", "batch"), None),
            P(("seq", "batch"), None),
            P(("seq", "batch")),
            P(("seq", "batch")),
            P(("seq", "batch")),
            P(("seq", "batch")),
            P(("seq", "batch")),
            P(("seq", "batch")),
            P(("seq", "batch")),
            P(("seq", "batch")),
            P(("seq", "batch")),
            P(("seq", "batch")),
            P(("seq", "batch")),
        ),
        check_vma=False,
    )
```

```python
import jax
import jax.numpy as jnp
from jax import lax
from jax.experimental import pallas as pl
from jax.experimental.pallas import tpu as pltpu
from jax.sharding import PartitionSpec as P

BOTH = ("seq", "batch")
MESH = pl.DeviceIdType.MESH
BF = jnp.bfloat16
F32 = jnp.float32
WIDE = 768
ROWS_MAIN = 224
ROWS_LAST = 96
GATHER_CHUNKS = ((0, 0, 80, 48), (0, 80, 48, 16), (0, 128, 48, 32), (0, 176, 48, 16), (1, 0, 48, 32), (1, 48, 48, 16))
SCATTER_CHUNKS = ((1, 0, 48, 32), (1, 48, 48, 16), (0, 128, 48, 32), (0, 176, 48, 16), (0, 80, 48, 16), (0, 0, 80, 48))
COUNT = len(GATHER_CHUNKS)


class Place:
    def __init__(self):
        self.s = lax.axis_index("seq")
        self.b = lax.axis_index("batch")
        self.z, self.c = self.s // 2, self.s % 2
        y, x = self.b // 2, self.b % 2
        self.bx, self.by, self.bd = y * 2 + 1 - x, (1 - y) * 2 + x, (1 - y) * 2 + 1 - x
        self.depth = lax.axis_size("seq") // 2
        self.x, self.y = (self.s, self.bx), (self.s, self.by)
        self.core = (self.z * 2 + 1 - self.c, self.b)

    def along(self, step):
        z = lax.rem(self.z + step, self.depth)
        return z, (z * 2 + self.c, self.b)

    def back(self, step):
        return lax.rem(self.z + self.depth - step, self.depth)


def rdma(src, dst, sems, send, recv, to):
    return pltpu.make_async_remote_copy(
        src_ref=src, dst_ref=dst, send_sem=sems.at[send], recv_sem=sems.at[recv], device_id=to, device_id_type=MESH
    )


def enter(place):
    barrier = pltpu.get_barrier_semaphore()
    count = 0
    peers = [place.x, place.y, place.core] + [place.along(d)[1] for d in range(1, place.depth)]
    for peer in peers:
        pl.semaphore_signal(barrier, inc=1, device_id=peer, device_id_type=MESH)
    pl.semaphore_wait(barrier, len(peers))


class Gather:
    def __init__(self, place, arrays, sems):
        self.p, self.arrays, self.sems = place, arrays, sems

    def copies(self, k):
        p, sems = self.p, self.sems.at[k]
        a, r0, n, nx = GATHER_CHUNKS[k]
        ref = self.arrays[a]
        whole, part_x, part_y = pl.ds(r0, n), pl.ds(r0, nx), pl.ds(r0 + nx, n - nx)
        own = ref.at[p.z, p.c, p.b, whole]
        col = lambda c, b, rows: ref.at[:, c, b, rows]
        out = {}
        for d in range(1, p.depth):
            out["z", d] = rdma(own, own, sems, 2 * d - 2, 2 * d - 1, p.along(d)[1])
        out["x"] = rdma(col(p.c, p.b, whole), col(p.c, p.b, whole), sems, 6, 7, p.x)
        out["y"] = rdma(col(p.c, p.b, whole), col(p.c, p.b, whole), sems, 8, 9, p.y)
        out["dx"] = rdma(col(p.c, p.by, part_x), col(p.c, p.by, part_x), sems, 10, 11, p.x)
        out["dy"] = rdma(col(p.c, p.bx, part_y), col(p.c, p.bx, part_y), sems, 12, 13, p.y)
        for j, b in enumerate((p.b, p.bx, p.by)):
            pass
        out["c", 0] = rdma(col(p.c, p.b, whole), col(p.c, p.b, whole), sems, 14, 15, p.core)
        out["c", 1] = rdma(col(p.c, p.bx, whole), col(p.c, p.bx, whole), sems, 16, 17, p.core)
        out["c", 2] = rdma(col(p.c, p.by, whole), col(p.c, p.by, whole), sems, 18, 19, p.core)
        out["c", 3] = rdma(col(p.c, p.bd, whole), col(p.c, p.bd, whole), sems, 20, 21, p.core)
        return out

    def arrivals(self, k):
        p, sems = self.p, self.sems.at[k]
        a, r0, n, nx = GATHER_CHUNKS[k]
        ref = self.arrays[a]
        whole, part_x, part_y = pl.ds(r0, n), pl.ds(r0, nx), pl.ds(r0 + nx, n - nx)
        col = lambda c, b, rows: ref.at[:, c, b, rows]
        at = lambda view, recv, to: rdma(view, view, sems, recv - 1, recv, to)
        out = {}
        for d in range(1, p.depth):
            out["z", d] = at(ref.at[p.back(d), p.c, p.b, whole], 2 * d - 1, p.along(d)[1])
        out["x"] = at(col(p.c, p.bx, whole), 7, p.x)
        out["y"] = at(col(p.c, p.by, whole), 9, p.y)
        out["dx"] = at(col(p.c, p.bd, part_x), 11, p.x)
        out["dy"] = at(col(p.c, p.bd, part_y), 13, p.y)
        for j, b in enumerate((p.b, p.bx, p.by, p.bd)):
            out["c", j] = at(col(1 - p.c, b, whole), 15 + 2 * j, p.core)
        return out

    def stage(self, number, k):
        if not 0 <= k < COUNT:
            return
        send, come = self.copies(k), self.arrivals(k)
        if number == 0:
            for d in range(1, self.p.depth):
                send["z", d].start()
        elif number == 1:
            for d in range(1, self.p.depth):
                come["z", d].wait_recv()
            send["x"].start()
            send["y"].start()
            send["c", 0].start()
        elif number == 2:
            come["x"].wait_recv()
            come["y"].wait_recv()
            send["dx"].start()
            send["dy"].start()
            send["c", 1].start()
            send["c", 2].start()
        elif number == 3:
            come["dx"].wait_recv()
            come["dy"].wait_recv()
            send["c", 3].start()
        elif number == 4:
            for j in range(4):
                come["c", j].wait_recv()
        elif number == 5:
            for copy in send.values():
                copy.wait_send()

    def tick(self, t):
        for number in range(5):
            self.stage(number, t - number)


class Scatter:
    def __init__(self, place, packed, from_core, near, diag, line, out, sems, credits):
        self.p, self.packed, self.from_core, self.near = place, packed, from_core, near
        self.diag, self.line, self.out, self.sems, self.credits = diag, line, out, sems, credits

    def stage(self, number, k):
        p, sems = self.p, self.sems.at[k]
        a, r0, n, nx = SCATTER_CHUNKS[k]
        ref, slot, depth = self.packed[a], k % 2, p.depth
        f0 = r0 if a == 0 else r0 + ROWS_MAIN
        whole, part_x, part_y = pl.ds(r0, n), pl.ds(r0, nx), pl.ds(r0 + nx, n - nx)
        core = lambda: rdma(ref.at[:, 1 - p.c, :, whole], self.from_core.at[slot, :, :, pl.ds(0, n)], sems, 0, 1, p.core)
        diag_x = lambda: rdma(ref.at[:, p.c, p.bd, part_x], self.diag.at[slot, :, pl.ds(0, nx)], sems, 2, 3, p.x)
        diag_y = lambda: rdma(ref.at[:, p.c, p.bd, part_y], self.diag.at[slot, :, pl.ds(nx, n - nx)], sems, 4, 5, p.y)
        near_x = lambda: rdma(ref.at[:, p.c, p.bx, whole], self.near.at[slot, 0, :, pl.ds(0, n)], sems, 6, 7, p.x)
        near_y = lambda: rdma(ref.at[:, p.c, p.by, whole], self.near.at[slot, 1, :, pl.ds(0, n)], sems, 8, 9, p.y)

        def along(d):
            z, to = p.along(d)
            return rdma(ref.at[z, p.c, p.b, whole], self.line.at[d - 1, pl.ds(f0, n)], sems, 8 + 2 * d, 9 + 2 * d, to)

        def ready(*which):
            if k >= 2:
                for w in which:
                    pl.semaphore_wait(self.credits.at[w], 1)

        def free(which, to):
            if k + 2 < COUNT:
                pl.semaphore_signal(self.credits.at[which], inc=1, device_id=to, device_id_type=MESH)

        if number == 0:
            ready(0)
            core().start()
        elif number == 1:
            core().wait_recv()

            @pl.loop(0, depth * 4)
            def _(i):
                z, b = i // 4, i % 4
                ref[z, p.c, b, r0 : r0 + n] = (
                    ref[z, p.c, b, r0 : r0 + n].astype(F32) + self.from_core[slot, z, b, 0:n].astype(F32)
                ).astype(BF)

            free(0, p.core)
            ready(1, 2)
            diag_x().start()
            diag_y().start()
        elif number == 2:
            diag_x().wait_recv()
            diag_y().wait_recv()

            @pl.loop(0, depth)
            def _(z):
                for b, s0, m in ((p.by, 0, nx), (p.bx, nx, n - nx)):
                    ref[z, p.c, b, r0 + s0 : r0 + s0 + m] = (
                        ref[z, p.c, b, r0 + s0 : r0 + s0 + m].astype(F32) + self.diag[slot, z, s0 : s0 + m].astype(F32)
                    ).astype(BF)

            free(1, p.x)
            free(2, p.y)
            ready(3, 4)
            near_x().start()
            near_y().start()
        elif number == 3:
            near_x().wait_recv()
            near_y().wait_recv()

            @pl.loop(0, depth)
            def _(z):
                ref[z, p.c, p.b, r0 : r0 + n] = (
                    ref[z, p.c, p.b, r0 : r0 + n].astype(F32)
                    + self.near[slot, 0, z, 0:n].astype(F32)
                    + self.near[slot, 1, z, 0:n].astype(F32)
                ).astype(BF)

            free(3, p.x)
            free(4, p.y)
            for d in range(1, depth):
                along(d).start()
        elif number == 4:
            for d in range(1, depth):
                along(d).wait_recv()
            total = ref[p.z, p.c, p.b, r0 : r0 + n].astype(F32)
            for d in range(1, depth):
                total = total + self.line[d - 1, f0 : f0 + n].astype(F32)
            self.out[f0 : f0 + n] = total
        elif number == 5:
            for each in (core, diag_x, diag_y, near_x, near_y):
                each().wait_send()
            for d in range(1, depth):
                along(d).wait_send()


EPSILON = 1e-05
TOK = 1024
SEQS = 4
SPAN = 256
STEPS = 32
SEG = 8
LANE = 128
WINDOW = 256
VECTORS = 11


def window_of(i):
    return min(i * 24 // LANE, WIDE // LANE - 2) * LANE


def spread_lanes(v):
    return jnp.concatenate([v] * (WIDE // LANE), axis=1)


def unit_norm(v):
    center = v - jnp.mean(v, axis=-1, keepdims=True)
    factor = lax.rsqrt(jnp.mean(center * center, axis=-1, keepdims=True) + EPSILON)
    return center * factor, factor


def sigmoid(v):
    return 1.0 / (1.0 + jnp.exp(-v))


def first_rows(halo_row, last_group):
    moved = pltpu.roll(last_group, 1, axis=0)
    at_top = lax.broadcasted_iota(jnp.int32, moved.shape, 0) == 0
    return jnp.where(at_top, halo_row, moved)


def permute_in(src, dst, tmp):
    @pl.loop(0, SEQS)
    def _(j):
        base = pl.multiple_of(j * SPAN, SPAN)
        for l in range(WIDE // LANE):
            tmp[l] = src[pl.ds(base, SPAN), l * LANE : (l + 1) * LANE].astype(F32)

        @pl.loop(0, STEPS // 2)
        def _(s):
            for l in range(WIDE // LANE):
                two = jnp.concatenate([tmp[l, pl.ds(2 * s, SEG, stride=STEPS), :], tmp[l, pl.ds(2 * s + 1, SEG, stride=STEPS), :]], axis=0)
                dst[pl.ds(pl.multiple_of(base + s * 16, 16), 16), l * LANE : (l + 1) * LANE] = two.astype(BF)


class Spill:
    def __init__(self, sems):
        self.sems, self.copies, self.used = sems, {}, 0

    def start(self, name, src, dst):
        self.copies[name] = pltpu.make_async_copy(src, dst, self.sems.at[self.used])
        self.used += 1
        self.copies[name].start()

    def wait(self, *names):
        for name in names or list(self.copies):
            self.copies.pop(name).wait()


class Line:
    def __init__(self, place):
        self.p = place
        self.n = lax.axis_size("seq")

    def all(self, buf, sems):
        p, copies = self.p, []
        for d in range(1, self.n):
            to = (lax.rem(p.s + d, self.n), p.b)
            copies.append(rdma(buf.at[p.s], buf.at[p.s], sems, d, self.n + d, to))
        return copies

    def shift(self, src, dst, sems, step):
        return rdma(src, dst, sems, 0, 1, (lax.rem(self.p.s + self.n + step, self.n), self.p.b))


def relayout(st, dst, depth, r0, n, targets):
    @pl.loop(0, depth * 2)
    def _(i):
        z, c = i // 2, i % 2
        slabs = [st[z, c, b, r0 : r0 + n].astype(F32) for b in range(4)]
        rows = pl.ds(pl.multiple_of(i * 96, 96), 96)
        for index, at in targets:
            dst[index, rows] = jnp.concatenate([v[at : at + 24] for v in slabs], axis=0).astype(BF)


def matmul(left, right, out, rows=512):
    @pl.loop(0, TOK // rows)
    def _(i):
        r = pl.ds(pl.multiple_of(i * rows, rows), rows)
        out[r] = jnp.dot(left[r], right[...], preferred_element_type=F32)


def forward_kernel(x_in, keep_in, up_in, vec_in, wk, wv, wr, wo, ws, we_in, wc_in,
                   o_w, o_e, o_c, o_ki, o_spa, o_spb, o_mixed, o_ei, o_si, o_gc, o_gs, o_xp, o_up, o_sq, o_pkc,
                   o_kvg, o_nd, o_first, o_vec, o_alive, o_bo,
                   st, cw, wd, we, u0, xp, u1, gyp, tmp, keep, xa, ki, kvg, nd, spb, vb, vec, states, alive, seg, carry, hx, hx_got, hb, hb_got,
                   gsems, vsems, asems, ssems, hsems, lsems):
    place = Place()
    line = Line(place)
    depth = place.depth
    devices = depth * 8
    me = place.s * 4 + place.b
    spill = Spill(lsems)
    spill.start("x", x_in, u0)
    spill.start("keep", keep_in, keep)
    spill.start("up", up_in, u1)
    barrier = pltpu.get_barrier_semaphore()
    for d in range(1, devices):
        other = lax.rem(me + d, devices)
        pl.semaphore_signal(barrier, inc=1, device_id=(other // 4, other % 4), device_id_type=MESH)
    z, c, b = place.z, place.c, place.b
    as32 = lambda ref: ref[...].astype(F32)
    join = lambda *v: jnp.concatenate(v, axis=0).astype(BF)
    st[z, c, b, 0:48] = join(as32(wk), as32(wv))
    st[z, c, b, 48:80] = join(as32(wr), jnp.zeros((8, WIDE), F32))
    st[z, c, b, 80:128] = join(as32(wo), as32(ws))
    e = as32(we_in)
    for h in range(2):
        st[z, c, b, 128 + 48 * h : 176 + 48 * h] = join(e[:, 2 * h * WIDE : (2 * h + 1) * WIDE], e[:, (2 * h + 1) * WIDE : (2 * h + 2) * WIDE])
    cw[z, c, b] = wc_in[...]
    start = me * 24
    low = jnp.minimum(start // LANE, WIDE // LANE - 2) * LANE
    wide = jnp.concatenate([vec_in[...], jnp.zeros((16, LANE), F32)], axis=1)
    vb[me] = pltpu.roll(wide, start - low, axis=1).astype(BF)
    pl.semaphore_wait(barrier, devices - 1)

    gather = Gather(place, (st, cw), gsems)
    vsend = []
    for d in range(1, devices):
        other = lax.rem(me + d, devices)
        copy = rdma(vb.at[me], vb.at[me], vsems, d, devices + d, (other // 4, other % 4))
        copy.start()
        vsend.append(copy)
    gather.tick(0)

    spill.wait("x")
    for j in range(SEQS):
        hx[j : j + 1] = u0[SPAN * j + SPAN - 16 : SPAN * j + SPAN].astype(F32)[15:16]
    hx[SEQS:8] = jnp.zeros((8 - SEQS, WIDE), F32)
    send_hx = line.shift(hx, hx_got, hsems.at[0], 1)
    send_hx.start()
    spill.wait("keep")
    for j in range(SEQS):
        low_keep = jnp.min(keep[SPAN * j : SPAN * (j + 1)], axis=0, keepdims=True)
        alive[place.s, j : j + 1] = low_keep
        alive[place.s, SEQS + j : SEQS + j + 1] = low_keep
    send_alive = line.all(alive, asems)
    for copy in send_alive:
        copy.start()
    permute_in(u0, xp, tmp)
    spill.start("xp", xp, o_xp)
    for d in range(1, devices):
        other = lax.rem(me + devices - d, devices)
        rdma(vb.at[other], vb.at[other], vsems, d, devices + d, (other // 4, other % 4)).wait_recv()
    vec[...] = jnp.zeros_like(vec)
    for i in range(devices):
        w = window_of(i)
        vec[:, w : w + WINDOW] += vb[i].astype(F32)
    spill.start("vec", vec, o_vec)
    gather.tick(1)

    gain_a, bias_a = vec[0:1], vec[1:2]

    def norm_rows(j, rows_of, gain, bias):
        @pl.loop(0, SPAN // 16)
        def _(t):
            v = rows_of(pl.ds(pl.multiple_of(j * SPAN + t * 16, 16), 16))
            xa[j, pl.ds(pl.multiple_of(8 + t * 16, 8), 16)] = unit_norm(v)[0] * gain + bias

    @pl.loop(0, SEQS)
    def _(j):
        norm_rows(j, lambda r: xp[r].astype(F32), gain_a, bias_a)

    not_first = jnp.where(place.s > 0, 1.0, 0.0).astype(F32)
    line.shift(hx, hx_got, hsems.at[0], 1).wait_recv()
    before = (unit_norm(hx_got[...])[0] * gain_a + bias_a) * not_first
    for j in range(SEQS):
        xa[j, 0:8] = first_rows(before[j : j + 1], xa[j, SPAN : SPAN + 8])

    def blends(j, ratios, outs, spread_out):
        @pl.loop(0, SPAN // 16)
        def _(t):
            r = pl.ds(pl.multiple_of(j * SPAN + t * 16, 16), 16)
            prev = xa[j, pl.ds(pl.multiple_of(t * 16, 8), 16)] * spread_lanes(keep[r])
            spread = xa[j, pl.ds(pl.multiple_of(8 + t * 16, 8), 16)] - prev
            spread_out[r] = spread.astype(BF)
            for ratio, out in zip(ratios, outs):
                out[r] = (prev + spread * ratio).astype(BF)

    gather.tick(2)

    @pl.loop(0, SEQS)
    def _(j):
        blends(j, [vec[4:5], vec[5:6], vec[6:7]], [ki.at[0], ki.at[1], ki.at[2]], u0)

    spill.start("ki", ki, o_ki)
    spill.start("spa", u0, o_spa)
    gather.tick(3)
    spill.wait("up")
    permute_in(u1, gyp, tmp)
    spill.start("gyp", gyp, o_up)
    gather.tick(4)
    relayout(st, wd, depth, 0, 48, ((0, 0), (1, 24)))
    relayout(st, wd, depth, 48, 32, ((2, 0),))
    for m in range(3):
        matmul(ki.at[m], wd.at[m], kvg.at[m])
    spill.start("kvg", kvg, o_kvg)
    gather.tick(5)

    shrink = jnp.exp(-vec[9:10])
    bonus = vec[10:11]
    shrink8 = jnp.broadcast_to(shrink, (SEG, WIDE))
    row = lax.broadcasted_iota(jnp.int32, (SEG, WIDE), 0)

    @pl.loop(0, SEQS)
    def _(j):
        def step(s, state):
            decay, numer, denom = state
            r = pl.ds(pl.multiple_of(j * SPAN + s * SEG, SEG), SEG)
            m = spread_lanes(keep[r]) * shrink8
            ek = jnp.exp(kvg[0, r])
            return decay * m, numer * m + ek * kvg[1, r], denom * m + ek

        zero = jnp.zeros((SEG, WIDE), F32)
        decay, numer, denom = lax.fori_loop(0, STEPS, step, (zero + 1.0, zero, zero), unroll=4)
        for d in (1, 2, 4):
            top = row < d
            numer, denom, decay = (
                numer + decay * jnp.where(top, 0.0, pltpu.roll(numer, d, axis=0)),
                denom + decay * jnp.where(top, 0.0, pltpu.roll(denom, d, axis=0)),
                decay * jnp.where(top, 1.0, pltpu.roll(decay, d, axis=0)),
            )
        states[place.s, pl.ds(j, 1)] = numer[SEG - 1 : SEG]
        states[place.s, pl.ds(SEQS + j, 1)] = denom[SEG - 1 : SEG]
        seg[j, 0] = jnp.where(row < 1, 1.0, pltpu.roll(decay, 1, axis=0))
        seg[j, 1] = jnp.where(row < 1, 0.0, pltpu.roll(numer, 1, axis=0))
        seg[j, 2] = jnp.where(row < 1, 0.0, pltpu.roll(denom, 1, axis=0))

    send_states = line.all(states, ssems)
    for copy in send_states:
        copy.start()
    relayout(st, wd, depth, 80, 48, ((3, 0), (4, 24)))
    spill.start("w", wd, o_w)
    for d in range(1, line.n):
        src = lax.rem(place.s + line.n - d, line.n)
        rdma(alive.at[src], alive.at[src], asems, d, line.n + d, (src, b)).wait_recv()
        rdma(states.at[src], states.at[src], ssems, d, line.n + d, (src, b)).wait_recv()
    spill.start("alive", alive, o_alive)
    whole = jnp.exp(-float(SPAN) * vec[9:10])
    arrived = jnp.zeros((SEG, WIDE), F32)
    for src in range(7):
        after = spread_lanes(alive[src]) * whole * arrived + states[src]
        arrived = jnp.where(src < place.s, after, arrived)
    carry[...] = arrived

    for j in range(SEQS):
        slot = j % 2
        if j >= 2:
            spill.wait(("nd", j - 2))
        into = nd.at[slot]
        base = j * SPAN
        numer0 = seg[j, 0] * carry[j : j + 1] + seg[j, 1]
        denom0 = seg[j, 0] * carry[SEQS + j : SEQS + j + 1] + seg[j, 2]

        def steps(i, state):
            numer, denom = state
            mixes = []
            for q in range(2):
                lo = pl.multiple_of(i * 16 + q * 8, 8)
                r = pl.ds(pl.multiple_of(base + lo, 8), SEG)
                kept = spread_lanes(keep[r])
                numer, denom = numer * kept, denom * kept
                into[0, pl.ds(lo, SEG)] = numer
                into[1, pl.ds(lo, SEG)] = denom
                k, v = kvg[0, r], kvg[1, r]
                now, ek = jnp.exp(bonus + k), jnp.exp(k)
                wkv = (numer + now * v) / (denom + now)
                mixes.append(sigmoid(kvg[2, r]) * wkv)
                numer, denom = shrink8 * numer + ek * v, shrink8 * denom + ek
            u1[pl.ds(pl.multiple_of(base + i * 16, 16), 16)] = jnp.concatenate(mixes, axis=0).astype(BF)
            return numer, denom

        lax.fori_loop(0, STEPS // 2, steps, (numer0, denom0))
        spill.start(("nd", j), into, o_nd.at[:, pl.ds(base, SPAN)])
        if j == 1:
            gather.tick(6)
    spill.start("mixed", u1, o_mixed)
    spill.wait("kvg")
    first = kvg.at[0]

    @pl.loop(0, TOK // 256)
    def _(i):
        r = pl.ds(pl.multiple_of(i * 256, 256), 256)
        first[r] = xp[r].astype(F32) + jnp.dot(u1[r], wd[3], preferred_element_type=F32)

    spill.start("first", first, o_first)

    @pl.loop(0, SEQS)
    def _(j):
        norm_rows(j, lambda r: first[r], vec[2:3], vec[3:4])

    for j in range(SEQS):
        hb[j : j + 1] = xa[j, SPAN : SPAN + 8][7:8]
    hb[SEQS:8] = jnp.zeros((8 - SEQS, WIDE), F32)
    send_hb = line.shift(hb, hb_got, hsems.at[1], 1)
    send_hb.start()
    gather.stage(0, COUNT)
    spill.wait("ki")
    send_hb.wait_recv()
    before_b = hb_got[...] * not_first
    for j in range(SEQS):
        xa[j, 0:8] = first_rows(before_b[j : j + 1], xa[j, SPAN : SPAN + 8])

    @pl.loop(0, SEQS)
    def _(j):
        blends(j, [vec[7:8], vec[8:9]], [ki.at[0], ki.at[1]], spb)

    spill.start("spb", spb, o_spb)
    spill.start("ei", ki.at[0], o_ei)
    spill.start("si", ki.at[1], o_si)
    sig = kvg.at[1]

    @pl.loop(0, TOK // 256)
    def _(i):
        r = pl.ds(pl.multiple_of(i * 256, 256), 256)
        chosen = sigmoid(jnp.dot(ki[1, r], wd[4], preferred_element_type=F32))
        sig[r] = chosen
        ki[2, r] = (gyp[r].astype(F32) * chosen).astype(BF)

    spill.start("gc", ki.at[2], o_gc)
    relayout(st, we, depth, 128, 48, ((0, 0), (1, 24)))
    gather.tick(7)
    relayout(st, we, depth, 176, 48, ((2, 0), (3, 24)))
    spill.start("e", we, o_e)
    for k in range(4):
        gather.stage(5, k)

    def square(f):
        @pl.loop(0, depth)
        def _(i):
            r = pl.ds(pl.multiple_of(i * 256, 256), 256)
            positive = jnp.maximum(jnp.dot(ki[0, r], we[f], preferred_element_type=F32), 0.0)
            st[i, :, :, 96 + 32 * f : 128 + 32 * f] = (positive * positive).astype(BF).reshape(2, 4, 32, WIDE)

    def contract_grad(f):
        left = st[:, :, :, 96 + 32 * f : 128 + 32 * f].reshape(TOK, WIDE)
        for h in range(2):
            got = lax.dot_general(left[:, 384 * h : 384 * (h + 1)], ki[2], (((0,), (0,)), ((), ())), preferred_element_type=F32)
            st[f, h, :, 0:96] = got.astype(BF).reshape(4, 96, WIDE)

    square(0)
    square(1)
    gather.tick(8)
    square(2)
    square(3)
    contract_grad(0)
    contract_grad(1)
    gather.tick(9)
    spill.start("c", cw, o_c)
    contract_grad(2)
    contract_grad(3)
    spill.start("pkc", st.at[:, :, :, pl.ds(0, 96)], o_pkc)
    spill.start("sq", st.at[:, :, :, pl.ds(96, 128)], o_sq)
    spill.wait("mixed", "spa")

    @pl.loop(0, depth)
    def _(i):
        r = pl.ds(pl.multiple_of(i * 256, 256), 256)
        total = jnp.zeros((256, WIDE), F32)
        for f in range(4):
            part = st[i, :, :, 96 + 32 * f : 128 + 32 * f].reshape(256, WIDE)
            total = total + jnp.dot(part, cw[f].reshape(WIDE, WIDE), preferred_element_type=F32)
        chosen = sig[r]
        u1[r] = (first[r] + chosen * total).astype(BF)
        u0[r] = (gyp[r].astype(F32) * total * chosen * (1.0 - chosen)).astype(BF)

    spill.start("gs", u0, o_gs)
    spill.start("bo", u1, o_bo)
    for copy in vsend + send_alive + send_states + [send_hx, send_hb]:
        copy.wait_send()
    for k in range(4, COUNT):
        gather.stage(5, k)
    spill.wait()


def forward_call(x, keep, up, vec, shards, depth):
    hbm, vmem = pl.BlockSpec(memory_space=pl.ANY), pl.BlockSpec(memory_space=pltpu.VMEM)
    s = jax.ShapeDtypeStruct
    seq = depth * 2
    devices = depth * 8
    rows = (TOK, WIDE)
    outs = dict(
        w=s((5, WIDE, WIDE), BF), e=s((4, WIDE, WIDE), BF), c=s((depth, 2, 4, 96, WIDE), BF), ki=s((3,) + rows, BF),
        spa=s(rows, BF), spb=s(rows, BF), mixed=s(rows, BF), ei=s(rows, BF), si=s(rows, BF), gc=s(rows, BF), gs=s(rows, BF),
        xp=s(rows, BF), up=s(rows, BF), sq=s((depth, 2, 4, 128, WIDE), BF), pkc=s((depth, 2, 4, 96, WIDE), BF),
        kvg=s((3,) + rows, F32), nd=s((2,) + rows, F32), first=s(rows, F32), vec=s((16, WIDE), F32), alive=s((seq, 8, LANE), F32),
        bo=s(rows, BF))
    scratch = [
        pltpu.VMEM((depth, 2, 4, ROWS_MAIN, WIDE), BF), pltpu.VMEM((depth, 2, 4, ROWS_LAST, WIDE), BF),
        pltpu.VMEM((5, WIDE, WIDE), BF), pltpu.VMEM((4, WIDE, WIDE), BF),
        pltpu.VMEM(rows, BF), pltpu.VMEM(rows, BF), pltpu.VMEM(rows, BF), pltpu.VMEM(rows, BF),
        pltpu.VMEM((6, SPAN, LANE), F32), pltpu.VMEM((TOK, LANE), F32), pltpu.VMEM((SEQS, SPAN + 8, WIDE), F32),
        pltpu.VMEM((3,) + rows, BF), pltpu.VMEM((3,) + rows, F32), pltpu.VMEM((2, 2, SPAN, WIDE), F32), pltpu.VMEM(rows, BF),
        pltpu.VMEM((devices, 16, WINDOW), BF), pltpu.VMEM((16, WIDE), F32), pltpu.VMEM((seq, 8, WIDE), F32), pltpu.VMEM((seq, 8, LANE), F32),
        pltpu.VMEM((SEQS, 3, SEG, WIDE), F32), pltpu.VMEM((8, WIDE), F32),
        pltpu.VMEM((8, WIDE), F32), pltpu.VMEM((8, WIDE), F32), pltpu.VMEM((8, WIDE), F32), pltpu.VMEM((8, WIDE), F32),
        pltpu.SemaphoreType.DMA((COUNT, 22)), pltpu.SemaphoreType.DMA((2 * devices,)), pltpu.SemaphoreType.DMA((2 * seq,)),
        pltpu.SemaphoreType.DMA((2 * seq,)), pltpu.SemaphoreType.DMA((2, 2)), pltpu.SemaphoreType.DMA((32,)),
    ]
    got = pl.pallas_call(
        forward_kernel,
        out_shape=tuple(outs.values()),
        in_specs=[hbm, hbm, hbm] + [vmem] * 8,
        out_specs=tuple(hbm for _ in outs),
        scratch_shapes=scratch,
        compiler_params=pltpu.CompilerParams(collective_id=0, has_side_effects=True, vmem_limit_bytes=62 << 20),
        cost_estimate=pl.CostEstimate(flops=2 * 1024 * 12 * 768 * 768, bytes_accessed=60 << 20, transcendentals=0),
    )(x, keep, up, vec, *shards)
    return dict(zip(outs, got))


NT = (((1,), (1,)), ((), ()))
TN = (((0,), (0,)), ((), ()))


def backward_kernel(i_w, i_e, i_c, i_ki, i_spa, i_spb, i_mixed, i_ei, i_si, i_gc, i_gs, i_xp, i_up, i_sq, i_pkc, i_kvg, i_nd, i_first, i_vec,
                    i_alive, i_keep,
                    o_out, o_tokens, o_vec,
                    main, last, from_core, near, diag, lines, out, we, cw, p, q, xg, keep, vec, alive, states, seg, vg, vr, hx, hx_got, hb, hb_got,
                    rsems, credits, ssems, hsems, zsems, lsems):
    place = Place()
    line = Line(place)
    depth = place.depth
    z, c, b = place.z, place.c, place.b
    spill = Spill(lsems)
    spill.start("pkc", i_pkc, last)
    spill.start("cw", i_c, cw)
    spill.start("keep", i_keep, keep)
    spill.start("vec", i_vec, vec)
    spill.start("alive", i_alive, alive)
    spill.start("we", i_e, we)
    barrier = pltpu.get_barrier_semaphore()
    peers = [place.x, place.y] + [(lax.rem(place.s + d, line.n), b) for d in range(1, line.n)]
    for peer in peers:
        pl.semaphore_signal(barrier, inc=1, device_id=peer, device_id_type=MESH)
    pl.semaphore_wait(barrier, len(peers))
    scatter = Scatter(place, (main, last), from_core, near, diag, lines, out, rsems, credits)
    run = scatter.stage
    vg[...] = jnp.zeros_like(vg)
    not_last = jnp.where(place.s < line.n - 1, 1.0, 0.0).astype(F32)

    def pack(first, second, r0):
        @pl.loop(0, depth * 2)
        def _(i):
            rows = pl.ds(pl.multiple_of(i * 96, 96), 96)
            u = first[rows].astype(F32)
            v = None if second is None else second[rows].astype(F32)
            for k in range(4):
                mine = u[24 * k : 24 * k + 24]
                other = jnp.zeros((8, WIDE), F32) if v is None else v[24 * k : 24 * k + 24]
                joined = jnp.concatenate([mine, other], axis=0)
                main[i // 2, i % 2, k, r0 : r0 + joined.shape[0]] = joined.astype(BF)

    def outer(left, right, into):
        for h in range(2):
            cols = slice(384 * h, 384 * h + 384)
            into[cols] = lax.dot_general(left[:, cols], right[...], TN, preferred_element_type=F32).astype(BF)

    def fold(v):
        return v[0:8] + v[8:16]

    def following_rows(halo):
        for j in range(SEQS):
            moved = pltpu.roll(xg[j, 0:8], SEG - 1, axis=0)
            at_end = lax.broadcasted_iota(jnp.int32, moved.shape, 0) == SEG - 1
            xg[j, SPAN : SPAN + 8] = jnp.where(at_end, halo[j : j + 1], moved)

    def send_first(src, dst, sems):
        for j in range(SEQS):
            src[j : j + 1] = xg[j, 0:8][0:1]
        src[SEQS:8] = jnp.zeros((8 - SEQS, WIDE), F32)
        copy = line.shift(src, dst, sems, -1)
        copy.start()
        return copy

    def norm_back(rows, gain, source, gain_at, bias_at, finish):
        @pl.loop(0, SEQS)
        def _(j):
            def tile(t, sums):
                r = pl.ds(pl.multiple_of(j * SPAN + t * 16, 16), 16)
                grad = rows[r] + xg[j, pl.ds(pl.multiple_of(t * 16 + 8, 8), 16)]
                unit, factor = unit_norm(source(r))
                h = grad * gain
                back = factor * (h - jnp.mean(h, axis=-1, keepdims=True) - unit * jnp.mean(h * unit, axis=-1, keepdims=True))
                finish(r, back)
                return sums[0] + fold(grad * unit), sums[1] + fold(grad)

            zero = jnp.zeros((8, WIDE), F32)
            sums = lax.fori_loop(0, SPAN // 16, tile, (zero, zero))
            vg[gain_at] += sums[0]
            vg[bias_at] += sums[1]

    def channel_mix(gc, ei, si, gs, sqb, ge, gt):
        load = lambda f: spill.start(("sq", f), i_sq.at[:, :, :, pl.ds(32 * f, 32)], sqb.at[f % 2])
        spill.start("gc", i_gc, gc)
        load(0)
        load(1)
        spill.start("ei", i_ei, ei)
        spill.start("si", i_si, si)
        spill.start("gs", i_gs, gs)
        spill.wait("pkc")
        run(0, 0)
        run(0, 1)
        spill.wait("cw", "gc")

        def expand_back(f):
            spill.wait(("sq", f))

            @pl.loop(0, TOK // 256)
            def _(i):
                r = pl.ds(pl.multiple_of(i * 256, 256), 256)
                grad = lax.dot_general(gc[r], cw[f].reshape(WIDE, WIDE), NT, preferred_element_type=F32)
                positive = jnp.sqrt(sqb[f % 2, i].reshape(256, WIDE).astype(F32))
                ge[r] = (2.0 * positive * grad).astype(BF)

            if f + 2 < 4:
                load(f + 2)

        def expand_in_back(f):
            @pl.loop(0, TOK // 512)
            def _(i):
                r = pl.ds(pl.multiple_of(i * 512, 512), 512)
                got = lax.dot_general(ge[r], we[f], NT, preferred_element_type=F32)
                p[r] = got if f == 0 else p[r] + got

        expand_back(0)
        run(1, 0)
        spill.wait("ei", "we")
        outer(ei, ge, gt.at[0])
        run(1, 1)
        run(2, 0)
        expand_in_back(0)
        spill.start("ws", i_w.at[4], we.at[0])
        expand_back(1)
        run(2, 1)
        run(3, 0)
        outer(ei, ge, gt.at[1])
        pack(gt.at[0], gt.at[1], 128)
        run(0, 2)
        expand_in_back(1)
        spill.start("wo", i_w.at[3], we.at[1])
        run(3, 1)
        run(4, 0)
        run(1, 2)
        expand_back(2)
        run(2, 2)
        outer(ei, ge, gt.at[0])
        run(4, 1)
        expand_in_back(2)
        expand_back(3)
        outer(ei, ge, gt.at[1])
        pack(gt.at[0], gt.at[1], 176)
        run(0, 3)
        run(3, 2)
        expand_in_back(3)
        run(1, 3)
        spill.wait("si", "gs", "ws", "wo")
        spill.start("wk", i_w.at[0], we.at[2])
        spill.start("wv", i_w.at[1], we.at[3])
        spill.start("spb", i_spb, gc)
        outer(si, gs, gt.at[1])
        run(2, 3)
        run(4, 2)

        @pl.loop(0, TOK // 512)
        def _(i):
            r = pl.ds(pl.multiple_of(i * 512, 512), 512)
            q[r] = lax.dot_general(gs[r], we[0], NT, preferred_element_type=F32)

        spill.start("wr", i_w.at[2], we.at[0])
        spill.start("gyp", i_up, ge)
        spill.start("mixed", i_mixed, ei)
        spill.wait("keep", "vec", "spb")
        run(3, 3)
        re, rs = vec[7:8], vec[8:9]

        @pl.loop(0, SEQS)
        def _(j):
            def tile(t, sums):
                r = pl.ds(pl.multiple_of(j * SPAN + t * 16, 16), 16)
                ge_in, gs_in, spread = p[r], q[r], gc[r].astype(F32)
                xg[j, pl.ds(pl.multiple_of(t * 16, 16), 16)] = (ge_in * (1.0 - re) + gs_in * (1.0 - rs)) * spread_lanes(keep[r])
                p[r] = ge_in * re + gs_in * rs
                return sums[0] + fold(ge_in * spread), sums[1] + fold(gs_in * spread)

            zero = jnp.zeros((8, WIDE), F32)
            sums = lax.fori_loop(0, SPAN // 16, tile, (zero, zero))
            vg[7] += sums[0]
            vg[8] += sums[1]

        send = send_first(hb, hb_got, hsems.at[0])
        spill.start("first", i_first, q)
        run(4, 3)
        spill.wait("gyp", "mixed", "first")
        send.wait_recv()
        following_rows(hb_got[...] * not_last)

        def finish(r, back):
            grad = ge[r].astype(F32) + back
            p[r] = grad
            si[r] = grad.astype(BF)

        norm_back(p, vec[2:3], lambda r: q[r], 2, 3, finish)
        send.wait_send()
        outer(ei, si, gt.at[0])
        pack(gt.at[0], gt.at[1], 80)
        run(0, 4)

        @pl.loop(0, TOK // 512)
        def _(i):
            r = pl.ds(pl.multiple_of(i * 512, 512), 512)
            q[r] = lax.dot_general(si[r], we[1], NT, preferred_element_type=F32)

        spill.wait("wk", "wv", "wr")

    unit = pltpu.VMEM((TOK, WIDE), BF)
    pl.run_scoped(channel_mix, unit, unit, unit, unit, pltpu.VMEM((2, depth, 2, 4, 32, WIDE), BF), unit,
                  pltpu.VMEM((2, WIDE, WIDE), BF))
    run(1, 4)
    spill.wait("alive")
    shrink = jnp.exp(-vec[9:10])
    shrink8 = jnp.broadcast_to(shrink, (SEG, WIDE))
    bonus = vec[10:11]
    row = lax.broadcasted_iota(jnp.int32, (SEG, WIDE), 0)
    zero = jnp.zeros((SEG, WIDE), F32)

    def time_mix(gkvg):
        def sweeps(buf):
            def load(j, name):
                spill.start((name, "kvg", j), i_kvg.at[:, pl.ds(j * SPAN, SPAN)], buf.at[j % 2, pl.ds(0, 3)])
                spill.start((name, "nd", j), i_nd.at[:, pl.ds(j * SPAN, SPAN)], buf.at[j % 2, pl.ds(3, 2)])

            def arrive(j, name):
                spill.wait((name, "kvg", j), (name, "nd", j))

            load(0, 1)
            load(1, 1)
            for j in range(SEQS):
                arrive(j, 1)
                at = buf.at[j % 2]

                def back(i, state):
                    decay, numer, denom, bonus_sum = state
                    gates = [None, None]
                    for h in (1, 0):
                        lo = pl.multiple_of((STEPS // 2 - 1 - i) * 16 + 8 * h, 8)
                        r = pl.ds(pl.multiple_of(j * SPAN + lo, 8), SEG)
                        here = pl.ds(lo, SEG)
                        kept = spread_lanes(keep[r])
                        k, v = at[0, here], at[1, here]
                        now = jnp.exp(bonus + k)
                        inverse = 1.0 / (at[4, here] + now)
                        wkv = (at[3, here] + now * v) * inverse
                        s = sigmoid(at[2, here])
                        gm = q[r]
                        gw = gm * s
                        gates[h] = gw * wkv * (1.0 - s)
                        dn = gw * inverse
                        dd = -dn * wkv
                        q[r] = dn
                        bonus_sum = bonus_sum + now * (dn * v + dd)
                        m = kept * shrink8
                        decay, numer, denom = decay * m, numer * m + kept * dn, denom * m + kept * dd
                    rows = pl.ds(pl.multiple_of(j * SPAN + (STEPS // 2 - 1 - i) * 16, 16), 16)
                    gkvg[2, rows] = jnp.concatenate(gates, axis=0).astype(BF)
                    return decay, numer, denom, bonus_sum

                decay, numer, denom, bonus_sum = lax.fori_loop(0, STEPS // 2, back, (zero + 1.0, zero, zero, zero))
                load(j + 2, 1) if j + 2 < SEQS else load(j - 2, 2)
                vg[10] += bonus_sum
                for d in (1, 2, 4):
                    end = row >= SEG - d
                    numer, denom, decay = (
                        numer + decay * jnp.where(end, 0.0, pltpu.roll(numer, SEG - d, axis=0)),
                        denom + decay * jnp.where(end, 0.0, pltpu.roll(denom, SEG - d, axis=0)),
                        decay * jnp.where(end, 1.0, pltpu.roll(decay, SEG - d, axis=0)),
                    )
                states[place.s, j : j + 1] = numer[0:1]
                states[place.s, SEQS + j : SEQS + j + 1] = denom[0:1]
                end = row >= SEG - 1
                seg[j, 0] = jnp.where(end, 1.0, pltpu.roll(decay, SEG - 1, axis=0))
                seg[j, 1] = jnp.where(end, 0.0, pltpu.roll(numer, SEG - 1, axis=0))
                seg[j, 2] = jnp.where(end, 0.0, pltpu.roll(denom, SEG - 1, axis=0))
                if j == 1:
                    run(2, 4)
            sent = line.all(states, ssems)
            for copy in sent:
                copy.start()
            run(3, 4)
            for d in range(1, line.n):
                src = lax.rem(place.s + line.n - d, line.n)
                rdma(states.at[src], states.at[src], ssems, d, line.n + d, (src, b)).wait_recv()
            whole = jnp.exp(-float(SPAN) * vec[9:10])
            arrived = zero
            for src in range(7, 0, -1):
                after = spread_lanes(alive[src]) * whole * arrived + states[src]
                arrived = jnp.where(src > place.s, after, arrived)
            for j in range(SEQS):
                arrive(j, 2)
                at = buf.at[j % 2]
                numer0 = seg[j, 0] * arrived[j : j + 1] + seg[j, 1]
                denom0 = seg[j, 0] * arrived[SEQS + j : SEQS + j + 1] + seg[j, 2]

                def back(i, state):
                    an, ad, decay_sum = state
                    keys, values = [None, None], [None, None]
                    for h in (1, 0):
                        lo = pl.multiple_of((STEPS // 2 - 1 - i) * 16 + 8 * h, 8)
                        r = pl.ds(pl.multiple_of(j * SPAN + lo, 8), SEG)
                        here = pl.ds(lo, SEG)
                        kept = spread_lanes(keep[r])
                        k, v, numer, denom = at[0, here], at[1, here], at[3, here], at[4, here]
                        now, ek = jnp.exp(bonus + k), jnp.exp(k)
                        wkv = (numer + now * v) / (denom + now)
                        dn = q[r]
                        dd = -dn * wkv
                        keys[h] = ek * (an * v + ad) + now * (dn * v + dd)
                        values[h] = ek * an + now * dn
                        decay_sum = decay_sum + an * numer + ad * denom
                        an, ad = kept * (dn + shrink8 * an), kept * (dd + shrink8 * ad)
                    rows = pl.ds(pl.multiple_of(j * SPAN + (STEPS // 2 - 1 - i) * 16, 16), 16)
                    gkvg[0, rows] = jnp.concatenate(keys, axis=0).astype(BF)
                    gkvg[1, rows] = jnp.concatenate(values, axis=0).astype(BF)
                    return an, ad, decay_sum

                _, _, decay_sum = lax.fori_loop(0, STEPS // 2, back, (numer0, denom0, zero))
                if j + 2 < SEQS:
                    load(j + 2, 2)
                vg[9] += -shrink * decay_sum
            for copy in sent:
                copy.wait_send()
            run(4, 4)

        pl.run_scoped(sweeps, pltpu.VMEM((2, 5, SPAN, WIDE), F32))

        def mixes(ki, spa, gt, parts):
            spill.start("ki0", i_ki.at[0], ki.at[0])
            spill.start("ki1", i_ki.at[1], ki.at[1])
            spill.start("spa", i_spa, spa)
            spill.wait("ki0")
            outer(ki.at[0], gkvg.at[0], gt.at[0])
            spill.start("ki2", i_ki.at[2], ki.at[0])
            spill.wait("ki1")
            outer(ki.at[1], gkvg.at[1], gt.at[1])
            spill.start("xp", i_xp, ki.at[1])
            pack(gt.at[0], gt.at[1], 0)
            spill.wait("ki2")
            outer(ki.at[0], gkvg.at[2], gt.at[0])
            pack(gt.at[0], None, 48)
            run(0, 5)
            spill.wait("spa")
            ratios = [vec[4 + m : 5 + m] for m in range(3)]
            for j in range(SEQS):
                rows = pl.ds(j * SPAN, SPAN)
                for m, w in enumerate((we.at[2], we.at[3], we.at[0])):
                    parts[m] = lax.dot_general(gkvg[m, rows], w[...], NT, preferred_element_type=F32)

                def tile(t, sums):
                    r = pl.ds(pl.multiple_of(j * SPAN + t * 16, 16), 16)
                    here = pl.ds(pl.multiple_of(t * 16, 16), 16)
                    spread = spa[r].astype(F32)
                    g = [parts[m, here] for m in range(3)]
                    shifted = g[0] * (1.0 - ratios[0]) + g[1] * (1.0 - ratios[1]) + g[2] * (1.0 - ratios[2])
                    xg[j, here] = shifted * spread_lanes(keep[r])
                    q[r] = g[0] * ratios[0] + g[1] * ratios[1] + g[2] * ratios[2]
                    return tuple(s + fold(v * spread) for s, v in zip(sums, g))

                sums = lax.fori_loop(0, SPAN // 16, tile, (zero, zero, zero))
                for m in range(3):
                    vg[4 + m] += sums[m]
                if j == 0:
                    run(1, 5)
                if j == 2:
                    run(2, 5)
            send = send_first(hx, hx_got, hsems.at[1])
            spill.wait("xp")
            send.wait_recv()
            following_rows(hx_got[...] * not_last)

            def finish(r, back):
                p[r] = p[r] + back

            norm_back(q, vec[0:1], lambda r: ki[1, r].astype(F32), 0, 1, finish)
            send.wait_send()

        unit2 = pltpu.VMEM((2, TOK, WIDE), BF)
        pl.run_scoped(mixes, unit2, unit, pltpu.VMEM((2, WIDE, WIDE), BF), pltpu.VMEM((3, SPAN, WIDE), F32))

    pl.run_scoped(time_mix, pltpu.VMEM((3, TOK, WIDE), BF))
    spill.start("tokens", p, o_tokens)
    vr[0, VECTORS:16] = jnp.zeros((16 - VECTORS, WIDE), F32)
    for i in range(VECTORS):
        vr[0, i : i + 1] = jnp.sum(vg[i], axis=0, keepdims=True)

    def exchange(src, slot, to):
        copy = rdma(vr.at[src], vr.at[slot], zsems.at[slot], 0, 1, to)
        copy.start()
        return copy

    one = exchange(0, 1, place.core)
    one.wait_recv()
    vr[2] = vr[0] + vr[1]
    two = exchange(2, 3, place.x)
    run(3, 5)
    two.wait_recv()
    vr[4] = vr[2] + vr[3]
    three = exchange(4, 5, place.y)
    three.wait_recv()
    vr[6] = vr[4] + vr[5]
    four = [exchange(6, 6 + d, place.along(d)[1]) for d in range(1, depth)]
    run(4, 5)
    total = vr[6]
    for d in range(1, depth):
        four[d - 1].wait_recv()
        total = total + vr[6 + d]
    vr[6 + depth] = total
    me = place.s * 4 + place.b
    start = me * 24
    low = pl.multiple_of(jnp.minimum(start // LANE, WIDE // LANE - 2) * LANE, LANE)
    mine = vr[6 + depth, :, pl.ds(low, WINDOW)]
    o_vec[...] = pltpu.roll(mine, WINDOW - (start - low), axis=1)[:, 0:LANE]
    spill.start("out", out, o_out)
    for copy in [one, two, three] + four:
        copy.wait_send()
    for k in range(COUNT):
        run(5, k)
    spill.wait()


BACK_INPUTS = ("w", "e", "c", "ki", "spa", "spb", "mixed", "ei", "si", "gc", "gs", "xp", "up", "sq", "pkc", "kvg", "nd", "first", "vec", "alive")


def backward_call(f, keep, depth):
    hbm, vmem = pl.BlockSpec(memory_space=pl.ANY), pl.BlockSpec(memory_space=pltpu.VMEM)
    s = jax.ShapeDtypeStruct
    seq, rows = depth * 2, ROWS_MAIN + ROWS_LAST
    top = max(n for _, _, n, _ in SCATTER_CHUNKS)
    row8 = pltpu.VMEM((8, WIDE), F32)
    return pl.pallas_call(
        backward_kernel,
        out_shape=(s((rows, WIDE), F32), s((TOK, WIDE), F32), s((16, LANE), F32)),
        in_specs=[hbm] * (len(BACK_INPUTS) + 1),
        out_specs=(hbm, hbm, vmem),
        scratch_shapes=[
            pltpu.VMEM((depth, 2, 4, ROWS_MAIN, WIDE), BF), pltpu.VMEM((depth, 2, 4, ROWS_LAST, WIDE), BF),
            pltpu.VMEM((2, depth, 4, top, WIDE), BF), pltpu.VMEM((2, 2, depth, top, WIDE), BF), pltpu.VMEM((2, depth, top, WIDE), BF),
            pltpu.VMEM((depth - 1, rows, WIDE), BF), pltpu.VMEM((rows, WIDE), F32),
            pltpu.VMEM((4, WIDE, WIDE), BF), pltpu.VMEM((depth, 2, 4, 96, WIDE), BF),
            pltpu.VMEM((TOK, WIDE), F32), pltpu.VMEM((TOK, WIDE), F32), pltpu.VMEM((SEQS, SPAN + 8, WIDE), F32),
            pltpu.VMEM((TOK, LANE), F32), pltpu.VMEM((16, WIDE), F32), pltpu.VMEM((seq, 8, LANE), F32), pltpu.VMEM((seq, 8, WIDE), F32),
            pltpu.VMEM((SEQS, 3, SEG, WIDE), F32), pltpu.VMEM((VECTORS, 8, WIDE), F32), pltpu.VMEM((7 + depth, 16, WIDE), F32),
            row8, row8, row8, row8,
            pltpu.SemaphoreType.DMA((COUNT, 16)), pltpu.SemaphoreType.REGULAR((5,)), pltpu.SemaphoreType.DMA((2 * seq,)),
            pltpu.SemaphoreType.DMA((2, 2)), pltpu.SemaphoreType.DMA((7 + depth, 2)), pltpu.SemaphoreType.DMA((56,)),
        ],
        compiler_params=pltpu.CompilerParams(collective_id=1, has_side_effects=True, vmem_limit_bytes=62 << 20),
        cost_estimate=pl.CostEstimate(flops=2 * 1024 * 26 * 768 * 768, bytes_accessed=60 << 20, transcendentals=0),
    )(*[f[n] for n in BACK_INPUTS], keep)


def fast_body(layer_inputs, document_openings, wk, wv, wr, wo, we, ws, wc, *rest):
    vectors, upstream = rest[:VECTORS], rest[VECTORS]
    depth = lax.axis_size("seq") // 2
    keep = 1.0 - document_openings.astype(F32)
    keep = keep.reshape(SEQS, SEG, STEPS).transpose(0, 2, 1).reshape(TOK, 1)
    keep = jnp.broadcast_to(keep, (TOK, LANE))
    vec = jnp.pad(jnp.stack(vectors).astype(F32), ((0, 16 - VECTORS), (0, LANE - 24)))
    got = forward_call(layer_inputs.reshape(TOK, WIDE), keep, upstream.reshape(TOK, WIDE), vec, (wk, wv, wr, wo, ws, we, wc), depth)
    out, tokens, small = backward_call(got, keep, depth)

    def natural(v):
        return v.reshape(SEQS, STEPS, SEG, WIDE).transpose(0, 2, 1, 3).reshape(SEQS, SPAN, WIDE)

    expand = jnp.concatenate([out[128 + 24 * i : 152 + 24 * i] for i in range(4)], axis=1)
    return (natural(got["bo"]), natural(tokens), out[0:24], out[24:48], out[48:72], out[80:104], expand, out[104:128], out[224:320]) + tuple(
        small[i, 0:24] for i in range(VECTORS))


def from_behind(block, axis, distance):
    devices = range(lax.axis_size(axis))
    route = [(i - distance, i) for i in devices if i - distance in devices]
    return lax.ppermute(block, axis, route)


def prefix(part, axis, combine, identity, reverse):
    count = lax.axis_size(axis)
    place = lax.axis_index(axis)
    ahead = count - 1 - place if reverse else place
    gathered = jax.tree.map(lambda a: lax.all_gather(a, axis), part)
    state = jax.tree.map(lambda a, e: jnp.zeros_like(a) + jnp.asarray(e, a.dtype), part, identity)

    def one(turn, state):
        source = count - 1 - turn if reverse else turn
        return combine(
            state, jax.tree.map(lambda a: lax.dynamic_index_in_dim(a, source, 0, False), gathered)
        )

    return lax.fori_loop(0, ahead, one, state)


def layer_norm(values, gain, offset):
    center = values - jnp.mean(values, axis=-1, keepdims=True)
    factor = lax.rsqrt(jnp.mean(center * center, axis=-1, keepdims=True) + EPSILON)
    normed = center * factor
    return (normed * gain + offset, normed, factor)


def norm_back(grad_out, normed, factor, gain):
    scaled = grad_out * gain
    centered = scaled - jnp.mean(scaled, axis=-1, keepdims=True)
    grad_in = factor * (centered - normed * jnp.mean(scaled * normed, axis=-1, keepdims=True))
    return (grad_in, jnp.sum(grad_out * normed, axis=(0, 1)), jnp.sum(grad_out, axis=(0, 1)))


def product(left, right):
    return jnp.einsum("scd,de->sce", left, right, preferred_element_type=jnp.float32)


def product_back(grad, right):
    return jnp.einsum("sce,de->scd", grad, right, preferred_element_type=jnp.float32)


def outer_sum(left, grad):
    return jnp.einsum("scd,sce->de", left, grad, preferred_element_type=jnp.float32)


def attach_previous(values, arriving, persisting_indicator):
    return jnp.concatenate([arriving, values[:, :-1]], axis=1) * persisting_indicator[..., None]


def attach_next(masked, arriving):
    return jnp.concatenate([masked[:, 1:], arriving], axis=1)


def make_combine(fading_multiplier):

    def combine(earlier, later):
        early_numer, early_denom, early_length, early_cut = earlier
        late_numer, late_denom, late_length, late_cut = later
        fading = jnp.exp(-late_length * fading_multiplier) * (1.0 - late_cut)
        return (
            late_numer + fading * early_numer,
            late_denom + fading * early_denom,
            early_length + late_length,
            jnp.maximum(early_cut, late_cut),
        )

    return combine


def affine_compose(first_step, second_step):
    first_mult, first_numer, first_denom = first_step
    second_mult, second_numer, second_denom = second_step
    return (
        first_mult * second_mult,
        second_mult * first_numer + second_numer,
        second_mult * first_denom + second_denom,
    )


def forward_sweep(exponentiated_lookup, payload_table_lines, persisting_indicator, shrink):
    multiplier = persisting_indicator[..., None] * shrink
    inclusive = lax.associative_scan(
        affine_compose,
        (multiplier, exponentiated_lookup * payload_table_lines, exponentiated_lookup),
        axis=1,
    )
    zeros = jnp.zeros_like(exponentiated_lookup[:, :1])
    numer_all = (
        jnp.concatenate([zeros, inclusive[1][:, :-1]], axis=1) * persisting_indicator[..., None]
    )
    denom_all = (
        jnp.concatenate([zeros, inclusive[2][:, :-1]], axis=1) * persisting_indicator[..., None]
    )
    return (numer_all, denom_all, inclusive[1][:, -1], inclusive[2][:, -1])


def reverse_sweep(adjoint_dividend, grad_denom, persisting_indicator, shrink):
    keep_now = persisting_indicator[..., None]
    inclusive = lax.associative_scan(
        affine_compose,
        (keep_now * shrink, keep_now * adjoint_dividend, keep_now * grad_denom),
        axis=1,
        reverse=True,
    )
    zeros = jnp.zeros_like(adjoint_dividend[:, :1])
    following_dividend = jnp.concatenate([inclusive[1][:, 1:], zeros], axis=1)
    next_denom = jnp.concatenate([inclusive[2][:, 1:], zeros], axis=1)
    return (following_dividend, next_denom, inclusive[1][:, 0], inclusive[2][:, 0])


def body(
    layer_inputs,
    document_openings,
    mixing_lookup_projection,
    mixing_payload_projection,
    mixing_acceptor_projection,
    mixing_result_projection,
    feedforward_lookup_projection,
    feedforward_acceptor_projection,
    feedforward_payload_projection,
    premix_layer_scaling,
    premix_layer_offset,
    postmix_layer_scaling,
    postmix_layer_offset,
    mixing_lookup_blend,
    mixing_payload_blend,
    mixing_acceptor_blend,
    feedforward_lookup_blend,
    feedforward_acceptor_blend,
    feature_fading_speed,
    present_token_reward,
    upstream_adjoint,
):
    gathered = (
        lax.all_gather(mixing_lookup_projection, BOTH, axis=0, tiled=True),
        lax.all_gather(mixing_payload_projection, BOTH, axis=0, tiled=True),
        lax.all_gather(mixing_acceptor_projection, BOTH, axis=0, tiled=True),
        lax.all_gather(mixing_result_projection, BOTH, axis=0, tiled=True),
        lax.all_gather(feedforward_lookup_projection, BOTH, axis=0, tiled=True),
        lax.all_gather(feedforward_acceptor_projection, BOTH, axis=0, tiled=True),
        lax.all_gather(feedforward_payload_projection, BOTH, axis=0, tiled=True),
        lax.all_gather(premix_layer_scaling, BOTH, axis=0, tiled=True),
        lax.all_gather(premix_layer_offset, BOTH, axis=0, tiled=True),
        lax.all_gather(postmix_layer_scaling, BOTH, axis=0, tiled=True),
        lax.all_gather(postmix_layer_offset, BOTH, axis=0, tiled=True),
        lax.all_gather(mixing_lookup_blend, BOTH, axis=0, tiled=True),
        lax.all_gather(mixing_payload_blend, BOTH, axis=0, tiled=True),
        lax.all_gather(mixing_acceptor_blend, BOTH, axis=0, tiled=True),
        lax.all_gather(feedforward_lookup_blend, BOTH, axis=0, tiled=True),
        lax.all_gather(feedforward_acceptor_blend, BOTH, axis=0, tiled=True),
        lax.all_gather(feature_fading_speed, BOTH, axis=0, tiled=True),
        lax.all_gather(present_token_reward, BOTH, axis=0, tiled=True),
    )
    full_key, full_value, full_gate, full_output, full_expand, full_select, full_contract = (
        gathered[:7]
    )
    vectors = [stream_element.astype(jnp.float32) for stream_element in gathered[7:]]
    (
        gain_first,
        bias_first,
        gain_second,
        bias_second,
        ratio_key,
        ratio_value,
        ratio_gate,
        ratio_expand,
        ratio_select,
        fading_multiplier,
        present_reward_term,
    ) = vectors
    inputs = layer_inputs.astype(jnp.float32)
    flags = document_openings.astype(jnp.float32)
    persisting_indicator = 1.0 - flags
    sequences = layer_inputs.shape[0]
    block_len = layer_inputs.shape[1]
    width = layer_inputs.shape[2]
    normed_a, unit_a, factor_a = layer_norm(inputs, gain_first, bias_first)
    arriving_a = from_behind(normed_a[:, -1:, :], "seq", 1)
    before_a = attach_previous(normed_a, arriving_a, persisting_indicator)
    spread_a = normed_a - before_a
    key_in = (before_a + spread_a * ratio_key).astype(jnp.bfloat16)
    value_in = (before_a + spread_a * ratio_value).astype(jnp.bfloat16)
    gate_in = (before_a + spread_a * ratio_gate).astype(jnp.bfloat16)
    lookup_table_lines = product(key_in, full_key)
    payload_table_lines = product(value_in, full_value)
    gate_rows = product(gate_in, full_gate)
    shrink = jnp.exp(-fading_multiplier)
    exponentiated_lookup = jnp.exp(lookup_table_lines)
    reward_scaled_pairs = jnp.exp(present_reward_term + lookup_table_lines)
    local_numer, local_denom, end_numer, end_denom = forward_sweep(
        exponentiated_lookup, payload_table_lines, persisting_indicator, shrink
    )
    cut = jnp.max(flags, axis=1, keepdims=True)
    length = jnp.full((1,), float(block_len), jnp.float32)
    zero_state = jnp.zeros((sequences, width), jnp.float32)
    identity = (
        zero_state,
        zero_state,
        jnp.zeros((1,), jnp.float32),
        jnp.zeros((sequences, 1), jnp.float32),
    )
    combine = make_combine(fading_multiplier)
    arrived = prefix((end_numer, end_denom, length, cut), "seq", combine, identity, False)
    positions = jnp.arange(block_len, dtype=jnp.float32)
    alive = 1.0 - lax.cummax(flags, axis=1)
    rising = jnp.exp(-positions[:, None] * fading_multiplier[None, :])
    running_dividend = local_numer + alive[..., None] * rising[None] * arrived[0][:, None, :]
    running_divisor = local_denom + alive[..., None] * rising[None] * arrived[1][:, None, :]
    accumulated_sum = running_divisor + reward_scaled_pairs
    recurrent_average = (
        running_dividend + reward_scaled_pairs * payload_table_lines
    ) / accumulated_sum
    gate_sig = jax.nn.sigmoid(gate_rows)
    mixed = (gate_sig * recurrent_average).astype(jnp.bfloat16)
    first = inputs + product(mixed, full_output)
    normed_b, unit_b, factor_b = layer_norm(first, gain_second, bias_second)
    arriving_b = from_behind(normed_b[:, -1:, :], "seq", 1)
    before_b = attach_previous(normed_b, arriving_b, persisting_indicator)
    spread_b = normed_b - before_b
    expand_in = (before_b + spread_b * ratio_expand).astype(jnp.bfloat16)
    select_in = (before_b + spread_b * ratio_select).astype(jnp.bfloat16)
    expanded = product(expand_in, full_expand)
    selected = product(select_in, full_select)
    positive = jax.nn.relu(expanded)
    squared = (positive * positive).astype(jnp.bfloat16)
    contracted = product(squared, full_contract)
    select_sig = jax.nn.sigmoid(selected)
    block_out = (first + select_sig * contracted).astype(jnp.bfloat16)
    again = (
        lax.all_gather(mixing_lookup_projection, BOTH, axis=0, tiled=True),
        lax.all_gather(mixing_payload_projection, BOTH, axis=0, tiled=True),
        lax.all_gather(mixing_acceptor_projection, BOTH, axis=0, tiled=True),
        lax.all_gather(mixing_result_projection, BOTH, axis=0, tiled=True),
        lax.all_gather(feedforward_lookup_projection, BOTH, axis=0, tiled=True),
        lax.all_gather(feedforward_acceptor_projection, BOTH, axis=0, tiled=True),
        lax.all_gather(feedforward_payload_projection, BOTH, axis=0, tiled=True),
    )
    full_key, full_value, full_gate, full_output, full_expand, full_select, full_contract = again
    upstream = upstream_adjoint.astype(jnp.float32)
    grad_contracted = (upstream * select_sig).astype(jnp.bfloat16)
    grad_selected = (upstream * contracted * select_sig * (1.0 - select_sig)).astype(jnp.bfloat16)
    grad_squared = product_back(grad_contracted, full_contract)
    grad_expanded = (2.0 * positive * grad_squared).astype(jnp.bfloat16)
    contract_grad = jnp.einsum(
        "scf,scd->fd", squared, grad_contracted, preferred_element_type=jnp.float32
    )
    expand_grad = outer_sum(expand_in, grad_expanded)
    select_grad = outer_sum(select_in, grad_selected)
    grad_expand_in = product_back(grad_expanded, full_expand)
    grad_select_in = product_back(grad_selected, full_select)
    expand_ratio_grad = jnp.sum(grad_expand_in * spread_b, axis=(0, 1))
    select_ratio_grad = jnp.sum(grad_select_in * spread_b, axis=(0, 1))
    grad_before_b = (
        grad_expand_in * (1.0 - ratio_expand) + grad_select_in * (1.0 - ratio_select)
    ) * persisting_indicator[..., None]
    arriving_gb = from_behind(grad_before_b[:, :1, :], "seq", -1)
    grad_normed_b = (
        grad_expand_in * ratio_expand
        + grad_select_in * ratio_select
        + attach_next(grad_before_b, arriving_gb)
    )
    grad_from_b, chan_gain_grad, chan_bias_grad = norm_back(
        grad_normed_b, unit_b, factor_b, gain_second
    )
    grad_first = upstream + grad_from_b
    grad_attended = grad_first.astype(jnp.bfloat16)
    output_grad = outer_sum(mixed, grad_attended)
    grad_mixed = product_back(grad_attended, full_output)
    grad_gates = (grad_mixed * recurrent_average * gate_sig * (1.0 - gate_sig)).astype(jnp.bfloat16)
    grad_wkv = grad_mixed * gate_sig
    adjoint_dividend = grad_wkv / accumulated_sum
    grad_denom = -grad_wkv * recurrent_average / accumulated_sum
    following_dividend, next_denom, lead_numer, lead_denom = reverse_sweep(
        adjoint_dividend, grad_denom, persisting_indicator, shrink
    )
    behind = prefix((lead_numer, lead_denom, length, cut), "seq", combine, identity, True)
    after = jnp.concatenate([flags[:, 1:], jnp.zeros_like(flags[:, :1])], axis=1)
    later_alive = 1.0 - lax.cummax(after, axis=1, reverse=True)
    falling = jnp.exp(-(block_len - 1.0 - positions)[:, None] * fading_multiplier[None, :])
    following_dividend = (
        following_dividend + later_alive[..., None] * falling[None] * behind[0][:, None, :]
    )
    next_denom = next_denom + later_alive[..., None] * falling[None] * behind[1][:, None, :]
    immediate_term = adjoint_dividend * payload_table_lines + grad_denom
    grad_keys = (
        exponentiated_lookup * (following_dividend * payload_table_lines + next_denom)
        + reward_scaled_pairs * immediate_term
    ).astype(jnp.bfloat16)
    adjoint_payloads = (
        exponentiated_lookup * following_dividend + reward_scaled_pairs * adjoint_dividend
    ).astype(jnp.bfloat16)
    present_reward_adjoint = jnp.sum(reward_scaled_pairs * immediate_term, axis=(0, 1))
    decay_grad = -shrink * jnp.sum(
        following_dividend * running_dividend + next_denom * running_divisor, axis=(0, 1)
    )
    key_grad = outer_sum(key_in, grad_keys)
    value_grad = outer_sum(value_in, adjoint_payloads)
    gate_grad = outer_sum(gate_in, grad_gates)
    grad_key_in = product_back(grad_keys, full_key)
    grad_value_in = product_back(adjoint_payloads, full_value)
    grad_gate_in = product_back(grad_gates, full_gate)
    key_ratio_grad = jnp.sum(grad_key_in * spread_a, axis=(0, 1))
    value_ratio_grad = jnp.sum(grad_value_in * spread_a, axis=(0, 1))
    gate_ratio_grad = jnp.sum(grad_gate_in * spread_a, axis=(0, 1))
    grad_before_a = (
        grad_key_in * (1.0 - ratio_key)
        + grad_value_in * (1.0 - ratio_value)
        + grad_gate_in * (1.0 - ratio_gate)
    ) * persisting_indicator[..., None]
    arriving_ga = from_behind(grad_before_a[:, :1, :], "seq", -1)
    grad_normed_a = (
        grad_key_in * ratio_key
        + grad_value_in * ratio_value
        + grad_gate_in * ratio_gate
        + attach_next(grad_before_a, arriving_ga)
    )
    grad_from_a, attn_gain_grad, attn_bias_grad = norm_back(
        grad_normed_a, unit_a, factor_a, gain_first
    )
    tokens_grad = grad_first + grad_from_a
    shares = (
        lax.psum_scatter(key_grad, BOTH, scatter_dimension=0, tiled=True),
        lax.psum_scatter(value_grad, BOTH, scatter_dimension=0, tiled=True),
        lax.psum_scatter(gate_grad, BOTH, scatter_dimension=0, tiled=True),
        lax.psum_scatter(output_grad, BOTH, scatter_dimension=0, tiled=True),
        lax.psum_scatter(expand_grad, BOTH, scatter_dimension=0, tiled=True),
        lax.psum_scatter(select_grad, BOTH, scatter_dimension=0, tiled=True),
        lax.psum_scatter(contract_grad, BOTH, scatter_dimension=0, tiled=True),
        lax.psum_scatter(attn_gain_grad, BOTH, scatter_dimension=0, tiled=True),
        lax.psum_scatter(attn_bias_grad, BOTH, scatter_dimension=0, tiled=True),
        lax.psum_scatter(chan_gain_grad, BOTH, scatter_dimension=0, tiled=True),
        lax.psum_scatter(chan_bias_grad, BOTH, scatter_dimension=0, tiled=True),
        lax.psum_scatter(key_ratio_grad, BOTH, scatter_dimension=0, tiled=True),
        lax.psum_scatter(value_ratio_grad, BOTH, scatter_dimension=0, tiled=True),
        lax.psum_scatter(gate_ratio_grad, BOTH, scatter_dimension=0, tiled=True),
        lax.psum_scatter(expand_ratio_grad, BOTH, scatter_dimension=0, tiled=True),
        lax.psum_scatter(select_ratio_grad, BOTH, scatter_dimension=0, tiled=True),
        lax.psum_scatter(decay_grad, BOTH, scatter_dimension=0, tiled=True),
        lax.psum_scatter(present_reward_adjoint, BOTH, scatter_dimension=0, tiled=True),
    )
    return (
        block_out,
        tokens_grad,
        shares[0],
        shares[1],
        shares[2],
        shares[3],
        shares[4],
        shares[5],
        shares[6],
        shares[7],
        shares[8],
        shares[9],
        shares[10],
        shares[11],
        shares[12],
        shares[13],
        shares[14],
        shares[15],
        shares[16],
        shares[17],
    )


def solution(mesh):
    fits = mesh.shape["seq"] == 8 and mesh.shape["batch"] == 4
    return jax.shard_map(
        fast_body if fits else body,
        mesh=mesh,
        in_specs=(
            P("batch", "seq", None),
            P("batch", "seq"),
            P(BOTH, None),
            P(BOTH, None),
            P(BOTH, None),
            P(BOTH, None),
            P(BOTH, None),
            P(BOTH, None),
            P(BOTH, None),
            P(BOTH),
            P(BOTH),
            P(BOTH),
            P(BOTH),
            P(BOTH),
            P(BOTH),
            P(BOTH),
            P(BOTH),
            P(BOTH),
            P(BOTH),
            P(BOTH),
            P("batch", "seq", None),
        ),
        out_specs=(
            P("batch", "seq", None),
            P("batch", "seq", None),
            P(BOTH, None),
            P(BOTH, None),
            P(BOTH, None),
            P(BOTH, None),
            P(BOTH, None),
            P(BOTH, None),
            P(BOTH, None),
            P(BOTH),
            P(BOTH),
            P(BOTH),
            P(BOTH),
            P(BOTH),
            P(BOTH),
            P(BOTH),
            P(BOTH),
            P(BOTH),
            P(BOTH),
            P(BOTH),
        ),
        check_vma=False,
    )
```

```python
import jax
import jax.numpy as jnp
from jax import lax
from jax.experimental import pallas as pl
from jax.experimental.pallas import tpu as pltpu
from jax.sharding import PartitionSpec as P

BOTH = ("seq", "batch")
MESH = pl.DeviceIdType.MESH
BF = jnp.bfloat16
F32 = jnp.float32
WIDE = 768
ROWS_MAIN = 224
ROWS_LAST = 96
GATHER_CHUNKS = (
    (0, 48, 32, 16), (0, 0, 48, 32), (0, 80, 48, 16), (0, 128, 48, 32), (0, 176, 48, 16), (1, 0, 48, 32), (1, 48, 48, 16))
SCATTER_CHUNKS = (
    (1, 0, 48, 32), (1, 48, 48, 16), (0, 128, 48, 32), (0, 176, 48, 16), (0, 80, 48, 32), (0, 0, 48, 16), (0, 48, 32, 16))
COUNT = len(GATHER_CHUNKS)


class Place:
    def __init__(self):
        self.s = lax.axis_index("seq")
        self.b = lax.axis_index("batch")
        self.z, self.c = self.s // 2, self.s % 2
        y, x = self.b // 2, self.b % 2
        self.bx, self.by, self.bd = y * 2 + 1 - x, (1 - y) * 2 + x, (1 - y) * 2 + 1 - x
        self.depth = lax.axis_size("seq") // 2
        self.x, self.y = (self.s, self.bx), (self.s, self.by)
        self.core = (self.z * 2 + 1 - self.c, self.b)

    def along(self, step):
        z = lax.rem(self.z + step, self.depth)
        return z, (z * 2 + self.c, self.b)

    def back(self, step):
        return lax.rem(self.z + self.depth - step, self.depth)


def rdma(src, dst, sems, send, recv, to):
    return pltpu.make_async_remote_copy(
        src_ref=src, dst_ref=dst, send_sem=sems.at[send], recv_sem=sems.at[recv], device_id=to, device_id_type=MESH
    )


def enter(place):
    barrier = pltpu.get_barrier_semaphore()
    n = lax.axis_size("seq")
    peers = [place.x, place.y] + [(lax.rem(place.s + d, n), place.b) for d in range(1, n)]
    for peer in peers:
        pl.semaphore_signal(barrier, inc=1, device_id=peer, device_id_type=MESH)
    pl.semaphore_wait(barrier, len(peers))


class Gather:
    def __init__(self, place, arrays, sems):
        self.p, self.arrays, self.sems = place, arrays, sems

    def stage(self, number, k):
        if not 0 <= k < COUNT:
            return
        p, sems = self.p, self.sems.at[k]
        a, r0, n, nx = GATHER_CHUNKS[k]
        ref = self.arrays[a]
        whole, part_x, part_y = pl.ds(r0, n), pl.ds(r0, nx), pl.ds(r0 + nx, n - nx)
        col = lambda c, b, rows: ref.at[:, c, b, rows]
        move = lambda view, at, to: rdma(view, view, sems, at, at + 1, to)
        one = lambda z, b: ref.at[z, p.c, b, whole]
        line = lambda d, z: move(one(z, p.b), 2 * d - 2, p.along(d)[1])
        near_x = lambda b: move(col(p.c, b, whole), 6, p.x)
        near_y = lambda b: move(col(p.c, b, whole), 8, p.y)
        diag_x = lambda b: move(col(p.c, b, part_x), 10, p.x)
        diag_y = lambda b: move(col(p.c, b, part_y), 12, p.y)
        core = lambda j, c, b: move(col(c, b, whole), 14 + 2 * j, p.core)
        single = k == 0
        steps = range(p.depth)
        lone = lambda d, z, b, c: (
            move(ref.at[z, c, b, whole], 22 + 6 * d, p.x), move(ref.at[z, c, b, whole], 24 + 6 * d, p.y),
            move(ref.at[z, c, b, whole], 26 + 6 * d, p.core))
        if number == 0:
            for d in range(1, p.depth):
                line(d, p.z).start()
            if single:
                for copy in lone(0, p.z, p.b, p.c):
                    copy.start()
        elif number == 1:
            for d in range(1, p.depth):
                line(d, p.back(d)).wait_recv()
                if single:
                    for copy in lone(d, p.back(d), p.b, p.c):
                        copy.start()
            if not single:
                near_x(p.b).start()
                near_y(p.b).start()
                core(0, p.c, p.b).start()
        elif number == 2:
            if single:
                for d in steps:
                    lone(d, p.back(d), p.bx, p.c)[0].wait_recv()
                    lone(d, p.back(d), p.by, p.c)[1].wait_recv()
            else:
                near_x(p.bx).wait_recv()
                near_y(p.by).wait_recv()
            diag_x(p.by).start()
            diag_y(p.bx).start()
            core(1, p.c, p.bx).start()
            core(2, p.c, p.by).start()
        elif number == 3:
            diag_x(p.bd).wait_recv()
            diag_y(p.bd).wait_recv()
            core(3, p.c, p.bd).start()
        elif number == 4:
            if single:
                for d in steps:
                    lone(d, p.back(d), p.b, 1 - p.c)[2].wait_recv()
            for j, b in enumerate((p.b, p.bx, p.by, p.bd)):
                if j or not single:
                    core(j, 1 - p.c, b).wait_recv()
        elif number == 5:
            for d in range(1, p.depth):
                line(d, p.z).wait_send()
            if single:
                for d in steps:
                    for copy in lone(d, p.back(d), p.b, p.c):
                        copy.wait_send()
            else:
                near_x(p.b).wait_send()
                near_y(p.b).wait_send()
                core(0, p.c, p.b).wait_send()
            diag_x(p.by).wait_send()
            diag_y(p.bx).wait_send()
            for j, b in ((1, p.bx), (2, p.by), (3, p.bd)):
                core(j, p.c, b).wait_send()

    def tick(self, t):
        for number in range(5):
            self.stage(number, t - number)


class Scatter:
    def __init__(self, place, packed, from_core, near, diag, line, out, sems, credits):
        self.p, self.packed, self.from_core, self.near = place, packed, from_core, near
        self.diag, self.line, self.out, self.sems, self.credits = diag, line, out, sems, credits

    def stage(self, number, k):
        p, sems = self.p, self.sems.at[k]
        a, r0, n, nx = SCATTER_CHUNKS[k]
        ref, slot, depth = self.packed[a], k % 2, p.depth
        f0 = r0 if a == 0 else r0 + ROWS_MAIN
        whole, part_x, part_y = pl.ds(r0, n), pl.ds(r0, nx), pl.ds(r0 + nx, n - nx)
        core = lambda: rdma(ref.at[:, 1 - p.c, :, whole], self.from_core.at[slot, :, :, pl.ds(0, n)], sems, 0, 1, p.core)
        diag_x = lambda: rdma(ref.at[:, p.c, p.bd, part_x], self.diag.at[slot, :, pl.ds(0, nx)], sems, 2, 3, p.x)
        diag_y = lambda: rdma(ref.at[:, p.c, p.bd, part_y], self.diag.at[slot, :, pl.ds(nx, n - nx)], sems, 4, 5, p.y)
        near_x = lambda: rdma(ref.at[:, p.c, p.bx, whole], self.near.at[slot, 0, :, pl.ds(0, n)], sems, 6, 7, p.x)
        near_y = lambda: rdma(ref.at[:, p.c, p.by, whole], self.near.at[slot, 1, :, pl.ds(0, n)], sems, 8, 9, p.y)

        def along(d):
            z, to = p.along(d)
            return rdma(ref.at[z, p.c, p.b, whole], self.line.at[d - 1, pl.ds(f0, n)], sems, 8 + 2 * d, 9 + 2 * d, to)

        def ready(*which):
            if k >= 2:
                for w in which:
                    pl.semaphore_wait(self.credits.at[w], 1)

        def free(which, to):
            if k + 2 < COUNT:
                pl.semaphore_signal(self.credits.at[which], inc=1, device_id=to, device_id_type=MESH)

        if number == 0:
            ready(0)
            core().start()
        elif number == 1:
            core().wait_recv()

            @pl.loop(0, depth * 4)
            def _(i):
                z, b = i // 4, i % 4
                ref[z, p.c, b, r0 : r0 + n] = (
                    ref[z, p.c, b, r0 : r0 + n].astype(F32) + self.from_core[slot, z, b, 0:n].astype(F32)
                ).astype(BF)

            free(0, p.core)
            ready(1, 2)
            diag_x().start()
            diag_y().start()
        elif number == 2:
            diag_x().wait_recv()
            diag_y().wait_recv()

            @pl.loop(0, depth)
            def _(z):
                for b, s0, m in ((p.by, 0, nx), (p.bx, nx, n - nx)):
                    ref[z, p.c, b, r0 + s0 : r0 + s0 + m] = (
                        ref[z, p.c, b, r0 + s0 : r0 + s0 + m].astype(F32) + self.diag[slot, z, s0 : s0 + m].astype(F32)
                    ).astype(BF)

            free(1, p.x)
            free(2, p.y)
            ready(3, 4)
            near_x().start()
            near_y().start()
        elif number == 3:
            near_x().wait_recv()
            near_y().wait_recv()

            @pl.loop(0, depth)
            def _(z):
                ref[z, p.c, p.b, r0 : r0 + n] = (
                    ref[z, p.c, p.b, r0 : r0 + n].astype(F32)
                    + self.near[slot, 0, z, 0:n].astype(F32)
                    + self.near[slot, 1, z, 0:n].astype(F32)
                ).astype(BF)

            free(3, p.x)
            free(4, p.y)
            for d in range(1, depth):
                along(d).start()
        elif number == 4:
            for d in range(1, depth):
                along(d).wait_recv()
            total = ref[p.z, p.c, p.b, r0 : r0 + n].astype(F32)
            for d in range(1, depth):
                total = total + self.line[d - 1, f0 : f0 + n].astype(F32)
            self.out[f0 : f0 + n] = total
        elif number == 5:
            for each in (core, diag_x, diag_y, near_x, near_y):
                each().wait_send()
            for d in range(1, depth):
                along(d).wait_send()


EPSILON = 1e-05
TOK = 1024
SEQS = 4
SPAN = 256
STEPS = 32
SEG = 8
LANE = 128
WINDOW = 256
VECTORS = 11


def window_of(i):
    return min(i * 24 // LANE, WIDE // LANE - 2) * LANE


def spread_lanes(v):
    return jnp.concatenate([v] * (WIDE // LANE), axis=1)


def unit_norm(v):
    center = v - jnp.mean(v, axis=-1, keepdims=True)
    factor = lax.rsqrt(jnp.mean(center * center, axis=-1, keepdims=True) + EPSILON)
    return center * factor, factor


def sigmoid(v):
    return 1.0 / (1.0 + jnp.exp(-v))


def first_rows(halo_row, last_group):
    moved = pltpu.roll(last_group, 1, axis=0)
    at_top = lax.broadcasted_iota(jnp.int32, moved.shape, 0) == 0
    return jnp.where(at_top, halo_row, moved)


def permute_in(src, dst, tmp):
    @pl.loop(0, SEQS)
    def _(j):
        base = pl.multiple_of(j * SPAN, SPAN)
        for l in range(WIDE // LANE):
            tmp[l] = src[pl.ds(base, SPAN), l * LANE : (l + 1) * LANE].astype(F32)

        @pl.loop(0, STEPS // 2)
        def _(s):
            for l in range(WIDE // LANE):
                two = jnp.concatenate([tmp[l, pl.ds(2 * s, SEG, stride=STEPS), :], tmp[l, pl.ds(2 * s + 1, SEG, stride=STEPS), :]], axis=0)
                dst[pl.ds(pl.multiple_of(base + s * 16, 16), 16), l * LANE : (l + 1) * LANE] = two.astype(BF)


class Spill:
    def __init__(self, sems):
        self.sems, self.copies, self.used = sems, {}, 0

    def start(self, name, src, dst):
        self.copies[name] = pltpu.make_async_copy(src, dst, self.sems.at[self.used])
        self.used += 1
        self.copies[name].start()

    def wait(self, *names):
        for name in names or list(self.copies):
            self.copies.pop(name).wait()


class Line:
    def __init__(self, place):
        self.p = place
        self.n = lax.axis_size("seq")

    def all(self, buf, sems):
        p, copies = self.p, []
        for d in range(1, self.n):
            to = (lax.rem(p.s + d, self.n), p.b)
            copies.append(rdma(buf.at[p.s], buf.at[p.s], sems, d, self.n + d, to))
        return copies

    def shift(self, src, dst, sems, step):
        return rdma(src, dst, sems, 0, 1, (lax.rem(self.p.s + self.n + step, self.n), self.p.b))


def relayout(st, dst, depth, r0, n, targets):
    @pl.loop(0, depth * 2)
    def _(i):
        z, c = i // 2, i % 2
        slabs = [st[z, c, b, r0 : r0 + n].astype(F32) for b in range(4)]
        rows = pl.ds(pl.multiple_of(i * 96, 96), 96)
        for index, at in targets:
            dst[index, rows] = jnp.concatenate([v[at : at + 24] for v in slabs], axis=0).astype(BF)


def matmul(left, right, out, rows=512):
    @pl.loop(0, TOK // rows)
    def _(i):
        r = pl.ds(pl.multiple_of(i * rows, rows), rows)
        out[r] = jnp.dot(left[r], right[...], preferred_element_type=F32)


def forward_kernel(x_in, keep_in, up_in, vec_in, wk, wv, wr, wo, ws, we_in, wc_in,
                   o_w, o_e, o_c, o_ki, o_spa, o_spb, o_mixed, o_ei, o_si, o_gc, o_gs, o_xp, o_up, o_sq, o_pkc,
                   o_kvg, o_nd, o_first, o_vec, o_alive, o_bo,
                   st, cw, wd, we, u0, xp, u1, gyp, tmp, keep, xa, ki, kvg, nd, spb, vec, states, alive, seg, carry, hx, hx_got, hb, hb_got,
                   gsems, asems, ssems, hsems, lsems):
    place = Place()
    line = Line(place)
    depth = place.depth
    devices = depth * 8
    me = place.s * 4 + place.b
    spill = Spill(lsems)
    spill.start("x", x_in, u0)
    spill.start("keep", keep_in, keep)
    spill.start("up", up_in, u1)
    z, c, b = place.z, place.c, place.b
    as32 = lambda ref: ref[...].astype(F32)
    join = lambda *v: jnp.concatenate(v, axis=0).astype(BF)
    start = me * 24
    low = jnp.minimum(start // LANE, WIDE // LANE - 2) * LANE
    wide = pltpu.roll(jnp.concatenate([vec_in[...], jnp.zeros((16, LANE), F32)], axis=1), start - low, axis=1)
    small = jnp.concatenate([wide[0:8], wide[8:16], jnp.zeros((8, WIDE - 2 * WINDOW), F32)], axis=1)
    st[z, c, b, 48:80] = join(as32(wr), small)
    st[z, c, b, 0:48] = join(as32(wk), as32(wv))
    enter(place)
    gather = Gather(place, (st, cw), gsems)
    gather.tick(0)
    st[z, c, b, 80:128] = join(as32(wo), as32(ws))
    e = as32(we_in)
    for h in range(2):
        st[z, c, b, 128 + 48 * h : 176 + 48 * h] = join(e[:, 2 * h * WIDE : (2 * h + 1) * WIDE], e[:, (2 * h + 1) * WIDE : (2 * h + 2) * WIDE])
    cw[z, c, b] = wc_in[...]

    spill.wait("x")
    for j in range(SEQS):
        hx[j : j + 1] = u0[SPAN * j + SPAN - 16 : SPAN * j + SPAN].astype(F32)[15:16]
    hx[SEQS:8] = jnp.zeros((8 - SEQS, WIDE), F32)
    send_hx = line.shift(hx, hx_got, hsems.at[0], 1)
    send_hx.start()
    spill.wait("keep")
    for j in range(SEQS):
        low_keep = jnp.min(keep[SPAN * j : SPAN * (j + 1)], axis=0, keepdims=True)
        alive[place.s, j : j + 1] = low_keep
        alive[place.s, SEQS + j : SEQS + j + 1] = low_keep
    send_alive = line.all(alive, asems)
    for copy in send_alive:
        copy.start()
    gather.tick(1)
    permute_in(u0, xp, tmp)
    spill.start("xp", xp, o_xp)
    gather.tick(2)
    spill.wait("up")
    permute_in(u1, gyp, tmp)
    spill.start("gyp", gyp, o_up)
    gather.tick(3)
    gather.tick(4)
    vec[...] = jnp.zeros_like(vec)
    for i in range(devices):
        w = window_of(i)
        got = st[i // 8, i // 4 % 2, i % 4, 64:80].astype(F32)[8:16]
        vec[0:8, w : w + WINDOW] += got[:, 0:WINDOW]
        vec[8:16, w : w + WINDOW] += got[:, WINDOW : 2 * WINDOW]
    spill.start("vec", vec, o_vec)

    gain_a, bias_a = vec[0:1], vec[1:2]

    def norm_rows(j, rows_of, gain, bias):
        @pl.loop(0, SPAN // 16, unroll=8)
        def _(t):
            v = rows_of(pl.ds(pl.multiple_of(j * SPAN + t * 16, 16), 16))
            xa[j, pl.ds(pl.multiple_of(8 + t * 16, 8), 16)] = unit_norm(v)[0] * gain + bias

    @pl.loop(0, SEQS)
    def _(j):
        norm_rows(j, lambda r: xp[r].astype(F32), gain_a, bias_a)

    not_first = jnp.where(place.s > 0, 1.0, 0.0).astype(F32)
    line.shift(hx, hx_got, hsems.at[0], 1).wait_recv()
    before = (unit_norm(hx_got[...])[0] * gain_a + bias_a) * not_first
    for j in range(SEQS):
        xa[j, 0:8] = first_rows(before[j : j + 1], xa[j, SPAN : SPAN + 8])

    def blends(j, ratios, outs, spread_out):
        @pl.loop(0, SPAN // 16)
        def _(t):
            r = pl.ds(pl.multiple_of(j * SPAN + t * 16, 16), 16)
            prev = xa[j, pl.ds(pl.multiple_of(t * 16, 8), 16)] * spread_lanes(keep[r])
            spread = xa[j, pl.ds(pl.multiple_of(8 + t * 16, 8), 16)] - prev
            spread_out[r] = spread.astype(BF)
            for ratio, out in zip(ratios, outs):
                out[r] = (prev + spread * ratio).astype(BF)

    @pl.loop(0, SEQS)
    def _(j):
        blends(j, [vec[4:5], vec[5:6], vec[6:7]], [ki.at[0], ki.at[1], ki.at[2]], u0)

    spill.start("ki", ki, o_ki)
    spill.start("spa", u0, o_spa)
    gather.tick(5)
    relayout(st, wd, depth, 0, 48, ((0, 0), (1, 24)))
    relayout(st, wd, depth, 48, 32, ((2, 0),))
    for m in range(3):
        matmul(ki.at[m], wd.at[m], kvg.at[m])
    spill.start("kvg", kvg, o_kvg)

    shrink = jnp.exp(-vec[9:10])
    bonus = vec[10:11]
    shrink8 = jnp.broadcast_to(shrink, (SEG, WIDE))
    row = lax.broadcasted_iota(jnp.int32, (SEG, WIDE), 0)

    @pl.loop(0, SEQS)
    def _(j):
        def step(s, state):
            decay, numer, denom = state
            r = pl.ds(pl.multiple_of(j * SPAN + s * SEG, SEG), SEG)
            m = spread_lanes(keep[r]) * shrink8
            ek = jnp.exp(kvg[0, r])
            return decay * m, numer * m + ek * kvg[1, r], denom * m + ek

        zero = jnp.zeros((SEG, WIDE), F32)
        decay, numer, denom = lax.fori_loop(0, STEPS, step, (zero + 1.0, zero, zero), unroll=4)
        for d in (1, 2, 4):
            top = row < d
            numer, denom, decay = (
                numer + decay * jnp.where(top, 0.0, pltpu.roll(numer, d, axis=0)),
                denom + decay * jnp.where(top, 0.0, pltpu.roll(denom, d, axis=0)),
                decay * jnp.where(top, 1.0, pltpu.roll(decay, d, axis=0)),
            )
        states[place.s, pl.ds(j, 1)] = numer[SEG - 1 : SEG]
        states[place.s, pl.ds(SEQS + j, 1)] = denom[SEG - 1 : SEG]
        seg[j, 0] = jnp.where(row < 1, 1.0, pltpu.roll(decay, 1, axis=0))
        seg[j, 1] = jnp.where(row < 1, 0.0, pltpu.roll(numer, 1, axis=0))
        seg[j, 2] = jnp.where(row < 1, 0.0, pltpu.roll(denom, 1, axis=0))

    send_states = line.all(states, ssems)
    for copy in send_states:
        copy.start()
    gather.tick(6)
    relayout(st, wd, depth, 80, 48, ((3, 0), (4, 24)))
    spill.start("w", wd, o_w)
    for d in range(1, line.n):
        src = lax.rem(place.s + line.n - d, line.n)
        rdma(alive.at[src], alive.at[src], asems, d, line.n + d, (src, b)).wait_recv()
        rdma(states.at[src], states.at[src], ssems, d, line.n + d, (src, b)).wait_recv()
    spill.start("alive", alive, o_alive)
    whole = jnp.exp(-float(SPAN) * vec[9:10])
    arrived = jnp.zeros((SEG, WIDE), F32)
    for src in range(7):
        after = spread_lanes(alive[src]) * whole * arrived + states[src]
        arrived = jnp.where(src < place.s, after, arrived)
    carry[...] = arrived

    for j in range(SEQS):
        slot = j % 2
        if j >= 2:
            spill.wait(("nd", j - 2))
        into = nd.at[slot]
        base = j * SPAN
        numer0 = seg[j, 0] * carry[j : j + 1] + seg[j, 1]
        denom0 = seg[j, 0] * carry[SEQS + j : SEQS + j + 1] + seg[j, 2]

        def steps(i, state):
            numer, denom = state
            mixes = []
            for q in range(2):
                lo = pl.multiple_of(i * 16 + q * 8, 8)
                r = pl.ds(pl.multiple_of(base + lo, 8), SEG)
                kept = spread_lanes(keep[r])
                numer, denom = numer * kept, denom * kept
                into[0, pl.ds(lo, SEG)] = numer
                into[1, pl.ds(lo, SEG)] = denom
                k, v = kvg[0, r], kvg[1, r]
                now, ek = jnp.exp(bonus + k), jnp.exp(k)
                wkv = (numer + now * v) / (denom + now)
                mixes.append(sigmoid(kvg[2, r]) * wkv)
                numer, denom = shrink8 * numer + ek * v, shrink8 * denom + ek
            u1[pl.ds(pl.multiple_of(base + i * 16, 16), 16)] = jnp.concatenate(mixes, axis=0).astype(BF)
            return numer, denom

        lax.fori_loop(0, STEPS // 2, steps, (numer0, denom0))
        spill.start(("nd", j), into, o_nd.at[:, pl.ds(base, SPAN)])
    spill.start("mixed", u1, o_mixed)
    spill.wait("kvg")
    first = kvg.at[0]

    @pl.loop(0, TOK // 256)
    def _(i):
        r = pl.ds(pl.multiple_of(i * 256, 256), 256)
        first[r] = xp[r].astype(F32) + jnp.dot(u1[r], wd[3], preferred_element_type=F32)

    spill.start("first", first, o_first)

    @pl.loop(0, SEQS)
    def _(j):
        norm_rows(j, lambda r: first[r], vec[2:3], vec[3:4])

    for j in range(SEQS):
        hb[j : j + 1] = xa[j, SPAN : SPAN + 8][7:8]
    hb[SEQS:8] = jnp.zeros((8 - SEQS, WIDE), F32)
    send_hb = line.shift(hb, hb_got, hsems.at[1], 1)
    send_hb.start()
    gather.tick(7)
    relayout(st, we, depth, 128, 48, ((0, 0), (1, 24)))
    spill.wait("ki")
    send_hb.wait_recv()
    before_b = hb_got[...] * not_first
    for j in range(SEQS):
        xa[j, 0:8] = first_rows(before_b[j : j + 1], xa[j, SPAN : SPAN + 8])

    @pl.loop(0, SEQS)
    def _(j):
        blends(j, [vec[7:8], vec[8:9]], [ki.at[0], ki.at[1]], spb)

    spill.start("spb", spb, o_spb)
    spill.start("ei", ki.at[0], o_ei)
    spill.start("si", ki.at[1], o_si)
    sig = kvg.at[1]

    @pl.loop(0, TOK // 256)
    def _(i):
        r = pl.ds(pl.multiple_of(i * 256, 256), 256)
        chosen = sigmoid(jnp.dot(ki[1, r], wd[4], preferred_element_type=F32))
        sig[r] = chosen
        ki[2, r] = (gyp[r].astype(F32) * chosen).astype(BF)

    spill.start("gc", ki.at[2], o_gc)
    def square(f):
        @pl.loop(0, depth, unroll=4)
        def _(i):
            r = pl.ds(pl.multiple_of(i * 256, 256), 256)
            positive = jnp.maximum(jnp.dot(ki[0, r], we[f], preferred_element_type=F32), 0.0)
            st[i, :, :, 96 + 32 * f : 128 + 32 * f] = (positive * positive).astype(BF).reshape(2, 4, 32, WIDE)

    def contract_grad(f):
        left = st[:, :, :, 96 + 32 * f : 128 + 32 * f].reshape(TOK, WIDE)
        for h in range(2):
            got = lax.dot_general(left[:, 384 * h : 384 * (h + 1)], ki[2], (((0,), (0,)), ((), ())), preferred_element_type=F32)
            st[f, h, :, 0:96] = got.astype(BF).reshape(4, 96, WIDE)

    for k in range(4):
        gather.stage(5, k)
    square(0)
    square(1)
    gather.tick(8)
    relayout(st, we, depth, 176, 48, ((2, 0), (3, 24)))
    spill.start("e", we, o_e)
    gather.stage(5, 4)
    square(2)
    square(3)
    contract_grad(0)
    contract_grad(1)
    gather.tick(9)
    contract_grad(2)
    contract_grad(3)
    gather.tick(10)
    spill.start("c", cw, o_c)
    spill.start("pkc", st.at[:, :, :, pl.ds(0, 96)], o_pkc)
    spill.start("sq", st.at[:, :, :, pl.ds(96, 128)], o_sq)
    spill.wait("mixed", "spa")

    @pl.loop(0, depth)
    def _(i):
        r = pl.ds(pl.multiple_of(i * 256, 256), 256)
        total = jnp.zeros((256, WIDE), F32)
        for f in range(4):
            part = st[i, :, :, 96 + 32 * f : 128 + 32 * f].reshape(256, WIDE)
            total = total + jnp.dot(part, cw[f].reshape(WIDE, WIDE), preferred_element_type=F32)
        chosen = sig[r]
        u1[r] = (first[r] + chosen * total).astype(BF)
        u0[r] = (gyp[r].astype(F32) * total * chosen * (1.0 - chosen)).astype(BF)

    spill.start("gs", u0, o_gs)
    spill.start("bo", u1, o_bo)
    for copy in send_alive + send_states + [send_hx, send_hb]:
        copy.wait_send()
    for k in range(5, COUNT):
        gather.stage(5, k)
    spill.wait()


def forward_call(x, keep, up, vec, shards, depth):
    hbm, vmem = pl.BlockSpec(memory_space=pl.ANY), pl.BlockSpec(memory_space=pltpu.VMEM)
    s = jax.ShapeDtypeStruct
    seq = depth * 2
    devices = depth * 8
    rows = (TOK, WIDE)
    outs = dict(
        w=s((5, WIDE, WIDE), BF), e=s((4, WIDE, WIDE), BF), c=s((depth, 2, 4, 96, WIDE), BF), ki=s((3,) + rows, BF),
        spa=s(rows, BF), spb=s(rows, BF), mixed=s(rows, BF), ei=s(rows, BF), si=s(rows, BF), gc=s(rows, BF), gs=s(rows, BF),
        xp=s(rows, BF), up=s(rows, BF), sq=s((depth, 2, 4, 128, WIDE), BF), pkc=s((depth, 2, 4, 96, WIDE), BF),
        kvg=s((3,) + rows, F32), nd=s((2,) + rows, F32), first=s(rows, F32), vec=s((16, WIDE), F32), alive=s((seq, 8, LANE), F32),
        bo=s(rows, BF))
    scratch = [
        pltpu.VMEM((depth, 2, 4, ROWS_MAIN, WIDE), BF), pltpu.VMEM((depth, 2, 4, ROWS_LAST, WIDE), BF),
        pltpu.VMEM((5, WIDE, WIDE), BF), pltpu.VMEM((4, WIDE, WIDE), BF),
        pltpu.VMEM(rows, BF), pltpu.VMEM(rows, BF), pltpu.VMEM(rows, BF), pltpu.VMEM(rows, BF),
        pltpu.VMEM((6, SPAN, LANE), F32), pltpu.VMEM((TOK, LANE), F32), pltpu.VMEM((SEQS, SPAN + 8, WIDE), F32),
        pltpu.VMEM((3,) + rows, BF), pltpu.VMEM((3,) + rows, F32), pltpu.VMEM((2, 2, SPAN, WIDE), F32), pltpu.VMEM(rows, BF),
        pltpu.VMEM((16, WIDE), F32), pltpu.VMEM((seq, 8, WIDE), F32), pltpu.VMEM((seq, 8, LANE), F32),
        pltpu.VMEM((SEQS, 3, SEG, WIDE), F32), pltpu.VMEM((8, WIDE), F32),
        pltpu.VMEM((8, WIDE), F32), pltpu.VMEM((8, WIDE), F32), pltpu.VMEM((8, WIDE), F32), pltpu.VMEM((8, WIDE), F32),
        pltpu.SemaphoreType.DMA((COUNT, 46)), pltpu.SemaphoreType.DMA((2 * seq,)),
        pltpu.SemaphoreType.DMA((2 * seq,)), pltpu.SemaphoreType.DMA((2, 2)), pltpu.SemaphoreType.DMA((32,)),
    ]
    got = pl.pallas_call(
        forward_kernel,
        out_shape=tuple(outs.values()),
        in_specs=[hbm, hbm, hbm] + [vmem] * 8,
        out_specs=tuple(hbm for _ in outs),
        scratch_shapes=scratch,
        compiler_params=pltpu.CompilerParams(collective_id=0, has_side_effects=True, vmem_limit_bytes=62 << 20),
        cost_estimate=pl.CostEstimate(flops=2 * 1024 * 12 * 768 * 768, bytes_accessed=60 << 20, transcendentals=0),
    )(x, keep, up, vec, *shards)
    return dict(zip(outs, got))


NT = (((1,), (1,)), ((), ()))
TN = (((0,), (0,)), ((), ()))


def backward_kernel(i_w, i_e, i_c, i_ki, i_spa, i_spb, i_mixed, i_ei, i_si, i_gc, i_gs, i_xp, i_up, i_sq, i_pkc, i_kvg, i_nd, i_first, i_vec,
                    i_alive, i_keep,
                    o_out, o_tokens, o_vec,
                    main, last, from_core, near, diag, lines, out, we, cw, p, q, xg, keep, vec, alive, states, seg, vg, vr, hx, hx_got, hb, hb_got,
                    rsems, credits, ssems, hsems, zsems, lsems):
    place = Place()
    line = Line(place)
    depth = place.depth
    z, c, b = place.z, place.c, place.b
    spill = Spill(lsems)
    spill.start("pkc", i_pkc, last)
    spill.start("cw", i_c, cw)
    spill.start("keep", i_keep, keep)
    spill.start("vec", i_vec, vec)
    spill.start("alive", i_alive, alive)
    spill.start("we", i_e, we)
    enter(place)
    scatter = Scatter(place, (main, last), from_core, near, diag, lines, out, rsems, credits)
    run = scatter.stage
    vg[...] = jnp.zeros_like(vg)
    not_last = jnp.where(place.s < line.n - 1, 1.0, 0.0).astype(F32)

    def pack(first, second, r0):
        @pl.loop(0, depth * 2)
        def _(i):
            rows = pl.ds(pl.multiple_of(i * 96, 96), 96)
            u = first[rows].astype(F32)
            v = None if second is None else second[rows].astype(F32)
            for k in range(4):
                mine = u[24 * k : 24 * k + 24]
                other = jnp.zeros((8, WIDE), F32) if v is None else v[24 * k : 24 * k + 24]
                joined = jnp.concatenate([mine, other], axis=0)
                main[i // 2, i % 2, k, r0 : r0 + joined.shape[0]] = joined.astype(BF)

    def outer(left, right, into):
        for h in range(2):
            cols = slice(384 * h, 384 * h + 384)
            into[cols] = lax.dot_general(left[:, cols], right[...], TN, preferred_element_type=F32).astype(BF)

    def fold(v):
        return v[0:8] + v[8:16]

    def following_rows(halo):
        for j in range(SEQS):
            moved = pltpu.roll(xg[j, 0:8], SEG - 1, axis=0)
            at_end = lax.broadcasted_iota(jnp.int32, moved.shape, 0) == SEG - 1
            xg[j, SPAN : SPAN + 8] = jnp.where(at_end, halo[j : j + 1], moved)

    def send_first(src, dst, sems):
        for j in range(SEQS):
            src[j : j + 1] = xg[j, 0:8][0:1]
        src[SEQS:8] = jnp.zeros((8 - SEQS, WIDE), F32)
        copy = line.shift(src, dst, sems, -1)
        copy.start()
        return copy

    def norm_back(rows, gain, source, gain_at, bias_at, finish):
        @pl.loop(0, SEQS)
        def _(j):
            def tile(t, sums):
                r = pl.ds(pl.multiple_of(j * SPAN + t * 16, 16), 16)
                grad = rows[r] + xg[j, pl.ds(pl.multiple_of(t * 16 + 8, 8), 16)]
                unit, factor = unit_norm(source(r))
                h = grad * gain
                back = factor * (h - jnp.mean(h, axis=-1, keepdims=True) - unit * jnp.mean(h * unit, axis=-1, keepdims=True))
                finish(r, back)
                return sums[0] + fold(grad * unit), sums[1] + fold(grad)

            zero = jnp.zeros((8, WIDE), F32)
            sums = lax.fori_loop(0, SPAN // 16, tile, (zero, zero), unroll=8)
            vg[gain_at] += sums[0]
            vg[bias_at] += sums[1]

    def channel_mix(gc, ei, si, gs, sqb, ge, gt):
        load = lambda f: spill.start(("sq", f), i_sq.at[:, :, :, pl.ds(32 * f, 32)], sqb.at[f % 2])
        spill.start("gc", i_gc, gc)
        load(0)
        load(1)
        spill.start("ei", i_ei, ei)
        spill.start("si", i_si, si)
        spill.start("gs", i_gs, gs)
        spill.wait("pkc")
        run(0, 0)
        run(0, 1)
        spill.wait("cw", "gc")

        def expand_back(f):
            spill.wait(("sq", f))

            @pl.loop(0, TOK // 256, unroll=4)
            def _(i):
                r = pl.ds(pl.multiple_of(i * 256, 256), 256)
                grad = lax.dot_general(gc[r], cw[f].reshape(WIDE, WIDE), NT, preferred_element_type=F32)
                positive = jnp.sqrt(sqb[f % 2, i].reshape(256, WIDE).astype(F32))
                ge[r] = (2.0 * positive * grad).astype(BF)

            if f + 2 < 4:
                load(f + 2)

        def expand_in_back(f):
            @pl.loop(0, TOK // 512)
            def _(i):
                r = pl.ds(pl.multiple_of(i * 512, 512), 512)
                got = lax.dot_general(ge[r], we[f], NT, preferred_element_type=F32)
                p[r] = got if f == 0 else p[r] + got

        expand_back(0)
        spill.wait("ei", "we")
        outer(ei, ge, gt.at[0])
        run(1, 0)
        expand_in_back(0)
        spill.start("ws", i_w.at[4], we.at[0])
        expand_back(1)
        outer(ei, ge, gt.at[1])
        pack(gt.at[0], gt.at[1], 128)
        run(2, 0)
        run(1, 1)
        run(0, 2)
        expand_in_back(1)
        spill.start("wo", i_w.at[3], we.at[1])
        expand_back(2)
        outer(ei, ge, gt.at[0])
        expand_in_back(2)
        run(2, 1)
        expand_back(3)
        run(1, 2)
        outer(ei, ge, gt.at[1])
        pack(gt.at[0], gt.at[1], 176)
        run(0, 3)
        run(3, 0)
        expand_in_back(3)
        spill.wait("si", "gs", "ws", "wo")
        spill.start("wk", i_w.at[0], we.at[2])
        spill.start("wv", i_w.at[1], we.at[3])
        spill.start("spb", i_spb, gc)
        outer(si, gs, gt.at[1])
        run(2, 2)

        @pl.loop(0, TOK // 512)
        def _(i):
            r = pl.ds(pl.multiple_of(i * 512, 512), 512)
            q[r] = lax.dot_general(gs[r], we[0], NT, preferred_element_type=F32)

        spill.start("wr", i_w.at[2], we.at[0])
        spill.start("gyp", i_up, ge)
        spill.start("mixed", i_mixed, ei)
        spill.wait("keep", "vec", "spb")
        run(1, 3)
        re, rs = vec[7:8], vec[8:9]

        @pl.loop(0, SEQS)
        def _(j):
            def tile(t, sums):
                r = pl.ds(pl.multiple_of(j * SPAN + t * 16, 16), 16)
                ge_in, gs_in, spread = p[r], q[r], gc[r].astype(F32)
                xg[j, pl.ds(pl.multiple_of(t * 16, 16), 16)] = (ge_in * (1.0 - re) + gs_in * (1.0 - rs)) * spread_lanes(keep[r])
                p[r] = ge_in * re + gs_in * rs
                return sums[0] + fold(ge_in * spread), sums[1] + fold(gs_in * spread)

            zero = jnp.zeros((8, WIDE), F32)
            sums = lax.fori_loop(0, SPAN // 16, tile, (zero, zero))
            vg[7] += sums[0]
            vg[8] += sums[1]

        send = send_first(hb, hb_got, hsems.at[0])
        spill.start("first", i_first, q)
        run(3, 1)
        run(4, 0)
        spill.wait("gyp", "mixed", "first")
        send.wait_recv()
        following_rows(hb_got[...] * not_last)

        def finish(r, back):
            grad = ge[r].astype(F32) + back
            p[r] = grad
            si[r] = grad.astype(BF)

        norm_back(p, vec[2:3], lambda r: q[r], 2, 3, finish)
        send.wait_send()
        run(2, 3)
        run(3, 2)
        outer(ei, si, gt.at[0])
        pack(gt.at[0], gt.at[1], 80)
        run(0, 4)
        run(4, 1)

        @pl.loop(0, TOK // 512)
        def _(i):
            r = pl.ds(pl.multiple_of(i * 512, 512), 512)
            q[r] = lax.dot_general(si[r], we[1], NT, preferred_element_type=F32)

        spill.wait("wk", "wv", "wr")

    unit = pltpu.VMEM((TOK, WIDE), BF)
    pl.run_scoped(channel_mix, unit, unit, unit, unit, pltpu.VMEM((2, depth, 2, 4, 32, WIDE), BF), unit,
                  pltpu.VMEM((2, WIDE, WIDE), BF))
    spill.wait("alive")
    shrink = jnp.exp(-vec[9:10])
    shrink8 = jnp.broadcast_to(shrink, (SEG, WIDE))
    bonus = vec[10:11]
    row = lax.broadcasted_iota(jnp.int32, (SEG, WIDE), 0)
    zero = jnp.zeros((SEG, WIDE), F32)

    def time_mix(gkvg):
        def sweeps(buf):
            def load(j, name):
                spill.start((name, "kvg", j), i_kvg.at[:, pl.ds(j * SPAN, SPAN)], buf.at[j % 2, pl.ds(0, 3)])
                spill.start((name, "nd", j), i_nd.at[:, pl.ds(j * SPAN, SPAN)], buf.at[j % 2, pl.ds(3, 2)])

            def arrive(j, name):
                spill.wait((name, "kvg", j), (name, "nd", j))

            load(0, 1)
            load(1, 1)
            for j in range(SEQS):
                arrive(j, 1)
                at = buf.at[j % 2]

                def back(i, state):
                    decay, numer, denom, bonus_sum = state
                    gates = [None, None]
                    for h in (1, 0):
                        lo = pl.multiple_of((STEPS // 2 - 1 - i) * 16 + 8 * h, 8)
                        r = pl.ds(pl.multiple_of(j * SPAN + lo, 8), SEG)
                        here = pl.ds(lo, SEG)
                        kept = spread_lanes(keep[r])
                        k, v = at[0, here], at[1, here]
                        now = jnp.exp(bonus + k)
                        inverse = 1.0 / (at[4, here] + now)
                        wkv = (at[3, here] + now * v) * inverse
                        s = sigmoid(at[2, here])
                        gm = q[r]
                        gw = gm * s
                        gates[h] = gw * wkv * (1.0 - s)
                        dn = gw * inverse
                        dd = -dn * wkv
                        q[r] = dn
                        bonus_sum = bonus_sum + now * (dn * v + dd)
                        m = kept * shrink8
                        decay, numer, denom = decay * m, numer * m + kept * dn, denom * m + kept * dd
                    rows = pl.ds(pl.multiple_of(j * SPAN + (STEPS // 2 - 1 - i) * 16, 16), 16)
                    gkvg[2, rows] = jnp.concatenate(gates, axis=0).astype(BF)
                    return decay, numer, denom, bonus_sum

                decay, numer, denom, bonus_sum = lax.fori_loop(0, STEPS // 2, back, (zero + 1.0, zero, zero, zero))
                load(j + 2, 1) if j + 2 < SEQS else load(j - 2, 2)
                vg[10] += bonus_sum
                for d in (1, 2, 4):
                    end = row >= SEG - d
                    numer, denom, decay = (
                        numer + decay * jnp.where(end, 0.0, pltpu.roll(numer, SEG - d, axis=0)),
                        denom + decay * jnp.where(end, 0.0, pltpu.roll(denom, SEG - d, axis=0)),
                        decay * jnp.where(end, 1.0, pltpu.roll(decay, SEG - d, axis=0)),
                    )
                states[place.s, j : j + 1] = numer[0:1]
                states[place.s, SEQS + j : SEQS + j + 1] = denom[0:1]
                end = row >= SEG - 1
                seg[j, 0] = jnp.where(end, 1.0, pltpu.roll(decay, SEG - 1, axis=0))
                seg[j, 1] = jnp.where(end, 0.0, pltpu.roll(numer, SEG - 1, axis=0))
                seg[j, 2] = jnp.where(end, 0.0, pltpu.roll(denom, SEG - 1, axis=0))
                if j == 0:
                    run(1, 4)
                if j == 3:
                    run(2, 4)
            sent = line.all(states, ssems)
            for copy in sent:
                copy.start()
            run(3, 3)
            run(4, 2)
            for d in range(1, line.n):
                src = lax.rem(place.s + line.n - d, line.n)
                rdma(states.at[src], states.at[src], ssems, d, line.n + d, (src, b)).wait_recv()
            whole = jnp.exp(-float(SPAN) * vec[9:10])
            arrived = zero
            for src in range(7, 0, -1):
                after = spread_lanes(alive[src]) * whole * arrived + states[src]
                arrived = jnp.where(src > place.s, after, arrived)
            for j in range(SEQS):
                arrive(j, 2)
                at = buf.at[j % 2]
                numer0 = seg[j, 0] * arrived[j : j + 1] + seg[j, 1]
                denom0 = seg[j, 0] * arrived[SEQS + j : SEQS + j + 1] + seg[j, 2]

                def back(i, state):
                    an, ad, decay_sum = state
                    keys, values = [None, None], [None, None]
                    for h in (1, 0):
                        lo = pl.multiple_of((STEPS // 2 - 1 - i) * 16 + 8 * h, 8)
                        r = pl.ds(pl.multiple_of(j * SPAN + lo, 8), SEG)
                        here = pl.ds(lo, SEG)
                        kept = spread_lanes(keep[r])
                        k, v, numer, denom = at[0, here], at[1, here], at[3, here], at[4, here]
                        now, ek = jnp.exp(bonus + k), jnp.exp(k)
                        wkv = (numer + now * v) / (denom + now)
                        dn = q[r]
                        dd = -dn * wkv
                        keys[h] = ek * (an * v + ad) + now * (dn * v + dd)
                        values[h] = ek * an + now * dn
                        decay_sum = decay_sum + an * numer + ad * denom
                        an, ad = kept * (dn + shrink8 * an), kept * (dd + shrink8 * ad)
                    rows = pl.ds(pl.multiple_of(j * SPAN + (STEPS // 2 - 1 - i) * 16, 16), 16)
                    gkvg[0, rows] = jnp.concatenate(keys, axis=0).astype(BF)
                    gkvg[1, rows] = jnp.concatenate(values, axis=0).astype(BF)
                    return an, ad, decay_sum

                _, _, decay_sum = lax.fori_loop(0, STEPS // 2, back, (numer0, denom0, zero))
                if j + 2 < SEQS:
                    load(j + 2, 2)
                vg[9] += -shrink * decay_sum
            for copy in sent:
                copy.wait_send()
            run(4, 3)
            run(3, 4)

        pl.run_scoped(sweeps, pltpu.VMEM((2, 5, SPAN, WIDE), F32))

        def mixes(ki, spa, gt, parts):
            spill.start("ki0", i_ki.at[0], ki.at[0])
            spill.start("ki1", i_ki.at[1], ki.at[1])
            spill.start("spa", i_spa, spa)
            spill.wait("ki0")
            outer(ki.at[0], gkvg.at[0], gt.at[0])
            spill.start("ki2", i_ki.at[2], ki.at[0])
            spill.wait("ki1")
            outer(ki.at[1], gkvg.at[1], gt.at[1])
            spill.start("xp", i_xp, ki.at[1])
            pack(gt.at[0], gt.at[1], 0)
            run(0, 5)
            spill.wait("ki2")
            outer(ki.at[0], gkvg.at[2], gt.at[0])
            pack(gt.at[0], None, 48)
            run(0, 6)
            spill.wait("spa")
            ratios = [vec[4 + m : 5 + m] for m in range(3)]
            for j in range(SEQS):
                rows = pl.ds(j * SPAN, SPAN)
                for m, w in enumerate((we.at[2], we.at[3], we.at[0])):
                    parts[m] = lax.dot_general(gkvg[m, rows], w[...], NT, preferred_element_type=F32)

                def tile(t, sums):
                    r = pl.ds(pl.multiple_of(j * SPAN + t * 16, 16), 16)
                    here = pl.ds(pl.multiple_of(t * 16, 16), 16)
                    spread = spa[r].astype(F32)
                    g = [parts[m, here] for m in range(3)]
                    shifted = g[0] * (1.0 - ratios[0]) + g[1] * (1.0 - ratios[1]) + g[2] * (1.0 - ratios[2])
                    xg[j, here] = shifted * spread_lanes(keep[r])
                    q[r] = g[0] * ratios[0] + g[1] * ratios[1] + g[2] * ratios[2]
                    return tuple(s + fold(v * spread) for s, v in zip(sums, g))

                sums = lax.fori_loop(0, SPAN // 16, tile, (zero, zero, zero))
                for m in range(3):
                    vg[4 + m] += sums[m]
                if j == 0:
                    run(1, 5)
                    run(1, 6)
                if j == 2:
                    run(2, 5)
                    run(4, 4)
                if j == 3:
                    run(2, 6)
            send = send_first(hx, hx_got, hsems.at[1])
            spill.wait("xp")
            send.wait_recv()
            following_rows(hx_got[...] * not_last)

            def finish(r, back):
                p[r] = p[r] + back

            norm_back(q, vec[0:1], lambda r: ki[1, r].astype(F32), 0, 1, finish)
            send.wait_send()

        unit2 = pltpu.VMEM((2, TOK, WIDE), BF)
        pl.run_scoped(mixes, unit2, unit, pltpu.VMEM((2, WIDE, WIDE), BF), pltpu.VMEM((3, SPAN, WIDE), F32))

    pl.run_scoped(time_mix, pltpu.VMEM((3, TOK, WIDE), BF))
    spill.start("tokens", p, o_tokens)
    vr[0, VECTORS:16] = jnp.zeros((16 - VECTORS, WIDE), F32)
    for i in range(VECTORS):
        vr[0, i : i + 1] = jnp.sum(vg[i], axis=0, keepdims=True)

    def exchange(src, slot, to):
        copy = rdma(vr.at[src], vr.at[slot], zsems.at[slot], 0, 1, to)
        copy.start()
        return copy

    one = exchange(0, 1, place.core)
    run(3, 5)
    one.wait_recv()
    vr[2] = vr[0] + vr[1]
    two = exchange(2, 3, place.x)
    run(3, 6)
    two.wait_recv()
    vr[4] = vr[2] + vr[3]
    three = exchange(4, 5, place.y)
    three.wait_recv()
    vr[6] = vr[4] + vr[5]
    four = [exchange(6, 6 + d, place.along(d)[1]) for d in range(1, depth)]
    run(4, 5)
    run(4, 6)
    total = vr[6]
    for d in range(1, depth):
        four[d - 1].wait_recv()
        total = total + vr[6 + d]
    vr[6 + depth] = total
    me = place.s * 4 + place.b
    start = me * 24
    low = pl.multiple_of(jnp.minimum(start // LANE, WIDE // LANE - 2) * LANE, LANE)
    mine = vr[6 + depth, :, pl.ds(low, WINDOW)]
    o_vec[...] = pltpu.roll(mine, WINDOW - (start - low), axis=1)[:, 0:LANE]
    spill.start("out", out, o_out)
    for copy in [one, two, three] + four:
        copy.wait_send()
    for k in range(COUNT):
        run(5, k)
    spill.wait()


BACK_INPUTS = ("w", "e", "c", "ki", "spa", "spb", "mixed", "ei", "si", "gc", "gs", "xp", "up", "sq", "pkc", "kvg", "nd", "first", "vec", "alive")


def backward_call(f, keep, depth):
    hbm, vmem = pl.BlockSpec(memory_space=pl.ANY), pl.BlockSpec(memory_space=pltpu.VMEM)
    s = jax.ShapeDtypeStruct
    seq, rows = depth * 2, ROWS_MAIN + ROWS_LAST
    top = max(n for _, _, n, _ in SCATTER_CHUNKS)
    row8 = pltpu.VMEM((8, WIDE), F32)
    return pl.pallas_call(
        backward_kernel,
        out_shape=(s((rows, WIDE), F32), s((TOK, WIDE), F32), s((16, LANE), F32)),
        in_specs=[hbm] * (len(BACK_INPUTS) + 1),
        out_specs=(hbm, hbm, vmem),
        scratch_shapes=[
            pltpu.VMEM((depth, 2, 4, ROWS_MAIN, WIDE), BF), pltpu.VMEM((depth, 2, 4, ROWS_LAST, WIDE), BF),
            pltpu.VMEM((2, depth, 4, top, WIDE), BF), pltpu.VMEM((2, 2, depth, top, WIDE), BF), pltpu.VMEM((2, depth, top, WIDE), BF),
            pltpu.VMEM((depth - 1, rows, WIDE), BF), pltpu.VMEM((rows, WIDE), F32),
            pltpu.VMEM((4, WIDE, WIDE), BF), pltpu.VMEM((depth, 2, 4, 96, WIDE), BF),
            pltpu.VMEM((TOK, WIDE), F32), pltpu.VMEM((TOK, WIDE), F32), pltpu.VMEM((SEQS, SPAN + 8, WIDE), F32),
            pltpu.VMEM((TOK, LANE), F32), pltpu.VMEM((16, WIDE), F32), pltpu.VMEM((seq, 8, LANE), F32), pltpu.VMEM((seq, 8, WIDE), F32),
            pltpu.VMEM((SEQS, 3, SEG, WIDE), F32), pltpu.VMEM((VECTORS, 8, WIDE), F32), pltpu.VMEM((7 + depth, 16, WIDE), F32),
            row8, row8, row8, row8,
            pltpu.SemaphoreType.DMA((COUNT, 16)), pltpu.SemaphoreType.REGULAR((5,)), pltpu.SemaphoreType.DMA((2 * seq,)),
            pltpu.SemaphoreType.DMA((2, 2)), pltpu.SemaphoreType.DMA((7 + depth, 2)), pltpu.SemaphoreType.DMA((56,)),
        ],
        compiler_params=pltpu.CompilerParams(collective_id=1, has_side_effects=True, vmem_limit_bytes=62 << 20),
        cost_estimate=pl.CostEstimate(flops=2 * 1024 * 26 * 768 * 768, bytes_accessed=60 << 20, transcendentals=0),
    )(*[f[n] for n in BACK_INPUTS], keep)


def fast_body(layer_inputs, document_openings, wk, wv, wr, wo, we, ws, wc, *rest):
    vectors, upstream = rest[:VECTORS], rest[VECTORS]
    depth = lax.axis_size("seq") // 2
    keep = 1.0 - document_openings.astype(F32)
    keep = keep.reshape(SEQS, SEG, STEPS).transpose(0, 2, 1).reshape(TOK, 1)
    keep = jnp.broadcast_to(keep, (TOK, LANE))
    vec = jnp.pad(jnp.stack(vectors).astype(F32), ((0, 16 - VECTORS), (0, LANE - 24)))
    got = forward_call(layer_inputs.reshape(TOK, WIDE), keep, upstream.reshape(TOK, WIDE), vec, (wk, wv, wr, wo, ws, we, wc), depth)
    out, tokens, small = backward_call(got, keep, depth)

    def natural(v):
        return v.reshape(SEQS, STEPS, SEG, WIDE).transpose(0, 2, 1, 3).reshape(SEQS, SPAN, WIDE)

    expand = jnp.concatenate([out[128 + 24 * i : 152 + 24 * i] for i in range(4)], axis=1)
    return (natural(got["bo"]), natural(tokens), out[0:24], out[24:48], out[48:72], out[80:104], expand, out[104:128], out[224:320]) + tuple(
        small[i, 0:24] for i in range(VECTORS))


def from_behind(block, axis, distance):
    devices = range(lax.axis_size(axis))
    route = [(i - distance, i) for i in devices if i - distance in devices]
    return lax.ppermute(block, axis, route)


def prefix(part, axis, combine, identity, reverse):
    count = lax.axis_size(axis)
    place = lax.axis_index(axis)
    ahead = count - 1 - place if reverse else place
    gathered = jax.tree.map(lambda a: lax.all_gather(a, axis), part)
    state = jax.tree.map(lambda a, e: jnp.zeros_like(a) + jnp.asarray(e, a.dtype), part, identity)

    def one(turn, state):
        source = count - 1 - turn if reverse else turn
        return combine(
            state, jax.tree.map(lambda a: lax.dynamic_index_in_dim(a, source, 0, False), gathered)
        )

    return lax.fori_loop(0, ahead, one, state)


def layer_norm(values, gain, offset):
    center = values - jnp.mean(values, axis=-1, keepdims=True)
    factor = lax.rsqrt(jnp.mean(center * center, axis=-1, keepdims=True) + EPSILON)
    normed = center * factor
    return (normed * gain + offset, normed, factor)


def norm_back(grad_out, normed, factor, gain):
    scaled = grad_out * gain
    centered = scaled - jnp.mean(scaled, axis=-1, keepdims=True)
    grad_in = factor * (centered - normed * jnp.mean(scaled * normed, axis=-1, keepdims=True))
    return (grad_in, jnp.sum(grad_out * normed, axis=(0, 1)), jnp.sum(grad_out, axis=(0, 1)))


def product(left, right):
    return jnp.einsum("scd,de->sce", left, right, preferred_element_type=jnp.float32)


def product_back(grad, right):
    return jnp.einsum("sce,de->scd", grad, right, preferred_element_type=jnp.float32)


def outer_sum(left, grad):
    return jnp.einsum("scd,sce->de", left, grad, preferred_element_type=jnp.float32)


def attach_previous(values, arriving, persisting_indicator):
    return jnp.concatenate([arriving, values[:, :-1]], axis=1) * persisting_indicator[..., None]


def attach_next(masked, arriving):
    return jnp.concatenate([masked[:, 1:], arriving], axis=1)


def make_combine(fading_multiplier):

    def combine(earlier, later):
        early_numer, early_denom, early_length, early_cut = earlier
        late_numer, late_denom, late_length, late_cut = later
        fading = jnp.exp(-late_length * fading_multiplier) * (1.0 - late_cut)
        return (
            late_numer + fading * early_numer,
            late_denom + fading * early_denom,
            early_length + late_length,
            jnp.maximum(early_cut, late_cut),
        )

    return combine


def affine_compose(first_step, second_step):
    first_mult, first_numer, first_denom = first_step
    second_mult, second_numer, second_denom = second_step
    return (
        first_mult * second_mult,
        second_mult * first_numer + second_numer,
        second_mult * first_denom + second_denom,
    )


def forward_sweep(exponentiated_lookup, payload_table_lines, persisting_indicator, shrink):
    multiplier = persisting_indicator[..., None] * shrink
    inclusive = lax.associative_scan(
        affine_compose,
        (multiplier, exponentiated_lookup * payload_table_lines, exponentiated_lookup),
        axis=1,
    )
    zeros = jnp.zeros_like(exponentiated_lookup[:, :1])
    numer_all = (
        jnp.concatenate([zeros, inclusive[1][:, :-1]], axis=1) * persisting_indicator[..., None]
    )
    denom_all = (
        jnp.concatenate([zeros, inclusive[2][:, :-1]], axis=1) * persisting_indicator[..., None]
    )
    return (numer_all, denom_all, inclusive[1][:, -1], inclusive[2][:, -1])


def reverse_sweep(adjoint_dividend, grad_denom, persisting_indicator, shrink):
    keep_now = persisting_indicator[..., None]
    inclusive = lax.associative_scan(
        affine_compose,
        (keep_now * shrink, keep_now * adjoint_dividend, keep_now * grad_denom),
        axis=1,
        reverse=True,
    )
    zeros = jnp.zeros_like(adjoint_dividend[:, :1])
    following_dividend = jnp.concatenate([inclusive[1][:, 1:], zeros], axis=1)
    next_denom = jnp.concatenate([inclusive[2][:, 1:], zeros], axis=1)
    return (following_dividend, next_denom, inclusive[1][:, 0], inclusive[2][:, 0])


def body(
    layer_inputs,
    document_openings,
    mixing_lookup_projection,
    mixing_payload_projection,
    mixing_acceptor_projection,
    mixing_result_projection,
    feedforward_lookup_projection,
    feedforward_acceptor_projection,
    feedforward_payload_projection,
    premix_layer_scaling,
    premix_layer_offset,
    postmix_layer_scaling,
    postmix_layer_offset,
    mixing_lookup_blend,
    mixing_payload_blend,
    mixing_acceptor_blend,
    feedforward_lookup_blend,
    feedforward_acceptor_blend,
    feature_fading_speed,
    present_token_reward,
    upstream_adjoint,
):
    gathered = (
        lax.all_gather(mixing_lookup_projection, BOTH, axis=0, tiled=True),
        lax.all_gather(mixing_payload_projection, BOTH, axis=0, tiled=True),
        lax.all_gather(mixing_acceptor_projection, BOTH, axis=0, tiled=True),
        lax.all_gather(mixing_result_projection, BOTH, axis=0, tiled=True),
        lax.all_gather(feedforward_lookup_projection, BOTH, axis=0, tiled=True),
        lax.all_gather(feedforward_acceptor_projection, BOTH, axis=0, tiled=True),
        lax.all_gather(feedforward_payload_projection, BOTH, axis=0, tiled=True),
        lax.all_gather(premix_layer_scaling, BOTH, axis=0, tiled=True),
        lax.all_gather(premix_layer_offset, BOTH, axis=0, tiled=True),
        lax.all_gather(postmix_layer_scaling, BOTH, axis=0, tiled=True),
        lax.all_gather(postmix_layer_offset, BOTH, axis=0, tiled=True),
        lax.all_gather(mixing_lookup_blend, BOTH, axis=0, tiled=True),
        lax.all_gather(mixing_payload_blend, BOTH, axis=0, tiled=True),
        lax.all_gather(mixing_acceptor_blend, BOTH, axis=0, tiled=True),
        lax.all_gather(feedforward_lookup_blend, BOTH, axis=0, tiled=True),
        lax.all_gather(feedforward_acceptor_blend, BOTH, axis=0, tiled=True),
        lax.all_gather(feature_fading_speed, BOTH, axis=0, tiled=True),
        lax.all_gather(present_token_reward, BOTH, axis=0, tiled=True),
    )
    full_key, full_value, full_gate, full_output, full_expand, full_select, full_contract = (
        gathered[:7]
    )
    vectors = [stream_element.astype(jnp.float32) for stream_element in gathered[7:]]
    (
        gain_first,
        bias_first,
        gain_second,
        bias_second,
        ratio_key,
        ratio_value,
        ratio_gate,
        ratio_expand,
        ratio_select,
        fading_multiplier,
        present_reward_term,
    ) = vectors
    inputs = layer_inputs.astype(jnp.float32)
    flags = document_openings.astype(jnp.float32)
    persisting_indicator = 1.0 - flags
    sequences = layer_inputs.shape[0]
    block_len = layer_inputs.shape[1]
    width = layer_inputs.shape[2]
    normed_a, unit_a, factor_a = layer_norm(inputs, gain_first, bias_first)
    arriving_a = from_behind(normed_a[:, -1:, :], "seq", 1)
    before_a = attach_previous(normed_a, arriving_a, persisting_indicator)
    spread_a = normed_a - before_a
    key_in = (before_a + spread_a * ratio_key).astype(jnp.bfloat16)
    value_in = (before_a + spread_a * ratio_value).astype(jnp.bfloat16)
    gate_in = (before_a + spread_a * ratio_gate).astype(jnp.bfloat16)
    lookup_table_lines = product(key_in, full_key)
    payload_table_lines = product(value_in, full_value)
    gate_rows = product(gate_in, full_gate)
    shrink = jnp.exp(-fading_multiplier)
    exponentiated_lookup = jnp.exp(lookup_table_lines)
    reward_scaled_pairs = jnp.exp(present_reward_term + lookup_table_lines)
    local_numer, local_denom, end_numer, end_denom = forward_sweep(
        exponentiated_lookup, payload_table_lines, persisting_indicator, shrink
    )
    cut = jnp.max(flags, axis=1, keepdims=True)
    length = jnp.full((1,), float(block_len), jnp.float32)
    zero_state = jnp.zeros((sequences, width), jnp.float32)
    identity = (
        zero_state,
        zero_state,
        jnp.zeros((1,), jnp.float32),
        jnp.zeros((sequences, 1), jnp.float32),
    )
    combine = make_combine(fading_multiplier)
    arrived = prefix((end_numer, end_denom, length, cut), "seq", combine, identity, False)
    positions = jnp.arange(block_len, dtype=jnp.float32)
    alive = 1.0 - lax.cummax(flags, axis=1)
    rising = jnp.exp(-positions[:, None] * fading_multiplier[None, :])
    running_dividend = local_numer + alive[..., None] * rising[None] * arrived[0][:, None, :]
    running_divisor = local_denom + alive[..., None] * rising[None] * arrived[1][:, None, :]
    accumulated_sum = running_divisor + reward_scaled_pairs
    recurrent_average = (
        running_dividend + reward_scaled_pairs * payload_table_lines
    ) / accumulated_sum
    gate_sig = jax.nn.sigmoid(gate_rows)
    mixed = (gate_sig * recurrent_average).astype(jnp.bfloat16)
    first = inputs + product(mixed, full_output)
    normed_b, unit_b, factor_b = layer_norm(first, gain_second, bias_second)
    arriving_b = from_behind(normed_b[:, -1:, :], "seq", 1)
    before_b = attach_previous(normed_b, arriving_b, persisting_indicator)
    spread_b = normed_b - before_b
    expand_in = (before_b + spread_b * ratio_expand).astype(jnp.bfloat16)
    select_in = (before_b + spread_b * ratio_select).astype(jnp.bfloat16)
    expanded = product(expand_in, full_expand)
    selected = product(select_in, full_select)
    positive = jax.nn.relu(expanded)
    squared = (positive * positive).astype(jnp.bfloat16)
    contracted = product(squared, full_contract)
    select_sig = jax.nn.sigmoid(selected)
    block_out = (first + select_sig * contracted).astype(jnp.bfloat16)
    again = (
        lax.all_gather(mixing_lookup_projection, BOTH, axis=0, tiled=True),
        lax.all_gather(mixing_payload_projection, BOTH, axis=0, tiled=True),
        lax.all_gather(mixing_acceptor_projection, BOTH, axis=0, tiled=True),
        lax.all_gather(mixing_result_projection, BOTH, axis=0, tiled=True),
        lax.all_gather(feedforward_lookup_projection, BOTH, axis=0, tiled=True),
        lax.all_gather(feedforward_acceptor_projection, BOTH, axis=0, tiled=True),
        lax.all_gather(feedforward_payload_projection, BOTH, axis=0, tiled=True),
    )
    full_key, full_value, full_gate, full_output, full_expand, full_select, full_contract = again
    upstream = upstream_adjoint.astype(jnp.float32)
    grad_contracted = (upstream * select_sig).astype(jnp.bfloat16)
    grad_selected = (upstream * contracted * select_sig * (1.0 - select_sig)).astype(jnp.bfloat16)
    grad_squared = product_back(grad_contracted, full_contract)
    grad_expanded = (2.0 * positive * grad_squared).astype(jnp.bfloat16)
    contract_grad = jnp.einsum(
        "scf,scd->fd", squared, grad_contracted, preferred_element_type=jnp.float32
    )
    expand_grad = outer_sum(expand_in, grad_expanded)
    select_grad = outer_sum(select_in, grad_selected)
    grad_expand_in = product_back(grad_expanded, full_expand)
    grad_select_in = product_back(grad_selected, full_select)
    expand_ratio_grad = jnp.sum(grad_expand_in * spread_b, axis=(0, 1))
    select_ratio_grad = jnp.sum(grad_select_in * spread_b, axis=(0, 1))
    grad_before_b = (
        grad_expand_in * (1.0 - ratio_expand) + grad_select_in * (1.0 - ratio_select)
    ) * persisting_indicator[..., None]
    arriving_gb = from_behind(grad_before_b[:, :1, :], "seq", -1)
    grad_normed_b = (
        grad_expand_in * ratio_expand
        + grad_select_in * ratio_select
        + attach_next(grad_before_b, arriving_gb)
    )
    grad_from_b, chan_gain_grad, chan_bias_grad = norm_back(
        grad_normed_b, unit_b, factor_b, gain_second
    )
    grad_first = upstream + grad_from_b
    grad_attended = grad_first.astype(jnp.bfloat16)
    output_grad = outer_sum(mixed, grad_attended)
    grad_mixed = product_back(grad_attended, full_output)
    grad_gates = (grad_mixed * recurrent_average * gate_sig * (1.0 - gate_sig)).astype(jnp.bfloat16)
    grad_wkv = grad_mixed * gate_sig
    adjoint_dividend = grad_wkv / accumulated_sum
    grad_denom = -grad_wkv * recurrent_average / accumulated_sum
    following_dividend, next_denom, lead_numer, lead_denom = reverse_sweep(
        adjoint_dividend, grad_denom, persisting_indicator, shrink
    )
    behind = prefix((lead_numer, lead_denom, length, cut), "seq", combine, identity, True)
    after = jnp.concatenate([flags[:, 1:], jnp.zeros_like(flags[:, :1])], axis=1)
    later_alive = 1.0 - lax.cummax(after, axis=1, reverse=True)
    falling = jnp.exp(-(block_len - 1.0 - positions)[:, None] * fading_multiplier[None, :])
    following_dividend = (
        following_dividend + later_alive[..., None] * falling[None] * behind[0][:, None, :]
    )
    next_denom = next_denom + later_alive[..., None] * falling[None] * behind[1][:, None, :]
    immediate_term = adjoint_dividend * payload_table_lines + grad_denom
    grad_keys = (
        exponentiated_lookup * (following_dividend * payload_table_lines + next_denom)
        + reward_scaled_pairs * immediate_term
    ).astype(jnp.bfloat16)
    adjoint_payloads = (
        exponentiated_lookup * following_dividend + reward_scaled_pairs * adjoint_dividend
    ).astype(jnp.bfloat16)
    present_reward_adjoint = jnp.sum(reward_scaled_pairs * immediate_term, axis=(0, 1))
    decay_grad = -shrink * jnp.sum(
        following_dividend * running_dividend + next_denom * running_divisor, axis=(0, 1)
    )
    key_grad = outer_sum(key_in, grad_keys)
    value_grad = outer_sum(value_in, adjoint_payloads)
    gate_grad = outer_sum(gate_in, grad_gates)
    grad_key_in = product_back(grad_keys, full_key)
    grad_value_in = product_back(adjoint_payloads, full_value)
    grad_gate_in = product_back(grad_gates, full_gate)
    key_ratio_grad = jnp.sum(grad_key_in * spread_a, axis=(0, 1))
    value_ratio_grad = jnp.sum(grad_value_in * spread_a, axis=(0, 1))
    gate_ratio_grad = jnp.sum(grad_gate_in * spread_a, axis=(0, 1))
    grad_before_a = (
        grad_key_in * (1.0 - ratio_key)
        + grad_value_in * (1.0 - ratio_value)
        + grad_gate_in * (1.0 - ratio_gate)
    ) * persisting_indicator[..., None]
    arriving_ga = from_behind(grad_before_a[:, :1, :], "seq", -1)
    grad_normed_a = (
        grad_key_in * ratio_key
        + grad_value_in * ratio_value
        + grad_gate_in * ratio_gate
        + attach_next(grad_before_a, arriving_ga)
    )
    grad_from_a, attn_gain_grad, attn_bias_grad = norm_back(
        grad_normed_a, unit_a, factor_a, gain_first
    )
    tokens_grad = grad_first + grad_from_a
    shares = (
        lax.psum_scatter(key_grad, BOTH, scatter_dimension=0, tiled=True),
        lax.psum_scatter(value_grad, BOTH, scatter_dimension=0, tiled=True),
        lax.psum_scatter(gate_grad, BOTH, scatter_dimension=0, tiled=True),
        lax.psum_scatter(output_grad, BOTH, scatter_dimension=0, tiled=True),
        lax.psum_scatter(expand_grad, BOTH, scatter_dimension=0, tiled=True),
        lax.psum_scatter(select_grad, BOTH, scatter_dimension=0, tiled=True),
        lax.psum_scatter(contract_grad, BOTH, scatter_dimension=0, tiled=True),
        lax.psum_scatter(attn_gain_grad, BOTH, scatter_dimension=0, tiled=True),
        lax.psum_scatter(attn_bias_grad, BOTH, scatter_dimension=0, tiled=True),
        lax.psum_scatter(chan_gain_grad, BOTH, scatter_dimension=0, tiled=True),
        lax.psum_scatter(chan_bias_grad, BOTH, scatter_dimension=0, tiled=True),
        lax.psum_scatter(key_ratio_grad, BOTH, scatter_dimension=0, tiled=True),
        lax.psum_scatter(value_ratio_grad, BOTH, scatter_dimension=0, tiled=True),
        lax.psum_scatter(gate_ratio_grad, BOTH, scatter_dimension=0, tiled=True),
        lax.psum_scatter(expand_ratio_grad, BOTH, scatter_dimension=0, tiled=True),
        lax.psum_scatter(select_ratio_grad, BOTH, scatter_dimension=0, tiled=True),
        lax.psum_scatter(decay_grad, BOTH, scatter_dimension=0, tiled=True),
        lax.psum_scatter(present_reward_adjoint, BOTH, scatter_dimension=0, tiled=True),
    )
    return (
        block_out,
        tokens_grad,
        shares[0],
        shares[1],
        shares[2],
        shares[3],
        shares[4],
        shares[5],
        shares[6],
        shares[7],
        shares[8],
        shares[9],
        shares[10],
        shares[11],
        shares[12],
        shares[13],
        shares[14],
        shares[15],
        shares[16],
        shares[17],
    )


def solution(mesh):
    fits = mesh.shape["seq"] == 8 and mesh.shape["batch"] == 4
    return jax.shard_map(
        fast_body if fits else body,
        mesh=mesh,
        in_specs=(
            P("batch", "seq", None),
            P("batch", "seq"),
            P(BOTH, None),
            P(BOTH, None),
            P(BOTH, None),
            P(BOTH, None),
            P(BOTH, None),
            P(BOTH, None),
            P(BOTH, None),
            P(BOTH),
            P(BOTH),
            P(BOTH),
            P(BOTH),
            P(BOTH),
            P(BOTH),
            P(BOTH),
            P(BOTH),
            P(BOTH),
            P(BOTH),
            P(BOTH),
            P("batch", "seq", None),
        ),
        out_specs=(
            P("batch", "seq", None),
            P("batch", "seq", None),
            P(BOTH, None),
            P(BOTH, None),
            P(BOTH, None),
            P(BOTH, None),
            P(BOTH, None),
            P(BOTH, None),
            P(BOTH, None),
            P(BOTH),
            P(BOTH),
            P(BOTH),
            P(BOTH),
            P(BOTH),
            P(BOTH),
            P(BOTH),
            P(BOTH),
            P(BOTH),
            P(BOTH),
            P(BOTH),
        ),
        check_vma=False,
    )
```

```python
import functools

import jax
import jax.numpy as jnp
from jax import lax
from jax.experimental import pallas as pl
from jax.experimental.pallas import tpu as pltpu
from jax.sharding import PartitionSpec as P

BOTH = ("seq", "batch")
MESH = pl.DeviceIdType.MESH
BF = jnp.bfloat16
F32 = jnp.float32
WIDE = 768
ROWS_MAIN = 224
ROWS_LAST = 96
GATHER_CHUNKS = (
    (0, 48, 32, 16), (0, 0, 48, 32), (0, 80, 48, 16), (0, 128, 48, 32), (0, 176, 48, 16), (1, 0, 48, 32), (1, 48, 48, 16))
SCATTER_CHUNKS = (
    (1, 0, 48, 32), (1, 48, 48, 16), (0, 128, 48, 32), (0, 176, 48, 16), (0, 80, 48, 32), (0, 48, 32, 16), (0, 0, 48, 16))
COUNT = len(GATHER_CHUNKS)


class Place:
    def __init__(self):
        self.s = lax.axis_index("seq")
        self.b = lax.axis_index("batch")
        self.z, self.c = self.s // 2, self.s % 2
        y, x = self.b // 2, self.b % 2
        self.bx, self.by, self.bd = y * 2 + 1 - x, (1 - y) * 2 + x, (1 - y) * 2 + 1 - x
        self.depth = lax.axis_size("seq") // 2
        self.x, self.y = (self.s, self.bx), (self.s, self.by)
        self.core = (self.z * 2 + 1 - self.c, self.b)

    def along(self, step):
        z = lax.rem(self.z + step, self.depth)
        return z, (z * 2 + self.c, self.b)

    def back(self, step):
        return lax.rem(self.z + self.depth - step, self.depth)


def rdma(src, dst, sems, send, recv, to):
    return pltpu.make_async_remote_copy(
        src_ref=src, dst_ref=dst, send_sem=sems.at[send], recv_sem=sems.at[recv], device_id=to, device_id_type=MESH
    )


def enter(place):
    barrier = pltpu.get_barrier_semaphore()
    n = lax.axis_size("seq")
    peers = [place.x, place.y] + [(lax.rem(place.s + d, n), place.b) for d in range(1, n)]
    for peer in peers:
        pl.semaphore_signal(barrier, inc=1, device_id=peer, device_id_type=MESH)
    pl.semaphore_wait(barrier, len(peers))


class Gather:
    def __init__(self, place, arrays, sems):
        self.p, self.arrays, self.sems = place, arrays, sems

    def stage(self, number, k):
        if not 0 <= k < COUNT:
            return
        p, sems = self.p, self.sems.at[k]
        a, r0, n, nx = GATHER_CHUNKS[k]
        ref = self.arrays[a]
        whole, part_x, part_y = pl.ds(r0, n), pl.ds(r0, nx), pl.ds(r0 + nx, n - nx)
        col = lambda c, b, rows: ref.at[:, c, b, rows]
        move = lambda view, at, to: rdma(view, view, sems, at, at + 1, to)
        one = lambda z, b: ref.at[z, p.c, b, whole]
        line = lambda d, z: move(one(z, p.b), 2 * d - 2, p.along(d)[1])
        near_x = lambda b: move(col(p.c, b, whole), 6, p.x)
        near_y = lambda b: move(col(p.c, b, whole), 8, p.y)
        diag_x = lambda b: move(col(p.c, b, part_x), 10, p.x)
        diag_y = lambda b: move(col(p.c, b, part_y), 12, p.y)
        core = lambda j, c, b: move(col(c, b, whole), 14 + 2 * j, p.core)
        single = k == 0
        steps = range(p.depth)
        lone = lambda d, z, b, c: (
            move(ref.at[z, c, b, whole], 22 + 6 * d, p.x), move(ref.at[z, c, b, whole], 24 + 6 * d, p.y),
            move(ref.at[z, c, b, whole], 26 + 6 * d, p.core))
        if number == 0:
            for d in range(1, p.depth):
                line(d, p.z).start()
            if single:
                for copy in lone(0, p.z, p.b, p.c):
                    copy.start()
        elif number == 1:
            for d in range(1, p.depth):
                line(d, p.back(d)).wait_recv()
                if single:
                    for copy in lone(d, p.back(d), p.b, p.c):
                        copy.start()
            if not single:
                near_x(p.b).start()
                near_y(p.b).start()
                core(0, p.c, p.b).start()
        elif number == 2:
            if single:
                for d in steps:
                    lone(d, p.back(d), p.bx, p.c)[0].wait_recv()
                    lone(d, p.back(d), p.by, p.c)[1].wait_recv()
            else:
                near_x(p.bx).wait_recv()
                near_y(p.by).wait_recv()
            diag_x(p.by).start()
            diag_y(p.bx).start()
            core(1, p.c, p.bx).start()
            core(2, p.c, p.by).start()
        elif number == 3:
            diag_x(p.bd).wait_recv()
            diag_y(p.bd).wait_recv()
            core(3, p.c, p.bd).start()
        elif number == 4:
            if single:
                for d in steps:
                    lone(d, p.back(d), p.b, 1 - p.c)[2].wait_recv()
            for j, b in enumerate((p.b, p.bx, p.by, p.bd)):
                if j or not single:
                    core(j, 1 - p.c, b).wait_recv()
        elif number == 5:
            for d in range(1, p.depth):
                line(d, p.z).wait_send()
            if single:
                for d in steps:
                    for copy in lone(d, p.back(d), p.b, p.c):
                        copy.wait_send()
            else:
                near_x(p.b).wait_send()
                near_y(p.b).wait_send()
                core(0, p.c, p.b).wait_send()
            diag_x(p.by).wait_send()
            diag_y(p.bx).wait_send()
            for j, b in ((1, p.bx), (2, p.by), (3, p.bd)):
                core(j, p.c, b).wait_send()

    def tick(self, t):
        for number in range(5):
            self.stage(number, t - number)


class Scatter:
    def __init__(self, place, packed, early, from_core, near, diag, line, out, sems, credits):
        self.early = early
        self.p, self.packed, self.from_core, self.near = place, packed, from_core, near
        self.diag, self.line, self.out, self.sems, self.credits = diag, line, out, sems, credits

    def stage(self, number, k):
        p, sems = self.p, self.sems.at[k]
        a, r0, n, nx = SCATTER_CHUNKS[k]
        ref, slot, depth = self.packed[a], k % 2, p.depth
        f0 = r0 if a == 0 else r0 + ROWS_MAIN
        whole, part_x, part_y = pl.ds(r0, n), pl.ds(r0, nx), pl.ds(r0 + nx, n - nx)
        whence = self.early if a == 1 else ref
        core = lambda: rdma(whence.at[:, 1 - p.c, :, whole], self.from_core.at[slot, :, :, pl.ds(0, n)], sems, 0, 1, p.core)
        diag_x = lambda: rdma(ref.at[:, p.c, p.bd, part_x], self.diag.at[slot, :, pl.ds(0, nx)], sems, 2, 3, p.x)
        diag_y = lambda: rdma(ref.at[:, p.c, p.bd, part_y], self.diag.at[slot, :, pl.ds(nx, n - nx)], sems, 4, 5, p.y)
        near_x = lambda: rdma(ref.at[:, p.c, p.bx, whole], self.near.at[slot, 0, :, pl.ds(0, n)], sems, 6, 7, p.x)
        near_y = lambda: rdma(ref.at[:, p.c, p.by, whole], self.near.at[slot, 1, :, pl.ds(0, n)], sems, 8, 9, p.y)

        def along(d):
            z, to = p.along(d)
            return rdma(ref.at[z, p.c, p.b, whole], self.line.at[d - 1, pl.ds(f0, n)], sems, 8 + 2 * d, 9 + 2 * d, to)

        def ready(*which):
            if k >= 2:
                for w in which:
                    pl.semaphore_wait(self.credits.at[w], 1)

        def free(which, to):
            if k + 2 < COUNT:
                pl.semaphore_signal(self.credits.at[which], inc=1, device_id=to, device_id_type=MESH)

        if number == 0:
            ready(0)
            core().start()
        elif number == 1:
            core().wait_recv()

            @pl.loop(0, depth * 4)
            def _(i):
                z, b = i // 4, i % 4
                ref[z, p.c, b, r0 : r0 + n] = ref[z, p.c, b, r0 : r0 + n] + self.from_core[slot, z, b, 0:n]

            free(0, p.core)
            ready(1, 2)
            diag_x().start()
            diag_y().start()
        elif number == 2:
            diag_x().wait_recv()
            diag_y().wait_recv()

            @pl.loop(0, depth)
            def _(z):
                for b, s0, m in ((p.by, 0, nx), (p.bx, nx, n - nx)):
                    ref[z, p.c, b, r0 + s0 : r0 + s0 + m] = ref[z, p.c, b, r0 + s0 : r0 + s0 + m] + self.diag[slot, z, s0 : s0 + m]

            free(1, p.x)
            free(2, p.y)
            ready(3, 4)
            near_x().start()
            near_y().start()
        elif number == 3:
            near_x().wait_recv()
            near_y().wait_recv()

            @pl.loop(0, depth)
            def _(z):
                ref[z, p.c, p.b, r0 : r0 + n] = (
                    ref[z, p.c, p.b, r0 : r0 + n].astype(F32)
                    + self.near[slot, 0, z, 0:n].astype(F32)
                    + self.near[slot, 1, z, 0:n].astype(F32)
                ).astype(BF)

            free(3, p.x)
            free(4, p.y)
            for d in range(1, depth):
                along(d).start()
        elif number == 4:
            for d in range(1, depth):
                along(d).wait_recv()
            total = ref[p.z, p.c, p.b, r0 : r0 + n].astype(F32)
            for d in range(1, depth):
                total = total + self.line[d - 1, f0 : f0 + n].astype(F32)
            self.out[f0 : f0 + n] = total
        elif number == 5:
            for each in (core, diag_x, diag_y, near_x, near_y):
                each().wait_send()
            for d in range(1, depth):
                along(d).wait_send()


EPSILON = 1e-05
TOK = 1024
SEQS = 4
SPAN = 256
STEPS = 32
SEG = 8
LANE = 128
WINDOW = 256
VECTORS = 11


def window_of(i):
    return min(i * 24 // LANE, WIDE // LANE - 2) * LANE


def spread_lanes(v):
    return jnp.concatenate([v] * (WIDE // LANE), axis=1)


def unit_norm(v):
    center = v - jnp.mean(v, axis=-1, keepdims=True)
    factor = lax.rsqrt(jnp.mean(center * center, axis=-1, keepdims=True) + EPSILON)
    return center * factor, factor


def sigmoid(v):
    return 1.0 / (1.0 + jnp.exp(-v))


def first_rows(halo_row, last_group):
    moved = pltpu.roll(last_group, 1, axis=0)
    at_top = lax.broadcasted_iota(jnp.int32, moved.shape, 0) == 0
    return jnp.where(at_top, halo_row, moved)


def permute_in(src, dst, tmp):
    @pl.loop(0, SEQS)
    def _(j):
        base = pl.multiple_of(j * SPAN, SPAN)
        for l in range(WIDE // LANE):
            tmp[l] = src[pl.ds(base, SPAN), l * LANE : (l + 1) * LANE].astype(F32)

        @pl.loop(0, STEPS // 2)
        def _(s):
            for l in range(WIDE // LANE):
                two = jnp.concatenate([tmp[l, pl.ds(2 * s, SEG, stride=STEPS), :], tmp[l, pl.ds(2 * s + 1, SEG, stride=STEPS), :]], axis=0)
                dst[pl.ds(pl.multiple_of(base + s * 16, 16), 16), l * LANE : (l + 1) * LANE] = two.astype(BF)


class Spill:
    def __init__(self, sems):
        self.sems, self.copies, self.used = sems, {}, 0

    def start(self, name, src, dst):
        self.copies[name] = pltpu.make_async_copy(src, dst, self.sems.at[self.used])
        self.used += 1
        self.copies[name].start()

    def wait(self, *names):
        for name in names or list(self.copies):
            self.copies.pop(name).wait()


class Line:
    def __init__(self, place):
        self.p = place
        self.n = lax.axis_size("seq")

    def all(self, buf, sems):
        p, copies = self.p, []
        for d in range(1, self.n):
            to = (lax.rem(p.s + d, self.n), p.b)
            copies.append(rdma(buf.at[p.s], buf.at[p.s], sems, d, self.n + d, to))
        return copies

    def shift(self, src, dst, sems, step):
        return rdma(src, dst, sems, 0, 1, (lax.rem(self.p.s + self.n + step, self.n), self.p.b))


def relayout(st, dst, depth, r0, n, targets):
    @pl.loop(0, depth * 2)
    def _(i):
        z, c = i // 2, i % 2
        slabs = [st[z, c, b, r0 : r0 + n].astype(F32) for b in range(4)]
        rows = pl.ds(pl.multiple_of(i * 96, 96), 96)
        for index, at in targets:
            dst[index, rows] = jnp.concatenate([v[at : at + 24] for v in slabs], axis=0).astype(BF)


def matmul(left, right, out, rows=512):
    @pl.loop(0, TOK // rows)
    def _(i):
        r = pl.ds(pl.multiple_of(i * rows, rows), rows)
        out[r] = jnp.dot(left[r], right[...], preferred_element_type=F32)


def forward_kernel(x_in, up_in, openings, vec_in, wk, wv, wr, wo, ws, we_in, wc_in,
                   o_w, o_e, o_c, o_ki, o_spa, o_spb, o_mixed, o_ei, o_si, o_gc, o_gs, o_up, o_sq, o_pkc,
                   o_kvg, o_nd, o_ua, o_ub, o_factors, o_keep, o_vec, o_alive, o_bo,
                   st, cw, wd, we, u0, xp, u1, gyp, tmp, keep, xa, ki, kvg, nd, spb, factors, vec, states, alive, seg, carry, hx, hx_got, hb, hb_got,
                   gsems, asems, ssems, hsems, lsems):
    place = Place()
    line = Line(place)
    depth = place.depth
    devices = depth * 8
    me = place.s * 4 + place.b
    spill = Spill(lsems)
    spill.start("x", x_in, u0)
    spill.start("up", up_in, u1)
    z, c, b = place.z, place.c, place.b
    as32 = lambda ref: ref[...].astype(F32)
    join = lambda *v: jnp.concatenate(v, axis=0).astype(BF)
    start = me * 24
    low = jnp.minimum(start // LANE, WIDE // LANE - 2) * LANE
    wide = pltpu.roll(jnp.concatenate([vec_in[...], jnp.zeros((16, LANE), F32)], axis=1), start - low, axis=1)
    small = jnp.concatenate([wide[0:8], wide[8:16], jnp.zeros((8, WIDE - 2 * WINDOW), F32)], axis=1)
    st[z, c, b, 48:80] = join(as32(wr), small)
    st[z, c, b, 0:48] = join(as32(wk), as32(wv))
    enter(place)
    gather = Gather(place, (st, cw), gsems)
    gather.tick(0)
    st[z, c, b, 80:128] = join(as32(wo), as32(ws))
    e = as32(we_in)
    for h in range(2):
        st[z, c, b, 128 + 48 * h : 176 + 48 * h] = join(e[:, 2 * h * WIDE : (2 * h + 1) * WIDE], e[:, (2 * h + 1) * WIDE : (2 * h + 2) * WIDE])
    cw[z, c, b] = wc_in[...]

    gather.tick(1)
    spill.wait("x")
    for j in range(SEQS):
        hx[j : j + 1] = u0[SPAN * j + SPAN - 16 : SPAN * j + SPAN].astype(F32)[15:16]
    hx[SEQS:8] = jnp.zeros((8 - SEQS, WIDE), F32)
    send_hx = line.shift(hx, hx_got, hsems.at[0], 1)
    send_hx.start()
    permute_in(u0, xp, tmp)
    gather.tick(2)
    for j in range(SEQS):
        flags = 1.0 - openings[j : j + 1].astype(F32)
        tmp[0] = jnp.broadcast_to(flags, (LANE, SPAN)).T
        for s in range(STEPS):
            keep[j * SPAN + s * SEG : j * SPAN + (s + 1) * SEG] = tmp[0, pl.ds(s, SEG, stride=STEPS), :]
    spill.start("keep", keep, o_keep)
    for j in range(SEQS):
        low_keep = jnp.min(keep[SPAN * j : SPAN * (j + 1)], axis=0, keepdims=True)
        alive[place.s, j : j + 1] = low_keep
        alive[place.s, SEQS + j : SEQS + j + 1] = low_keep
    send_alive = line.all(alive, asems)
    for copy in send_alive:
        copy.start()
    gather.tick(3)
    spill.wait("up")
    permute_in(u1, gyp, tmp)
    spill.start("gyp", gyp, o_up)
    gather.tick(4)
    vec[...] = jnp.zeros_like(vec)
    for i in range(devices):
        w = window_of(i)
        got = st[i // 8, i // 4 % 2, i % 4, 64:80].astype(F32)[8:16]
        vec[0:8, w : w + WINDOW] += got[:, 0:WINDOW]
        vec[8:16, w : w + WINDOW] += got[:, WINDOW : 2 * WINDOW]
    spill.start("vec", vec, o_vec)

    gain_a, bias_a = vec[0:1], vec[1:2]

    def norm_rows(j, rows_of, gain, bias, unit_out, factor_out):
        @pl.loop(0, SPAN // 16, unroll=8)
        def _(t):
            r = pl.ds(pl.multiple_of(j * SPAN + t * 16, 16), 16)
            unit, factor = unit_norm(rows_of(r))
            unit_out(j, t, unit)
            factor_out[r] = jnp.broadcast_to(factor, (16, LANE))
            xa[j, pl.ds(pl.multiple_of(8 + t * 16, 8), 16)] = unit * gain + bias

    def store_a(j, t, unit):
        spb[pl.ds(pl.multiple_of(j * SPAN + t * 16, 16), 16)] = unit.astype(BF)

    def store_b(j, t, unit):
        nd[j // 2, j % 2, pl.ds(pl.multiple_of(t * 16, 16), 16)] = unit

    @pl.loop(0, SEQS)
    def _(j):
        norm_rows(j, lambda r: xp[r].astype(F32), gain_a, bias_a, store_a, factors.at[0])

    spill.start("ua", spb, o_ua)
    not_first = jnp.where(place.s > 0, 1.0, 0.0).astype(F32)
    line.shift(hx, hx_got, hsems.at[0], 1).wait_recv()
    before = (unit_norm(hx_got[...])[0] * gain_a + bias_a) * not_first
    for j in range(SEQS):
        xa[j, 0:8] = first_rows(before[j : j + 1], xa[j, SPAN : SPAN + 8])

    def blends(j, ratios, outs, spread_out):
        @pl.loop(0, SPAN // 16)
        def _(t):
            r = pl.ds(pl.multiple_of(j * SPAN + t * 16, 16), 16)
            prev = xa[j, pl.ds(pl.multiple_of(t * 16, 8), 16)] * spread_lanes(keep[r])
            spread = xa[j, pl.ds(pl.multiple_of(8 + t * 16, 8), 16)] - prev
            spread_out[r] = spread.astype(BF)
            for ratio, out in zip(ratios, outs):
                out[r] = (prev + spread * ratio).astype(BF)

    @pl.loop(0, SEQS)
    def _(j):
        blends(j, [vec[4:5], vec[5:6], vec[6:7]], [ki.at[0], ki.at[1], ki.at[2]], u0)

    spill.start("ki", ki, o_ki)
    spill.start("spa", u0, o_spa)
    gather.tick(5)
    relayout(st, wd, depth, 0, 48, ((0, 0), (1, 24)))
    relayout(st, wd, depth, 48, 32, ((2, 0),))
    for m in range(3):
        matmul(ki.at[m], wd.at[m], kvg.at[m])
    spill.start("kvg", kvg, o_kvg)

    shrink = jnp.exp(-vec[9:10])
    bonus = vec[10:11]
    shrink8 = jnp.broadcast_to(shrink, (SEG, WIDE))
    row = lax.broadcasted_iota(jnp.int32, (SEG, WIDE), 0)

    @pl.loop(0, SEQS)
    def _(j):
        def step(s, state):
            decay, numer, denom = state
            r = pl.ds(pl.multiple_of(j * SPAN + s * SEG, SEG), SEG)
            m = spread_lanes(keep[r]) * shrink8
            ek = jnp.exp(kvg[0, r])
            return decay * m, numer * m + ek * kvg[1, r], denom * m + ek

        zero = jnp.zeros((SEG, WIDE), F32)
        decay, numer, denom = lax.fori_loop(0, STEPS, step, (zero + 1.0, zero, zero), unroll=4)
        for d in (1, 2, 4):
            top = row < d
            numer, denom, decay = (
                numer + decay * jnp.where(top, 0.0, pltpu.roll(numer, d, axis=0)),
                denom + decay * jnp.where(top, 0.0, pltpu.roll(denom, d, axis=0)),
                decay * jnp.where(top, 1.0, pltpu.roll(decay, d, axis=0)),
            )
        states[place.s, pl.ds(j, 1)] = numer[SEG - 1 : SEG]
        states[place.s, pl.ds(SEQS + j, 1)] = denom[SEG - 1 : SEG]
        seg[j, 0] = jnp.where(row < 1, 1.0, pltpu.roll(decay, 1, axis=0))
        seg[j, 1] = jnp.where(row < 1, 0.0, pltpu.roll(numer, 1, axis=0))
        seg[j, 2] = jnp.where(row < 1, 0.0, pltpu.roll(denom, 1, axis=0))

    send_states = line.all(states, ssems)
    for copy in send_states:
        copy.start()
    gather.tick(6)
    relayout(st, wd, depth, 80, 48, ((3, 0), (4, 24)))
    spill.start("w", wd, o_w)
    for d in range(1, line.n):
        src = lax.rem(place.s + line.n - d, line.n)
        rdma(alive.at[src], alive.at[src], asems, d, line.n + d, (src, b)).wait_recv()
        rdma(states.at[src], states.at[src], ssems, d, line.n + d, (src, b)).wait_recv()
    spill.start("alive", alive, o_alive)
    whole = jnp.exp(-float(SPAN) * vec[9:10])
    arrived = jnp.zeros((SEG, WIDE), F32)
    for src in range(7):
        after = spread_lanes(alive[src]) * whole * arrived + states[src]
        arrived = jnp.where(src < place.s, after, arrived)
    carry[...] = arrived

    for j in range(SEQS):
        slot = j % 2
        if j >= 2:
            spill.wait(("nd", j - 2))
        into = nd.at[slot]
        base = j * SPAN
        numer0 = seg[j, 0] * carry[j : j + 1] + seg[j, 1]
        denom0 = seg[j, 0] * carry[SEQS + j : SEQS + j + 1] + seg[j, 2]

        def steps(i, state):
            numer, denom = state
            mixes = []
            for q in range(2):
                lo = pl.multiple_of(i * 16 + q * 8, 8)
                r = pl.ds(pl.multiple_of(base + lo, 8), SEG)
                kept = spread_lanes(keep[r])
                numer, denom = numer * kept, denom * kept
                into[0, pl.ds(lo, SEG)] = numer
                into[1, pl.ds(lo, SEG)] = denom
                k, v = kvg[0, r], kvg[1, r]
                now, ek = jnp.exp(bonus + k), jnp.exp(k)
                wkv = (numer + now * v) / (denom + now)
                mixes.append(sigmoid(kvg[2, r]) * wkv)
                numer, denom = shrink8 * numer + ek * v, shrink8 * denom + ek
            u1[pl.ds(pl.multiple_of(base + i * 16, 16), 16)] = jnp.concatenate(mixes, axis=0).astype(BF)
            return numer, denom

        lax.fori_loop(0, STEPS // 2, steps, (numer0, denom0))
        spill.start(("nd", j), into, o_nd.at[:, pl.ds(base, SPAN)])
    spill.start("mixed", u1, o_mixed)
    spill.wait("kvg", ("nd", 2), ("nd", 3))
    first = kvg.at[0]

    @pl.loop(0, TOK // 256)
    def _(i):
        r = pl.ds(pl.multiple_of(i * 256, 256), 256)
        first[r] = xp[r].astype(F32) + jnp.dot(u1[r], wd[3], preferred_element_type=F32)

    @pl.loop(0, SEQS)
    def _(j):
        norm_rows(j, lambda r: first[r], vec[2:3], vec[3:4], store_b, factors.at[1])

    for j in range(SEQS):
        spill.start(("ub", j), nd.at[j // 2, j % 2], o_ub.at[pl.ds(j * SPAN, SPAN)])
    spill.start("factors", factors, o_factors)
    spill.wait("ua")
    for j in range(SEQS):
        hb[j : j + 1] = xa[j, SPAN : SPAN + 8][7:8]
    hb[SEQS:8] = jnp.zeros((8 - SEQS, WIDE), F32)
    send_hb = line.shift(hb, hb_got, hsems.at[1], 1)
    send_hb.start()
    gather.tick(7)
    relayout(st, we, depth, 128, 48, ((0, 0), (1, 24)))
    spill.wait("ki")
    send_hb.wait_recv()
    before_b = hb_got[...] * not_first
    for j in range(SEQS):
        xa[j, 0:8] = first_rows(before_b[j : j + 1], xa[j, SPAN : SPAN + 8])

    @pl.loop(0, SEQS)
    def _(j):
        blends(j, [vec[7:8], vec[8:9]], [ki.at[0], ki.at[1]], spb)

    spill.start("spb", spb, o_spb)
    spill.start("ei", ki.at[0], o_ei)
    spill.start("si", ki.at[1], o_si)
    sig = kvg.at[1]

    @pl.loop(0, TOK // 256)
    def _(i):
        r = pl.ds(pl.multiple_of(i * 256, 256), 256)
        chosen = sigmoid(jnp.dot(ki[1, r], wd[4], preferred_element_type=F32))
        sig[r] = chosen
        ki[2, r] = (gyp[r].astype(F32) * chosen).astype(BF)

    spill.start("gc", ki.at[2], o_gc)
    def square(f):
        @pl.loop(0, depth, unroll=4)
        def _(i):
            r = pl.ds(pl.multiple_of(i * 256, 256), 256)
            positive = jnp.maximum(jnp.dot(ki[0, r], we[f], preferred_element_type=F32), 0.0)
            st[i, :, :, 96 + 32 * f : 128 + 32 * f] = (positive * positive).astype(BF).reshape(2, 4, 32, WIDE)

    def contract_grad(f):
        left = st[:, :, :, 96 + 32 * f : 128 + 32 * f].reshape(TOK, WIDE)
        for h in range(2):
            got = lax.dot_general(left[:, 384 * h : 384 * (h + 1)], ki[2], (((0,), (0,)), ((), ())), preferred_element_type=F32)
            st[f, h, :, 0:96] = got.astype(BF).reshape(4, 96, WIDE)

    for k in range(4):
        gather.stage(5, k)
    square(0)
    square(1)
    gather.tick(8)
    relayout(st, we, depth, 176, 48, ((2, 0), (3, 24)))
    spill.start("e", we, o_e)
    gather.stage(5, 4)
    square(2)
    square(3)
    contract_grad(0)
    contract_grad(1)
    gather.tick(9)
    contract_grad(2)
    contract_grad(3)
    spill.start("pkc", st.at[:, :, :, pl.ds(0, 96)], o_pkc)
    spill.start("sq", st.at[:, :, :, pl.ds(96, 128)], o_sq)
    spill.wait("mixed", "spa")

    def contract(h):
        cols = slice(h * (WIDE // 2), (h + 1) * (WIDE // 2))
        half = pl.ds(h * (WIDE // 2), WIDE // 2)
        spill.start(("c", h), cw.at[:, :, :, :, half], o_c.at[:, :, :, :, half])

        @pl.loop(0, depth)
        def _(i):
            r = pl.ds(pl.multiple_of(i * 256, 256), 256)
            total = jnp.zeros((256, WIDE // 2), F32)
            for f in range(4):
                part = st[i, :, :, 96 + 32 * f : 128 + 32 * f].reshape(256, WIDE)
                total = total + jnp.dot(part, cw[f, :, :, :, cols].reshape(WIDE, WIDE // 2), preferred_element_type=F32)
            chosen = sig[r, cols]
            u1[r, cols] = (first[r, cols] + chosen * total).astype(BF)
            u0[r, cols] = (gyp[r, cols].astype(F32) * total * chosen * (1.0 - chosen)).astype(BF)

    gather.tick(10)
    contract(0)
    contract(1)
    spill.start("gs", u0, o_gs)
    spill.start("bo", u1, o_bo)
    for copy in send_alive + send_states + [send_hx, send_hb]:
        copy.wait_send()
    for k in range(5, COUNT):
        gather.stage(5, k)
    spill.wait()


def forward_call(x, openings, up, vec, shards, depth):
    hbm, vmem = pl.BlockSpec(memory_space=pl.ANY), pl.BlockSpec(memory_space=pltpu.VMEM)
    s = jax.ShapeDtypeStruct
    seq = depth * 2
    devices = depth * 8
    rows = (TOK, WIDE)
    outs = dict(
        w=s((5, WIDE, WIDE), BF), e=s((4, WIDE, WIDE), BF), c=s((depth, 2, 4, 96, WIDE), BF), ki=s((3,) + rows, BF),
        spa=s(rows, BF), spb=s(rows, BF), mixed=s(rows, BF), ei=s(rows, BF), si=s(rows, BF), gc=s(rows, BF), gs=s(rows, BF),
        up=s(rows, BF), sq=s((depth, 2, 4, 128, WIDE), BF), pkc=s((depth, 2, 4, 96, WIDE), BF),
        kvg=s((3,) + rows, F32), nd=s((2,) + rows, F32), ua=s(rows, BF), ub=s(rows, F32), factors=s((2, TOK, LANE), F32), keep=s((TOK, LANE), F32), vec=s((16, WIDE), F32), alive=s((seq, 8, LANE), F32),
        bo=s(rows, BF))
    scratch = [
        pltpu.VMEM((depth, 2, 4, ROWS_MAIN, WIDE), BF), pltpu.VMEM((depth, 2, 4, ROWS_LAST, WIDE), BF),
        pltpu.VMEM((5, WIDE, WIDE), BF), pltpu.VMEM((4, WIDE, WIDE), BF),
        pltpu.VMEM(rows, BF), pltpu.VMEM(rows, BF), pltpu.VMEM(rows, BF), pltpu.VMEM(rows, BF),
        pltpu.VMEM((6, SPAN, LANE), F32), pltpu.VMEM((TOK, LANE), F32), pltpu.VMEM((SEQS, SPAN + 8, WIDE), F32),
        pltpu.VMEM((3,) + rows, BF), pltpu.VMEM((3,) + rows, F32), pltpu.VMEM((2, 2, SPAN, WIDE), F32), pltpu.VMEM(rows, BF), pltpu.VMEM((2, TOK, LANE), F32),
        pltpu.VMEM((16, WIDE), F32), pltpu.VMEM((seq, 8, WIDE), F32), pltpu.VMEM((seq, 8, LANE), F32),
        pltpu.VMEM((SEQS, 3, SEG, WIDE), F32), pltpu.VMEM((8, WIDE), F32),
        pltpu.VMEM((8, WIDE), F32), pltpu.VMEM((8, WIDE), F32), pltpu.VMEM((8, WIDE), F32), pltpu.VMEM((8, WIDE), F32),
        pltpu.SemaphoreType.DMA((COUNT, 46)), pltpu.SemaphoreType.DMA((2 * seq,)),
        pltpu.SemaphoreType.DMA((2 * seq,)), pltpu.SemaphoreType.DMA((2, 2)), pltpu.SemaphoreType.DMA((32,)),
    ]
    got = pl.pallas_call(
        forward_kernel,
        out_shape=tuple(outs.values()),
        in_specs=[hbm, hbm] + [vmem] * 9,
        out_specs=tuple(hbm for _ in outs),
        scratch_shapes=scratch,
        compiler_params=pltpu.CompilerParams(collective_id=0, has_side_effects=True, vmem_limit_bytes=62 << 20),
        cost_estimate=pl.CostEstimate(flops=2 * 1024 * 12 * 768 * 768, bytes_accessed=60 << 20, transcendentals=0),
    )(x, up, openings, vec, *shards)
    return dict(zip(outs, got))


NT = (((1,), (1,)), ((), ()))
TN = (((0,), (0,)), ((), ()))


def backward_kernel(i_w, i_e, i_c, i_ki, i_spa, i_spb, i_mixed, i_ei, i_si, i_gc, i_gs, i_up, i_sq, i_pkc, i_kvg, i_nd, i_ua, i_ub, i_factors, i_keep, i_vec,
                    i_alive,
                    o_out, o_tokens, o_vec,
                    main, last, from_core, near, diag, lines, out, we, cw, p, q, xg, keep, factors, vec, alive, states, seg, vg, vr, hx, hx_got, hb, hb_got,
                    rsems, credits, ssems, hsems, zsems, lsems):
    place = Place()
    line = Line(place)
    depth = place.depth
    z, c, b = place.z, place.c, place.b
    spill = Spill(lsems)
    spill.start("cw", i_c, cw)
    enter(place)
    scatter = Scatter(place, (main, last), i_pkc, from_core, near, diag, lines, out, rsems, credits)
    run = scatter.stage
    run(0, 0)
    run(0, 1)
    spill.start("alive", i_alive, alive)
    vg[...] = jnp.zeros_like(vg)
    not_last = jnp.where(place.s < line.n - 1, 1.0, 0.0).astype(F32)

    def pack(first, second, r0):
        @pl.loop(0, depth * 2)
        def _(i):
            rows = pl.ds(pl.multiple_of(i * 96, 96), 96)
            u = first[rows].astype(F32)
            v = None if second is None else second[rows].astype(F32)
            for k in range(4):
                mine = u[24 * k : 24 * k + 24]
                other = jnp.zeros((8, WIDE), F32) if v is None else v[24 * k : 24 * k + 24]
                joined = jnp.concatenate([mine, other], axis=0)
                main[i // 2, i % 2, k, r0 : r0 + joined.shape[0]] = joined.astype(BF)

    def outer(left, right, into):
        for h in range(2):
            cols = slice(384 * h, 384 * h + 384)
            into[cols] = lax.dot_general(left[:, cols], right[...], TN, preferred_element_type=F32).astype(BF)

    def fold(v):
        return v[0:8] + v[8:16]

    def following_rows(halo):
        for j in range(SEQS):
            moved = pltpu.roll(xg[j, 0:8], SEG - 1, axis=0)
            at_end = lax.broadcasted_iota(jnp.int32, moved.shape, 0) == SEG - 1
            xg[j, SPAN : SPAN + 8] = jnp.where(at_end, halo[j : j + 1], moved)

    def send_first(src, dst, sems):
        for j in range(SEQS):
            src[j : j + 1] = xg[j, 0:8][0:1]
        src[SEQS:8] = jnp.zeros((8 - SEQS, WIDE), F32)
        copy = line.shift(src, dst, sems, -1)
        copy.start()
        return copy

    def norm_back(rows, gain, source, factor_of, gain_at, bias_at, finish, middle=None):
        def one(j):
            def tile(t, sums):
                done = []
                for u in range(4):
                    r = pl.ds(pl.multiple_of(j * SPAN + t * 64 + 16 * u, 16), 16)
                    grad = rows[r] + xg[j, pl.ds(pl.multiple_of(t * 64 + 16 * u + 8, 8), 16)]
                    unit, factor = source(r), spread_lanes(factor_of[r])
                    h = grad * gain
                    back = factor * (h - jnp.mean(h, axis=-1, keepdims=True) - unit * jnp.mean(h * unit, axis=-1, keepdims=True))
                    done.append((r, back))
                    sums = sums[0] + fold(grad * unit), sums[1] + fold(grad)
                for r, back in done:
                    finish(r, back)
                return sums

            zero = jnp.zeros((8, WIDE), F32)
            sums = lax.fori_loop(0, SPAN // 64, tile, (zero, zero))
            vg[gain_at] += sums[0]
            vg[bias_at] += sums[1]

        pl.loop(0, 2)(one)
        if middle:
            middle()
        pl.loop(2, SEQS)(one)

    def channel_mix(units, gc, sqb, ge, gt):
        ei, si, gs = units.at[0], units.at[1], units.at[2]
        load = lambda f: spill.start(("sq", f), i_sq.at[:, :, :, pl.ds(32 * f, 32)], sqb.at[f % 2])
        spill.start("gc", i_gc, gc)
        load(0)
        spill.start("pkc", i_pkc, last)
        spill.start("ei", i_ei, ei)
        spill.start("we", i_e, we)
        load(1)
        spill.start("keep", i_keep, keep)
        spill.start("vec", i_vec, vec)
        spill.start("factors", i_factors, factors)
        spill.start("si", i_si, si)
        spill.start("gs", i_gs, gs)
        spill.wait("cw", "gc")

        def expand_back(f):
            spill.wait(("sq", f))

            @pl.loop(0, TOK // 256, unroll=4)
            def _(i):
                r = pl.ds(pl.multiple_of(i * 256, 256), 256)
                grad = lax.dot_general(gc[r], cw[f].reshape(WIDE, WIDE), NT, preferred_element_type=F32)
                positive = jnp.sqrt(sqb[f % 2, i].reshape(256, WIDE).astype(F32))
                ge[r] = (2.0 * positive * grad).astype(BF)

            if f + 2 < 4:
                load(f + 2)

        def expand_in_back(f):
            @pl.loop(0, TOK // 512)
            def _(i):
                r = pl.ds(pl.multiple_of(i * 512, 512), 512)
                got = lax.dot_general(ge[r], we[f], NT, preferred_element_type=F32)
                p[r] = got if f == 0 else p[r] + got

        expand_back(0)
        spill.wait("ei", "we")
        outer(ei, ge, gt.at[0])
        spill.wait("pkc")
        run(1, 0)
        expand_in_back(0)
        spill.start("ws", i_w.at[4], we.at[0])
        expand_back(1)
        outer(ei, ge, gt.at[1])
        pack(gt.at[0], gt.at[1], 128)
        run(2, 0)
        run(1, 1)
        run(0, 2)
        expand_in_back(1)
        spill.start("wo", i_w.at[3], we.at[1])
        expand_back(2)
        outer(ei, ge, gt.at[0])
        expand_in_back(2)
        expand_back(3)
        outer(ei, ge, gt.at[1])
        pack(gt.at[0], gt.at[1], 176)
        run(2, 1)
        run(1, 2)
        run(0, 3)
        run(3, 0)
        expand_in_back(3)
        spill.wait("si", "gs", "ws", "wo")
        spill.start("wk", i_w.at[0], we.at[2])
        spill.start("wv", i_w.at[1], we.at[3])
        spill.start("spb", i_spb, gc)
        outer(si, gs, gt.at[1])

        @pl.loop(0, TOK // 512)
        def _(i):
            r = pl.ds(pl.multiple_of(i * 512, 512), 512)
            q[r] = lax.dot_general(gs[r], we[0], NT, preferred_element_type=F32)

        spill.start("wr", i_w.at[2], we.at[0])
        spill.start("gyp", i_up, ge)
        spill.start("mixed", i_mixed, ei)
        spill.wait("keep", "vec", "spb")
        re, rs = vec[7:8], vec[8:9]

        @pl.loop(0, SEQS)
        def _(j):
            def tile(t, sums):
                r = pl.ds(pl.multiple_of(j * SPAN + t * 16, 16), 16)
                ge_in, gs_in, spread = p[r], q[r], gc[r].astype(F32)
                xg[j, pl.ds(pl.multiple_of(t * 16, 16), 16)] = (ge_in * (1.0 - re) + gs_in * (1.0 - rs)) * spread_lanes(keep[r])
                p[r] = ge_in * re + gs_in * rs
                return sums[0] + fold(ge_in * spread), sums[1] + fold(gs_in * spread)

            zero = jnp.zeros((8, WIDE), F32)
            sums = lax.fori_loop(0, SPAN // 16, tile, (zero, zero))
            vg[7] += sums[0]
            vg[8] += sums[1]

        send = send_first(hb, hb_got, hsems.at[0])
        spill.start("ub", i_ub, q)
        spill.wait("gyp", "mixed", "ub", "factors")
        send.wait_recv()
        following_rows(hb_got[...] * not_last)

        def finish(r, back):
            grad = ge[r].astype(F32) + back
            p[r] = grad
            si[r] = grad.astype(BF)

        norm_back(p, vec[2:3], lambda r: q[r], factors.at[1], 2, 3, finish, lambda: [run(*v) for v in ((2, 2), (1, 3), (3, 1), (4, 0))])
        send.wait_send()
        outer(ei, si, gt.at[0])
        pack(gt.at[0], gt.at[1], 80)
        run(0, 4)

        spill.wait("wk", "wv", "wr")

    unit = pltpu.VMEM((TOK, WIDE), BF)

    def time_mix(gkvg, gt1):
        pl.run_scoped(functools.partial(channel_mix, gkvg), unit, pltpu.VMEM((2, depth, 2, 4, 32, WIDE), BF), unit, pltpu.VMEM((2, WIDE, WIDE), BF))
        spill.wait("alive")
        shrink = jnp.exp(-vec[9:10])
        shrink8 = jnp.broadcast_to(shrink, (SEG, WIDE))
        bonus = vec[10:11]
        row = lax.broadcasted_iota(jnp.int32, (SEG, WIDE), 0)
        zero = jnp.zeros((SEG, WIDE), F32)

        def sweeps(buf):
            def load(j, name):
                many = 4 - name
                spill.start((name, "kvg", j), i_kvg.at[pl.ds(0, many), pl.ds(j * SPAN, SPAN)], buf.at[j % 2, pl.ds(0, many)])
                spill.start((name, "nd", j), i_nd.at[:, pl.ds(j * SPAN, SPAN)], buf.at[j % 2, pl.ds(3, 2)])

            def arrive(j, name):
                spill.wait((name, "kvg", j), (name, "nd", j))

            load(0, 1)
            load(1, 1)

            @pl.loop(0, TOK // 512)
            def _(i):
                r = pl.ds(pl.multiple_of(i * 512, 512), 512)
                q[r] = lax.dot_general(gkvg[1, r], we[1], NT, preferred_element_type=F32)

            spill.start("ki2", i_ki.at[2], gkvg.at[0])
            for j in range(SEQS):
                arrive(j, 1)
                at = buf.at[j % 2]

                def back(i, state):
                    decay, numer, denom, bonus_sum = state
                    gates = [None, None]
                    for h in (1, 0):
                        lo = pl.multiple_of((STEPS // 2 - 1 - i) * 16 + 8 * h, 8)
                        r = pl.ds(pl.multiple_of(j * SPAN + lo, 8), SEG)
                        here = pl.ds(lo, SEG)
                        kept = spread_lanes(keep[r])
                        k, v = at[0, here], at[1, here]
                        now = jnp.exp(bonus + k)
                        inverse = 1.0 / (at[4, here] + now)
                        wkv = (at[3, here] + now * v) * inverse
                        s = sigmoid(at[2, here])
                        gm = q[r]
                        gw = gm * s
                        gates[h] = gw * wkv * (1.0 - s)
                        dn = gw * inverse
                        dd = -dn * wkv
                        q[r] = dn
                        bonus_sum = bonus_sum + now * (dn * v + dd)
                        m = kept * shrink8
                        decay, numer, denom = decay * m, numer * m + kept * dn, denom * m + kept * dd
                    rows = pl.ds(pl.multiple_of(j * SPAN + (STEPS // 2 - 1 - i) * 16, 16), 16)
                    gkvg[2, rows] = jnp.concatenate(gates, axis=0).astype(BF)
                    return decay, numer, denom, bonus_sum

                decay, numer, denom, bonus_sum = lax.fori_loop(0, STEPS // 2, back, (zero + 1.0, zero, zero, zero))
                load(j + 2, 1) if j + 2 < SEQS else load(j - 2, 2)
                vg[10] += bonus_sum
                for d in (1, 2, 4):
                    end = row >= SEG - d
                    numer, denom, decay = (
                        numer + decay * jnp.where(end, 0.0, pltpu.roll(numer, SEG - d, axis=0)),
                        denom + decay * jnp.where(end, 0.0, pltpu.roll(denom, SEG - d, axis=0)),
                        decay * jnp.where(end, 1.0, pltpu.roll(decay, SEG - d, axis=0)),
                    )
                states[place.s, j : j + 1] = numer[0:1]
                states[place.s, SEQS + j : SEQS + j + 1] = denom[0:1]
                end = row >= SEG - 1
                seg[j, 0] = jnp.where(end, 1.0, pltpu.roll(decay, SEG - 1, axis=0))
                seg[j, 1] = jnp.where(end, 0.0, pltpu.roll(numer, SEG - 1, axis=0))
                seg[j, 2] = jnp.where(end, 0.0, pltpu.roll(denom, SEG - 1, axis=0))
                if j == 1:
                    run(2, 3)
                    run(1, 4)
                    run(3, 2)
                    run(4, 1)
            sent = line.all(states, ssems)
            for copy in sent:
                copy.start()
            spill.wait("ki2")
            outer(gkvg.at[0], gkvg.at[2], gt1)
            pack(gt1, None, 48)
            run(0, 5)
            for d in range(1, line.n):
                src = lax.rem(place.s + line.n - d, line.n)
                rdma(states.at[src], states.at[src], ssems, d, line.n + d, (src, b)).wait_recv()
            run(3, 3)
            run(4, 2)
            whole = jnp.exp(-float(SPAN) * vec[9:10])
            arrived = zero
            for src in range(7, 0, -1):
                after = spread_lanes(alive[src]) * whole * arrived + states[src]
                arrived = jnp.where(src > place.s, after, arrived)
            for j in range(SEQS):
                arrive(j, 2)
                at = buf.at[j % 2]
                numer0 = seg[j, 0] * arrived[j : j + 1] + seg[j, 1]
                denom0 = seg[j, 0] * arrived[SEQS + j : SEQS + j + 1] + seg[j, 2]

                def back(i, state):
                    an, ad, decay_sum = state
                    keys, values = [None, None], [None, None]
                    for h in (1, 0):
                        lo = pl.multiple_of((STEPS // 2 - 1 - i) * 16 + 8 * h, 8)
                        r = pl.ds(pl.multiple_of(j * SPAN + lo, 8), SEG)
                        here = pl.ds(lo, SEG)
                        kept = spread_lanes(keep[r])
                        k, v, numer, denom = at[0, here], at[1, here], at[3, here], at[4, here]
                        now, ek = jnp.exp(bonus + k), jnp.exp(k)
                        wkv = (numer + now * v) / (denom + now)
                        dn = q[r]
                        dd = -dn * wkv
                        keys[h] = ek * (an * v + ad) + now * (dn * v + dd)
                        values[h] = ek * an + now * dn
                        decay_sum = decay_sum + an * numer + ad * denom
                        an, ad = kept * (dn + shrink8 * an), kept * (dd + shrink8 * ad)
                    rows = pl.ds(pl.multiple_of(j * SPAN + (STEPS // 2 - 1 - i) * 16, 16), 16)
                    gkvg[0, rows] = jnp.concatenate(keys, axis=0).astype(BF)
                    gkvg[1, rows] = jnp.concatenate(values, axis=0).astype(BF)
                    return an, ad, decay_sum

                _, _, decay_sum = lax.fori_loop(0, STEPS // 2, back, (numer0, denom0, zero))
                if j + 2 < SEQS:
                    load(j + 2, 2)
                vg[9] += -shrink * decay_sum
                if j == 1:
                    run(2, 4)
                    run(1, 5)
            for copy in sent:
                copy.wait_send()
            run(4, 3)

        pl.run_scoped(sweeps, pltpu.VMEM((2, 5, SPAN, WIDE), F32))

        def mixes(ki, spa, gt, parts):
            spill.start("ki0", i_ki.at[0], ki.at[0])
            spill.start("ki1", i_ki.at[1], ki.at[1])
            spill.start("spa", i_spa, spa)
            spill.wait("ki0")
            outer(ki.at[0], gkvg.at[0], gt.at[0])
            spill.wait("ki1")
            outer(ki.at[1], gkvg.at[1], gt.at[1])
            spill.start("ua", i_ua, ki.at[1])
            pack(gt.at[0], gt.at[1], 0)
            run(0, 6)
            run(2, 5)
            run(3, 4)
            spill.wait("spa")
            ratios = [vec[4 + m : 5 + m] for m in range(3)]
            for j in range(SEQS):
                rows = pl.ds(j * SPAN, SPAN)
                for m, w in enumerate((we.at[2], we.at[3], we.at[0])):
                    parts[m] = lax.dot_general(gkvg[m, rows], w[...], NT, preferred_element_type=F32)

                def tile(t, sums):
                    r = pl.ds(pl.multiple_of(j * SPAN + t * 16, 16), 16)
                    here = pl.ds(pl.multiple_of(t * 16, 16), 16)
                    spread = spa[r].astype(F32)
                    g = [parts[m, here] for m in range(3)]
                    shifted = g[0] * (1.0 - ratios[0]) + g[1] * (1.0 - ratios[1]) + g[2] * (1.0 - ratios[2])
                    xg[j, here] = shifted * spread_lanes(keep[r])
                    q[r] = g[0] * ratios[0] + g[1] * ratios[1] + g[2] * ratios[2]
                    return tuple(s + fold(v * spread) for s, v in zip(sums, g))

                sums = lax.fori_loop(0, SPAN // 16, tile, (zero, zero, zero))
                for m in range(3):
                    vg[4 + m] += sums[m]
                if j == 0:
                    run(1, 6)
                if j == 1:
                    run(3, 5)
                    run(4, 4)
                if j == 2:
                    run(2, 6)
            send = send_first(hx, hx_got, hsems.at[1])
            spill.wait("ua")
            send.wait_recv()
            following_rows(hx_got[...] * not_last)

            def finish(r, back):
                p[r] = p[r] + back

            norm_back(q, vec[0:1], lambda r: ki[1, r].astype(F32), factors.at[0], 0, 1, finish, lambda: (run(3, 6), run(4, 5)))
            send.wait_send()

        unit2 = pltpu.VMEM((2, TOK, WIDE), BF)
        pl.run_scoped(mixes, unit2, unit, pltpu.VMEM((2, WIDE, WIDE), BF), pltpu.VMEM((3, SPAN, WIDE), F32))

    pl.run_scoped(time_mix, pltpu.VMEM((3, TOK, WIDE), BF), pltpu.VMEM((WIDE, WIDE), BF))
    spill.start("tokens", p, o_tokens)
    vr[0, VECTORS:16] = jnp.zeros((16 - VECTORS, WIDE), F32)
    for i in range(VECTORS):
        vr[0, i : i + 1] = jnp.sum(vg[i], axis=0, keepdims=True)

    def exchange(src, slot, to):
        copy = rdma(vr.at[src], vr.at[slot], zsems.at[slot], 0, 1, to)
        copy.start()
        return copy

    one = exchange(0, 1, place.core)
    one.wait_recv()
    vr[2] = vr[0] + vr[1]
    two = exchange(2, 3, place.x)
    two.wait_recv()
    vr[4] = vr[2] + vr[3]
    three = exchange(4, 5, place.y)
    three.wait_recv()
    vr[6] = vr[4] + vr[5]
    four = [exchange(6, 6 + d, place.along(d)[1]) for d in range(1, depth)]
    run(4, 6)
    total = vr[6]
    for d in range(1, depth):
        four[d - 1].wait_recv()
        total = total + vr[6 + d]
    vr[6 + depth] = total
    me = place.s * 4 + place.b
    start = me * 24
    low = pl.multiple_of(jnp.minimum(start // LANE, WIDE // LANE - 2) * LANE, LANE)
    mine = vr[6 + depth, :, pl.ds(low, WINDOW)]
    o_vec[...] = pltpu.roll(mine, WINDOW - (start - low), axis=1)[:, 0:LANE]
    spill.start("out", out, o_out)
    for copy in [one, two, three] + four:
        copy.wait_send()
    for k in range(COUNT):
        run(5, k)
    spill.wait()


BACK_INPUTS = ("w", "e", "c", "ki", "spa", "spb", "mixed", "ei", "si", "gc", "gs", "up", "sq", "pkc", "kvg", "nd", "ua", "ub", "factors", "keep", "vec", "alive")


def backward_call(f, depth):
    hbm, vmem = pl.BlockSpec(memory_space=pl.ANY), pl.BlockSpec(memory_space=pltpu.VMEM)
    s = jax.ShapeDtypeStruct
    seq, rows = depth * 2, ROWS_MAIN + ROWS_LAST
    top = max(n for _, _, n, _ in SCATTER_CHUNKS)
    row8 = pltpu.VMEM((8, WIDE), F32)
    return pl.pallas_call(
        backward_kernel,
        out_shape=(s((rows, WIDE), F32), s((TOK, WIDE), F32), s((16, LANE), F32)),
        in_specs=[hbm] * len(BACK_INPUTS),
        out_specs=(hbm, hbm, vmem),
        scratch_shapes=[
            pltpu.VMEM((depth, 2, 4, ROWS_MAIN, WIDE), BF), pltpu.VMEM((depth, 2, 4, ROWS_LAST, WIDE), BF),
            pltpu.VMEM((2, depth, 4, top, WIDE), BF), pltpu.VMEM((2, 2, depth, top, WIDE), BF), pltpu.VMEM((2, depth, top, WIDE), BF),
            pltpu.VMEM((depth - 1, rows, WIDE), BF), pltpu.VMEM((rows, WIDE), F32),
            pltpu.VMEM((4, WIDE, WIDE), BF), pltpu.VMEM((depth, 2, 4, 96, WIDE), BF),
            pltpu.VMEM((TOK, WIDE), F32), pltpu.VMEM((TOK, WIDE), F32), pltpu.VMEM((SEQS, SPAN + 8, WIDE), F32),
            pltpu.VMEM((TOK, LANE), F32), pltpu.VMEM((2, TOK, LANE), F32), pltpu.VMEM((16, WIDE), F32), pltpu.VMEM((seq, 8, LANE), F32), pltpu.VMEM((seq, 8, WIDE), F32),
            pltpu.VMEM((SEQS, 3, SEG, WIDE), F32), pltpu.VMEM((VECTORS, 8, WIDE), F32), pltpu.VMEM((7 + depth, 16, WIDE), F32),
            row8, row8, row8, row8,
            pltpu.SemaphoreType.DMA((COUNT, 16)), pltpu.SemaphoreType.REGULAR((5,)), pltpu.SemaphoreType.DMA((2 * seq,)),
            pltpu.SemaphoreType.DMA((2, 2)), pltpu.SemaphoreType.DMA((7 + depth, 2)), pltpu.SemaphoreType.DMA((56,)),
        ],
        compiler_params=pltpu.CompilerParams(collective_id=1, has_side_effects=True, vmem_limit_bytes=62 << 20),
        cost_estimate=pl.CostEstimate(flops=2 * 1024 * 26 * 768 * 768, bytes_accessed=60 << 20, transcendentals=0),
    )(*[f[n] for n in BACK_INPUTS])


def fast_body(layer_inputs, document_openings, wk, wv, wr, wo, we, ws, wc, *rest):
    vectors, upstream = rest[:VECTORS], rest[VECTORS]
    depth = lax.axis_size("seq") // 2
    rows = [lax.pad(v.astype(F32).reshape(1, 24), jnp.float32(0), ((i, 15 - i, 0), (0, LANE - 24, 0))) for i, v in enumerate(vectors)]
    vec = sum(rows[1:], rows[0])
    got = forward_call(layer_inputs.reshape(TOK, WIDE), document_openings, upstream.reshape(TOK, WIDE), vec, (wk, wv, wr, wo, ws, we, wc), depth)
    out, tokens, small = backward_call(got, depth)

    def natural(v):
        return v.reshape(SEQS, STEPS, SEG, WIDE).transpose(0, 2, 1, 3).reshape(SEQS, SPAN, WIDE)

    expand = jnp.concatenate([out[128 + 24 * i : 152 + 24 * i] for i in range(4)], axis=1)
    return (natural(got["bo"]), natural(tokens), out[0:24], out[24:48], out[48:72], out[80:104], expand, out[104:128], out[224:320]) + tuple(
        small[i, 0:24] for i in range(VECTORS))


def from_behind(block, axis, distance):
    devices = range(lax.axis_size(axis))
    route = [(i - distance, i) for i in devices if i - distance in devices]
    return lax.ppermute(block, axis, route)


def prefix(part, axis, combine, identity, reverse):
    count = lax.axis_size(axis)
    place = lax.axis_index(axis)
    ahead = count - 1 - place if reverse else place
    gathered = jax.tree.map(lambda a: lax.all_gather(a, axis), part)
    state = jax.tree.map(lambda a, e: jnp.zeros_like(a) + jnp.asarray(e, a.dtype), part, identity)

    def one(turn, state):
        source = count - 1 - turn if reverse else turn
        return combine(
            state, jax.tree.map(lambda a: lax.dynamic_index_in_dim(a, source, 0, False), gathered)
        )

    return lax.fori_loop(0, ahead, one, state)


def layer_norm(values, gain, offset):
    center = values - jnp.mean(values, axis=-1, keepdims=True)
    factor = lax.rsqrt(jnp.mean(center * center, axis=-1, keepdims=True) + EPSILON)
    normed = center * factor
    return (normed * gain + offset, normed, factor)


def norm_back(grad_out, normed, factor, gain):
    scaled = grad_out * gain
    centered = scaled - jnp.mean(scaled, axis=-1, keepdims=True)
    grad_in = factor * (centered - normed * jnp.mean(scaled * normed, axis=-1, keepdims=True))
    return (grad_in, jnp.sum(grad_out * normed, axis=(0, 1)), jnp.sum(grad_out, axis=(0, 1)))


def product(left, right):
    return jnp.einsum("scd,de->sce", left, right, preferred_element_type=jnp.float32)


def product_back(grad, right):
    return jnp.einsum("sce,de->scd", grad, right, preferred_element_type=jnp.float32)


def outer_sum(left, grad):
    return jnp.einsum("scd,sce->de", left, grad, preferred_element_type=jnp.float32)


def attach_previous(values, arriving, persisting_indicator):
    return jnp.concatenate([arriving, values[:, :-1]], axis=1) * persisting_indicator[..., None]


def attach_next(masked, arriving):
    return jnp.concatenate([masked[:, 1:], arriving], axis=1)


def make_combine(fading_multiplier):

    def combine(earlier, later):
        early_numer, early_denom, early_length, early_cut = earlier
        late_numer, late_denom, late_length, late_cut = later
        fading = jnp.exp(-late_length * fading_multiplier) * (1.0 - late_cut)
        return (
            late_numer + fading * early_numer,
            late_denom + fading * early_denom,
            early_length + late_length,
            jnp.maximum(early_cut, late_cut),
        )

    return combine


def affine_compose(first_step, second_step):
    first_mult, first_numer, first_denom = first_step
    second_mult, second_numer, second_denom = second_step
    return (
        first_mult * second_mult,
        second_mult * first_numer + second_numer,
        second_mult * first_denom + second_denom,
    )


def forward_sweep(exponentiated_lookup, payload_table_lines, persisting_indicator, shrink):
    multiplier = persisting_indicator[..., None] * shrink
    inclusive = lax.associative_scan(
        affine_compose,
        (multiplier, exponentiated_lookup * payload_table_lines, exponentiated_lookup),
        axis=1,
    )
    zeros = jnp.zeros_like(exponentiated_lookup[:, :1])
    numer_all = (
        jnp.concatenate([zeros, inclusive[1][:, :-1]], axis=1) * persisting_indicator[..., None]
    )
    denom_all = (
        jnp.concatenate([zeros, inclusive[2][:, :-1]], axis=1) * persisting_indicator[..., None]
    )
    return (numer_all, denom_all, inclusive[1][:, -1], inclusive[2][:, -1])


def reverse_sweep(adjoint_dividend, grad_denom, persisting_indicator, shrink):
    keep_now = persisting_indicator[..., None]
    inclusive = lax.associative_scan(
        affine_compose,
        (keep_now * shrink, keep_now * adjoint_dividend, keep_now * grad_denom),
        axis=1,
        reverse=True,
    )
    zeros = jnp.zeros_like(adjoint_dividend[:, :1])
    following_dividend = jnp.concatenate([inclusive[1][:, 1:], zeros], axis=1)
    next_denom = jnp.concatenate([inclusive[2][:, 1:], zeros], axis=1)
    return (following_dividend, next_denom, inclusive[1][:, 0], inclusive[2][:, 0])


def body(
    layer_inputs,
    document_openings,
    mixing_lookup_projection,
    mixing_payload_projection,
    mixing_acceptor_projection,
    mixing_result_projection,
    feedforward_lookup_projection,
    feedforward_acceptor_projection,
    feedforward_payload_projection,
    premix_layer_scaling,
    premix_layer_offset,
    postmix_layer_scaling,
    postmix_layer_offset,
    mixing_lookup_blend,
    mixing_payload_blend,
    mixing_acceptor_blend,
    feedforward_lookup_blend,
    feedforward_acceptor_blend,
    feature_fading_speed,
    present_token_reward,
    upstream_adjoint,
):
    gathered = (
        lax.all_gather(mixing_lookup_projection, BOTH, axis=0, tiled=True),
        lax.all_gather(mixing_payload_projection, BOTH, axis=0, tiled=True),
        lax.all_gather(mixing_acceptor_projection, BOTH, axis=0, tiled=True),
        lax.all_gather(mixing_result_projection, BOTH, axis=0, tiled=True),
        lax.all_gather(feedforward_lookup_projection, BOTH, axis=0, tiled=True),
        lax.all_gather(feedforward_acceptor_projection, BOTH, axis=0, tiled=True),
        lax.all_gather(feedforward_payload_projection, BOTH, axis=0, tiled=True),
        lax.all_gather(premix_layer_scaling, BOTH, axis=0, tiled=True),
        lax.all_gather(premix_layer_offset, BOTH, axis=0, tiled=True),
        lax.all_gather(postmix_layer_scaling, BOTH, axis=0, tiled=True),
        lax.all_gather(postmix_layer_offset, BOTH, axis=0, tiled=True),
        lax.all_gather(mixing_lookup_blend, BOTH, axis=0, tiled=True),
        lax.all_gather(mixing_payload_blend, BOTH, axis=0, tiled=True),
        lax.all_gather(mixing_acceptor_blend, BOTH, axis=0, tiled=True),
        lax.all_gather(feedforward_lookup_blend, BOTH, axis=0, tiled=True),
        lax.all_gather(feedforward_acceptor_blend, BOTH, axis=0, tiled=True),
        lax.all_gather(feature_fading_speed, BOTH, axis=0, tiled=True),
        lax.all_gather(present_token_reward, BOTH, axis=0, tiled=True),
    )
    full_key, full_value, full_gate, full_output, full_expand, full_select, full_contract = (
        gathered[:7]
    )
    vectors = [stream_element.astype(jnp.float32) for stream_element in gathered[7:]]
    (
        gain_first,
        bias_first,
        gain_second,
        bias_second,
        ratio_key,
        ratio_value,
        ratio_gate,
        ratio_expand,
        ratio_select,
        fading_multiplier,
        present_reward_term,
    ) = vectors
    inputs = layer_inputs.astype(jnp.float32)
    flags = document_openings.astype(jnp.float32)
    persisting_indicator = 1.0 - flags
    sequences = layer_inputs.shape[0]
    block_len = layer_inputs.shape[1]
    width = layer_inputs.shape[2]
    normed_a, unit_a, factor_a = layer_norm(inputs, gain_first, bias_first)
    arriving_a = from_behind(normed_a[:, -1:, :], "seq", 1)
    before_a = attach_previous(normed_a, arriving_a, persisting_indicator)
    spread_a = normed_a - before_a
    key_in = (before_a + spread_a * ratio_key).astype(jnp.bfloat16)
    value_in = (before_a + spread_a * ratio_value).astype(jnp.bfloat16)
    gate_in = (before_a + spread_a * ratio_gate).astype(jnp.bfloat16)
    lookup_table_lines = product(key_in, full_key)
    payload_table_lines = product(value_in, full_value)
    gate_rows = product(gate_in, full_gate)
    shrink = jnp.exp(-fading_multiplier)
    exponentiated_lookup = jnp.exp(lookup_table_lines)
    reward_scaled_pairs = jnp.exp(present_reward_term + lookup_table_lines)
    local_numer, local_denom, end_numer, end_denom = forward_sweep(
        exponentiated_lookup, payload_table_lines, persisting_indicator, shrink
    )
    cut = jnp.max(flags, axis=1, keepdims=True)
    length = jnp.full((1,), float(block_len), jnp.float32)
    zero_state = jnp.zeros((sequences, width), jnp.float32)
    identity = (
        zero_state,
        zero_state,
        jnp.zeros((1,), jnp.float32),
        jnp.zeros((sequences, 1), jnp.float32),
    )
    combine = make_combine(fading_multiplier)
    arrived = prefix((end_numer, end_denom, length, cut), "seq", combine, identity, False)
    positions = jnp.arange(block_len, dtype=jnp.float32)
    alive = 1.0 - lax.cummax(flags, axis=1)
    rising = jnp.exp(-positions[:, None] * fading_multiplier[None, :])
    running_dividend = local_numer + alive[..., None] * rising[None] * arrived[0][:, None, :]
    running_divisor = local_denom + alive[..., None] * rising[None] * arrived[1][:, None, :]
    accumulated_sum = running_divisor + reward_scaled_pairs
    recurrent_average = (
        running_dividend + reward_scaled_pairs * payload_table_lines
    ) / accumulated_sum
    gate_sig = jax.nn.sigmoid(gate_rows)
    mixed = (gate_sig * recurrent_average).astype(jnp.bfloat16)
    first = inputs + product(mixed, full_output)
    normed_b, unit_b, factor_b = layer_norm(first, gain_second, bias_second)
    arriving_b = from_behind(normed_b[:, -1:, :], "seq", 1)
    before_b = attach_previous(normed_b, arriving_b, persisting_indicator)
    spread_b = normed_b - before_b
    expand_in = (before_b + spread_b * ratio_expand).astype(jnp.bfloat16)
    select_in = (before_b + spread_b * ratio_select).astype(jnp.bfloat16)
    expanded = product(expand_in, full_expand)
    selected = product(select_in, full_select)
    positive = jax.nn.relu(expanded)
    squared = (positive * positive).astype(jnp.bfloat16)
    contracted = product(squared, full_contract)
    select_sig = jax.nn.sigmoid(selected)
    block_out = (first + select_sig * contracted).astype(jnp.bfloat16)
    again = (
        lax.all_gather(mixing_lookup_projection, BOTH, axis=0, tiled=True),
        lax.all_gather(mixing_payload_projection, BOTH, axis=0, tiled=True),
        lax.all_gather(mixing_acceptor_projection, BOTH, axis=0, tiled=True),
        lax.all_gather(mixing_result_projection, BOTH, axis=0, tiled=True),
        lax.all_gather(feedforward_lookup_projection, BOTH, axis=0, tiled=True),
        lax.all_gather(feedforward_acceptor_projection, BOTH, axis=0, tiled=True),
        lax.all_gather(feedforward_payload_projection, BOTH, axis=0, tiled=True),
    )
    full_key, full_value, full_gate, full_output, full_expand, full_select, full_contract = again
    upstream = upstream_adjoint.astype(jnp.float32)
    grad_contracted = (upstream * select_sig).astype(jnp.bfloat16)
    grad_selected = (upstream * contracted * select_sig * (1.0 - select_sig)).astype(jnp.bfloat16)
    grad_squared = product_back(grad_contracted, full_contract)
    grad_expanded = (2.0 * positive * grad_squared).astype(jnp.bfloat16)
    contract_grad = jnp.einsum(
        "scf,scd->fd", squared, grad_contracted, preferred_element_type=jnp.float32
    )
    expand_grad = outer_sum(expand_in, grad_expanded)
    select_grad = outer_sum(select_in, grad_selected)
    grad_expand_in = product_back(grad_expanded, full_expand)
    grad_select_in = product_back(grad_selected, full_select)
    expand_ratio_grad = jnp.sum(grad_expand_in * spread_b, axis=(0, 1))
    select_ratio_grad = jnp.sum(grad_select_in * spread_b, axis=(0, 1))
    grad_before_b = (
        grad_expand_in * (1.0 - ratio_expand) + grad_select_in * (1.0 - ratio_select)
    ) * persisting_indicator[..., None]
    arriving_gb = from_behind(grad_before_b[:, :1, :], "seq", -1)
    grad_normed_b = (
        grad_expand_in * ratio_expand
        + grad_select_in * ratio_select
        + attach_next(grad_before_b, arriving_gb)
    )
    grad_from_b, chan_gain_grad, chan_bias_grad = norm_back(
        grad_normed_b, unit_b, factor_b, gain_second
    )
    grad_first = upstream + grad_from_b
    grad_attended = grad_first.astype(jnp.bfloat16)
    output_grad = outer_sum(mixed, grad_attended)
    grad_mixed = product_back(grad_attended, full_output)
    grad_gates = (grad_mixed * recurrent_average * gate_sig * (1.0 - gate_sig)).astype(jnp.bfloat16)
    grad_wkv = grad_mixed * gate_sig
    adjoint_dividend = grad_wkv / accumulated_sum
    grad_denom = -grad_wkv * recurrent_average / accumulated_sum
    following_dividend, next_denom, lead_numer, lead_denom = reverse_sweep(
        adjoint_dividend, grad_denom, persisting_indicator, shrink
    )
    behind = prefix((lead_numer, lead_denom, length, cut), "seq", combine, identity, True)
    after = jnp.concatenate([flags[:, 1:], jnp.zeros_like(flags[:, :1])], axis=1)
    later_alive = 1.0 - lax.cummax(after, axis=1, reverse=True)
    falling = jnp.exp(-(block_len - 1.0 - positions)[:, None] * fading_multiplier[None, :])
    following_dividend = (
        following_dividend + later_alive[..., None] * falling[None] * behind[0][:, None, :]
    )
    next_denom = next_denom + later_alive[..., None] * falling[None] * behind[1][:, None, :]
    immediate_term = adjoint_dividend * payload_table_lines + grad_denom
    grad_keys = (
        exponentiated_lookup * (following_dividend * payload_table_lines + next_denom)
        + reward_scaled_pairs * immediate_term
    ).astype(jnp.bfloat16)
    adjoint_payloads = (
        exponentiated_lookup * following_dividend + reward_scaled_pairs * adjoint_dividend
    ).astype(jnp.bfloat16)
    present_reward_adjoint = jnp.sum(reward_scaled_pairs * immediate_term, axis=(0, 1))
    decay_grad = -shrink * jnp.sum(
        following_dividend * running_dividend + next_denom * running_divisor, axis=(0, 1)
    )
    key_grad = outer_sum(key_in, grad_keys)
    value_grad = outer_sum(value_in, adjoint_payloads)
    gate_grad = outer_sum(gate_in, grad_gates)
    grad_key_in = product_back(grad_keys, full_key)
    grad_value_in = product_back(adjoint_payloads, full_value)
    grad_gate_in = product_back(grad_gates, full_gate)
    key_ratio_grad = jnp.sum(grad_key_in * spread_a, axis=(0, 1))
    value_ratio_grad = jnp.sum(grad_value_in * spread_a, axis=(0, 1))
    gate_ratio_grad = jnp.sum(grad_gate_in * spread_a, axis=(0, 1))
    grad_before_a = (
        grad_key_in * (1.0 - ratio_key)
        + grad_value_in * (1.0 - ratio_value)
        + grad_gate_in * (1.0 - ratio_gate)
    ) * persisting_indicator[..., None]
    arriving_ga = from_behind(grad_before_a[:, :1, :], "seq", -1)
    grad_normed_a = (
        grad_key_in * ratio_key
        + grad_value_in * ratio_value
        + grad_gate_in * ratio_gate
        + attach_next(grad_before_a, arriving_ga)
    )
    grad_from_a, attn_gain_grad, attn_bias_grad = norm_back(
        grad_normed_a, unit_a, factor_a, gain_first
    )
    tokens_grad = grad_first + grad_from_a
    shares = (
        lax.psum_scatter(key_grad, BOTH, scatter_dimension=0, tiled=True),
        lax.psum_scatter(value_grad, BOTH, scatter_dimension=0, tiled=True),
        lax.psum_scatter(gate_grad, BOTH, scatter_dimension=0, tiled=True),
        lax.psum_scatter(output_grad, BOTH, scatter_dimension=0, tiled=True),
        lax.psum_scatter(expand_grad, BOTH, scatter_dimension=0, tiled=True),
        lax.psum_scatter(select_grad, BOTH, scatter_dimension=0, tiled=True),
        lax.psum_scatter(contract_grad, BOTH, scatter_dimension=0, tiled=True),
        lax.psum_scatter(attn_gain_grad, BOTH, scatter_dimension=0, tiled=True),
        lax.psum_scatter(attn_bias_grad, BOTH, scatter_dimension=0, tiled=True),
        lax.psum_scatter(chan_gain_grad, BOTH, scatter_dimension=0, tiled=True),
        lax.psum_scatter(chan_bias_grad, BOTH, scatter_dimension=0, tiled=True),
        lax.psum_scatter(key_ratio_grad, BOTH, scatter_dimension=0, tiled=True),
        lax.psum_scatter(value_ratio_grad, BOTH, scatter_dimension=0, tiled=True),
        lax.psum_scatter(gate_ratio_grad, BOTH, scatter_dimension=0, tiled=True),
        lax.psum_scatter(expand_ratio_grad, BOTH, scatter_dimension=0, tiled=True),
        lax.psum_scatter(select_ratio_grad, BOTH, scatter_dimension=0, tiled=True),
        lax.psum_scatter(decay_grad, BOTH, scatter_dimension=0, tiled=True),
        lax.psum_scatter(present_reward_adjoint, BOTH, scatter_dimension=0, tiled=True),
    )
    return (
        block_out,
        tokens_grad,
        shares[0],
        shares[1],
        shares[2],
        shares[3],
        shares[4],
        shares[5],
        shares[6],
        shares[7],
        shares[8],
        shares[9],
        shares[10],
        shares[11],
        shares[12],
        shares[13],
        shares[14],
        shares[15],
        shares[16],
        shares[17],
    )


def solution(mesh):
    fits = mesh.shape["seq"] == 8 and mesh.shape["batch"] == 4
    return jax.shard_map(
        fast_body if fits else body,
        mesh=mesh,
        in_specs=(
            P("batch", "seq", None),
            P("batch", "seq"),
            P(BOTH, None),
            P(BOTH, None),
            P(BOTH, None),
            P(BOTH, None),
            P(BOTH, None),
            P(BOTH, None),
            P(BOTH, None),
            P(BOTH),
            P(BOTH),
            P(BOTH),
            P(BOTH),
            P(BOTH),
            P(BOTH),
            P(BOTH),
            P(BOTH),
            P(BOTH),
            P(BOTH),
            P(BOTH),
            P("batch", "seq", None),
        ),
        out_specs=(
            P("batch", "seq", None),
            P("batch", "seq", None),
            P(BOTH, None),
            P(BOTH, None),
            P(BOTH, None),
            P(BOTH, None),
            P(BOTH, None),
            P(BOTH, None),
            P(BOTH, None),
            P(BOTH),
            P(BOTH),
            P(BOTH),
            P(BOTH),
            P(BOTH),
            P(BOTH),
            P(BOTH),
            P(BOTH),
            P(BOTH),
            P(BOTH),
            P(BOTH),
        ),
        check_vma=False,
    )
```

```python
import functools

import jax
import jax.numpy as jnp
from jax import lax
from jax.experimental import pallas as pl
from jax.experimental.pallas import tpu as pltpu
from jax.sharding import PartitionSpec as P

BOTH = ("seq", "batch")
MESH = pl.DeviceIdType.MESH
BF = jnp.bfloat16
F32 = jnp.float32
WIDE = 768
ROWS_MAIN = 224
ROWS_LAST = 96
GATHER_CHUNKS = (
    (0, 48, 32, 16), (0, 0, 48, 32), (0, 80, 48, 16), (0, 128, 48, 32), (0, 176, 48, 16), (1, 0, 64, 32), (1, 64, 32, 16))
SCATTER_CHUNKS = (
    (1, 0, 48, 32), (1, 48, 48, 16), (0, 128, 48, 32), (0, 176, 48, 16), (0, 80, 48, 32), (0, 48, 32, 16), (0, 0, 48, 16))
COUNT = len(GATHER_CHUNKS)


class Place:
    def __init__(self):
        self.s = lax.axis_index("seq")
        self.b = lax.axis_index("batch")
        self.z, self.c = self.s // 2, self.s % 2
        y, x = self.b // 2, self.b % 2
        self.bx, self.by, self.bd = y * 2 + 1 - x, (1 - y) * 2 + x, (1 - y) * 2 + 1 - x
        self.depth = lax.axis_size("seq") // 2
        self.x, self.y = (self.s, self.bx), (self.s, self.by)
        self.core = (self.z * 2 + 1 - self.c, self.b)

    def along(self, step):
        z = lax.rem(self.z + step, self.depth)
        return z, (z * 2 + self.c, self.b)

    def back(self, step):
        return lax.rem(self.z + self.depth - step, self.depth)


def rdma(src, dst, sems, send, recv, to):
    return pltpu.make_async_remote_copy(
        src_ref=src, dst_ref=dst, send_sem=sems.at[send], recv_sem=sems.at[recv], device_id=to, device_id_type=MESH
    )


def enter(place):
    barrier = pltpu.get_barrier_semaphore()
    n = lax.axis_size("seq")
    peers = [place.x, place.y, (place.s, place.bd)] + [(lax.rem(place.s + d, n), place.b) for d in range(1, n)]
    for peer in peers:
        pl.semaphore_signal(barrier, inc=1, device_id=peer, device_id_type=MESH)
    pl.semaphore_wait(barrier, len(peers))


class Gather:
    def __init__(self, place, arrays, sems):
        self.p, self.arrays, self.sems = place, arrays, sems

    def stage(self, number, k):
        if not 0 <= k < COUNT:
            return
        p, sems = self.p, self.sems.at[k]
        a, r0, n, nx = GATHER_CHUNKS[k]
        ref = self.arrays[a]
        whole, part_x, part_y = pl.ds(r0, n), pl.ds(r0, nx), pl.ds(r0 + nx, n - nx)
        col = lambda c, b, rows: ref.at[:, c, b, rows]
        move = lambda view, at, to: rdma(view, view, sems, at, at + 1, to)
        one = lambda z, b: ref.at[z, p.c, b, whole]
        line = lambda d, z: move(one(z, p.b), 2 * d - 2, p.along(d)[1])
        near_x = lambda b: move(col(p.c, b, whole), 6, p.x)
        near_y = lambda b: move(col(p.c, b, whole), 8, p.y)
        diag_x = lambda b: move(col(p.c, b, part_x), 10, p.x)
        diag_y = lambda b: move(col(p.c, b, part_y), 12, p.y)
        core = lambda j, c, b: move(col(c, b, whole), 14 + 2 * j, p.core)
        single = k == 0
        steps = range(p.depth)
        lone = lambda d, z, b, c: (
            move(ref.at[z, c, b, whole], 22 + 6 * d, p.x), move(ref.at[z, c, b, whole], 24 + 6 * d, p.y),
            move(ref.at[z, c, b, whole], 26 + 6 * d, p.core))
        if number == 0:
            for d in range(1, p.depth):
                line(d, p.z).start()
            if single:
                for copy in lone(0, p.z, p.b, p.c):
                    copy.start()
        elif number == 1:
            for d in range(1, p.depth):
                line(d, p.back(d)).wait_recv()
                if single:
                    for copy in lone(d, p.back(d), p.b, p.c):
                        copy.start()
            if not single:
                near_x(p.b).start()
                near_y(p.b).start()
                core(0, p.c, p.b).start()
        elif number == 2:
            if single:
                for d in steps:
                    lone(d, p.back(d), p.bx, p.c)[0].wait_recv()
                    lone(d, p.back(d), p.by, p.c)[1].wait_recv()
            else:
                near_x(p.bx).wait_recv()
                near_y(p.by).wait_recv()
            diag_x(p.by).start()
            diag_y(p.bx).start()
            core(1, p.c, p.bx).start()
            core(2, p.c, p.by).start()
        elif number == 3:
            diag_x(p.bd).wait_recv()
            diag_y(p.bd).wait_recv()
            core(3, p.c, p.bd).start()
        elif number == 4:
            if single:
                for d in steps:
                    lone(d, p.back(d), p.b, 1 - p.c)[2].wait_recv()
            for j, b in enumerate((p.b, p.bx, p.by, p.bd)):
                if j or not single:
                    core(j, 1 - p.c, b).wait_recv()
        elif number == 5:
            for d in range(1, p.depth):
                line(d, p.z).wait_send()
            if single:
                for d in steps:
                    for copy in lone(d, p.back(d), p.b, p.c):
                        copy.wait_send()
            else:
                near_x(p.b).wait_send()
                near_y(p.b).wait_send()
                core(0, p.c, p.b).wait_send()
            diag_x(p.by).wait_send()
            diag_y(p.bx).wait_send()
            for j, b in ((1, p.bx), (2, p.by), (3, p.bd)):
                core(j, p.c, b).wait_send()

    def tick(self, t):
        for number in range(5):
            self.stage(number, t - number)


class Scatter:
    def __init__(self, place, packed, early, from_core, near, diag, line, out, sems, credits):
        self.early = early
        self.p, self.packed, self.from_core, self.near = place, packed, from_core, near
        self.diag, self.line, self.out, self.sems, self.credits = diag, line, out, sems, credits

    def stage(self, number, k):
        p, sems = self.p, self.sems.at[k]
        a, r0, n, nx = SCATTER_CHUNKS[k]
        ref, slot, depth = self.packed[a], k % 2, p.depth
        f0 = r0 if a == 0 else r0 + ROWS_MAIN
        whole, part_x, part_y = pl.ds(r0, n), pl.ds(r0, nx), pl.ds(r0 + nx, n - nx)
        whence = self.early if a == 1 else ref
        core = lambda: rdma(whence.at[:, 1 - p.c, :, whole], self.from_core.at[slot, :, :, pl.ds(0, n)], sems, 0, 1, p.core)
        diag_x = lambda: rdma(ref.at[:, p.c, p.bd, part_x], self.diag.at[slot, :, pl.ds(0, nx)], sems, 2, 3, p.x)
        diag_y = lambda: rdma(ref.at[:, p.c, p.bd, part_y], self.diag.at[slot, :, pl.ds(nx, n - nx)], sems, 4, 5, p.y)
        near_x = lambda: rdma(ref.at[:, p.c, p.bx, whole], self.near.at[slot, 0, :, pl.ds(0, n)], sems, 6, 7, p.x)
        near_y = lambda: rdma(ref.at[:, p.c, p.by, whole], self.near.at[slot, 1, :, pl.ds(0, n)], sems, 8, 9, p.y)

        def along(d):
            z, to = p.along(d)
            return rdma(ref.at[z, p.c, p.b, whole], self.line.at[d - 1, pl.ds(f0, n)], sems, 8 + 2 * d, 9 + 2 * d, to)

        def ready(*which):
            if k >= 2:
                for w in which:
                    pl.semaphore_wait(self.credits.at[w], 1)

        def free(which, to):
            if k + 2 < COUNT:
                pl.semaphore_signal(self.credits.at[which], inc=1, device_id=to, device_id_type=MESH)

        if number == 0:
            ready(0)
            core().start()
        elif number == 1:
            core().wait_recv()

            @pl.loop(0, depth * 4)
            def _(i):
                z, b = i // 4, i % 4
                ref[z, p.c, b, r0 : r0 + n] = ref[z, p.c, b, r0 : r0 + n] + self.from_core[slot, z, b, 0:n]

            free(0, p.core)
            ready(1, 2)
            diag_x().start()
            diag_y().start()
        elif number == 2:
            diag_x().wait_recv()
            diag_y().wait_recv()

            @pl.loop(0, depth)
            def _(z):
                for b, s0, m in ((p.by, 0, nx), (p.bx, nx, n - nx)):
                    ref[z, p.c, b, r0 + s0 : r0 + s0 + m] = ref[z, p.c, b, r0 + s0 : r0 + s0 + m] + self.diag[slot, z, s0 : s0 + m]

            free(1, p.x)
            free(2, p.y)
            ready(3, 4)
            near_x().start()
            near_y().start()
        elif number == 3:
            near_x().wait_recv()
            near_y().wait_recv()

            @pl.loop(0, depth)
            def _(z):
                ref[z, p.c, p.b, r0 : r0 + n] = (
                    ref[z, p.c, p.b, r0 : r0 + n].astype(F32)
                    + self.near[slot, 0, z, 0:n].astype(F32)
                    + self.near[slot, 1, z, 0:n].astype(F32)
                ).astype(BF)

            free(3, p.x)
            free(4, p.y)
            for d in range(1, depth):
                along(d).start()
        elif number == 4:
            for d in range(1, depth):
                along(d).wait_recv()
            total = ref[p.z, p.c, p.b, r0 : r0 + n].astype(F32)
            for d in range(1, depth):
                total = total + self.line[d - 1, f0 : f0 + n].astype(F32)
            self.out[f0 : f0 + n] = total
        elif number == 5:
            for each in (core, diag_x, diag_y, near_x, near_y):
                each().wait_send()
            for d in range(1, depth):
                along(d).wait_send()


EPSILON = 1e-05
TOK = 1024
SEQS = 4
SPAN = 256
STEPS = 32
SEG = 8
LANE = 128
WINDOW = 256
VECTORS = 11


def window_of(i):
    return min(i * 24 // LANE, WIDE // LANE - 2) * LANE


def spread_lanes(v):
    return jnp.concatenate([v] * (WIDE // LANE), axis=1)


def unit_norm(v):
    center = v - jnp.mean(v, axis=-1, keepdims=True)
    factor = lax.rsqrt(jnp.mean(center * center, axis=-1, keepdims=True) + EPSILON)
    return center * factor, factor


def sigmoid(v):
    return 1.0 / (1.0 + jnp.exp(-v))


def first_rows(halo_row, last_group):
    moved = pltpu.roll(last_group, 1, axis=0)
    at_top = lax.broadcasted_iota(jnp.int32, moved.shape, 0) == 0
    return jnp.where(at_top, halo_row, moved)


def permute_in(src, dst, tmp):
    @pl.loop(0, SEQS)
    def _(j):
        base = pl.multiple_of(j * SPAN, SPAN)
        for l in range(WIDE // LANE):
            tmp[l] = src[pl.ds(base, SPAN), l * LANE : (l + 1) * LANE].astype(F32)

        @pl.loop(0, STEPS // 2)
        def _(s):
            for l in range(WIDE // LANE):
                two = jnp.concatenate([tmp[l, pl.ds(2 * s, SEG, stride=STEPS), :], tmp[l, pl.ds(2 * s + 1, SEG, stride=STEPS), :]], axis=0)
                dst[pl.ds(pl.multiple_of(base + s * 16, 16), 16), l * LANE : (l + 1) * LANE] = two.astype(BF)


class Spill:
    def __init__(self, sems):
        self.sems, self.copies, self.used = sems, {}, 0

    def start(self, name, src, dst):
        self.copies[name] = pltpu.make_async_copy(src, dst, self.sems.at[self.used])
        self.used += 1
        self.copies[name].start()

    def wait(self, *names):
        for name in names or list(self.copies):
            self.copies.pop(name).wait()


class Line:
    def __init__(self, place):
        self.p = place
        self.n = lax.axis_size("seq")

    def all(self, buf, sems):
        p, copies = self.p, []
        for d in range(1, self.n):
            to = (lax.rem(p.s + d, self.n), p.b)
            copies.append(rdma(buf.at[p.s], buf.at[p.s], sems, d, self.n + d, to))
        return copies

    def shift(self, src, dst, sems, step):
        return rdma(src, dst, sems, 0, 1, (lax.rem(self.p.s + self.n + step, self.n), self.p.b))


def relayout(st, dst, depth, r0, n, targets):
    @pl.loop(0, depth * 2)
    def _(i):
        z, c = i // 2, i % 2
        slabs = [st[z, c, b, r0 : r0 + n].astype(F32) for b in range(4)]
        rows = pl.ds(pl.multiple_of(i * 96, 96), 96)
        for index, at in targets:
            dst[index, rows] = jnp.concatenate([v[at : at + 24] for v in slabs], axis=0).astype(BF)


def matmul(left, right, out, rows=512):
    @pl.loop(0, TOK // rows, unroll=2)
    def _(i):
        r = pl.ds(pl.multiple_of(i * rows, rows), rows)
        out[r] = jnp.dot(left[r], right[...], preferred_element_type=F32)


def forward_kernel(x_in, up_in, openings, vec_in, wk, wv, wr, wo, ws, we_in, wc_in,
                   o_w, o_e, o_c, o_ki, o_spa, o_spb, o_mixed, o_ei, o_si, o_gc, o_gs, o_up, o_sq, o_pkc,
                   o_kvg, o_nd, o_ua, o_ub, o_factors, o_keep, o_vec, o_alive, o_bo,
                   st, cw, wd, we, u0, xp, u1, gyp, tmp, keep, xa, ki, kvg, nd, spb, factors, vec, states, alive, seg, carry, hx, hx_got, hb, hb_got,
                   gsems, asems, ssems, hsems, lsems):
    place = Place()
    line = Line(place)
    depth = place.depth
    devices = depth * 8
    me = place.s * 4 + place.b
    spill = Spill(lsems)
    spill.start("x", x_in, u0)
    spill.start("up", up_in, u1)
    z, c, b = place.z, place.c, place.b
    as32 = lambda ref: ref[...].astype(F32)
    join = lambda *v: jnp.concatenate(v, axis=0).astype(BF)
    start = me * 24
    low = jnp.minimum(start // LANE, WIDE // LANE - 2) * LANE
    wide = pltpu.roll(jnp.concatenate([vec_in[...], jnp.zeros((16, LANE), F32)], axis=1), start - low, axis=1)
    small = jnp.concatenate([wide[0:8], wide[8:16], jnp.zeros((8, WIDE - 2 * WINDOW), F32)], axis=1)
    st[z, c, b, 48:80] = join(as32(wr), small)
    st[z, c, b, 0:48] = join(as32(wk), as32(wv))
    enter(place)
    gather = Gather(place, (st, cw), gsems)
    gather.tick(0)
    st[z, c, b, 80:128] = join(as32(wo), as32(ws))
    e = as32(we_in)
    for h in range(2):
        st[z, c, b, 128 + 48 * h : 176 + 48 * h] = join(e[:, 2 * h * WIDE : (2 * h + 1) * WIDE], e[:, (2 * h + 1) * WIDE : (2 * h + 2) * WIDE])
    cw[z, c, b] = wc_in[...]

    gather.tick(1)
    spill.wait("x")
    for j in range(SEQS):
        hx[j : j + 1] = u0[SPAN * j + SPAN - 16 : SPAN * j + SPAN].astype(F32)[15:16]
    hx[SEQS:8] = jnp.zeros((8 - SEQS, WIDE), F32)
    send_hx = line.shift(hx, hx_got, hsems.at[0], 1)
    send_hx.start()
    permute_in(u0, xp, tmp)
    gather.tick(2)
    for j in range(SEQS):
        flags = 1.0 - openings[j : j + 1].astype(F32)
        tmp[0] = jnp.broadcast_to(flags, (LANE, SPAN)).T
        for s in range(STEPS):
            keep[j * SPAN + s * SEG : j * SPAN + (s + 1) * SEG] = tmp[0, pl.ds(s, SEG, stride=STEPS), :]
    spill.start("keep", keep, o_keep)
    for j in range(SEQS):
        low_keep = jnp.min(keep[SPAN * j : SPAN * (j + 1)], axis=0, keepdims=True)
        alive[place.s, j : j + 1] = low_keep
        alive[place.s, SEQS + j : SEQS + j + 1] = low_keep
    send_alive = line.all(alive, asems)
    for copy in send_alive:
        copy.start()
    gather.tick(3)
    spill.wait("up")
    permute_in(u1, gyp, tmp)
    spill.start("gyp", gyp, o_up)
    gather.tick(4)
    vec[...] = jnp.zeros_like(vec)
    for i in range(devices):
        w = window_of(i)
        got = st[i // 8, i // 4 % 2, i % 4, 64:80].astype(F32)[8:16]
        vec[0:8, w : w + WINDOW] += got[:, 0:WINDOW]
        vec[8:16, w : w + WINDOW] += got[:, WINDOW : 2 * WINDOW]
    spill.start("vec", vec, o_vec)

    gain_a, bias_a = vec[0:1], vec[1:2]

    def norm_rows(j, rows_of, gain, bias, unit_out, factor_out):
        @pl.loop(0, SPAN // 16, unroll=8)
        def _(t):
            r = pl.ds(pl.multiple_of(j * SPAN + t * 16, 16), 16)
            unit, factor = unit_norm(rows_of(r))
            unit_out(j, t, unit)
            factor_out[r] = jnp.broadcast_to(factor, (16, LANE))
            xa[j, pl.ds(pl.multiple_of(8 + t * 16, 8), 16)] = unit * gain + bias

    def store_a(j, t, unit):
        spb[pl.ds(pl.multiple_of(j * SPAN + t * 16, 16), 16)] = unit.astype(BF)

    def store_b(j, t, unit):
        nd[j // 2, j % 2, pl.ds(pl.multiple_of(t * 16, 16), 16)] = unit

    @pl.loop(0, SEQS)
    def _(j):
        norm_rows(j, lambda r: xp[r].astype(F32), gain_a, bias_a, store_a, factors.at[0])

    spill.start("ua", spb, o_ua)
    not_first = jnp.where(place.s > 0, 1.0, 0.0).astype(F32)
    line.shift(hx, hx_got, hsems.at[0], 1).wait_recv()
    before = (unit_norm(hx_got[...])[0] * gain_a + bias_a) * not_first
    for j in range(SEQS):
        xa[j, 0:8] = first_rows(before[j : j + 1], xa[j, SPAN : SPAN + 8])

    def blends(j, ratios, outs, spread_out):
        @pl.loop(0, SPAN // 16, unroll=4)
        def _(t):
            r = pl.ds(pl.multiple_of(j * SPAN + t * 16, 16), 16)
            prev = xa[j, pl.ds(pl.multiple_of(t * 16, 8), 16)] * spread_lanes(keep[r])
            spread = xa[j, pl.ds(pl.multiple_of(8 + t * 16, 8), 16)] - prev
            spread_out[r] = spread.astype(BF)
            for ratio, out in zip(ratios, outs):
                out[r] = (prev + spread * ratio).astype(BF)

    @pl.loop(0, SEQS)
    def _(j):
        blends(j, [vec[4:5], vec[5:6], vec[6:7]], [ki.at[0], ki.at[1], ki.at[2]], u0)

    spill.start("ki", ki, o_ki)
    spill.start("spa", u0, o_spa)
    gather.tick(5)
    relayout(st, wd, depth, 0, 48, ((0, 0), (1, 24)))
    relayout(st, wd, depth, 48, 32, ((2, 0),))
    for m in range(3):
        matmul(ki.at[m], wd.at[m], kvg.at[m])
    spill.start("kvg", kvg, o_kvg)

    shrink = jnp.exp(-vec[9:10])
    bonus = vec[10:11]
    shrink8 = jnp.broadcast_to(shrink, (SEG, WIDE))
    row = lax.broadcasted_iota(jnp.int32, (SEG, WIDE), 0)

    @pl.loop(0, SEQS)
    def _(j):
        def step(s, state):
            decay, numer, denom = state
            r = pl.ds(pl.multiple_of(j * SPAN + s * SEG, SEG), SEG)
            m = spread_lanes(keep[r]) * shrink8
            ek = jnp.exp(kvg[0, r])
            return decay * m, numer * m + ek * kvg[1, r], denom * m + ek

        zero = jnp.zeros((SEG, WIDE), F32)
        decay, numer, denom = lax.fori_loop(0, STEPS, step, (zero + 1.0, zero, zero), unroll=4)
        for d in (1, 2, 4):
            top = row < d
            numer, denom, decay = (
                numer + decay * jnp.where(top, 0.0, pltpu.roll(numer, d, axis=0)),
                denom + decay * jnp.where(top, 0.0, pltpu.roll(denom, d, axis=0)),
                decay * jnp.where(top, 1.0, pltpu.roll(decay, d, axis=0)),
            )
        states[place.s, pl.ds(j, 1)] = numer[SEG - 1 : SEG]
        states[place.s, pl.ds(SEQS + j, 1)] = denom[SEG - 1 : SEG]
        seg[j, 0] = jnp.where(row < 1, 1.0, pltpu.roll(decay, 1, axis=0))
        seg[j, 1] = jnp.where(row < 1, 0.0, pltpu.roll(numer, 1, axis=0))
        seg[j, 2] = jnp.where(row < 1, 0.0, pltpu.roll(denom, 1, axis=0))

    send_states = line.all(states, ssems)
    for copy in send_states:
        copy.start()
    gather.tick(6)
    relayout(st, wd, depth, 80, 48, ((3, 0), (4, 24)))
    spill.start("w", wd, o_w)
    for d in range(1, line.n):
        src = lax.rem(place.s + line.n - d, line.n)
        rdma(alive.at[src], alive.at[src], asems, d, line.n + d, (src, b)).wait_recv()
        rdma(states.at[src], states.at[src], ssems, d, line.n + d, (src, b)).wait_recv()
    spill.start("alive", alive, o_alive)
    whole = jnp.exp(-float(SPAN) * vec[9:10])
    arrived = jnp.zeros((SEG, WIDE), F32)
    for src in range(7):
        after = spread_lanes(alive[src]) * whole * arrived + states[src]
        arrived = jnp.where(src < place.s, after, arrived)
    carry[...] = arrived

    for j in range(SEQS):
        slot = j % 2
        if j >= 2:
            spill.wait(("nd", j - 2))
        into = nd.at[slot]
        base = j * SPAN
        numer0 = seg[j, 0] * carry[j : j + 1] + seg[j, 1]
        denom0 = seg[j, 0] * carry[SEQS + j : SEQS + j + 1] + seg[j, 2]

        def steps(i, state):
            numer, denom = state
            mixes = []
            for q in range(2):
                lo = pl.multiple_of(i * 16 + q * 8, 8)
                r = pl.ds(pl.multiple_of(base + lo, 8), SEG)
                kept = spread_lanes(keep[r])
                numer, denom = numer * kept, denom * kept
                into[0, pl.ds(lo, SEG)] = numer
                into[1, pl.ds(lo, SEG)] = denom
                k, v = kvg[0, r], kvg[1, r]
                now, ek = jnp.exp(bonus + k), jnp.exp(k)
                wkv = (numer + now * v) / (denom + now)
                mixes.append(sigmoid(kvg[2, r]) * wkv)
                numer, denom = shrink8 * numer + ek * v, shrink8 * denom + ek
            u1[pl.ds(pl.multiple_of(base + i * 16, 16), 16)] = jnp.concatenate(mixes, axis=0).astype(BF)
            return numer, denom

        lax.fori_loop(0, STEPS // 2, steps, (numer0, denom0), unroll=2)
        spill.start(("nd", j), into, o_nd.at[:, pl.ds(base, SPAN)])
    spill.start("mixed", u1, o_mixed)
    spill.wait("kvg", ("nd", 2), ("nd", 3))
    first = kvg.at[0]

    @pl.loop(0, TOK // 256, unroll=2)
    def _(i):
        r = pl.ds(pl.multiple_of(i * 256, 256), 256)
        first[r] = xp[r].astype(F32) + jnp.dot(u1[r], wd[3], preferred_element_type=F32)

    @pl.loop(0, SEQS)
    def _(j):
        norm_rows(j, lambda r: first[r], vec[2:3], vec[3:4], store_b, factors.at[1])

    for j in range(SEQS):
        spill.start(("ub", j), nd.at[j // 2, j % 2], o_ub.at[pl.ds(j * SPAN, SPAN)])
    spill.start("factors", factors, o_factors)
    spill.wait("ua")
    for j in range(SEQS):
        hb[j : j + 1] = xa[j, SPAN : SPAN + 8][7:8]
    hb[SEQS:8] = jnp.zeros((8 - SEQS, WIDE), F32)
    send_hb = line.shift(hb, hb_got, hsems.at[1], 1)
    send_hb.start()
    gather.tick(7)
    relayout(st, we, depth, 128, 48, ((0, 0), (1, 24)))
    spill.wait("ki")
    send_hb.wait_recv()
    before_b = hb_got[...] * not_first
    for j in range(SEQS):
        xa[j, 0:8] = first_rows(before_b[j : j + 1], xa[j, SPAN : SPAN + 8])

    @pl.loop(0, SEQS)
    def _(j):
        blends(j, [vec[7:8], vec[8:9]], [ki.at[0], ki.at[1]], spb)

    spill.start("spb", spb, o_spb)
    spill.start("ei", ki.at[0], o_ei)
    spill.start("si", ki.at[1], o_si)
    sig = kvg.at[1]

    @pl.loop(0, TOK // 256, unroll=2)
    def _(i):
        r = pl.ds(pl.multiple_of(i * 256, 256), 256)
        chosen = sigmoid(jnp.dot(ki[1, r], wd[4], preferred_element_type=F32))
        sig[r] = chosen
        ki[2, r] = (gyp[r].astype(F32) * chosen).astype(BF)

    spill.start("gc", ki.at[2], o_gc)
    def square(f):
        @pl.loop(0, depth, unroll=4)
        def _(i):
            r = pl.ds(pl.multiple_of(i * 256, 256), 256)
            positive = jnp.maximum(jnp.dot(ki[0, r], we[f], preferred_element_type=F32), 0.0)
            st[i, :, :, 96 + 32 * f : 128 + 32 * f] = (positive * positive).astype(BF).reshape(2, 4, 32, WIDE)

    def contract_grad(f):
        left = st[:, :, :, 96 + 32 * f : 128 + 32 * f].reshape(TOK, WIDE)
        for h in range(2):
            got = lax.dot_general(left[:, 384 * h : 384 * (h + 1)], ki[2], (((0,), (0,)), ((), ())), preferred_element_type=F32)
            st[f, h, :, 0:96] = got.astype(BF).reshape(4, 96, WIDE)

    for k in range(4):
        gather.stage(5, k)
    square(0)
    square(1)
    gather.tick(8)
    relayout(st, we, depth, 176, 48, ((2, 0), (3, 24)))
    spill.start("e", we, o_e)
    gather.stage(5, 4)
    square(2)
    square(3)
    contract_grad(0)
    contract_grad(1)
    gather.tick(9)
    contract_grad(2)
    contract_grad(3)
    spill.start("pkc", st.at[:, :, :, pl.ds(0, 96)], o_pkc)
    spill.start("sq", st.at[:, :, :, pl.ds(96, 128)], o_sq)
    spill.wait("mixed", "spa")

    gather.tick(10)
    spill.start("c", cw, o_c)

    @pl.loop(0, depth, unroll=2)
    def _(i):
        r = pl.ds(pl.multiple_of(i * 256, 256), 256)
        total = jnp.zeros((256, WIDE), F32)
        for f in range(4):
            part = st[i, :, :, 96 + 32 * f : 128 + 32 * f].reshape(256, WIDE)
            total = total + jnp.dot(part, cw[f].reshape(WIDE, WIDE), preferred_element_type=F32)
        chosen = sig[r]
        u1[r] = (first[r] + chosen * total).astype(BF)
        u0[r] = (gyp[r].astype(F32) * total * chosen * (1.0 - chosen)).astype(BF)

    spill.start("gs", u0, o_gs)
    spill.start("bo", u1, o_bo)
    for copy in send_alive + send_states + [send_hx, send_hb]:
        copy.wait_send()
    for k in range(5, COUNT):
        gather.stage(5, k)
    spill.wait()


def forward_call(x, openings, up, vec, shards, depth):
    hbm, vmem = pl.BlockSpec(memory_space=pl.ANY), pl.BlockSpec(memory_space=pltpu.VMEM)
    s = jax.ShapeDtypeStruct
    seq = depth * 2
    devices = depth * 8
    rows = (TOK, WIDE)
    outs = dict(
        w=s((5, WIDE, WIDE), BF), e=s((4, WIDE, WIDE), BF), c=s((depth, 2, 4, 96, WIDE), BF), ki=s((3,) + rows, BF),
        spa=s(rows, BF), spb=s(rows, BF), mixed=s(rows, BF), ei=s(rows, BF), si=s(rows, BF), gc=s(rows, BF), gs=s(rows, BF),
        up=s(rows, BF), sq=s((depth, 2, 4, 128, WIDE), BF), pkc=s((depth, 2, 4, 96, WIDE), BF),
        kvg=s((3,) + rows, F32), nd=s((2,) + rows, F32), ua=s(rows, BF), ub=s(rows, F32), factors=s((2, TOK, LANE), F32), keep=s((TOK, LANE), F32), vec=s((16, WIDE), F32), alive=s((seq, 8, LANE), F32),
        bo=s(rows, BF))
    scratch = [
        pltpu.VMEM((depth, 2, 4, ROWS_MAIN, WIDE), BF), pltpu.VMEM((depth, 2, 4, ROWS_LAST, WIDE), BF),
        pltpu.VMEM((5, WIDE, WIDE), BF), pltpu.VMEM((4, WIDE, WIDE), BF),
        pltpu.VMEM(rows, BF), pltpu.VMEM(rows, BF), pltpu.VMEM(rows, BF), pltpu.VMEM(rows, BF),
        pltpu.VMEM((6, SPAN, LANE), F32), pltpu.VMEM((TOK, LANE), F32), pltpu.VMEM((SEQS, SPAN + 8, WIDE), F32),
        pltpu.VMEM((3,) + rows, BF), pltpu.VMEM((3,) + rows, F32), pltpu.VMEM((2, 2, SPAN, WIDE), F32), pltpu.VMEM(rows, BF), pltpu.VMEM((2, TOK, LANE), F32),
        pltpu.VMEM((16, WIDE), F32), pltpu.VMEM((seq, 8, WIDE), F32), pltpu.VMEM((seq, 8, LANE), F32),
        pltpu.VMEM((SEQS, 3, SEG, WIDE), F32), pltpu.VMEM((8, WIDE), F32),
        pltpu.VMEM((8, WIDE), F32), pltpu.VMEM((8, WIDE), F32), pltpu.VMEM((8, WIDE), F32), pltpu.VMEM((8, WIDE), F32),
        pltpu.SemaphoreType.DMA((COUNT, 46)), pltpu.SemaphoreType.DMA((2 * seq,)),
        pltpu.SemaphoreType.DMA((2 * seq,)), pltpu.SemaphoreType.DMA((2, 2)), pltpu.SemaphoreType.DMA((32,)),
    ]
    got = pl.pallas_call(
        forward_kernel,
        out_shape=tuple(outs.values()),
        in_specs=[hbm, hbm] + [vmem] * 9,
        out_specs=tuple(hbm for _ in outs),
        scratch_shapes=scratch,
        compiler_params=pltpu.CompilerParams(collective_id=0, has_side_effects=True, vmem_limit_bytes=62 << 20),
        cost_estimate=pl.CostEstimate(flops=2 * 1024 * 12 * 768 * 768, bytes_accessed=60 << 20, transcendentals=0),
    )(x, up, openings, vec, *shards)
    return dict(zip(outs, got))


NT = (((1,), (1,)), ((), ()))
TN = (((0,), (0,)), ((), ()))


def backward_kernel(i_w, i_e, i_c, i_ki, i_spa, i_spb, i_mixed, i_ei, i_si, i_gc, i_gs, i_up, i_sq, i_pkc, i_kvg, i_nd, i_ua, i_ub, i_factors, i_keep, i_vec,
                    i_alive,
                    o_out, o_tokens, o_vec,
                    main, last, from_core, near, diag, lines, out, we, cw, p, q, xg, keep, factors, vec, alive, states, seg, vg, vr, hx, hx_got, hb, hb_got,
                    rsems, credits, ssems, hsems, zsems, lsems):
    place = Place()
    line = Line(place)
    depth = place.depth
    z, c, b = place.z, place.c, place.b
    spill = Spill(lsems)
    spill.start("cw", i_c, cw)
    enter(place)
    scatter = Scatter(place, (main, last), i_pkc, from_core, near, diag, lines, out, rsems, credits)
    run = scatter.stage
    run(0, 0)
    run(0, 1)
    spill.start("alive", i_alive, alive)
    vg[...] = jnp.zeros_like(vg)
    not_last = jnp.where(place.s < line.n - 1, 1.0, 0.0).astype(F32)

    def pack(first, second, r0):
        @pl.loop(0, depth * 2)
        def _(i):
            rows = pl.ds(pl.multiple_of(i * 96, 96), 96)
            u = first[rows].astype(F32)
            v = None if second is None else second[rows].astype(F32)
            for k in range(4):
                mine = u[24 * k : 24 * k + 24]
                other = jnp.zeros((8, WIDE), F32) if v is None else v[24 * k : 24 * k + 24]
                joined = jnp.concatenate([mine, other], axis=0)
                main[i // 2, i % 2, k, r0 : r0 + joined.shape[0]] = joined.astype(BF)

    def outer(left, right, into):
        for h in range(2):
            cols = slice(384 * h, 384 * h + 384)
            into[cols] = lax.dot_general(left[:, cols], right[...], TN, preferred_element_type=F32).astype(BF)

    def fold(v):
        return v[0:8] + v[8:16]

    def following_rows(halo):
        for j in range(SEQS):
            moved = pltpu.roll(xg[j, 0:8], SEG - 1, axis=0)
            at_end = lax.broadcasted_iota(jnp.int32, moved.shape, 0) == SEG - 1
            xg[j, SPAN : SPAN + 8] = jnp.where(at_end, halo[j : j + 1], moved)

    def send_first(src, dst, sems):
        for j in range(SEQS):
            src[j : j + 1] = xg[j, 0:8][0:1]
        src[SEQS:8] = jnp.zeros((8 - SEQS, WIDE), F32)
        copy = line.shift(src, dst, sems, -1)
        copy.start()
        return copy

    def norm_back(rows, gain, source, factor_of, gain_at, bias_at, finish, middle=None):
        def one(j):
            def tile(t, sums):
                done = []
                for u in range(4):
                    r = pl.ds(pl.multiple_of(j * SPAN + t * 64 + 16 * u, 16), 16)
                    grad = rows[r] + xg[j, pl.ds(pl.multiple_of(t * 64 + 16 * u + 8, 8), 16)]
                    unit, factor = source(r), spread_lanes(factor_of[r])
                    h = grad * gain
                    back = factor * (h - jnp.mean(h, axis=-1, keepdims=True) - unit * jnp.mean(h * unit, axis=-1, keepdims=True))
                    done.append((r, back))
                    sums = sums[0] + fold(grad * unit), sums[1] + fold(grad)
                for r, back in done:
                    finish(r, back)
                return sums

            zero = jnp.zeros((8, WIDE), F32)
            sums = lax.fori_loop(0, SPAN // 64, tile, (zero, zero))
            vg[gain_at] += sums[0]
            vg[bias_at] += sums[1]

        pl.loop(0, 2)(one)
        if middle:
            middle()
        pl.loop(2, SEQS)(one)

    def channel_mix(units, gc, sqb, ge, gt):
        ei, si, gs = units.at[0], units.at[1], units.at[2]
        load = lambda f: spill.start(("sq", f), i_sq.at[:, :, :, pl.ds(32 * f, 32)], sqb.at[f % 2])
        spill.start("gc", i_gc, gc)
        load(0)
        spill.start("pkc", i_pkc, last)
        spill.start("ei", i_ei, ei)
        spill.start("we", i_e, we)
        load(1)
        spill.start("keep", i_keep, keep)
        spill.start("vec", i_vec, vec)
        spill.start("factors", i_factors, factors)
        spill.start("si", i_si, si)
        spill.start("gs", i_gs, gs)
        spill.wait("cw", "gc")

        def expand_back(f):
            spill.wait(("sq", f))

            @pl.loop(0, TOK // 256, unroll=4)
            def _(i):
                r = pl.ds(pl.multiple_of(i * 256, 256), 256)
                grad = lax.dot_general(gc[r], cw[f].reshape(WIDE, WIDE), NT, preferred_element_type=F32)
                positive = jnp.sqrt(sqb[f % 2, i].reshape(256, WIDE).astype(F32))
                ge[r] = (2.0 * positive * grad).astype(BF)

            if f + 2 < 4:
                load(f + 2)

        def expand_in_back(f):
            @pl.loop(0, TOK // 512, unroll=2)
            def _(i):
                r = pl.ds(pl.multiple_of(i * 512, 512), 512)
                got = lax.dot_general(ge[r], we[f], NT, preferred_element_type=F32)
                p[r] = got if f == 0 else p[r] + got

        expand_back(0)
        spill.wait("ei", "we")
        outer(ei, ge, gt.at[0])
        spill.wait("pkc")
        run(1, 0)
        expand_in_back(0)
        spill.start("ws", i_w.at[4], we.at[0])
        expand_back(1)
        outer(ei, ge, gt.at[1])
        pack(gt.at[0], gt.at[1], 128)
        run(2, 0)
        run(1, 1)
        run(0, 2)
        expand_in_back(1)
        spill.start("wo", i_w.at[3], we.at[1])
        expand_back(2)
        outer(ei, ge, gt.at[0])
        expand_in_back(2)
        expand_back(3)
        outer(ei, ge, gt.at[1])
        pack(gt.at[0], gt.at[1], 176)
        run(2, 1)
        run(1, 2)
        run(0, 3)
        run(3, 0)
        expand_in_back(3)
        spill.wait("si", "gs", "ws", "wo")
        spill.start("wk", i_w.at[0], we.at[2])
        spill.start("wv", i_w.at[1], we.at[3])
        spill.start("spb", i_spb, gc)
        outer(si, gs, gt.at[1])

        @pl.loop(0, TOK // 512, unroll=2)
        def _(i):
            r = pl.ds(pl.multiple_of(i * 512, 512), 512)
            q[r] = lax.dot_general(gs[r], we[0], NT, preferred_element_type=F32)

        spill.start("wr", i_w.at[2], we.at[0])
        spill.start("gyp", i_up, ge)
        spill.start("mixed", i_mixed, ei)
        spill.wait("keep", "vec", "spb")
        re, rs = vec[7:8], vec[8:9]

        @pl.loop(0, SEQS)
        def _(j):
            def tile(t, sums):
                r = pl.ds(pl.multiple_of(j * SPAN + t * 16, 16), 16)
                ge_in, gs_in, spread = p[r], q[r], gc[r].astype(F32)
                xg[j, pl.ds(pl.multiple_of(t * 16, 16), 16)] = (ge_in * (1.0 - re) + gs_in * (1.0 - rs)) * spread_lanes(keep[r])
                p[r] = ge_in * re + gs_in * rs
                return sums[0] + fold(ge_in * spread), sums[1] + fold(gs_in * spread)

            zero = jnp.zeros((8, WIDE), F32)
            sums = lax.fori_loop(0, SPAN // 16, tile, (zero, zero), unroll=4)
            vg[7] += sums[0]
            vg[8] += sums[1]

        send = send_first(hb, hb_got, hsems.at[0])
        spill.start("ub", i_ub, q)
        spill.wait("gyp", "mixed", "ub", "factors")
        send.wait_recv()
        following_rows(hb_got[...] * not_last)

        def finish(r, back):
            grad = ge[r].astype(F32) + back
            p[r] = grad
            si[r] = grad.astype(BF)

        norm_back(p, vec[2:3], lambda r: q[r], factors.at[1], 2, 3, finish, lambda: [run(*v) for v in ((2, 2), (1, 3), (3, 1), (4, 0))])
        send.wait_send()
        outer(ei, si, gt.at[0])
        pack(gt.at[0], gt.at[1], 80)
        run(0, 4)

        spill.wait("wk", "wv", "wr")

    unit = pltpu.VMEM((TOK, WIDE), BF)

    def time_mix(gkvg, gt1):
        pl.run_scoped(functools.partial(channel_mix, gkvg), unit, pltpu.VMEM((2, depth, 2, 4, 32, WIDE), BF), unit, pltpu.VMEM((2, WIDE, WIDE), BF))
        spill.wait("alive")
        shrink = jnp.exp(-vec[9:10])
        shrink8 = jnp.broadcast_to(shrink, (SEG, WIDE))
        bonus = vec[10:11]
        row = lax.broadcasted_iota(jnp.int32, (SEG, WIDE), 0)
        zero = jnp.zeros((SEG, WIDE), F32)

        def sweeps(buf):
            def load(j, name):
                many = 4 - name
                spill.start((name, "kvg", j), i_kvg.at[pl.ds(0, many), pl.ds(j * SPAN, SPAN)], buf.at[j % 2, pl.ds(0, many)])
                spill.start((name, "nd", j), i_nd.at[:, pl.ds(j * SPAN, SPAN)], buf.at[j % 2, pl.ds(3, 2)])

            def arrive(j, name):
                spill.wait((name, "kvg", j), (name, "nd", j))

            load(0, 1)
            load(1, 1)

            @pl.loop(0, TOK // 512, unroll=2)
            def _(i):
                r = pl.ds(pl.multiple_of(i * 512, 512), 512)
                q[r] = lax.dot_general(gkvg[1, r], we[1], NT, preferred_element_type=F32)

            spill.start("ki2", i_ki.at[2], gkvg.at[0])
            for j in range(SEQS):
                arrive(j, 1)
                at = buf.at[j % 2]

                def back(i, state):
                    decay, numer, denom, bonus_sum = state
                    gates = [None, None]
                    for h in (1, 0):
                        lo = pl.multiple_of((STEPS // 2 - 1 - i) * 16 + 8 * h, 8)
                        r = pl.ds(pl.multiple_of(j * SPAN + lo, 8), SEG)
                        here = pl.ds(lo, SEG)
                        kept = spread_lanes(keep[r])
                        k, v = at[0, here], at[1, here]
                        now = jnp.exp(bonus + k)
                        inverse = 1.0 / (at[4, here] + now)
                        wkv = (at[3, here] + now * v) * inverse
                        s = sigmoid(at[2, here])
                        gm = q[r]
                        gw = gm * s
                        gates[h] = gw * wkv * (1.0 - s)
                        dn = gw * inverse
                        dd = -dn * wkv
                        q[r] = dn
                        bonus_sum = bonus_sum + now * (dn * v + dd)
                        m = kept * shrink8
                        decay, numer, denom = decay * m, numer * m + kept * dn, denom * m + kept * dd
                    rows = pl.ds(pl.multiple_of(j * SPAN + (STEPS // 2 - 1 - i) * 16, 16), 16)
                    gkvg[2, rows] = jnp.concatenate(gates, axis=0).astype(BF)
                    return decay, numer, denom, bonus_sum

                decay, numer, denom, bonus_sum = lax.fori_loop(0, STEPS // 2, back, (zero + 1.0, zero, zero, zero))
                load(j + 2, 1) if j + 2 < SEQS else load(j - 2, 2)
                vg[10] += bonus_sum
                for d in (1, 2, 4):
                    end = row >= SEG - d
                    numer, denom, decay = (
                        numer + decay * jnp.where(end, 0.0, pltpu.roll(numer, SEG - d, axis=0)),
                        denom + decay * jnp.where(end, 0.0, pltpu.roll(denom, SEG - d, axis=0)),
                        decay * jnp.where(end, 1.0, pltpu.roll(decay, SEG - d, axis=0)),
                    )
                states[place.s, j : j + 1] = numer[0:1]
                states[place.s, SEQS + j : SEQS + j + 1] = denom[0:1]
                end = row >= SEG - 1
                seg[j, 0] = jnp.where(end, 1.0, pltpu.roll(decay, SEG - 1, axis=0))
                seg[j, 1] = jnp.where(end, 0.0, pltpu.roll(numer, SEG - 1, axis=0))
                seg[j, 2] = jnp.where(end, 0.0, pltpu.roll(denom, SEG - 1, axis=0))
                if j == 1:
                    run(2, 3)
                    run(1, 4)
                    run(3, 2)
                    run(4, 1)
            sent = line.all(states, ssems)
            for copy in sent:
                copy.start()
            spill.wait("ki2")
            outer(gkvg.at[0], gkvg.at[2], gt1)
            pack(gt1, None, 48)
            run(0, 5)
            for d in range(1, line.n):
                src = lax.rem(place.s + line.n - d, line.n)
                rdma(states.at[src], states.at[src], ssems, d, line.n + d, (src, b)).wait_recv()
            run(3, 3)
            run(4, 2)
            whole = jnp.exp(-float(SPAN) * vec[9:10])
            arrived = zero
            for src in range(7, 0, -1):
                after = spread_lanes(alive[src]) * whole * arrived + states[src]
                arrived = jnp.where(src > place.s, after, arrived)
            for j in range(SEQS):
                arrive(j, 2)
                at = buf.at[j % 2]
                numer0 = seg[j, 0] * arrived[j : j + 1] + seg[j, 1]
                denom0 = seg[j, 0] * arrived[SEQS + j : SEQS + j + 1] + seg[j, 2]

                def back(i, state):
                    an, ad, decay_sum = state
                    keys, values = [None, None], [None, None]
                    for h in (1, 0):
                        lo = pl.multiple_of((STEPS // 2 - 1 - i) * 16 + 8 * h, 8)
                        r = pl.ds(pl.multiple_of(j * SPAN + lo, 8), SEG)
                        here = pl.ds(lo, SEG)
                        kept = spread_lanes(keep[r])
                        k, v, numer, denom = at[0, here], at[1, here], at[3, here], at[4, here]
                        now, ek = jnp.exp(bonus + k), jnp.exp(k)
                        wkv = (numer + now * v) / (denom + now)
                        dn = q[r]
                        dd = -dn * wkv
                        keys[h] = ek * (an * v + ad) + now * (dn * v + dd)
                        values[h] = ek * an + now * dn
                        decay_sum = decay_sum + an * numer + ad * denom
                        an, ad = kept * (dn + shrink8 * an), kept * (dd + shrink8 * ad)
                    rows = pl.ds(pl.multiple_of(j * SPAN + (STEPS // 2 - 1 - i) * 16, 16), 16)
                    gkvg[0, rows] = jnp.concatenate(keys, axis=0).astype(BF)
                    gkvg[1, rows] = jnp.concatenate(values, axis=0).astype(BF)
                    return an, ad, decay_sum

                _, _, decay_sum = lax.fori_loop(0, STEPS // 2, back, (numer0, denom0, zero))
                if j + 2 < SEQS:
                    load(j + 2, 2)
                vg[9] += -shrink * decay_sum
                if j == 1:
                    run(2, 4)
                    run(1, 5)
            for copy in sent:
                copy.wait_send()
            run(4, 3)

        pl.run_scoped(sweeps, pltpu.VMEM((2, 5, SPAN, WIDE), F32))

        def mixes(ki, spa, gt, parts):
            spill.start("ki0", i_ki.at[0], ki.at[0])
            spill.start("ki1", i_ki.at[1], ki.at[1])
            spill.start("spa", i_spa, spa)
            spill.wait("ki0")
            outer(ki.at[0], gkvg.at[0], gt.at[0])
            spill.wait("ki1")
            outer(ki.at[1], gkvg.at[1], gt.at[1])
            spill.start("ua", i_ua, ki.at[1])
            pack(gt.at[0], gt.at[1], 0)
            run(0, 6)
            run(2, 5)
            run(3, 4)
            spill.wait("spa")
            ratios = [vec[4 + m : 5 + m] for m in range(3)]
            for j in range(SEQS):
                rows = pl.ds(j * SPAN, SPAN)
                for m, w in enumerate((we.at[2], we.at[3], we.at[0])):
                    parts[m] = lax.dot_general(gkvg[m, rows], w[...], NT, preferred_element_type=F32)

                def tile(t, sums):
                    r = pl.ds(pl.multiple_of(j * SPAN + t * 16, 16), 16)
                    here = pl.ds(pl.multiple_of(t * 16, 16), 16)
                    spread = spa[r].astype(F32)
                    g = [parts[m, here] for m in range(3)]
                    shifted = g[0] * (1.0 - ratios[0]) + g[1] * (1.0 - ratios[1]) + g[2] * (1.0 - ratios[2])
                    xg[j, here] = shifted * spread_lanes(keep[r])
                    q[r] = g[0] * ratios[0] + g[1] * ratios[1] + g[2] * ratios[2]
                    return tuple(s + fold(v * spread) for s, v in zip(sums, g))

                sums = lax.fori_loop(0, SPAN // 16, tile, (zero, zero, zero), unroll=4)
                for m in range(3):
                    vg[4 + m] += sums[m]
                if j == 0:
                    run(1, 6)
                if j == 1:
                    run(3, 5)
                    run(4, 4)
                if j == 2:
                    run(2, 6)
            send = send_first(hx, hx_got, hsems.at[1])
            spill.wait("ua")
            send.wait_recv()
            following_rows(hx_got[...] * not_last)

            def finish(r, back):
                p[r] = p[r] + back

            norm_back(q, vec[0:1], lambda r: ki[1, r].astype(F32), factors.at[0], 0, 1, finish, lambda: (run(3, 6), run(4, 5)))
            send.wait_send()

        unit2 = pltpu.VMEM((2, TOK, WIDE), BF)
        pl.run_scoped(mixes, unit2, unit, pltpu.VMEM((2, WIDE, WIDE), BF), pltpu.VMEM((3, SPAN, WIDE), F32))

    pl.run_scoped(time_mix, pltpu.VMEM((3, TOK, WIDE), BF), pltpu.VMEM((WIDE, WIDE), BF))
    spill.start("tokens", p, o_tokens)
    vr[0, VECTORS:16] = jnp.zeros((16 - VECTORS, WIDE), F32)
    for i in range(VECTORS):
        vr[0, i : i + 1] = jnp.sum(vg[i], axis=0, keepdims=True)

    def exchange(src, slot, to):
        copy = rdma(vr.at[src], vr.at[slot], zsems.at[slot], 0, 1, to)
        copy.start()
        return copy

    one = exchange(0, 1, place.core)
    one.wait_recv()
    vr[2] = vr[0] + vr[1]
    two = [exchange(2, 3 + i, (place.s, other)) for i, other in enumerate((place.bx, place.by, place.bd))]
    for copy in two:
        copy.wait_recv()
    vr[6] = vr[2] + vr[3] + vr[4] + vr[5]
    four = [exchange(6, 6 + d, place.along(d)[1]) for d in range(1, depth)]
    run(4, 6)
    total = vr[6]
    for d in range(1, depth):
        four[d - 1].wait_recv()
        total = total + vr[6 + d]
    vr[6 + depth] = total
    me = place.s * 4 + place.b
    start = me * 24
    low = pl.multiple_of(jnp.minimum(start // LANE, WIDE // LANE - 2) * LANE, LANE)
    mine = vr[6 + depth, :, pl.ds(low, WINDOW)]
    o_vec[...] = pltpu.roll(mine, WINDOW - (start - low), axis=1)[:, 0:LANE]
    spill.start("out", out, o_out)
    for copy in [one] + two + four:
        copy.wait_send()
    for k in range(COUNT):
        run(5, k)
    spill.wait()


BACK_INPUTS = ("w", "e", "c", "ki", "spa", "spb", "mixed", "ei", "si", "gc", "gs", "up", "sq", "pkc", "kvg", "nd", "ua", "ub", "factors", "keep", "vec", "alive")


def backward_call(f, depth):
    hbm, vmem = pl.BlockSpec(memory_space=pl.ANY), pl.BlockSpec(memory_space=pltpu.VMEM)
    s = jax.ShapeDtypeStruct
    seq, rows = depth * 2, ROWS_MAIN + ROWS_LAST
    top = max(n for _, _, n, _ in SCATTER_CHUNKS)
    row8 = pltpu.VMEM((8, WIDE), F32)
    return pl.pallas_call(
        backward_kernel,
        out_shape=(s((rows, WIDE), F32), s((TOK, WIDE), F32), s((16, LANE), F32)),
        in_specs=[hbm] * len(BACK_INPUTS),
        out_specs=(hbm, hbm, vmem),
        scratch_shapes=[
            pltpu.VMEM((depth, 2, 4, ROWS_MAIN, WIDE), BF), pltpu.VMEM((depth, 2, 4, ROWS_LAST, WIDE), BF),
            pltpu.VMEM((2, depth, 4, top, WIDE), BF), pltpu.VMEM((2, 2, depth, top, WIDE), BF), pltpu.VMEM((2, depth, top, WIDE), BF),
            pltpu.VMEM((depth - 1, rows, WIDE), BF), pltpu.VMEM((rows, WIDE), F32),
            pltpu.VMEM((4, WIDE, WIDE), BF), pltpu.VMEM((depth, 2, 4, 96, WIDE), BF),
            pltpu.VMEM((TOK, WIDE), F32), pltpu.VMEM((TOK, WIDE), F32), pltpu.VMEM((SEQS, SPAN + 8, WIDE), F32),
            pltpu.VMEM((TOK, LANE), F32), pltpu.VMEM((2, TOK, LANE), F32), pltpu.VMEM((16, WIDE), F32), pltpu.VMEM((seq, 8, LANE), F32), pltpu.VMEM((seq, 8, WIDE), F32),
            pltpu.VMEM((SEQS, 3, SEG, WIDE), F32), pltpu.VMEM((VECTORS, 8, WIDE), F32), pltpu.VMEM((7 + depth, 16, WIDE), F32),
            row8, row8, row8, row8,
            pltpu.SemaphoreType.DMA((COUNT, 16)), pltpu.SemaphoreType.REGULAR((5,)), pltpu.SemaphoreType.DMA((2 * seq,)),
            pltpu.SemaphoreType.DMA((2, 2)), pltpu.SemaphoreType.DMA((7 + depth, 2)), pltpu.SemaphoreType.DMA((56,)),
        ],
        compiler_params=pltpu.CompilerParams(collective_id=1, has_side_effects=True, vmem_limit_bytes=62 << 20),
        cost_estimate=pl.CostEstimate(flops=2 * 1024 * 26 * 768 * 768, bytes_accessed=60 << 20, transcendentals=0),
    )(*[f[n] for n in BACK_INPUTS])


def fast_body(layer_inputs, document_openings, wk, wv, wr, wo, we, ws, wc, *rest):
    vectors, upstream = rest[:VECTORS], rest[VECTORS]
    depth = lax.axis_size("seq") // 2
    rows = [lax.pad(v.astype(F32).reshape(1, 24), jnp.float32(0), ((i, 15 - i, 0), (0, LANE - 24, 0))) for i, v in enumerate(vectors)]
    vec = sum(rows[1:], rows[0])
    got = forward_call(layer_inputs.reshape(TOK, WIDE), document_openings, upstream.reshape(TOK, WIDE), vec, (wk, wv, wr, wo, ws, we, wc), depth)
    out, tokens, small = backward_call(got, depth)

    def natural(v):
        return v.reshape(SEQS, STEPS, SEG, WIDE).transpose(0, 2, 1, 3).reshape(SEQS, SPAN, WIDE)

    expand = jnp.concatenate([out[128 + 24 * i : 152 + 24 * i] for i in range(4)], axis=1)
    return (natural(got["bo"]), natural(tokens), out[0:24], out[24:48], out[48:72], out[80:104], expand, out[104:128], out[224:320]) + tuple(
        small[i, 0:24] for i in range(VECTORS))


def from_behind(block, axis, distance):
    devices = range(lax.axis_size(axis))
    route = [(i - distance, i) for i in devices if i - distance in devices]
    return lax.ppermute(block, axis, route)


def prefix(part, axis, combine, identity, reverse):
    count = lax.axis_size(axis)
    place = lax.axis_index(axis)
    ahead = count - 1 - place if reverse else place
    gathered = jax.tree.map(lambda a: lax.all_gather(a, axis), part)
    state = jax.tree.map(lambda a, e: jnp.zeros_like(a) + jnp.asarray(e, a.dtype), part, identity)

    def one(turn, state):
        source = count - 1 - turn if reverse else turn
        return combine(
            state, jax.tree.map(lambda a: lax.dynamic_index_in_dim(a, source, 0, False), gathered)
        )

    return lax.fori_loop(0, ahead, one, state)


def layer_norm(values, gain, offset):
    center = values - jnp.mean(values, axis=-1, keepdims=True)
    factor = lax.rsqrt(jnp.mean(center * center, axis=-1, keepdims=True) + EPSILON)
    normed = center * factor
    return (normed * gain + offset, normed, factor)


def norm_back(grad_out, normed, factor, gain):
    scaled = grad_out * gain
    centered = scaled - jnp.mean(scaled, axis=-1, keepdims=True)
    grad_in = factor * (centered - normed * jnp.mean(scaled * normed, axis=-1, keepdims=True))
    return (grad_in, jnp.sum(grad_out * normed, axis=(0, 1)), jnp.sum(grad_out, axis=(0, 1)))


def product(left, right):
    return jnp.einsum("scd,de->sce", left, right, preferred_element_type=jnp.float32)


def product_back(grad, right):
    return jnp.einsum("sce,de->scd", grad, right, preferred_element_type=jnp.float32)


def outer_sum(left, grad):
    return jnp.einsum("scd,sce->de", left, grad, preferred_element_type=jnp.float32)


def attach_previous(values, arriving, persisting_indicator):
    return jnp.concatenate([arriving, values[:, :-1]], axis=1) * persisting_indicator[..., None]


def attach_next(masked, arriving):
    return jnp.concatenate([masked[:, 1:], arriving], axis=1)


def make_combine(fading_multiplier):

    def combine(earlier, later):
        early_numer, early_denom, early_length, early_cut = earlier
        late_numer, late_denom, late_length, late_cut = later
        fading = jnp.exp(-late_length * fading_multiplier) * (1.0 - late_cut)
        return (
            late_numer + fading * early_numer,
            late_denom + fading * early_denom,
            early_length + late_length,
            jnp.maximum(early_cut, late_cut),
        )

    return combine


def affine_compose(first_step, second_step):
    first_mult, first_numer, first_denom = first_step
    second_mult, second_numer, second_denom = second_step
    return (
        first_mult * second_mult,
        second_mult * first_numer + second_numer,
        second_mult * first_denom + second_denom,
    )


def forward_sweep(exponentiated_lookup, payload_table_lines, persisting_indicator, shrink):
    multiplier = persisting_indicator[..., None] * shrink
    inclusive = lax.associative_scan(
        affine_compose,
        (multiplier, exponentiated_lookup * payload_table_lines, exponentiated_lookup),
        axis=1,
    )
    zeros = jnp.zeros_like(exponentiated_lookup[:, :1])
    numer_all = (
        jnp.concatenate([zeros, inclusive[1][:, :-1]], axis=1) * persisting_indicator[..., None]
    )
    denom_all = (
        jnp.concatenate([zeros, inclusive[2][:, :-1]], axis=1) * persisting_indicator[..., None]
    )
    return (numer_all, denom_all, inclusive[1][:, -1], inclusive[2][:, -1])


def reverse_sweep(adjoint_dividend, grad_denom, persisting_indicator, shrink):
    keep_now = persisting_indicator[..., None]
    inclusive = lax.associative_scan(
        affine_compose,
        (keep_now * shrink, keep_now * adjoint_dividend, keep_now * grad_denom),
        axis=1,
        reverse=True,
    )
    zeros = jnp.zeros_like(adjoint_dividend[:, :1])
    following_dividend = jnp.concatenate([inclusive[1][:, 1:], zeros], axis=1)
    next_denom = jnp.concatenate([inclusive[2][:, 1:], zeros], axis=1)
    return (following_dividend, next_denom, inclusive[1][:, 0], inclusive[2][:, 0])


def body(
    layer_inputs,
    document_openings,
    mixing_lookup_projection,
    mixing_payload_projection,
    mixing_acceptor_projection,
    mixing_result_projection,
    feedforward_lookup_projection,
    feedforward_acceptor_projection,
    feedforward_payload_projection,
    premix_layer_scaling,
    premix_layer_offset,
    postmix_layer_scaling,
    postmix_layer_offset,
    mixing_lookup_blend,
    mixing_payload_blend,
    mixing_acceptor_blend,
    feedforward_lookup_blend,
    feedforward_acceptor_blend,
    feature_fading_speed,
    present_token_reward,
    upstream_adjoint,
):
    gathered = (
        lax.all_gather(mixing_lookup_projection, BOTH, axis=0, tiled=True),
        lax.all_gather(mixing_payload_projection, BOTH, axis=0, tiled=True),
        lax.all_gather(mixing_acceptor_projection, BOTH, axis=0, tiled=True),
        lax.all_gather(mixing_result_projection, BOTH, axis=0, tiled=True),
        lax.all_gather(feedforward_lookup_projection, BOTH, axis=0, tiled=True),
        lax.all_gather(feedforward_acceptor_projection, BOTH, axis=0, tiled=True),
        lax.all_gather(feedforward_payload_projection, BOTH, axis=0, tiled=True),
        lax.all_gather(premix_layer_scaling, BOTH, axis=0, tiled=True),
        lax.all_gather(premix_layer_offset, BOTH, axis=0, tiled=True),
        lax.all_gather(postmix_layer_scaling, BOTH, axis=0, tiled=True),
        lax.all_gather(postmix_layer_offset, BOTH, axis=0, tiled=True),
        lax.all_gather(mixing_lookup_blend, BOTH, axis=0, tiled=True),
        lax.all_gather(mixing_payload_blend, BOTH, axis=0, tiled=True),
        lax.all_gather(mixing_acceptor_blend, BOTH, axis=0, tiled=True),
        lax.all_gather(feedforward_lookup_blend, BOTH, axis=0, tiled=True),
        lax.all_gather(feedforward_acceptor_blend, BOTH, axis=0, tiled=True),
        lax.all_gather(feature_fading_speed, BOTH, axis=0, tiled=True),
        lax.all_gather(present_token_reward, BOTH, axis=0, tiled=True),
    )
    full_key, full_value, full_gate, full_output, full_expand, full_select, full_contract = (
        gathered[:7]
    )
    vectors = [stream_element.astype(jnp.float32) for stream_element in gathered[7:]]
    (
        gain_first,
        bias_first,
        gain_second,
        bias_second,
        ratio_key,
        ratio_value,
        ratio_gate,
        ratio_expand,
        ratio_select,
        fading_multiplier,
        present_reward_term,
    ) = vectors
    inputs = layer_inputs.astype(jnp.float32)
    flags = document_openings.astype(jnp.float32)
    persisting_indicator = 1.0 - flags
    sequences = layer_inputs.shape[0]
    block_len = layer_inputs.shape[1]
    width = layer_inputs.shape[2]
    normed_a, unit_a, factor_a = layer_norm(inputs, gain_first, bias_first)
    arriving_a = from_behind(normed_a[:, -1:, :], "seq", 1)
    before_a = attach_previous(normed_a, arriving_a, persisting_indicator)
    spread_a = normed_a - before_a
    key_in = (before_a + spread_a * ratio_key).astype(jnp.bfloat16)
    value_in = (before_a + spread_a * ratio_value).astype(jnp.bfloat16)
    gate_in = (before_a + spread_a * ratio_gate).astype(jnp.bfloat16)
    lookup_table_lines = product(key_in, full_key)
    payload_table_lines = product(value_in, full_value)
    gate_rows = product(gate_in, full_gate)
    shrink = jnp.exp(-fading_multiplier)
    exponentiated_lookup = jnp.exp(lookup_table_lines)
    reward_scaled_pairs = jnp.exp(present_reward_term + lookup_table_lines)
    local_numer, local_denom, end_numer, end_denom = forward_sweep(
        exponentiated_lookup, payload_table_lines, persisting_indicator, shrink
    )
    cut = jnp.max(flags, axis=1, keepdims=True)
    length = jnp.full((1,), float(block_len), jnp.float32)
    zero_state = jnp.zeros((sequences, width), jnp.float32)
    identity = (
        zero_state,
        zero_state,
        jnp.zeros((1,), jnp.float32),
        jnp.zeros((sequences, 1), jnp.float32),
    )
    combine = make_combine(fading_multiplier)
    arrived = prefix((end_numer, end_denom, length, cut), "seq", combine, identity, False)
    positions = jnp.arange(block_len, dtype=jnp.float32)
    alive = 1.0 - lax.cummax(flags, axis=1)
    rising = jnp.exp(-positions[:, None] * fading_multiplier[None, :])
    running_dividend = local_numer + alive[..., None] * rising[None] * arrived[0][:, None, :]
    running_divisor = local_denom + alive[..., None] * rising[None] * arrived[1][:, None, :]
    accumulated_sum = running_divisor + reward_scaled_pairs
    recurrent_average = (
        running_dividend + reward_scaled_pairs * payload_table_lines
    ) / accumulated_sum
    gate_sig = jax.nn.sigmoid(gate_rows)
    mixed = (gate_sig * recurrent_average).astype(jnp.bfloat16)
    first = inputs + product(mixed, full_output)
    normed_b, unit_b, factor_b = layer_norm(first, gain_second, bias_second)
    arriving_b = from_behind(normed_b[:, -1:, :], "seq", 1)
    before_b = attach_previous(normed_b, arriving_b, persisting_indicator)
    spread_b = normed_b - before_b
    expand_in = (before_b + spread_b * ratio_expand).astype(jnp.bfloat16)
    select_in = (before_b + spread_b * ratio_select).astype(jnp.bfloat16)
    expanded = product(expand_in, full_expand)
    selected = product(select_in, full_select)
    positive = jax.nn.relu(expanded)
    squared = (positive * positive).astype(jnp.bfloat16)
    contracted = product(squared, full_contract)
    select_sig = jax.nn.sigmoid(selected)
    block_out = (first + select_sig * contracted).astype(jnp.bfloat16)
    again = (
        lax.all_gather(mixing_lookup_projection, BOTH, axis=0, tiled=True),
        lax.all_gather(mixing_payload_projection, BOTH, axis=0, tiled=True),
        lax.all_gather(mixing_acceptor_projection, BOTH, axis=0, tiled=True),
        lax.all_gather(mixing_result_projection, BOTH, axis=0, tiled=True),
        lax.all_gather(feedforward_lookup_projection, BOTH, axis=0, tiled=True),
        lax.all_gather(feedforward_acceptor_projection, BOTH, axis=0, tiled=True),
        lax.all_gather(feedforward_payload_projection, BOTH, axis=0, tiled=True),
    )
    full_key, full_value, full_gate, full_output, full_expand, full_select, full_contract = again
    upstream = upstream_adjoint.astype(jnp.float32)
    grad_contracted = (upstream * select_sig).astype(jnp.bfloat16)
    grad_selected = (upstream * contracted * select_sig * (1.0 - select_sig)).astype(jnp.bfloat16)
    grad_squared = product_back(grad_contracted, full_contract)
    grad_expanded = (2.0 * positive * grad_squared).astype(jnp.bfloat16)
    contract_grad = jnp.einsum(
        "scf,scd->fd", squared, grad_contracted, preferred_element_type=jnp.float32
    )
    expand_grad = outer_sum(expand_in, grad_expanded)
    select_grad = outer_sum(select_in, grad_selected)
    grad_expand_in = product_back(grad_expanded, full_expand)
    grad_select_in = product_back(grad_selected, full_select)
    expand_ratio_grad = jnp.sum(grad_expand_in * spread_b, axis=(0, 1))
    select_ratio_grad = jnp.sum(grad_select_in * spread_b, axis=(0, 1))
    grad_before_b = (
        grad_expand_in * (1.0 - ratio_expand) + grad_select_in * (1.0 - ratio_select)
    ) * persisting_indicator[..., None]
    arriving_gb = from_behind(grad_before_b[:, :1, :], "seq", -1)
    grad_normed_b = (
        grad_expand_in * ratio_expand
        + grad_select_in * ratio_select
        + attach_next(grad_before_b, arriving_gb)
    )
    grad_from_b, chan_gain_grad, chan_bias_grad = norm_back(
        grad_normed_b, unit_b, factor_b, gain_second
    )
    grad_first = upstream + grad_from_b
    grad_attended = grad_first.astype(jnp.bfloat16)
    output_grad = outer_sum(mixed, grad_attended)
    grad_mixed = product_back(grad_attended, full_output)
    grad_gates = (grad_mixed * recurrent_average * gate_sig * (1.0 - gate_sig)).astype(jnp.bfloat16)
    grad_wkv = grad_mixed * gate_sig
    adjoint_dividend = grad_wkv / accumulated_sum
    grad_denom = -grad_wkv * recurrent_average / accumulated_sum
    following_dividend, next_denom, lead_numer, lead_denom = reverse_sweep(
        adjoint_dividend, grad_denom, persisting_indicator, shrink
    )
    behind = prefix((lead_numer, lead_denom, length, cut), "seq", combine, identity, True)
    after = jnp.concatenate([flags[:, 1:], jnp.zeros_like(flags[:, :1])], axis=1)
    later_alive = 1.0 - lax.cummax(after, axis=1, reverse=True)
    falling = jnp.exp(-(block_len - 1.0 - positions)[:, None] * fading_multiplier[None, :])
    following_dividend = (
        following_dividend + later_alive[..., None] * falling[None] * behind[0][:, None, :]
    )
    next_denom = next_denom + later_alive[..., None] * falling[None] * behind[1][:, None, :]
    immediate_term = adjoint_dividend * payload_table_lines + grad_denom
    grad_keys = (
        exponentiated_lookup * (following_dividend * payload_table_lines + next_denom)
        + reward_scaled_pairs * immediate_term
    ).astype(jnp.bfloat16)
    adjoint_payloads = (
        exponentiated_lookup * following_dividend + reward_scaled_pairs * adjoint_dividend
    ).astype(jnp.bfloat16)
    present_reward_adjoint = jnp.sum(reward_scaled_pairs * immediate_term, axis=(0, 1))
    decay_grad = -shrink * jnp.sum(
        following_dividend * running_dividend + next_denom * running_divisor, axis=(0, 1)
    )
    key_grad = outer_sum(key_in, grad_keys)
    value_grad = outer_sum(value_in, adjoint_payloads)
    gate_grad = outer_sum(gate_in, grad_gates)
    grad_key_in = product_back(grad_keys, full_key)
    grad_value_in = product_back(adjoint_payloads, full_value)
    grad_gate_in = product_back(grad_gates, full_gate)
    key_ratio_grad = jnp.sum(grad_key_in * spread_a, axis=(0, 1))
    value_ratio_grad = jnp.sum(grad_value_in * spread_a, axis=(0, 1))
    gate_ratio_grad = jnp.sum(grad_gate_in * spread_a, axis=(0, 1))
    grad_before_a = (
        grad_key_in * (1.0 - ratio_key)
        + grad_value_in * (1.0 - ratio_value)
        + grad_gate_in * (1.0 - ratio_gate)
    ) * persisting_indicator[..., None]
    arriving_ga = from_behind(grad_before_a[:, :1, :], "seq", -1)
    grad_normed_a = (
        grad_key_in * ratio_key
        + grad_value_in * ratio_value
        + grad_gate_in * ratio_gate
        + attach_next(grad_before_a, arriving_ga)
    )
    grad_from_a, attn_gain_grad, attn_bias_grad = norm_back(
        grad_normed_a, unit_a, factor_a, gain_first
    )
    tokens_grad = grad_first + grad_from_a
    shares = (
        lax.psum_scatter(key_grad, BOTH, scatter_dimension=0, tiled=True),
        lax.psum_scatter(value_grad, BOTH, scatter_dimension=0, tiled=True),
        lax.psum_scatter(gate_grad, BOTH, scatter_dimension=0, tiled=True),
        lax.psum_scatter(output_grad, BOTH, scatter_dimension=0, tiled=True),
        lax.psum_scatter(expand_grad, BOTH, scatter_dimension=0, tiled=True),
        lax.psum_scatter(select_grad, BOTH, scatter_dimension=0, tiled=True),
        lax.psum_scatter(contract_grad, BOTH, scatter_dimension=0, tiled=True),
        lax.psum_scatter(attn_gain_grad, BOTH, scatter_dimension=0, tiled=True),
        lax.psum_scatter(attn_bias_grad, BOTH, scatter_dimension=0, tiled=True),
        lax.psum_scatter(chan_gain_grad, BOTH, scatter_dimension=0, tiled=True),
        lax.psum_scatter(chan_bias_grad, BOTH, scatter_dimension=0, tiled=True),
        lax.psum_scatter(key_ratio_grad, BOTH, scatter_dimension=0, tiled=True),
        lax.psum_scatter(value_ratio_grad, BOTH, scatter_dimension=0, tiled=True),
        lax.psum_scatter(gate_ratio_grad, BOTH, scatter_dimension=0, tiled=True),
        lax.psum_scatter(expand_ratio_grad, BOTH, scatter_dimension=0, tiled=True),
        lax.psum_scatter(select_ratio_grad, BOTH, scatter_dimension=0, tiled=True),
        lax.psum_scatter(decay_grad, BOTH, scatter_dimension=0, tiled=True),
        lax.psum_scatter(present_reward_adjoint, BOTH, scatter_dimension=0, tiled=True),
    )
    return (
        block_out,
        tokens_grad,
        shares[0],
        shares[1],
        shares[2],
        shares[3],
        shares[4],
        shares[5],
        shares[6],
        shares[7],
        shares[8],
        shares[9],
        shares[10],
        shares[11],
        shares[12],
        shares[13],
        shares[14],
        shares[15],
        shares[16],
        shares[17],
    )


def solution(mesh):
    fits = mesh.shape["seq"] == 8 and mesh.shape["batch"] == 4
    return jax.shard_map(
        fast_body if fits else body,
        mesh=mesh,
        in_specs=(
            P("batch", "seq", None),
            P("batch", "seq"),
            P(BOTH, None),
            P(BOTH, None),
            P(BOTH, None),
            P(BOTH, None),
            P(BOTH, None),
            P(BOTH, None),
            P(BOTH, None),
            P(BOTH),
            P(BOTH),
            P(BOTH),
            P(BOTH),
            P(BOTH),
            P(BOTH),
            P(BOTH),
            P(BOTH),
            P(BOTH),
            P(BOTH),
            P(BOTH),
            P("batch", "seq", None),
        ),
        out_specs=(
            P("batch", "seq", None),
            P("batch", "seq", None),
            P(BOTH, None),
            P(BOTH, None),
            P(BOTH, None),
            P(BOTH, None),
            P(BOTH, None),
            P(BOTH, None),
            P(BOTH, None),
            P(BOTH),
            P(BOTH),
            P(BOTH),
            P(BOTH),
            P(BOTH),
            P(BOTH),
            P(BOTH),
            P(BOTH),
            P(BOTH),
            P(BOTH),
            P(BOTH),
        ),
        check_vma=False,
    )
```

```python
import functools

import jax
import jax.numpy as jnp
from jax import lax
from jax.experimental import pallas as pl
from jax.experimental.pallas import tpu as pltpu
from jax.sharding import PartitionSpec as P

BOTH = ("seq", "batch")
MESH = pl.DeviceIdType.MESH
BF = jnp.bfloat16
F32 = jnp.float32
WIDE = 768
ROWS_MAIN = 224
ROWS_LAST = 96
GATHER_CHUNKS = (
    (0, 48, 32, 16), (0, 0, 48, 32), (0, 80, 48, 16), (0, 128, 48, 32), (0, 176, 48, 16), (1, 0, 64, 32), (1, 64, 32, 16))
SCATTER_CHUNKS = (
    (1, 0, 48, 32), (1, 48, 48, 16), (0, 128, 48, 32), (0, 176, 48, 16), (0, 80, 48, 32), (0, 48, 32, 16), (0, 0, 48, 16))
COUNT = len(GATHER_CHUNKS)


class Place:
    def __init__(self):
        self.s = lax.axis_index("seq")
        self.b = lax.axis_index("batch")
        self.z, self.c = self.s // 2, self.s % 2
        y, x = self.b // 2, self.b % 2
        self.bx, self.by, self.bd = y * 2 + 1 - x, (1 - y) * 2 + x, (1 - y) * 2 + 1 - x
        self.depth = lax.axis_size("seq") // 2
        self.x, self.y = (self.s, self.bx), (self.s, self.by)
        self.core = (self.z * 2 + 1 - self.c, self.b)

    def along(self, step):
        z = lax.rem(self.z + step, self.depth)
        return z, (z * 2 + self.c, self.b)

    def back(self, step):
        return lax.rem(self.z + self.depth - step, self.depth)


def rdma(src, dst, sems, send, recv, to):
    return pltpu.make_async_remote_copy(
        src_ref=src, dst_ref=dst, send_sem=sems.at[send], recv_sem=sems.at[recv], device_id=to, device_id_type=MESH
    )


def enter(place):
    barrier = pltpu.get_barrier_semaphore()
    n = lax.axis_size("seq")
    peers = [place.x, place.y, (place.s, place.bd)] + [(lax.rem(place.s + d, n), place.b) for d in range(1, n)]
    for peer in peers:
        pl.semaphore_signal(barrier, inc=1, device_id=peer, device_id_type=MESH)
    pl.semaphore_wait(barrier, len(peers))


class Gather:
    def __init__(self, place, arrays, sems):
        self.p, self.arrays, self.sems = place, arrays, sems

    def stage(self, number, k):
        if not 0 <= k < COUNT:
            return
        p, sems = self.p, self.sems.at[k]
        a, r0, n, nx = GATHER_CHUNKS[k]
        ref = self.arrays[a]
        whole, part_x, part_y = pl.ds(r0, n), pl.ds(r0, nx), pl.ds(r0 + nx, n - nx)
        col = lambda c, b, rows: ref.at[:, c, b, rows]
        move = lambda view, at, to: rdma(view, view, sems, at, at + 1, to)
        one = lambda z, b: ref.at[z, p.c, b, whole]
        line = lambda d, z: move(one(z, p.b), 2 * d - 2, p.along(d)[1])
        near_x = lambda b: move(col(p.c, b, whole), 6, p.x)
        near_y = lambda b: move(col(p.c, b, whole), 8, p.y)
        diag_x = lambda b: move(col(p.c, b, part_x), 10, p.x)
        diag_y = lambda b: move(col(p.c, b, part_y), 12, p.y)
        core = lambda j, c, b: move(col(c, b, whole), 14 + 2 * j, p.core)
        single = k == 0
        steps = range(p.depth)
        lone = lambda d, z, b, c: (
            move(ref.at[z, c, b, whole], 22 + 6 * d, p.x), move(ref.at[z, c, b, whole], 24 + 6 * d, p.y),
            move(ref.at[z, c, b, whole], 26 + 6 * d, p.core))
        if number == 0:
            for d in range(1, p.depth):
                line(d, p.z).start()
            if single:
                for copy in lone(0, p.z, p.b, p.c):
                    copy.start()
        elif number == 1:
            for d in range(1, p.depth):
                line(d, p.back(d)).wait_recv()
                if single:
                    for copy in lone(d, p.back(d), p.b, p.c):
                        copy.start()
            if not single:
                near_x(p.b).start()
                near_y(p.b).start()
                core(0, p.c, p.b).start()
        elif number == 2:
            if single:
                for d in steps:
                    lone(d, p.back(d), p.bx, p.c)[0].wait_recv()
                    lone(d, p.back(d), p.by, p.c)[1].wait_recv()
            else:
                near_x(p.bx).wait_recv()
                near_y(p.by).wait_recv()
            diag_x(p.by).start()
            diag_y(p.bx).start()
            core(1, p.c, p.bx).start()
            core(2, p.c, p.by).start()
        elif number == 3:
            diag_x(p.bd).wait_recv()
            diag_y(p.bd).wait_recv()
            core(3, p.c, p.bd).start()
        elif number == 4:
            if single:
                for d in steps:
                    lone(d, p.back(d), p.b, 1 - p.c)[2].wait_recv()
            for j, b in enumerate((p.b, p.bx, p.by, p.bd)):
                if j or not single:
                    core(j, 1 - p.c, b).wait_recv()
        elif number == 5:
            for d in range(1, p.depth):
                line(d, p.z).wait_send()
            if single:
                for d in steps:
                    for copy in lone(d, p.back(d), p.b, p.c):
                        copy.wait_send()
            else:
                near_x(p.b).wait_send()
                near_y(p.b).wait_send()
                core(0, p.c, p.b).wait_send()
            diag_x(p.by).wait_send()
            diag_y(p.bx).wait_send()
            for j, b in ((1, p.bx), (2, p.by), (3, p.bd)):
                core(j, p.c, b).wait_send()

    def tick(self, t):
        for number in range(5):
            self.stage(number, t - number)


class Scatter:
    def __init__(self, place, packed, early, from_core, near, diag, line, out, sems, credits):
        self.early = early
        self.p, self.packed, self.from_core, self.near = place, packed, from_core, near
        self.diag, self.line, self.out, self.sems, self.credits = diag, line, out, sems, credits

    def stage(self, number, k):
        p, sems = self.p, self.sems.at[k]
        a, r0, n, nx = SCATTER_CHUNKS[k]
        ref, slot, depth = self.packed[a], k % 2, p.depth
        f0 = r0 if a == 0 else r0 + ROWS_MAIN
        whole, part_x, part_y = pl.ds(r0, n), pl.ds(r0, nx), pl.ds(r0 + nx, n - nx)
        whence = self.early if a == 1 else ref
        core = lambda: rdma(whence.at[:, 1 - p.c, :, whole], self.from_core.at[slot, :, :, pl.ds(0, n)], sems, 0, 1, p.core)
        diag_x = lambda: rdma(ref.at[:, p.c, p.bd, part_x], self.diag.at[slot, :, pl.ds(0, nx)], sems, 2, 3, p.x)
        diag_y = lambda: rdma(ref.at[:, p.c, p.bd, part_y], self.diag.at[slot, :, pl.ds(nx, n - nx)], sems, 4, 5, p.y)
        near_x = lambda: rdma(ref.at[:, p.c, p.bx, whole], self.near.at[slot, 0, :, pl.ds(0, n)], sems, 6, 7, p.x)
        near_y = lambda: rdma(ref.at[:, p.c, p.by, whole], self.near.at[slot, 1, :, pl.ds(0, n)], sems, 8, 9, p.y)

        def along(d):
            z, to = p.along(d)
            return rdma(ref.at[z, p.c, p.b, whole], self.line.at[d - 1, pl.ds(f0, n)], sems, 8 + 2 * d, 9 + 2 * d, to)

        def ready(*which):
            if k >= 2:
                for w in which:
                    pl.semaphore_wait(self.credits.at[w], 1)

        def free(which, to):
            if k + 2 < COUNT:
                pl.semaphore_signal(self.credits.at[which], inc=1, device_id=to, device_id_type=MESH)

        if number == 0:
            ready(0)
            core().start()
        elif number == 1:
            core().wait_recv()

            @pl.loop(0, depth * 4)
            def _(i):
                z, b = i // 4, i % 4
                ref[z, p.c, b, r0 : r0 + n] = ref[z, p.c, b, r0 : r0 + n] + self.from_core[slot, z, b, 0:n]

            free(0, p.core)
            ready(1, 2)
            diag_x().start()
            diag_y().start()
        elif number == 2:
            diag_x().wait_recv()
            diag_y().wait_recv()

            @pl.loop(0, depth)
            def _(z):
                for b, s0, m in ((p.by, 0, nx), (p.bx, nx, n - nx)):
                    ref[z, p.c, b, r0 + s0 : r0 + s0 + m] = ref[z, p.c, b, r0 + s0 : r0 + s0 + m] + self.diag[slot, z, s0 : s0 + m]

            free(1, p.x)
            free(2, p.y)
            ready(3, 4)
            near_x().start()
            near_y().start()
        elif number == 3:
            near_x().wait_recv()
            near_y().wait_recv()

            @pl.loop(0, depth)
            def _(z):
                ref[z, p.c, p.b, r0 : r0 + n] = (
                    ref[z, p.c, p.b, r0 : r0 + n].astype(F32)
                    + self.near[slot, 0, z, 0:n].astype(F32)
                    + self.near[slot, 1, z, 0:n].astype(F32)
                ).astype(BF)

            free(3, p.x)
            free(4, p.y)
            for d in range(1, depth):
                along(d).start()
        elif number == 4:
            for d in range(1, depth):
                along(d).wait_recv()
            total = ref[p.z, p.c, p.b, r0 : r0 + n].astype(F32)
            for d in range(1, depth):
                total = total + self.line[d - 1, f0 : f0 + n].astype(F32)
            self.out[f0 : f0 + n] = total
        elif number == 5:
            for each in (core, diag_x, diag_y, near_x, near_y):
                each().wait_send()
            for d in range(1, depth):
                along(d).wait_send()


EPSILON = 1e-05
TOK = 1024
SEQS = 4
SPAN = 256
STEPS = 32
SEG = 8
LANE = 128
WINDOW = 256
VECTORS = 11


def window_of(i):
    return min(i * 24 // LANE, WIDE // LANE - 2) * LANE


def spread_lanes(v):
    return jnp.concatenate([v] * (WIDE // LANE), axis=1)


def unit_norm(v):
    center = v - jnp.mean(v, axis=-1, keepdims=True)
    factor = lax.rsqrt(jnp.mean(center * center, axis=-1, keepdims=True) + EPSILON)
    return center * factor, factor


def sigmoid(v):
    return 1.0 / (1.0 + jnp.exp(-v))


def first_rows(halo_row, last_group):
    moved = pltpu.roll(last_group, 1, axis=0)
    at_top = lax.broadcasted_iota(jnp.int32, moved.shape, 0) == 0
    return jnp.where(at_top, halo_row, moved)


def permute_in(src, dst, tmp):
    @pl.loop(0, SEQS)
    def _(j):
        base = pl.multiple_of(j * SPAN, SPAN)
        for l in range(WIDE // LANE):
            tmp[l] = src[pl.ds(base, SPAN), l * LANE : (l + 1) * LANE].astype(F32)

        @pl.loop(0, STEPS // 2)
        def _(s):
            for l in range(WIDE // LANE):
                two = jnp.concatenate([tmp[l, pl.ds(2 * s, SEG, stride=STEPS), :], tmp[l, pl.ds(2 * s + 1, SEG, stride=STEPS), :]], axis=0)
                dst[pl.ds(pl.multiple_of(base + s * 16, 16), 16), l * LANE : (l + 1) * LANE] = two.astype(BF)


class Spill:
    def __init__(self, sems):
        self.sems, self.copies, self.used = sems, {}, 0

    def start(self, name, src, dst):
        self.copies[name] = pltpu.make_async_copy(src, dst, self.sems.at[self.used])
        self.used += 1
        self.copies[name].start()

    def wait(self, *names):
        for name in names or list(self.copies):
            self.copies.pop(name).wait()


class Line:
    def __init__(self, place):
        self.p = place
        self.n = lax.axis_size("seq")

    def all(self, buf, sems):
        p, copies = self.p, []
        for d in range(1, self.n):
            to = (lax.rem(p.s + d, self.n), p.b)
            copies.append(rdma(buf.at[p.s], buf.at[p.s], sems, d, self.n + d, to))
        return copies

    def shift(self, src, dst, sems, step):
        return rdma(src, dst, sems, 0, 1, (lax.rem(self.p.s + self.n + step, self.n), self.p.b))


def relayout(st, dst, depth, r0, n, targets):
    @pl.loop(0, depth * 2)
    def _(i):
        z, c = i // 2, i % 2
        slabs = [st[z, c, b, r0 : r0 + n].astype(F32) for b in range(4)]
        rows = pl.ds(pl.multiple_of(i * 96, 96), 96)
        for index, at in targets:
            dst[index, rows] = jnp.concatenate([v[at : at + 24] for v in slabs], axis=0).astype(BF)


def matmul(left, right, out, rows=512):
    @pl.loop(0, TOK // rows, unroll=2)
    def _(i):
        r = pl.ds(pl.multiple_of(i * rows, rows), rows)
        out[r] = jnp.dot(left[r], right[...], preferred_element_type=F32)


def forward_kernel(x_in, up_in, openings, vec_in, wk, wv, wr, wo, ws, we_in, wc_in,
                   o_w, o_e, o_c, o_ki, o_spa, o_spb, o_mixed, o_ei, o_si, o_gc, o_gs, o_up, o_sq, o_pkc,
                   o_kvg, o_nd, o_ua, o_ub, o_factors, o_keep, o_vec, o_alive, o_bo,
                   st, cw, wd, we, u0, xp, u1, gyp, tmp, keep, xa, ki, kvg, nd, spb, factors, vec, states, alive, seg, carry, hx, hx_got, hb, hb_got,
                   gsems, asems, ssems, hsems, lsems):
    place = Place()
    line = Line(place)
    depth = place.depth
    devices = depth * 8
    me = place.s * 4 + place.b
    spill = Spill(lsems)
    spill.start("x", x_in, u0)
    spill.start("up", up_in, u1)
    z, c, b = place.z, place.c, place.b
    as32 = lambda ref: ref[...].astype(F32)
    join = lambda *v: jnp.concatenate(v, axis=0).astype(BF)
    start = me * 24
    low = jnp.minimum(start // LANE, WIDE // LANE - 2) * LANE
    wide = pltpu.roll(jnp.concatenate([vec_in[...], jnp.zeros((16, LANE), F32)], axis=1), start - low, axis=1)
    small = jnp.concatenate([wide[0:8], wide[8:16], jnp.zeros((8, WIDE - 2 * WINDOW), F32)], axis=1)
    st[z, c, b, 48:80] = join(as32(wr), small)
    st[z, c, b, 0:48] = join(as32(wk), as32(wv))
    enter(place)
    gather = Gather(place, (st, cw), gsems)
    gather.tick(0)
    st[z, c, b, 80:128] = join(as32(wo), as32(ws))
    e = as32(we_in)
    for h in range(2):
        st[z, c, b, 128 + 48 * h : 176 + 48 * h] = join(e[:, 2 * h * WIDE : (2 * h + 1) * WIDE], e[:, (2 * h + 1) * WIDE : (2 * h + 2) * WIDE])
    cw[z, c, b] = wc_in[...]

    gather.tick(1)
    spill.wait("x")
    for j in range(SEQS):
        hx[j : j + 1] = u0[SPAN * j + SPAN - 16 : SPAN * j + SPAN].astype(F32)[15:16]
    hx[SEQS:8] = jnp.zeros((8 - SEQS, WIDE), F32)
    send_hx = line.shift(hx, hx_got, hsems.at[0], 1)
    send_hx.start()
    permute_in(u0, xp, tmp)
    gather.tick(2)
    for j in range(SEQS):
        flags = 1.0 - openings[j : j + 1].astype(F32)
        tmp[0] = jnp.broadcast_to(flags, (LANE, SPAN)).T
        for s in range(STEPS):
            keep[j * SPAN + s * SEG : j * SPAN + (s + 1) * SEG] = tmp[0, pl.ds(s, SEG, stride=STEPS), :]
    spill.start("keep", keep, o_keep)
    for j in range(SEQS):
        low_keep = jnp.min(keep[SPAN * j : SPAN * (j + 1)], axis=0, keepdims=True)
        alive[place.s, j : j + 1] = low_keep
        alive[place.s, SEQS + j : SEQS + j + 1] = low_keep
    send_alive = line.all(alive, asems)
    for copy in send_alive:
        copy.start()
    gather.tick(3)
    spill.wait("up")
    permute_in(u1, gyp, tmp)
    spill.start("gyp", gyp, o_up)
    gather.tick(4)
    vec[...] = jnp.zeros_like(vec)
    for i in range(devices):
        w = window_of(i)
        got = st[i // 8, i // 4 % 2, i % 4, 64:80].astype(F32)[8:16]
        vec[0:8, w : w + WINDOW] += got[:, 0:WINDOW]
        vec[8:16, w : w + WINDOW] += got[:, WINDOW : 2 * WINDOW]
    spill.start("vec", vec, o_vec)

    gain_a, bias_a = vec[0:1], vec[1:2]

    def norm_rows(j, rows_of, gain, bias, unit_out, factor_out):
        @pl.loop(0, SPAN // 16, unroll=8)
        def _(t):
            r = pl.ds(pl.multiple_of(j * SPAN + t * 16, 16), 16)
            unit, factor = unit_norm(rows_of(r))
            unit_out(j, t, unit)
            factor_out[r] = jnp.broadcast_to(factor, (16, LANE))
            xa[j, pl.ds(pl.multiple_of(8 + t * 16, 8), 16)] = unit * gain + bias

    def store_a(j, t, unit):
        spb[pl.ds(pl.multiple_of(j * SPAN + t * 16, 16), 16)] = unit.astype(BF)

    def store_b(j, t, unit):
        nd[j // 2, j % 2, pl.ds(pl.multiple_of(t * 16, 16), 16)] = unit

    @pl.loop(0, SEQS)
    def _(j):
        norm_rows(j, lambda r: xp[r].astype(F32), gain_a, bias_a, store_a, factors.at[0])

    spill.start("ua", spb, o_ua)
    not_first = jnp.where(place.s > 0, 1.0, 0.0).astype(F32)
    line.shift(hx, hx_got, hsems.at[0], 1).wait_recv()
    before = (unit_norm(hx_got[...])[0] * gain_a + bias_a) * not_first
    for j in range(SEQS):
        xa[j, 0:8] = first_rows(before[j : j + 1], xa[j, SPAN : SPAN + 8])

    def blends(j, ratios, outs, spread_out):
        @pl.loop(0, SPAN // 16, unroll=4)
        def _(t):
            r = pl.ds(pl.multiple_of(j * SPAN + t * 16, 16), 16)
            prev = xa[j, pl.ds(pl.multiple_of(t * 16, 8), 16)] * spread_lanes(keep[r])
            spread = xa[j, pl.ds(pl.multiple_of(8 + t * 16, 8), 16)] - prev
            spread_out[r] = spread.astype(BF)
            for ratio, out in zip(ratios, outs):
                out[r] = (prev + spread * ratio).astype(BF)

    @pl.loop(0, SEQS)
    def _(j):
        blends(j, [vec[4:5], vec[5:6], vec[6:7]], [ki.at[0], ki.at[1], ki.at[2]], u0)

    spill.start("ki", ki, o_ki)
    spill.start("spa", u0, o_spa)
    gather.tick(5)
    relayout(st, wd, depth, 0, 48, ((0, 0), (1, 24)))
    relayout(st, wd, depth, 48, 32, ((2, 0),))
    for m in range(3):
        matmul(ki.at[m], wd.at[m], kvg.at[m])
    spill.start("kvg", kvg, o_kvg)

    shrink = jnp.exp(-vec[9:10])
    bonus = vec[10:11]
    shrink8 = jnp.broadcast_to(shrink, (SEG, WIDE))
    row = lax.broadcasted_iota(jnp.int32, (SEG, WIDE), 0)

    @pl.loop(0, SEQS)
    def _(j):
        def step(s, state):
            decay, numer, denom = state
            r = pl.ds(pl.multiple_of(j * SPAN + s * SEG, SEG), SEG)
            m = spread_lanes(keep[r]) * shrink8
            ek = jnp.exp(kvg[0, r])
            return decay * m, numer * m + ek * kvg[1, r], denom * m + ek

        zero = jnp.zeros((SEG, WIDE), F32)
        decay, numer, denom = lax.fori_loop(0, STEPS, step, (zero + 1.0, zero, zero), unroll=4)
        for d in (1, 2, 4):
            top = row < d
            numer, denom, decay = (
                numer + decay * jnp.where(top, 0.0, pltpu.roll(numer, d, axis=0)),
                denom + decay * jnp.where(top, 0.0, pltpu.roll(denom, d, axis=0)),
                decay * jnp.where(top, 1.0, pltpu.roll(decay, d, axis=0)),
            )
        states[place.s, pl.ds(j, 1)] = numer[SEG - 1 : SEG]
        states[place.s, pl.ds(SEQS + j, 1)] = denom[SEG - 1 : SEG]
        seg[j, 0] = jnp.where(row < 1, 1.0, pltpu.roll(decay, 1, axis=0))
        seg[j, 1] = jnp.where(row < 1, 0.0, pltpu.roll(numer, 1, axis=0))
        seg[j, 2] = jnp.where(row < 1, 0.0, pltpu.roll(denom, 1, axis=0))

    send_states = line.all(states, ssems)
    for copy in send_states:
        copy.start()
    gather.tick(6)
    relayout(st, wd, depth, 80, 48, ((3, 0), (4, 24)))
    spill.start("w", wd, o_w)
    for d in range(1, line.n):
        src = lax.rem(place.s + line.n - d, line.n)
        rdma(alive.at[src], alive.at[src], asems, d, line.n + d, (src, b)).wait_recv()
        rdma(states.at[src], states.at[src], ssems, d, line.n + d, (src, b)).wait_recv()
    spill.start("alive", alive, o_alive)
    whole = jnp.exp(-float(SPAN) * vec[9:10])
    arrived = jnp.zeros((SEG, WIDE), F32)
    for src in range(7):
        after = spread_lanes(alive[src]) * whole * arrived + states[src]
        arrived = jnp.where(src < place.s, after, arrived)
    carry[...] = arrived

    for j in range(SEQS):
        slot = j % 2
        if j >= 2:
            spill.wait(("nd", j - 2))
        into = nd.at[slot]
        base = j * SPAN
        numer0 = seg[j, 0] * carry[j : j + 1] + seg[j, 1]
        denom0 = seg[j, 0] * carry[SEQS + j : SEQS + j + 1] + seg[j, 2]

        def steps(i, state):
            numer, denom = state
            mixes = []
            for q in range(2):
                lo = pl.multiple_of(i * 16 + q * 8, 8)
                r = pl.ds(pl.multiple_of(base + lo, 8), SEG)
                kept = spread_lanes(keep[r])
                numer, denom = numer * kept, denom * kept
                into[0, pl.ds(lo, SEG)] = numer
                into[1, pl.ds(lo, SEG)] = denom
                k, v = kvg[0, r], kvg[1, r]
                now, ek = jnp.exp(bonus + k), jnp.exp(k)
                wkv = (numer + now * v) / (denom + now)
                mixes.append(sigmoid(kvg[2, r]) * wkv)
                numer, denom = shrink8 * numer + ek * v, shrink8 * denom + ek
            u1[pl.ds(pl.multiple_of(base + i * 16, 16), 16)] = jnp.concatenate(mixes, axis=0).astype(BF)
            return numer, denom

        lax.fori_loop(0, STEPS // 2, steps, (numer0, denom0), unroll=2)
        spill.start(("nd", j), into, o_nd.at[:, pl.ds(base, SPAN)])
    spill.start("mixed", u1, o_mixed)
    spill.wait("kvg", ("nd", 2), ("nd", 3))
    first = kvg.at[0]

    @pl.loop(0, TOK // 256, unroll=2)
    def _(i):
        r = pl.ds(pl.multiple_of(i * 256, 256), 256)
        first[r] = xp[r].astype(F32) + jnp.dot(u1[r], wd[3], preferred_element_type=F32)

    @pl.loop(0, SEQS)
    def _(j):
        norm_rows(j, lambda r: first[r], vec[2:3], vec[3:4], store_b, factors.at[1])

    for j in range(SEQS):
        spill.start(("ub", j), nd.at[j // 2, j % 2], o_ub.at[pl.ds(j * SPAN, SPAN)])
    spill.start("factors", factors, o_factors)
    spill.wait("ua")
    for j in range(SEQS):
        hb[j : j + 1] = xa[j, SPAN : SPAN + 8][7:8]
    hb[SEQS:8] = jnp.zeros((8 - SEQS, WIDE), F32)
    send_hb = line.shift(hb, hb_got, hsems.at[1], 1)
    send_hb.start()
    gather.tick(7)
    relayout(st, we, depth, 128, 48, ((0, 0), (1, 24)))
    spill.wait("ki")
    send_hb.wait_recv()
    before_b = hb_got[...] * not_first
    for j in range(SEQS):
        xa[j, 0:8] = first_rows(before_b[j : j + 1], xa[j, SPAN : SPAN + 8])

    @pl.loop(0, SEQS)
    def _(j):
        blends(j, [vec[7:8], vec[8:9]], [ki.at[0], ki.at[1]], spb)

    spill.start("spb", spb, o_spb)
    spill.start("ei", ki.at[0], o_ei)
    spill.start("si", ki.at[1], o_si)
    sig = kvg.at[1]

    @pl.loop(0, TOK // 256, unroll=2)
    def _(i):
        r = pl.ds(pl.multiple_of(i * 256, 256), 256)
        chosen = sigmoid(jnp.dot(ki[1, r], wd[4], preferred_element_type=F32))
        sig[r] = chosen
        ki[2, r] = (gyp[r].astype(F32) * chosen).astype(BF)

    spill.start("gc", ki.at[2], o_gc)
    def square(f):
        @pl.loop(0, depth, unroll=4)
        def _(i):
            r = pl.ds(pl.multiple_of(i * 256, 256), 256)
            positive = jnp.maximum(jnp.dot(ki[0, r], we[f], preferred_element_type=F32), 0.0)
            st[i, :, :, 96 + 32 * f : 128 + 32 * f] = (positive * positive).astype(BF).reshape(2, 4, 32, WIDE)

    def contract_grad(f):
        left = st[:, :, :, 96 + 32 * f : 128 + 32 * f].reshape(TOK, WIDE)
        for h in range(2):
            got = lax.dot_general(left[:, 384 * h : 384 * (h + 1)], ki[2], (((0,), (0,)), ((), ())), preferred_element_type=F32)
            st[f, h, :, 0:96] = got.astype(BF).reshape(4, 96, WIDE)

    for k in range(4):
        gather.stage(5, k)
    square(0)
    square(1)
    contract_grad(0)
    contract_grad(1)
    gather.tick(8)
    relayout(st, we, depth, 176, 48, ((2, 0), (3, 24)))
    spill.start("e", we, o_e)
    gather.stage(5, 4)
    square(2)
    square(3)
    gather.tick(9)
    contract_grad(2)
    contract_grad(3)
    spill.start("pkc", st.at[:, :, :, pl.ds(0, 96)], o_pkc)
    spill.start("sq", st.at[:, :, :, pl.ds(96, 128)], o_sq)
    spill.wait("mixed", "spa")

    gather.tick(10)
    spill.start("c", cw, o_c)

    @pl.loop(0, depth, unroll=2)
    def _(i):
        r = pl.ds(pl.multiple_of(i * 256, 256), 256)
        total = jnp.zeros((256, WIDE), F32)
        for f in range(4):
            part = st[i, :, :, 96 + 32 * f : 128 + 32 * f].reshape(256, WIDE)
            total = total + jnp.dot(part, cw[f].reshape(WIDE, WIDE), preferred_element_type=F32)
        chosen = sig[r]
        u1[r] = (first[r] + chosen * total).astype(BF)
        u0[r] = (gyp[r].astype(F32) * total * chosen * (1.0 - chosen)).astype(BF)

    spill.start("gs", u0, o_gs)
    spill.start("bo", u1, o_bo)
    for copy in send_alive + send_states + [send_hx, send_hb]:
        copy.wait_send()
    for k in range(5, COUNT):
        gather.stage(5, k)
    spill.wait()


def forward_call(x, openings, up, vec, shards, depth):
    hbm, vmem = pl.BlockSpec(memory_space=pl.ANY), pl.BlockSpec(memory_space=pltpu.VMEM)
    s = jax.ShapeDtypeStruct
    seq = depth * 2
    devices = depth * 8
    rows = (TOK, WIDE)
    outs = dict(
        w=s((5, WIDE, WIDE), BF), e=s((4, WIDE, WIDE), BF), c=s((depth, 2, 4, 96, WIDE), BF), ki=s((3,) + rows, BF),
        spa=s(rows, BF), spb=s(rows, BF), mixed=s(rows, BF), ei=s(rows, BF), si=s(rows, BF), gc=s(rows, BF), gs=s(rows, BF),
        up=s(rows, BF), sq=s((depth, 2, 4, 128, WIDE), BF), pkc=s((depth, 2, 4, 96, WIDE), BF),
        kvg=s((3,) + rows, F32), nd=s((2,) + rows, F32), ua=s(rows, BF), ub=s(rows, F32), factors=s((2, TOK, LANE), F32), keep=s((TOK, LANE), F32), vec=s((16, WIDE), F32), alive=s((seq, 8, LANE), F32),
        bo=s(rows, BF))
    scratch = [
        pltpu.VMEM((depth, 2, 4, ROWS_MAIN, WIDE), BF), pltpu.VMEM((depth, 2, 4, ROWS_LAST, WIDE), BF),
        pltpu.VMEM((5, WIDE, WIDE), BF), pltpu.VMEM((4, WIDE, WIDE), BF),
        pltpu.VMEM(rows, BF), pltpu.VMEM(rows, BF), pltpu.VMEM(rows, BF), pltpu.VMEM(rows, BF),
        pltpu.VMEM((6, SPAN, LANE), F32), pltpu.VMEM((TOK, LANE), F32), pltpu.VMEM((SEQS, SPAN + 8, WIDE), F32),
        pltpu.VMEM((3,) + rows, BF), pltpu.VMEM((3,) + rows, F32), pltpu.VMEM((2, 2, SPAN, WIDE), F32), pltpu.VMEM(rows, BF), pltpu.VMEM((2, TOK, LANE), F32),
        pltpu.VMEM((16, WIDE), F32), pltpu.VMEM((seq, 8, WIDE), F32), pltpu.VMEM((seq, 8, LANE), F32),
        pltpu.VMEM((SEQS, 3, SEG, WIDE), F32), pltpu.VMEM((8, WIDE), F32),
        pltpu.VMEM((8, WIDE), F32), pltpu.VMEM((8, WIDE), F32), pltpu.VMEM((8, WIDE), F32), pltpu.VMEM((8, WIDE), F32),
        pltpu.SemaphoreType.DMA((COUNT, 46)), pltpu.SemaphoreType.DMA((2 * seq,)),
        pltpu.SemaphoreType.DMA((2 * seq,)), pltpu.SemaphoreType.DMA((2, 2)), pltpu.SemaphoreType.DMA((32,)),
    ]
    got = pl.pallas_call(
        forward_kernel,
        out_shape=tuple(outs.values()),
        in_specs=[hbm, hbm] + [vmem] * 9,
        out_specs=tuple(hbm for _ in outs),
        scratch_shapes=scratch,
        compiler_params=pltpu.CompilerParams(collective_id=0, has_side_effects=True, vmem_limit_bytes=62 << 20),
        cost_estimate=pl.CostEstimate(flops=2 * 1024 * 12 * 768 * 768, bytes_accessed=60 << 20, transcendentals=0),
    )(x, up, openings, vec, *shards)
    return dict(zip(outs, got))


NT = (((1,), (1,)), ((), ()))
TN = (((0,), (0,)), ((), ()))


def backward_kernel(i_w, i_e, i_c, i_ki, i_spa, i_spb, i_mixed, i_ei, i_si, i_gc, i_gs, i_up, i_sq, i_pkc, i_kvg, i_nd, i_ua, i_ub, i_factors, i_keep, i_vec,
                    i_alive,
                    o_out, o_tokens, o_vec,
                    main, last, from_core, near, diag, lines, out, we, cw, p, q, xg, keep, factors, vec, alive, states, seg, vg, vr, hx, hx_got, hb, hb_got,
                    rsems, credits, ssems, hsems, zsems, lsems):
    place = Place()
    line = Line(place)
    depth = place.depth
    z, c, b = place.z, place.c, place.b
    spill = Spill(lsems)
    spill.start("cw", i_c.at[0], cw.at[0])
    enter(place)
    scatter = Scatter(place, (main, last), i_pkc, from_core, near, diag, lines, out, rsems, credits)
    run = scatter.stage
    run(0, 0)
    run(0, 1)
    spill.start("alive", i_alive, alive)
    vg[...] = jnp.zeros_like(vg)
    not_last = jnp.where(place.s < line.n - 1, 1.0, 0.0).astype(F32)

    def pack(first, second, r0):
        @pl.loop(0, depth * 2)
        def _(i):
            rows = pl.ds(pl.multiple_of(i * 96, 96), 96)
            u = first[rows].astype(F32)
            v = None if second is None else second[rows].astype(F32)
            for k in range(4):
                mine = u[24 * k : 24 * k + 24]
                other = jnp.zeros((8, WIDE), F32) if v is None else v[24 * k : 24 * k + 24]
                joined = jnp.concatenate([mine, other], axis=0)
                main[i // 2, i % 2, k, r0 : r0 + joined.shape[0]] = joined.astype(BF)

    def outer(left, right, into):
        for h in range(2):
            cols = slice(384 * h, 384 * h + 384)
            into[cols] = lax.dot_general(left[:, cols], right[...], TN, preferred_element_type=F32).astype(BF)

    def fold(v):
        return v[0:8] + v[8:16]

    def following_rows(halo):
        for j in range(SEQS):
            moved = pltpu.roll(xg[j, 0:8], SEG - 1, axis=0)
            at_end = lax.broadcasted_iota(jnp.int32, moved.shape, 0) == SEG - 1
            xg[j, SPAN : SPAN + 8] = jnp.where(at_end, halo[j : j + 1], moved)

    def send_first(src, dst, sems):
        for j in range(SEQS):
            src[j : j + 1] = xg[j, 0:8][0:1]
        src[SEQS:8] = jnp.zeros((8 - SEQS, WIDE), F32)
        copy = line.shift(src, dst, sems, -1)
        copy.start()
        return copy

    def norm_back(rows, gain, source, factor_of, gain_at, bias_at, finish, middle=None):
        def one(j):
            def tile(t, sums):
                done = []
                for u in range(4):
                    r = pl.ds(pl.multiple_of(j * SPAN + t * 64 + 16 * u, 16), 16)
                    grad = rows[r] + xg[j, pl.ds(pl.multiple_of(t * 64 + 16 * u + 8, 8), 16)]
                    unit, factor = source(r), spread_lanes(factor_of[r])
                    h = grad * gain
                    back = factor * (h - jnp.mean(h, axis=-1, keepdims=True) - unit * jnp.mean(h * unit, axis=-1, keepdims=True))
                    done.append((r, back))
                    sums = sums[0] + fold(grad * unit), sums[1] + fold(grad)
                for r, back in done:
                    finish(r, back)
                return sums

            zero = jnp.zeros((8, WIDE), F32)
            sums = lax.fori_loop(0, SPAN // 64, tile, (zero, zero))
            vg[gain_at] += sums[0]
            vg[bias_at] += sums[1]

        pl.loop(0, 2)(one)
        if middle:
            middle()
        pl.loop(2, SEQS)(one)

    def channel_mix(units, gc, sqb, ge, gt):
        ei, si, gs = units.at[0], units.at[1], units.at[2]
        load = lambda f: spill.start(("sq", f), i_sq.at[:, :, :, pl.ds(32 * f, 32)], sqb.at[f % 2])
        spill.start("gc", i_gc, gc)
        load(0)
        rest = pl.ds(1, depth - 1)
        spill.start("cr", i_c.at[rest], cw.at[rest])
        spill.start("pkc", i_pkc, last)
        spill.start("ei", i_ei, ei)
        spill.start("we", i_e, we)
        load(1)
        spill.start("keep", i_keep, keep)
        spill.start("vec", i_vec, vec)
        spill.start("factors", i_factors, factors)
        spill.start("si", i_si, si)
        spill.start("gs", i_gs, gs)
        spill.wait("cw", "gc")

        def expand_back(f):
            spill.wait(("sq", f))

            @pl.loop(0, TOK // 256, unroll=4)
            def _(i):
                r = pl.ds(pl.multiple_of(i * 256, 256), 256)
                grad = lax.dot_general(gc[r], cw[f].reshape(WIDE, WIDE), NT, preferred_element_type=F32)
                positive = jnp.sqrt(sqb[f % 2, i].reshape(256, WIDE).astype(F32))
                ge[r] = (2.0 * positive * grad).astype(BF)

            if f + 2 < 4:
                load(f + 2)

        def expand_in_back(f):
            @pl.loop(0, TOK // 512, unroll=2)
            def _(i):
                r = pl.ds(pl.multiple_of(i * 512, 512), 512)
                got = lax.dot_general(ge[r], we[f], NT, preferred_element_type=F32)
                p[r] = got if f == 0 else p[r] + got

        expand_back(0)
        spill.wait("ei", "we", "cr")
        outer(ei, ge, gt.at[0])
        spill.wait("pkc")
        run(1, 0)
        expand_in_back(0)
        spill.start("ws", i_w.at[4], we.at[0])
        expand_back(1)
        outer(ei, ge, gt.at[1])
        pack(gt.at[0], gt.at[1], 128)
        run(2, 0)
        run(1, 1)
        run(0, 2)
        expand_in_back(1)
        spill.start("wo", i_w.at[3], we.at[1])
        expand_back(2)
        outer(ei, ge, gt.at[0])
        expand_in_back(2)
        expand_back(3)
        outer(ei, ge, gt.at[1])
        pack(gt.at[0], gt.at[1], 176)
        run(2, 1)
        run(1, 2)
        run(0, 3)
        run(3, 0)
        expand_in_back(3)
        spill.wait("si", "gs", "ws", "wo")
        spill.start("wk", i_w.at[0], we.at[2])
        spill.start("wv", i_w.at[1], we.at[3])
        spill.start("spb", i_spb, gc)
        outer(si, gs, gt.at[1])

        @pl.loop(0, TOK // 512, unroll=2)
        def _(i):
            r = pl.ds(pl.multiple_of(i * 512, 512), 512)
            q[r] = lax.dot_general(gs[r], we[0], NT, preferred_element_type=F32)

        spill.start("wr", i_w.at[2], we.at[0])
        spill.start("gyp", i_up, ge)
        spill.start("mixed", i_mixed, ei)
        spill.wait("keep", "vec", "spb")
        re, rs = vec[7:8], vec[8:9]

        @pl.loop(0, SEQS)
        def _(j):
            def tile(t, sums):
                r = pl.ds(pl.multiple_of(j * SPAN + t * 16, 16), 16)
                ge_in, gs_in, spread = p[r], q[r], gc[r].astype(F32)
                xg[j, pl.ds(pl.multiple_of(t * 16, 16), 16)] = (ge_in * (1.0 - re) + gs_in * (1.0 - rs)) * spread_lanes(keep[r])
                p[r] = ge_in * re + gs_in * rs
                return sums[0] + fold(ge_in * spread), sums[1] + fold(gs_in * spread)

            zero = jnp.zeros((8, WIDE), F32)
            sums = lax.fori_loop(0, SPAN // 16, tile, (zero, zero), unroll=4)
            vg[7] += sums[0]
            vg[8] += sums[1]

        send = send_first(hb, hb_got, hsems.at[0])
        spill.start("ub", i_ub, q)
        spill.wait("gyp", "mixed", "ub", "factors")
        send.wait_recv()
        following_rows(hb_got[...] * not_last)

        def finish(r, back):
            grad = ge[r].astype(F32) + back
            p[r] = grad
            si[r] = grad.astype(BF)

        norm_back(p, vec[2:3], lambda r: q[r], factors.at[1], 2, 3, finish, lambda: [run(*v) for v in ((2, 2), (1, 3), (3, 1), (4, 0))])
        send.wait_send()
        outer(ei, si, gt.at[0])
        pack(gt.at[0], gt.at[1], 80)
        run(0, 4)

        spill.wait("wk", "wv", "wr")

    unit = pltpu.VMEM((TOK, WIDE), BF)

    def time_mix(gkvg, gt1):
        pl.run_scoped(functools.partial(channel_mix, gkvg), unit, pltpu.VMEM((2, depth, 2, 4, 32, WIDE), BF), unit, pltpu.VMEM((2, WIDE, WIDE), BF))
        spill.wait("alive")
        shrink = jnp.exp(-vec[9:10])
        shrink8 = jnp.broadcast_to(shrink, (SEG, WIDE))
        bonus = vec[10:11]
        row = lax.broadcasted_iota(jnp.int32, (SEG, WIDE), 0)
        zero = jnp.zeros((SEG, WIDE), F32)

        def sweeps(buf):
            def load(j, name):
                many = 4 - name
                spill.start((name, "kvg", j), i_kvg.at[pl.ds(0, many), pl.ds(j * SPAN, SPAN)], buf.at[j % 2, pl.ds(0, many)])
                spill.start((name, "nd", j), i_nd.at[:, pl.ds(j * SPAN, SPAN)], buf.at[j % 2, pl.ds(3, 2)])

            def arrive(j, name):
                spill.wait((name, "kvg", j), (name, "nd", j))

            load(0, 1)
            load(1, 1)

            @pl.loop(0, TOK // 512, unroll=2)
            def _(i):
                r = pl.ds(pl.multiple_of(i * 512, 512), 512)
                q[r] = lax.dot_general(gkvg[1, r], we[1], NT, preferred_element_type=F32)

            spill.start("ki2", i_ki.at[2], gkvg.at[0])
            for j in range(SEQS):
                arrive(j, 1)
                at = buf.at[j % 2]

                def back(i, state):
                    decay, numer, denom, bonus_sum = state
                    gates = [None, None]
                    for h in (1, 0):
                        lo = pl.multiple_of((STEPS // 2 - 1 - i) * 16 + 8 * h, 8)
                        r = pl.ds(pl.multiple_of(j * SPAN + lo, 8), SEG)
                        here = pl.ds(lo, SEG)
                        kept = spread_lanes(keep[r])
                        k, v = at[0, here], at[1, here]
                        now = jnp.exp(bonus + k)
                        inverse = 1.0 / (at[4, here] + now)
                        wkv = (at[3, here] + now * v) * inverse
                        s = sigmoid(at[2, here])
                        gm = q[r]
                        gw = gm * s
                        gates[h] = gw * wkv * (1.0 - s)
                        dn = gw * inverse
                        dd = -dn * wkv
                        q[r] = dn
                        bonus_sum = bonus_sum + now * (dn * v + dd)
                        m = kept * shrink8
                        decay, numer, denom = decay * m, numer * m + kept * dn, denom * m + kept * dd
                    rows = pl.ds(pl.multiple_of(j * SPAN + (STEPS // 2 - 1 - i) * 16, 16), 16)
                    gkvg[2, rows] = jnp.concatenate(gates, axis=0).astype(BF)
                    return decay, numer, denom, bonus_sum

                decay, numer, denom, bonus_sum = lax.fori_loop(0, STEPS // 2, back, (zero + 1.0, zero, zero, zero))
                load(j + 2, 1) if j + 2 < SEQS else load(j - 2, 2)
                vg[10] += bonus_sum
                for d in (1, 2, 4):
                    end = row >= SEG - d
                    numer, denom, decay = (
                        numer + decay * jnp.where(end, 0.0, pltpu.roll(numer, SEG - d, axis=0)),
                        denom + decay * jnp.where(end, 0.0, pltpu.roll(denom, SEG - d, axis=0)),
                        decay * jnp.where(end, 1.0, pltpu.roll(decay, SEG - d, axis=0)),
                    )
                states[place.s, j : j + 1] = numer[0:1]
                states[place.s, SEQS + j : SEQS + j + 1] = denom[0:1]
                end = row >= SEG - 1
                seg[j, 0] = jnp.where(end, 1.0, pltpu.roll(decay, SEG - 1, axis=0))
                seg[j, 1] = jnp.where(end, 0.0, pltpu.roll(numer, SEG - 1, axis=0))
                seg[j, 2] = jnp.where(end, 0.0, pltpu.roll(denom, SEG - 1, axis=0))
                if j == 1:
                    run(2, 3)
                    run(1, 4)
                    run(3, 2)
                    run(4, 1)
            sent = line.all(states, ssems)
            for copy in sent:
                copy.start()
            spill.wait("ki2")
            outer(gkvg.at[0], gkvg.at[2], gt1)
            pack(gt1, None, 48)
            run(0, 5)
            for d in range(1, line.n):
                src = lax.rem(place.s + line.n - d, line.n)
                rdma(states.at[src], states.at[src], ssems, d, line.n + d, (src, b)).wait_recv()
            run(3, 3)
            run(4, 2)
            whole = jnp.exp(-float(SPAN) * vec[9:10])
            arrived = zero
            for src in range(7, 0, -1):
                after = spread_lanes(alive[src]) * whole * arrived + states[src]
                arrived = jnp.where(src > place.s, after, arrived)
            for j in range(SEQS):
                arrive(j, 2)
                at = buf.at[j % 2]
                numer0 = seg[j, 0] * arrived[j : j + 1] + seg[j, 1]
                denom0 = seg[j, 0] * arrived[SEQS + j : SEQS + j + 1] + seg[j, 2]

                def back(i, state):
                    an, ad, decay_sum = state
                    keys, values = [None, None], [None, None]
                    for h in (1, 0):
                        lo = pl.multiple_of((STEPS // 2 - 1 - i) * 16 + 8 * h, 8)
                        r = pl.ds(pl.multiple_of(j * SPAN + lo, 8), SEG)
                        here = pl.ds(lo, SEG)
                        kept = spread_lanes(keep[r])
                        k, v, numer, denom = at[0, here], at[1, here], at[3, here], at[4, here]
                        now, ek = jnp.exp(bonus + k), jnp.exp(k)
                        wkv = (numer + now * v) / (denom + now)
                        dn = q[r]
                        dd = -dn * wkv
                        keys[h] = ek * (an * v + ad) + now * (dn * v + dd)
                        values[h] = ek * an + now * dn
                        decay_sum = decay_sum + an * numer + ad * denom
                        an, ad = kept * (dn + shrink8 * an), kept * (dd + shrink8 * ad)
                    rows = pl.ds(pl.multiple_of(j * SPAN + (STEPS // 2 - 1 - i) * 16, 16), 16)
                    gkvg[0, rows] = jnp.concatenate(keys, axis=0).astype(BF)
                    gkvg[1, rows] = jnp.concatenate(values, axis=0).astype(BF)
                    return an, ad, decay_sum

                _, _, decay_sum = lax.fori_loop(0, STEPS // 2, back, (numer0, denom0, zero))
                if j + 2 < SEQS:
                    load(j + 2, 2)
                vg[9] += -shrink * decay_sum
                if j == 1:
                    run(2, 4)
                    run(1, 5)
            for copy in sent:
                copy.wait_send()
            run(4, 3)

        pl.run_scoped(sweeps, pltpu.VMEM((2, 5, SPAN, WIDE), F32))

        def mixes(ki, spa, gt, parts):
            spill.start("ki0", i_ki.at[0], ki.at[0])
            spill.start("ki1", i_ki.at[1], ki.at[1])
            spill.start("spa", i_spa, spa)
            spill.wait("ki0")
            outer(ki.at[0], gkvg.at[0], gt.at[0])
            spill.wait("ki1")
            outer(ki.at[1], gkvg.at[1], gt.at[1])
            spill.start("ua", i_ua, ki.at[1])
            pack(gt.at[0], gt.at[1], 0)
            run(0, 6)
            run(2, 5)
            run(3, 4)
            spill.wait("spa")
            ratios = [vec[4 + m : 5 + m] for m in range(3)]
            for j in range(SEQS):
                rows = pl.ds(j * SPAN, SPAN)
                for m, w in enumerate((we.at[2], we.at[3], we.at[0])):
                    parts[m] = lax.dot_general(gkvg[m, rows], w[...], NT, preferred_element_type=F32)

                def tile(t, sums):
                    r = pl.ds(pl.multiple_of(j * SPAN + t * 16, 16), 16)
                    here = pl.ds(pl.multiple_of(t * 16, 16), 16)
                    spread = spa[r].astype(F32)
                    g = [parts[m, here] for m in range(3)]
                    shifted = g[0] * (1.0 - ratios[0]) + g[1] * (1.0 - ratios[1]) + g[2] * (1.0 - ratios[2])
                    xg[j, here] = shifted * spread_lanes(keep[r])
                    q[r] = g[0] * ratios[0] + g[1] * ratios[1] + g[2] * ratios[2]
                    return tuple(s + fold(v * spread) for s, v in zip(sums, g))

                sums = lax.fori_loop(0, SPAN // 16, tile, (zero, zero, zero), unroll=4)
                for m in range(3):
                    vg[4 + m] += sums[m]
                if j == 0:
                    run(1, 6)
                if j == 1:
                    run(3, 5)
                    run(4, 4)
                if j == 2:
                    run(2, 6)
            send = send_first(hx, hx_got, hsems.at[1])
            spill.wait("ua")
            send.wait_recv()
            following_rows(hx_got[...] * not_last)

            def finish(r, back):
                p[r] = p[r] + back

            norm_back(q, vec[0:1], lambda r: ki[1, r].astype(F32), factors.at[0], 0, 1, finish, lambda: (run(3, 6), run(4, 5)))
            send.wait_send()

        unit2 = pltpu.VMEM((2, TOK, WIDE), BF)
        pl.run_scoped(mixes, unit2, unit, pltpu.VMEM((2, WIDE, WIDE), BF), pltpu.VMEM((3, SPAN, WIDE), F32))

    pl.run_scoped(time_mix, pltpu.VMEM((3, TOK, WIDE), BF), pltpu.VMEM((WIDE, WIDE), BF))
    spill.start("tokens", p, o_tokens)
    vr[0, VECTORS:16] = jnp.zeros((16 - VECTORS, WIDE), F32)
    for i in range(VECTORS):
        vr[0, i : i + 1] = jnp.sum(vg[i], axis=0, keepdims=True)

    def exchange(src, slot, to):
        copy = rdma(vr.at[src], vr.at[slot], zsems.at[slot], 0, 1, to)
        copy.start()
        return copy

    one = exchange(0, 1, place.core)
    one.wait_recv()
    vr[2] = vr[0] + vr[1]
    two = [exchange(2, 3 + i, (place.s, other)) for i, other in enumerate((place.bx, place.by, place.bd))]
    for copy in two:
        copy.wait_recv()
    vr[6] = vr[2] + vr[3] + vr[4] + vr[5]
    four = [exchange(6, 6 + d, place.along(d)[1]) for d in range(1, depth)]
    run(4, 6)
    total = vr[6]
    for d in range(1, depth):
        four[d - 1].wait_recv()
        total = total + vr[6 + d]
    vr[6 + depth] = total
    me = place.s * 4 + place.b
    start = me * 24
    low = pl.multiple_of(jnp.minimum(start // LANE, WIDE // LANE - 2) * LANE, LANE)
    mine = vr[6 + depth, :, pl.ds(low, WINDOW)]
    o_vec[...] = pltpu.roll(mine, WINDOW - (start - low), axis=1)[:, 0:LANE]
    spill.start("out", out, o_out)
    for copy in [one] + two + four:
        copy.wait_send()
    for k in range(COUNT):
        run(5, k)
    spill.wait()


BACK_INPUTS = ("w", "e", "c", "ki", "spa", "spb", "mixed", "ei", "si", "gc", "gs", "up", "sq", "pkc", "kvg", "nd", "ua", "ub", "factors", "keep", "vec", "alive")


def backward_call(f, depth):
    hbm, vmem = pl.BlockSpec(memory_space=pl.ANY), pl.BlockSpec(memory_space=pltpu.VMEM)
    s = jax.ShapeDtypeStruct
    seq, rows = depth * 2, ROWS_MAIN + ROWS_LAST
    top = max(n for _, _, n, _ in SCATTER_CHUNKS)
    row8 = pltpu.VMEM((8, WIDE), F32)
    return pl.pallas_call(
        backward_kernel,
        out_shape=(s((rows, WIDE), F32), s((TOK, WIDE), F32), s((16, LANE), F32)),
        in_specs=[hbm] * len(BACK_INPUTS),
        out_specs=(hbm, hbm, vmem),
        scratch_shapes=[
            pltpu.VMEM((depth, 2, 4, ROWS_MAIN, WIDE), BF), pltpu.VMEM((depth, 2, 4, ROWS_LAST, WIDE), BF),
            pltpu.VMEM((2, depth, 4, top, WIDE), BF), pltpu.VMEM((2, 2, depth, top, WIDE), BF), pltpu.VMEM((2, depth, top, WIDE), BF),
            pltpu.VMEM((depth - 1, rows, WIDE), BF), pltpu.VMEM((rows, WIDE), F32),
            pltpu.VMEM((4, WIDE, WIDE), BF), pltpu.VMEM((depth, 2, 4, 96, WIDE), BF),
            pltpu.VMEM((TOK, WIDE), F32), pltpu.VMEM((TOK, WIDE), F32), pltpu.VMEM((SEQS, SPAN + 8, WIDE), F32),
            pltpu.VMEM((TOK, LANE), F32), pltpu.VMEM((2, TOK, LANE), F32), pltpu.VMEM((16, WIDE), F32), pltpu.VMEM((seq, 8, LANE), F32), pltpu.VMEM((seq, 8, WIDE), F32),
            pltpu.VMEM((SEQS, 3, SEG, WIDE), F32), pltpu.VMEM((VECTORS, 8, WIDE), F32), pltpu.VMEM((7 + depth, 16, WIDE), F32),
            row8, row8, row8, row8,
            pltpu.SemaphoreType.DMA((COUNT, 16)), pltpu.SemaphoreType.REGULAR((5,)), pltpu.SemaphoreType.DMA((2 * seq,)),
            pltpu.SemaphoreType.DMA((2, 2)), pltpu.SemaphoreType.DMA((7 + depth, 2)), pltpu.SemaphoreType.DMA((56,)),
        ],
        compiler_params=pltpu.CompilerParams(collective_id=1, has_side_effects=True, vmem_limit_bytes=62 << 20),
        cost_estimate=pl.CostEstimate(flops=2 * 1024 * 26 * 768 * 768, bytes_accessed=60 << 20, transcendentals=0),
    )(*[f[n] for n in BACK_INPUTS])


def fast_body(layer_inputs, document_openings, wk, wv, wr, wo, we, ws, wc, *rest):
    vectors, upstream = rest[:VECTORS], rest[VECTORS]
    depth = lax.axis_size("seq") // 2
    rows = [lax.pad(v.astype(F32).reshape(1, 24), jnp.float32(0), ((i, 15 - i, 0), (0, LANE - 24, 0))) for i, v in enumerate(vectors)]
    vec = sum(rows[1:], rows[0])
    got = forward_call(layer_inputs.reshape(TOK, WIDE), document_openings, upstream.reshape(TOK, WIDE), vec, (wk, wv, wr, wo, ws, we, wc), depth)
    out, tokens, small = backward_call(got, depth)

    def natural(v):
        return v.reshape(SEQS, STEPS, SEG, WIDE).transpose(0, 2, 1, 3).reshape(SEQS, SPAN, WIDE)

    expand = jnp.concatenate([out[128 + 24 * i : 152 + 24 * i] for i in range(4)], axis=1)
    return (natural(got["bo"]), natural(tokens), out[0:24], out[24:48], out[48:72], out[80:104], expand, out[104:128], out[224:320]) + tuple(
        small[i, 0:24] for i in range(VECTORS))


def from_behind(block, axis, distance):
    devices = range(lax.axis_size(axis))
    route = [(i - distance, i) for i in devices if i - distance in devices]
    return lax.ppermute(block, axis, route)


def prefix(part, axis, combine, identity, reverse):
    count = lax.axis_size(axis)
    place = lax.axis_index(axis)
    ahead = count - 1 - place if reverse else place
    gathered = jax.tree.map(lambda a: lax.all_gather(a, axis), part)
    state = jax.tree.map(lambda a, e: jnp.zeros_like(a) + jnp.asarray(e, a.dtype), part, identity)

    def one(turn, state):
        source = count - 1 - turn if reverse else turn
        return combine(
            state, jax.tree.map(lambda a: lax.dynamic_index_in_dim(a, source, 0, False), gathered)
        )

    return lax.fori_loop(0, ahead, one, state)


def layer_norm(values, gain, offset):
    center = values - jnp.mean(values, axis=-1, keepdims=True)
    factor = lax.rsqrt(jnp.mean(center * center, axis=-1, keepdims=True) + EPSILON)
    normed = center * factor
    return (normed * gain + offset, normed, factor)


def norm_back(grad_out, normed, factor, gain):
    scaled = grad_out * gain
    centered = scaled - jnp.mean(scaled, axis=-1, keepdims=True)
    grad_in = factor * (centered - normed * jnp.mean(scaled * normed, axis=-1, keepdims=True))
    return (grad_in, jnp.sum(grad_out * normed, axis=(0, 1)), jnp.sum(grad_out, axis=(0, 1)))


def product(left, right):
    return jnp.einsum("scd,de->sce", left, right, preferred_element_type=jnp.float32)


def product_back(grad, right):
    return jnp.einsum("sce,de->scd", grad, right, preferred_element_type=jnp.float32)


def outer_sum(left, grad):
    return jnp.einsum("scd,sce->de", left, grad, preferred_element_type=jnp.float32)


def attach_previous(values, arriving, persisting_indicator):
    return jnp.concatenate([arriving, values[:, :-1]], axis=1) * persisting_indicator[..., None]


def attach_next(masked, arriving):
    return jnp.concatenate([masked[:, 1:], arriving], axis=1)


def make_combine(fading_multiplier):

    def combine(earlier, later):
        early_numer, early_denom, early_length, early_cut = earlier
        late_numer, late_denom, late_length, late_cut = later
        fading = jnp.exp(-late_length * fading_multiplier) * (1.0 - late_cut)
        return (
            late_numer + fading * early_numer,
            late_denom + fading * early_denom,
            early_length + late_length,
            jnp.maximum(early_cut, late_cut),
        )

    return combine


def affine_compose(first_step, second_step):
    first_mult, first_numer, first_denom = first_step
    second_mult, second_numer, second_denom = second_step
    return (
        first_mult * second_mult,
        second_mult * first_numer + second_numer,
        second_mult * first_denom + second_denom,
    )


def forward_sweep(exponentiated_lookup, payload_table_lines, persisting_indicator, shrink):
    multiplier = persisting_indicator[..., None] * shrink
    inclusive = lax.associative_scan(
        affine_compose,
        (multiplier, exponentiated_lookup * payload_table_lines, exponentiated_lookup),
        axis=1,
    )
    zeros = jnp.zeros_like(exponentiated_lookup[:, :1])
    numer_all = (
        jnp.concatenate([zeros, inclusive[1][:, :-1]], axis=1) * persisting_indicator[..., None]
    )
    denom_all = (
        jnp.concatenate([zeros, inclusive[2][:, :-1]], axis=1) * persisting_indicator[..., None]
    )
    return (numer_all, denom_all, inclusive[1][:, -1], inclusive[2][:, -1])


def reverse_sweep(adjoint_dividend, grad_denom, persisting_indicator, shrink):
    keep_now = persisting_indicator[..., None]
    inclusive = lax.associative_scan(
        affine_compose,
        (keep_now * shrink, keep_now * adjoint_dividend, keep_now * grad_denom),
        axis=1,
        reverse=True,
    )
    zeros = jnp.zeros_like(adjoint_dividend[:, :1])
    following_dividend = jnp.concatenate([inclusive[1][:, 1:], zeros], axis=1)
    next_denom = jnp.concatenate([inclusive[2][:, 1:], zeros], axis=1)
    return (following_dividend, next_denom, inclusive[1][:, 0], inclusive[2][:, 0])


def body(
    layer_inputs,
    document_openings,
    mixing_lookup_projection,
    mixing_payload_projection,
    mixing_acceptor_projection,
    mixing_result_projection,
    feedforward_lookup_projection,
    feedforward_acceptor_projection,
    feedforward_payload_projection,
    premix_layer_scaling,
    premix_layer_offset,
    postmix_layer_scaling,
    postmix_layer_offset,
    mixing_lookup_blend,
    mixing_payload_blend,
    mixing_acceptor_blend,
    feedforward_lookup_blend,
    feedforward_acceptor_blend,
    feature_fading_speed,
    present_token_reward,
    upstream_adjoint,
):
    gathered = (
        lax.all_gather(mixing_lookup_projection, BOTH, axis=0, tiled=True),
        lax.all_gather(mixing_payload_projection, BOTH, axis=0, tiled=True),
        lax.all_gather(mixing_acceptor_projection, BOTH, axis=0, tiled=True),
        lax.all_gather(mixing_result_projection, BOTH, axis=0, tiled=True),
        lax.all_gather(feedforward_lookup_projection, BOTH, axis=0, tiled=True),
        lax.all_gather(feedforward_acceptor_projection, BOTH, axis=0, tiled=True),
        lax.all_gather(feedforward_payload_projection, BOTH, axis=0, tiled=True),
        lax.all_gather(premix_layer_scaling, BOTH, axis=0, tiled=True),
        lax.all_gather(premix_layer_offset, BOTH, axis=0, tiled=True),
        lax.all_gather(postmix_layer_scaling, BOTH, axis=0, tiled=True),
        lax.all_gather(postmix_layer_offset, BOTH, axis=0, tiled=True),
        lax.all_gather(mixing_lookup_blend, BOTH, axis=0, tiled=True),
        lax.all_gather(mixing_payload_blend, BOTH, axis=0, tiled=True),
        lax.all_gather(mixing_acceptor_blend, BOTH, axis=0, tiled=True),
        lax.all_gather(feedforward_lookup_blend, BOTH, axis=0, tiled=True),
        lax.all_gather(feedforward_acceptor_blend, BOTH, axis=0, tiled=True),
        lax.all_gather(feature_fading_speed, BOTH, axis=0, tiled=True),
        lax.all_gather(present_token_reward, BOTH, axis=0, tiled=True),
    )
    full_key, full_value, full_gate, full_output, full_expand, full_select, full_contract = (
        gathered[:7]
    )
    vectors = [stream_element.astype(jnp.float32) for stream_element in gathered[7:]]
    (
        gain_first,
        bias_first,
        gain_second,
        bias_second,
        ratio_key,
        ratio_value,
        ratio_gate,
        ratio_expand,
        ratio_select,
        fading_multiplier,
        present_reward_term,
    ) = vectors
    inputs = layer_inputs.astype(jnp.float32)
    flags = document_openings.astype(jnp.float32)
    persisting_indicator = 1.0 - flags
    sequences = layer_inputs.shape[0]
    block_len = layer_inputs.shape[1]
    width = layer_inputs.shape[2]
    normed_a, unit_a, factor_a = layer_norm(inputs, gain_first, bias_first)
    arriving_a = from_behind(normed_a[:, -1:, :], "seq", 1)
    before_a = attach_previous(normed_a, arriving_a, persisting_indicator)
    spread_a = normed_a - before_a
    key_in = (before_a + spread_a * ratio_key).astype(jnp.bfloat16)
    value_in = (before_a + spread_a * ratio_value).astype(jnp.bfloat16)
    gate_in = (before_a + spread_a * ratio_gate).astype(jnp.bfloat16)
    lookup_table_lines = product(key_in, full_key)
    payload_table_lines = product(value_in, full_value)
    gate_rows = product(gate_in, full_gate)
    shrink = jnp.exp(-fading_multiplier)
    exponentiated_lookup = jnp.exp(lookup_table_lines)
    reward_scaled_pairs = jnp.exp(present_reward_term + lookup_table_lines)
    local_numer, local_denom, end_numer, end_denom = forward_sweep(
        exponentiated_lookup, payload_table_lines, persisting_indicator, shrink
    )
    cut = jnp.max(flags, axis=1, keepdims=True)
    length = jnp.full((1,), float(block_len), jnp.float32)
    zero_state = jnp.zeros((sequences, width), jnp.float32)
    identity = (
        zero_state,
        zero_state,
        jnp.zeros((1,), jnp.float32),
        jnp.zeros((sequences, 1), jnp.float32),
    )
    combine = make_combine(fading_multiplier)
    arrived = prefix((end_numer, end_denom, length, cut), "seq", combine, identity, False)
    positions = jnp.arange(block_len, dtype=jnp.float32)
    alive = 1.0 - lax.cummax(flags, axis=1)
    rising = jnp.exp(-positions[:, None] * fading_multiplier[None, :])
    running_dividend = local_numer + alive[..., None] * rising[None] * arrived[0][:, None, :]
    running_divisor = local_denom + alive[..., None] * rising[None] * arrived[1][:, None, :]
    accumulated_sum = running_divisor + reward_scaled_pairs
    recurrent_average = (
        running_dividend + reward_scaled_pairs * payload_table_lines
    ) / accumulated_sum
    gate_sig = jax.nn.sigmoid(gate_rows)
    mixed = (gate_sig * recurrent_average).astype(jnp.bfloat16)
    first = inputs + product(mixed, full_output)
    normed_b, unit_b, factor_b = layer_norm(first, gain_second, bias_second)
    arriving_b = from_behind(normed_b[:, -1:, :], "seq", 1)
    before_b = attach_previous(normed_b, arriving_b, persisting_indicator)
    spread_b = normed_b - before_b
    expand_in = (before_b + spread_b * ratio_expand).astype(jnp.bfloat16)
    select_in = (before_b + spread_b * ratio_select).astype(jnp.bfloat16)
    expanded = product(expand_in, full_expand)
    selected = product(select_in, full_select)
    positive = jax.nn.relu(expanded)
    squared = (positive * positive).astype(jnp.bfloat16)
    contracted = product(squared, full_contract)
    select_sig = jax.nn.sigmoid(selected)
    block_out = (first + select_sig * contracted).astype(jnp.bfloat16)
    again = (
        lax.all_gather(mixing_lookup_projection, BOTH, axis=0, tiled=True),
        lax.all_gather(mixing_payload_projection, BOTH, axis=0, tiled=True),
        lax.all_gather(mixing_acceptor_projection, BOTH, axis=0, tiled=True),
        lax.all_gather(mixing_result_projection, BOTH, axis=0, tiled=True),
        lax.all_gather(feedforward_lookup_projection, BOTH, axis=0, tiled=True),
        lax.all_gather(feedforward_acceptor_projection, BOTH, axis=0, tiled=True),
        lax.all_gather(feedforward_payload_projection, BOTH, axis=0, tiled=True),
    )
    full_key, full_value, full_gate, full_output, full_expand, full_select, full_contract = again
    upstream = upstream_adjoint.astype(jnp.float32)
    grad_contracted = (upstream * select_sig).astype(jnp.bfloat16)
    grad_selected = (upstream * contracted * select_sig * (1.0 - select_sig)).astype(jnp.bfloat16)
    grad_squared = product_back(grad_contracted, full_contract)
    grad_expanded = (2.0 * positive * grad_squared).astype(jnp.bfloat16)
    contract_grad = jnp.einsum(
        "scf,scd->fd", squared, grad_contracted, preferred_element_type=jnp.float32
    )
    expand_grad = outer_sum(expand_in, grad_expanded)
    select_grad = outer_sum(select_in, grad_selected)
    grad_expand_in = product_back(grad_expanded, full_expand)
    grad_select_in = product_back(grad_selected, full_select)
    expand_ratio_grad = jnp.sum(grad_expand_in * spread_b, axis=(0, 1))
    select_ratio_grad = jnp.sum(grad_select_in * spread_b, axis=(0, 1))
    grad_before_b = (
        grad_expand_in * (1.0 - ratio_expand) + grad_select_in * (1.0 - ratio_select)
    ) * persisting_indicator[..., None]
    arriving_gb = from_behind(grad_before_b[:, :1, :], "seq", -1)
    grad_normed_b = (
        grad_expand_in * ratio_expand
        + grad_select_in * ratio_select
        + attach_next(grad_before_b, arriving_gb)
    )
    grad_from_b, chan_gain_grad, chan_bias_grad = norm_back(
        grad_normed_b, unit_b, factor_b, gain_second
    )
    grad_first = upstream + grad_from_b
    grad_attended = grad_first.astype(jnp.bfloat16)
    output_grad = outer_sum(mixed, grad_attended)
    grad_mixed = product_back(grad_attended, full_output)
    grad_gates = (grad_mixed * recurrent_average * gate_sig * (1.0 - gate_sig)).astype(jnp.bfloat16)
    grad_wkv = grad_mixed * gate_sig
    adjoint_dividend = grad_wkv / accumulated_sum
    grad_denom = -grad_wkv * recurrent_average / accumulated_sum
    following_dividend, next_denom, lead_numer, lead_denom = reverse_sweep(
        adjoint_dividend, grad_denom, persisting_indicator, shrink
    )
    behind = prefix((lead_numer, lead_denom, length, cut), "seq", combine, identity, True)
    after = jnp.concatenate([flags[:, 1:], jnp.zeros_like(flags[:, :1])], axis=1)
    later_alive = 1.0 - lax.cummax(after, axis=1, reverse=True)
    falling = jnp.exp(-(block_len - 1.0 - positions)[:, None] * fading_multiplier[None, :])
    following_dividend = (
        following_dividend + later_alive[..., None] * falling[None] * behind[0][:, None, :]
    )
    next_denom = next_denom + later_alive[..., None] * falling[None] * behind[1][:, None, :]
    immediate_term = adjoint_dividend * payload_table_lines + grad_denom
    grad_keys = (
        exponentiated_lookup * (following_dividend * payload_table_lines + next_denom)
        + reward_scaled_pairs * immediate_term
    ).astype(jnp.bfloat16)
    adjoint_payloads = (
        exponentiated_lookup * following_dividend + reward_scaled_pairs * adjoint_dividend
    ).astype(jnp.bfloat16)
    present_reward_adjoint = jnp.sum(reward_scaled_pairs * immediate_term, axis=(0, 1))
    decay_grad = -shrink * jnp.sum(
        following_dividend * running_dividend + next_denom * running_divisor, axis=(0, 1)
    )
    key_grad = outer_sum(key_in, grad_keys)
    value_grad = outer_sum(value_in, adjoint_payloads)
    gate_grad = outer_sum(gate_in, grad_gates)
    grad_key_in = product_back(grad_keys, full_key)
    grad_value_in = product_back(adjoint_payloads, full_value)
    grad_gate_in = product_back(grad_gates, full_gate)
    key_ratio_grad = jnp.sum(grad_key_in * spread_a, axis=(0, 1))
    value_ratio_grad = jnp.sum(grad_value_in * spread_a, axis=(0, 1))
    gate_ratio_grad = jnp.sum(grad_gate_in * spread_a, axis=(0, 1))
    grad_before_a = (
        grad_key_in * (1.0 - ratio_key)
        + grad_value_in * (1.0 - ratio_value)
        + grad_gate_in * (1.0 - ratio_gate)
    ) * persisting_indicator[..., None]
    arriving_ga = from_behind(grad_before_a[:, :1, :], "seq", -1)
    grad_normed_a = (
        grad_key_in * ratio_key
        + grad_value_in * ratio_value
        + grad_gate_in * ratio_gate
        + attach_next(grad_before_a, arriving_ga)
    )
    grad_from_a, attn_gain_grad, attn_bias_grad = norm_back(
        grad_normed_a, unit_a, factor_a, gain_first
    )
    tokens_grad = grad_first + grad_from_a
    shares = (
        lax.psum_scatter(key_grad, BOTH, scatter_dimension=0, tiled=True),
        lax.psum_scatter(value_grad, BOTH, scatter_dimension=0, tiled=True),
        lax.psum_scatter(gate_grad, BOTH, scatter_dimension=0, tiled=True),
        lax.psum_scatter(output_grad, BOTH, scatter_dimension=0, tiled=True),
        lax.psum_scatter(expand_grad, BOTH, scatter_dimension=0, tiled=True),
        lax.psum_scatter(select_grad, BOTH, scatter_dimension=0, tiled=True),
        lax.psum_scatter(contract_grad, BOTH, scatter_dimension=0, tiled=True),
        lax.psum_scatter(attn_gain_grad, BOTH, scatter_dimension=0, tiled=True),
        lax.psum_scatter(attn_bias_grad, BOTH, scatter_dimension=0, tiled=True),
        lax.psum_scatter(chan_gain_grad, BOTH, scatter_dimension=0, tiled=True),
        lax.psum_scatter(chan_bias_grad, BOTH, scatter_dimension=0, tiled=True),
        lax.psum_scatter(key_ratio_grad, BOTH, scatter_dimension=0, tiled=True),
        lax.psum_scatter(value_ratio_grad, BOTH, scatter_dimension=0, tiled=True),
        lax.psum_scatter(gate_ratio_grad, BOTH, scatter_dimension=0, tiled=True),
        lax.psum_scatter(expand_ratio_grad, BOTH, scatter_dimension=0, tiled=True),
        lax.psum_scatter(select_ratio_grad, BOTH, scatter_dimension=0, tiled=True),
        lax.psum_scatter(decay_grad, BOTH, scatter_dimension=0, tiled=True),
        lax.psum_scatter(present_reward_adjoint, BOTH, scatter_dimension=0, tiled=True),
    )
    return (
        block_out,
        tokens_grad,
        shares[0],
        shares[1],
        shares[2],
        shares[3],
        shares[4],
        shares[5],
        shares[6],
        shares[7],
        shares[8],
        shares[9],
        shares[10],
        shares[11],
        shares[12],
        shares[13],
        shares[14],
        shares[15],
        shares[16],
        shares[17],
    )


def solution(mesh):
    fits = mesh.shape["seq"] == 8 and mesh.shape["batch"] == 4
    return jax.shard_map(
        fast_body if fits else body,
        mesh=mesh,
        in_specs=(
            P("batch", "seq", None),
            P("batch", "seq"),
            P(BOTH, None),
            P(BOTH, None),
            P(BOTH, None),
            P(BOTH, None),
            P(BOTH, None),
            P(BOTH, None),
            P(BOTH, None),
            P(BOTH),
            P(BOTH),
            P(BOTH),
            P(BOTH),
            P(BOTH),
            P(BOTH),
            P(BOTH),
            P(BOTH),
            P(BOTH),
            P(BOTH),
            P(BOTH),
            P("batch", "seq", None),
        ),
        out_specs=(
            P("batch", "seq", None),
            P("batch", "seq", None),
            P(BOTH, None),
            P(BOTH, None),
            P(BOTH, None),
            P(BOTH, None),
            P(BOTH, None),
            P(BOTH, None),
            P(BOTH, None),
            P(BOTH),
            P(BOTH),
            P(BOTH),
            P(BOTH),
            P(BOTH),
            P(BOTH),
            P(BOTH),
            P(BOTH),
            P(BOTH),
            P(BOTH),
            P(BOTH),
        ),
        check_vma=False,
    )
```
